32 devices in a mesh: section: 4 (over y, x), dp: 8 (over z, core).
Axes of the slice: x: 2, y: 2, z: 4, core: 2. Of those that a mesh axis runs over, the one named last changes fastest.
Arguments:
- stream_in: bfloat16 [3, 2048, 1024], P(None, 'dp'), may hold values from -6 to 6
- segment_ids: int32 [3, 2048], replicated, may hold values from 0 to 7, as said below
- chosen_rows: int32 [3, 256], replicated, may hold values from 0 to 2047, as said below
- cotangent: bfloat16 [3, 2048, 1024], P(None, 'dp'), may hold values from -6 to 6
- dense_prenorm: bfloat16 [1024], P('dp'), may hold values from 0.5 to 1.5
- dense_query: bfloat16 [1024, 1024], P('dp'), may hold values from -0.1875 to 0.1875
- dense_keys: bfloat16 [1024, 1024], P('dp'), may hold values from -0.1875 to 0.1875
- dense_values: bfloat16 [1024, 1024], P('dp'), may hold values from -0.1875 to 0.1875
- dense_output: bfloat16 [1024, 1024], P('dp'), may hold values from -1 to 1
- dense_midnorm: bfloat16 [1024], P('dp'), may hold values from 0.5 to 1.5
- dense_expand: bfloat16 [1024, 4096], P('dp'), may hold values from -0.1875 to 0.1875
- dense_shrink: bfloat16 [4096, 1024], P('dp'), may hold values from -0.09375 to 0.09375
- routed_prenorm: bfloat16 [1024], P('dp'), may hold values from 0.5 to 1.5
- routed_query: bfloat16 [1024, 1024], P('dp'), may hold values from -0.1875 to 0.1875
- routed_keys: bfloat16 [1024, 1024], P('dp'), may hold values from -0.1875 to 0.1875
- routed_values: bfloat16 [1024, 1024], P('dp'), may hold values from -0.1875 to 0.1875
- routed_output: bfloat16 [1024, 1024], P('dp'), may hold values from -0.75 to 0.75
- routed_midnorm: bfloat16 [1024], P('dp'), may hold values from 0.5 to 1.5
- routed_expand: bfloat16 [1024, 4096], P('dp'), may hold values from -0.1875 to 0.1875
- routed_shrink: bfloat16 [4096, 1024], P('dp'), may hold values from -0.1875 to 0.1875
- router_weight: bfloat16 [1024], P('dp'), may hold values from -0.1875 to 0.1875
Outputs:
- stream_out: bfloat16 [3, 2048, 1024], P(None, 'dp', 'section')
- stream_grad: bfloat16 [3, 2048, 1024], P(None, 'dp', 'section')
- grad_dense_prenorm: float32 [1024], P('dp')
- grad_dense_query: float32 [1024, 1024], P('dp')
- grad_dense_keys: float32 [1024, 1024], P('dp')
- grad_dense_values: float32 [1024, 1024], P('dp')
- grad_dense_output: float32 [1024, 1024], P('dp')
- grad_dense_midnorm: float32 [1024], P('dp')
- grad_dense_expand: float32 [1024, 4096], P('dp')
- grad_dense_shrink: float32 [4096, 1024], P('dp')
- grad_routed_prenorm: float32 [1024], P('dp')
- grad_routed_query: float32 [1024, 1024], P('dp')
- grad_routed_keys: float32 [1024, 1024], P('dp')
- grad_routed_values: float32 [1024, 1024], P('dp')
- grad_routed_output: float32 [1024, 1024], P('dp')
- grad_routed_midnorm: float32 [1024], P('dp')
- grad_routed_expand: float32 [1024, 4096], P('dp')
- grad_routed_shrink: float32 [4096, 1024], P('dp')
- grad_router_weight: float32 [1024], P('dp')
The draws below stay inside these ranges and needn't reach their ends.
Inputs may be any that keep to these rules, and one draw needn't show every extreme that they name: `segment_ids`: within each sequence the ids start at 0 and never fall; one sequence, drawn from the seed, is a single document, each other one holds exactly 8 documents. `chosen_rows`: each sequence's 256 positions are distinct and ascending and include 0 and 2047.
All inputs are finite; a program needn't handle non-finite values.
Results may differ from the reference program's by a relative error of at most 0.035.
Values may be sent and summed in bfloat16 or wider, within the bound.
A program may use at most 320 MiB of HBM per device.

```python
import jax
import jax.numpy as jnp
from jax import lax

D = 1024
HEADS = 16
HDIM = 64
FF = 4096
DOCS = 8
SEQS = 3
LEN = 2048
SEL = 256


def draw_segment_ids(key, part):
    key = jax.random.fold_in(key, 11)
    whole_key, cut_key = jax.random.split(key)
    single = jax.random.randint(whole_key, (), 0, SEQS)

    def one(piece_key):
        marks = jax.random.permutation(piece_key, LEN - 1)[:DOCS - 1] + 1
        places = jnp.arange(LEN)
        return jnp.sum((places[:, None] >= marks[None, :]).astype(jnp.int32), axis=1)
    ids = jax.vmap(one)(jax.random.split(cut_key, SEQS))
    keep = jnp.arange(SEQS)[:, None] != single
    return jnp.where(keep, ids, 0).astype(jnp.int32)


def draw_chosen_rows(key, part):
    key = jax.random.fold_in(key, 23)

    def one(piece_key):
        inner = (jax.random.permutation(piece_key, LEN - 2)[:SEL - 2] + 1).astype(jnp.int32)
        rows = jnp.concatenate([jnp.zeros((1,), jnp.int32), inner, jnp.full((1,), LEN - 1, jnp.int32)])
        return jnp.sort(rows)
    return jax.vmap(one)(jax.random.split(key, SEQS)).astype(jnp.int32)


def level_of(rng, shape, pieces, low, largest):
    factor_of = 1.0
    for dim, shards_of in pieces:
        draws = jax.random.uniform(jax.random.fold_in(jax.random.fold_in(rng, 6), dim), (shards_of,), jnp.float32, low / len(pieces), largest / len(pieces))
        factor_of = factor_of * jnp.repeat(jnp.exp(draws), shape[dim] // shards_of).reshape((-1,) + (1,) * (len(shape) - 1 - dim))
    return factor_of


def centred(key, dims, scale, bound, cuts=(), held_as=jnp.bfloat16):
    level = level_of(key, dims, cuts, -0.22, 0.18) if cuts else 1.0
    entries = jax.random.normal(key, dims, jnp.float32) * scale * level
    return jnp.minimum(jnp.maximum(entries, -bound), bound).astype(held_as)


def setup_inputs(seed: int = 0) -> dict:
    seeds = jax.random.split(jax.random.key(seed), 22)
    stream_in = centred(seeds[0], (SEQS, LEN, D), 1.0, 6.0, ((1, 8),))
    segment_ids = draw_segment_ids(jax.random.fold_in(seeds[21], 71), 0)
    chosen_rows = draw_chosen_rows(jax.random.fold_in(seeds[21], 71), 0)
    cotangent = centred(seeds[3], (SEQS, LEN, D), 1.0, 6.0, ((1, 8),))
    dense_prenorm = jnp.clip(1.0 + 0.1 * jax.random.normal(seeds[4], (D,), jnp.float32), 0.5, 1.5).astype(jnp.bfloat16)
    dense_query = centred(seeds[5], (D, D), D ** -0.5, 0.1875, ((0, 8),))
    dense_keys = centred(seeds[6], (D, D), D ** -0.5, 0.1875, ((0, 8),))
    dense_values = centred(seeds[7], (D, D), D ** -0.5, 0.1875, ((0, 8),))
    dense_output = centred(seeds[8], (D, D), (max(1, D * 8 * DOCS // LEN)) ** -0.5, 1.0, ((0, 8),))
    dense_midnorm = jnp.clip(1.0 + 0.1 * jax.random.normal(seeds[9], (D,), jnp.float32), 0.5, 1.5).astype(jnp.bfloat16)
    dense_expand = centred(seeds[10], (D, FF), D ** -0.5, 0.1875, ((0, 8),))
    dense_shrink = centred(seeds[11], (FF, D), FF ** -0.5, 0.09375, ((0, 8),))
    routed_prenorm = jnp.clip(1.0 + 0.1 * jax.random.normal(seeds[12], (D,), jnp.float32), 0.5, 1.5).astype(jnp.bfloat16)
    routed_query = centred(seeds[13], (D, D), D ** -0.5, 0.1875, ((0, 8),))
    routed_keys = centred(seeds[14], (D, D), D ** -0.5, 0.1875, ((0, 8),))
    routed_values = centred(seeds[15], (D, D), D ** -0.5, 0.1875, ((0, 8),))
    routed_output = centred(seeds[16], (D, D), (max(1, D * 2 * DOCS // SEL)) ** -0.5, 0.75, ((0, 8),))
    routed_midnorm = jnp.clip(1.0 + 0.1 * jax.random.normal(seeds[17], (D,), jnp.float32), 0.5, 1.5).astype(jnp.bfloat16)
    routed_expand = centred(seeds[18], (D, FF), D ** -0.5, 0.1875, ((0, 8),))
    routed_shrink = centred(seeds[19], (FF, D), (FF // 4) ** -0.5, 0.1875, ((0, 8),))
    router_weight = centred(seeds[20], (D,), D ** -0.5, 0.1875, ((0, 8),))
    return {"stream_in": stream_in, "segment_ids": segment_ids, "chosen_rows": chosen_rows, "cotangent": cotangent, "dense_prenorm": dense_prenorm, "dense_query": dense_query, "dense_keys": dense_keys, "dense_values": dense_values, "dense_output": dense_output, "dense_midnorm": dense_midnorm, "dense_expand": dense_expand, "dense_shrink": dense_shrink, "routed_prenorm": routed_prenorm, "routed_query": routed_query, "routed_keys": routed_keys, "routed_values": routed_values, "routed_output": routed_output, "routed_midnorm": routed_midnorm, "routed_expand": routed_expand, "routed_shrink": routed_shrink, "router_weight": router_weight}


@jax.custom_vjp
def low(v):
    return lax.optimization_barrier(v.astype(jnp.bfloat16)).astype(jnp.float32)

@jax.custom_vjp
def low_back(v):
    return v

def low_keep(v):
    return (low(v), None)

def low_pass(kept, grad):
    return (grad,)

def back_keep(v):
    return (v, None)

def back_low(kept, grad):
    return (low(grad),)
low.defvjp(low_keep, low_pass)
low_back.defvjp(back_keep, back_low)
EPS = 1e-06
HIGH = lax.Precision.HIGHEST

def matmul(left, right):
    return jnp.dot(left, right, precision=HIGH)

def rms(value, gain):
    return value * lax.rsqrt(lax.optimization_barrier(jnp.mean(value * value, axis=-1, keepdims=True)) + EPS) * gain

def attention(q, k, v, qpos, kpos, qseg, kseg):
    rows = q.shape[0]
    size = min(512, rows)
    scale = HDIM ** (-0.5)
    key_heads = k.reshape(-1, HEADS, HDIM)
    value_heads = v.reshape(-1, HEADS, HDIM)

    def one(item):
        query_block, pos_block, seg_block = item
        scores = jnp.einsum('bhd,khd->hbk', query_block, key_heads, precision=HIGH) * scale
        scores = low_back(scores)
        allowed = (kpos[None, :] <= pos_block[:, None]) & (kseg[None, :] == seg_block[:, None])
        scores = jnp.where(allowed[None], scores, -1e+30)
        probs = low(jax.nn.softmax(scores, axis=-1))
        mixed = jnp.einsum('hbk,khd->bhd', probs, value_heads, precision=HIGH)
        return mixed.reshape(size, HEADS * HDIM)
    blocks = lax.map(jax.checkpoint(one), (q.reshape(rows // size, size, HEADS, HDIM), qpos.reshape(rows // size, size), qseg.reshape(rows // size, size)))
    return blocks.reshape(rows, HEADS * HDIM)

def branch(value, pos, seg, weights):
    prenorm, query, keys, values, output, midnorm, expand, shrink = weights
    normed = low(rms(value, prenorm))
    q = low_back(low(matmul(normed, query)))
    k = low_back(low(matmul(normed, keys)))
    v = low_back(low(matmul(normed, values)))
    mixed = low_back(low(attention(q, k, v, pos, pos, seg, seg)))
    attended = low_back(matmul(mixed, output))
    middle = value + attended
    normed_mid = low(rms(middle, midnorm))
    hidden_pre = low_back(matmul(normed_mid, expand))
    hidden = low(jax.nn.gelu(hidden_pre))
    fed = low_back(matmul(hidden, shrink))
    return (attended, middle, fed)

def sequence(value, seg, chosen, dense, routed, router):
    places = jnp.arange(LEN, dtype=jnp.int32)
    attended, middle, fed = branch(value, places, seg, dense)
    after_dense = middle + fed
    picked = low_back(after_dense[chosen])
    routed_attended, routed_middle, routed_fed = branch(picked, chosen, seg[chosen], routed)
    delta = routed_attended + routed_fed
    gate = jax.nn.sigmoid(matmul(picked, router))
    sent = low(gate[:, None] * delta)
    return after_dense.at[chosen].add(sent)

def reference(stream_in, segment_ids, chosen_rows, cotangent, dense_prenorm, dense_query, dense_keys, dense_values, dense_output, dense_midnorm, dense_expand, dense_shrink, routed_prenorm, routed_query, routed_keys, routed_values, routed_output, routed_midnorm, routed_expand, routed_shrink, router_weight):
    dense = tuple((w.astype(jnp.float32) for w in (dense_prenorm, dense_query, dense_keys, dense_values, dense_output, dense_midnorm, dense_expand, dense_shrink)))
    routed = tuple((w.astype(jnp.float32) for w in (routed_prenorm, routed_query, routed_keys, routed_values, routed_output, routed_midnorm, routed_expand, routed_shrink)))
    router = router_weight.astype(jnp.float32)
    streams = stream_in.astype(jnp.float32)
    grads_in = cotangent.astype(jnp.float32)

    def step(total, item):
        value, seg, chosen, grad_out = item

        def forward(v, dw, rw, gw):
            return sequence(v, seg, chosen, dw, rw, gw)
        result, pull = jax.vjp(forward, value, dense, routed, router)
        grad_value, grad_dense, grad_routed, grad_router = pull(grad_out)
        total = jax.tree.map(jnp.add, total, (grad_dense, grad_routed, grad_router))
        return (total, (result.astype(jnp.bfloat16), grad_value.astype(jnp.bfloat16)))
    zeros = jax.tree.map(jnp.zeros_like, (dense, routed, router))
    total, (results, grad_values) = lax.scan(step, zeros, (streams, segment_ids, chosen_rows, grads_in))
    gd, gr, gg = total
    return (results, grad_values, gd[0], gd[1], gd[2], gd[3], gd[4], gd[5], gd[6], gd[7], gr[0], gr[1], gr[2], gr[3], gr[4], gr[5], gr[6], gr[7], gg)
```

```python
import functools

import jax
import jax.numpy as jnp
from jax import lax
from jax.experimental import pallas as pl
from jax.experimental.pallas import tpu as pltpu
from jax.sharding import PartitionSpec as P

HEADS = 16
HDIM = 64
DOCS = 8
EPS = 1e-06
NEG = -1e30
SCALE = HDIM ** (-0.5)
VMEM = 56 * 2**20
MESH = pl.DeviceIdType.MESH
BF = jnp.bfloat16
F32 = jnp.float32


def matmul(left, right):
    return jnp.dot(left, right, preferred_element_type=F32)


def contract(left, right, ldim, rdim):
    return lax.dot_general(left, right, (((ldim,), (rdim,)), ((), ())), preferred_element_type=F32)


class Line:
    def __init__(self, kind, dp, group):
        self.axis = "section" if kind == "section" else "dp"
        self.kind = kind
        self.stride = dp // group
        self.size = {"section": lax.axis_size("section"), "dp": dp, "z": group, "core": dp // group}[kind]

    def place(self):
        index = lax.axis_index(self.axis)
        if self.kind == "z":
            return index // self.stride
        if self.kind == "core":
            return lax.rem(index, self.stride)
        return index

    def coordinate(self, place):
        index = lax.axis_index(self.axis)
        if self.kind == "z":
            return place * self.stride + lax.rem(index, self.stride)
        if self.kind == "core":
            return (index // self.stride) * self.stride + place
        return place


def exchange_kernel(line, plan, n_in, n_out, *refs):
    ins, outs = refs[:n_in], refs[n_in : n_in + n_out]
    send, recv, local = refs[n_in + n_out :]
    count = line.size
    me = line.place()
    barrier = pltpu.get_barrier_semaphore()
    peers = [lax.rem(me + step, count) for step in range(1, count)]
    for peer in peers:
        pl.semaphore_signal(
            barrier, inc=1, device_id={line.axis: line.coordinate(peer)}, device_id_type=MESH
        )
    pl.semaphore_wait(barrier, count - 1)
    copies = []
    for step, peer in enumerate(peers):
        for item, (i, src, o, dst) in enumerate(plan):
            copy = pltpu.make_async_remote_copy(
                src_ref=src(ins[i], peer),
                dst_ref=dst(outs[o], me),
                send_sem=send.at[step, item],
                recv_sem=recv.at[step, item],
                device_id={line.axis: line.coordinate(peer)},
                device_id_type=MESH,
            )
            copy.start()
            copies.append(copy)
    for item, (i, src, o, dst) in enumerate(plan):
        copy = pltpu.make_async_copy(src(ins[i], me), dst(outs[o], me), local.at[item])
        copy.start()
        copies.append(copy)
    for copy in copies:
        copy.wait()


class Exchanger:
    def __init__(self, dp, group):
        self.dp, self.group, self.next_id = dp, group, 1

    def __call__(self, kind, arrays, shapes, plan, name):
        line = Line(kind, self.dp, self.group)
        ident = self.next_id
        self.next_id += 1
        if line.size == 1:
            return list(arrays)
        items = len(plan)
        return pl.pallas_call(
            functools.partial(exchange_kernel, line, plan, len(arrays), len(shapes)),
            out_shape=[jax.ShapeDtypeStruct(s, d) for s, d in shapes],
            in_specs=[pl.BlockSpec(memory_space=pl.ANY)] * len(arrays),
            out_specs=[pl.BlockSpec(memory_space=pl.ANY)] * len(shapes),
            scratch_shapes=[
                pltpu.SemaphoreType.DMA((line.size - 1, items)),
                pltpu.SemaphoreType.DMA((line.size - 1, items)),
                pltpu.SemaphoreType.DMA((items,)),
            ],
            compiler_params=pltpu.CompilerParams(collective_id=ident, has_side_effects=True),
            name=name,
        )(*arrays)


def whole(ref, place):
    return ref


def slot(ref, place):
    return ref.at[place]


def columns(width):
    def view(ref, place):
        return ref.at[:, pl.ds(pl.multiple_of(place * width, width), width)]

    return view


def middle(width):
    def view(ref, place):
        return ref.at[:, pl.ds(pl.multiple_of(place * width, width), width), :]

    return view


def gather_columns(swap, parts, name):
    size = lax.axis_size("section")
    shapes = [((p.shape[0], size * p.shape[1]), p.dtype) for p in parts]
    plan = [(i, whole, i, columns(p.shape[1])) for i, p in enumerate(parts)]
    return swap("section", parts, shapes, plan, name)


def scatter_columns(swap, part, extra, name):
    size = lax.axis_size("section")
    width = part.shape[1] // size
    arrays = [part] + ([] if extra is None else [extra])
    shapes = [((size, part.shape[0], width), part.dtype)]
    plan = [(0, columns(width), 0, slot)]
    if extra is not None:
        shapes.append(((size,) + extra.shape, extra.dtype))
        plan.append((1, whole, 1, slot))
    got = swap("section", arrays, shapes, plan, name)
    total = jnp.sum(got[0].astype(F32), axis=0)
    if extra is None:
        return total
    return total, jnp.sum(got[1].astype(F32), axis=0)


def unpack_low(packed):
    lane = lax.broadcasted_iota(jnp.int32, packed.shape, 1)
    zero = jnp.zeros_like(packed)
    low = jnp.where(lane < HDIM, packed, zero)
    turned = jnp.concatenate([packed[:, HDIM:], packed[:, :HDIM]], axis=1)
    high = jnp.where(lane < HDIM, turned, zero)
    return jnp.concatenate([low, high], axis=0)


def unpack_high(packed):
    lane = lax.broadcasted_iota(jnp.int32, packed.shape, 1)
    zero = jnp.zeros_like(packed)
    turned = jnp.concatenate([packed[:, HDIM:], packed[:, :HDIM]], axis=1)
    low = jnp.where(lane >= HDIM, turned, zero)
    high = jnp.where(lane >= HDIM, packed, zero)
    return jnp.concatenate([low, high], axis=0)


def pack_turned(turned):
    half = turned.shape[1] // 2
    return jnp.concatenate([turned[:, :half], turned[:, half:]], axis=0).T


def forward_block(query, pieces, qpos, start, causal):
    scores = []
    peak = None
    for index, (pair, _, first) in enumerate(pieces):
        item = contract(pair, query, 1, 1)
        kpos = first + lax.broadcasted_iota(jnp.int32, item.shape, 0)
        allowed = kpos >= start
        if causal[index]:
            allowed = allowed & (kpos <= qpos)
        item = jnp.where(allowed, item, NEG)
        top = jnp.max(item, axis=0, keepdims=True)
        peak = top if peak is None else jnp.maximum(peak, top)
        scores.append(item)
    total = jnp.zeros_like(peak)
    mixed = None
    for item, (_, turned, _) in zip(scores, pieces):
        weight = jnp.exp(item - peak)
        total = total + jnp.sum(weight, axis=0, keepdims=True)
        part = matmul(turned[HDIM:], weight.astype(BF))
        mixed = part if mixed is None else mixed + part
    return mixed / total, peak + jnp.log(total)


def backward_block(query, grad, grad_turned, mixed_turned, lse, pieces, qpos, start, causal):
    row_sum = jnp.sum(grad_turned.astype(F32) * mixed_turned.astype(F32), axis=0, keepdims=True)
    grad_query = None
    grads = []
    for index, (pair, turned, first) in enumerate(pieces):
        scores = contract(pair, query, 1, 1)
        kpos = first + lax.broadcasted_iota(jnp.int32, scores.shape, 0)
        allowed = kpos >= start
        if causal[index]:
            allowed = allowed & (kpos <= qpos)
        probs = jnp.where(allowed, jnp.exp(scores - lse), 0.0)
        grad_probs = contract(pair, grad, 1, 1)
        grad_scores = (probs * (grad_probs - row_sum)).astype(BF)
        grads.append(matmul(grad_scores, query) + matmul(probs.astype(BF), grad))
        part = matmul(turned[:HDIM], grad_scores)
        grad_query = part if grad_query is None else grad_query + part
    return grad_query * SCALE, grads


def dense_forward_kernel(place_ref, q_ref, kv_ref, start_ref, out_ref, turned_ref, lse_ref):
    group, _, half, _ = q_ref.shape
    ring, _, _, block, _ = kv_ref.shape
    place = place_ref[0]
    span = ring * block
    pieces = []
    for g in range(group):
        pair = kv_ref[:, g, 0].reshape(span, 2 * HDIM)
        pieces.append((pair, pair.T, g * span))
    for g in range(group):
        query = unpack_low(q_ref[g, 0]) * jnp.asarray(SCALE, BF)
        qpos = g * span + place * block + lax.broadcasted_iota(jnp.int32, (1, block), 1)
        mixed, lse = forward_block(
            query, pieces[: g + 1], qpos, start_ref[0, g], [i == g for i in range(g + 1)]
        )
        turned_ref[0, g] = mixed.astype(BF)
        lse_ref[0, g] = lse
        out_ref[g, 0] = pack_turned(mixed).astype(BF)


def dense_forward(place, q, kv, start):
    group, seqs, half, lanes = q.shape
    ring, _, _, block, _ = kv.shape
    grid = pltpu.PrefetchScalarGridSpec(
        num_scalar_prefetch=1,
        grid=(seqs,),
        in_specs=[
            pl.BlockSpec((group, 1, half, lanes), lambda s, _: (0, s, 0, 0)),
            pl.BlockSpec((ring, group, 1, block, lanes), lambda s, _: (0, 0, s, 0, 0)),
            pl.BlockSpec((1, group, 1, block), lambda s, _: (s, 0, 0, 0)),
        ],
        out_specs=[
            pl.BlockSpec((group, 1, half, lanes), lambda s, _: (0, s, 0, 0)),
            pl.BlockSpec((1, group, HDIM, block), lambda s, _: (s, 0, 0, 0)),
            pl.BlockSpec((1, group, 1, block), lambda s, _: (s, 0, 0, 0)),
        ],
    )
    return pl.pallas_call(
        dense_forward_kernel,
        grid_spec=grid,
        out_shape=[
            jax.ShapeDtypeStruct(q.shape, BF),
            jax.ShapeDtypeStruct((seqs, group, HDIM, block), BF),
            jax.ShapeDtypeStruct((seqs, group, 1, block), F32),
        ],
        compiler_params=pltpu.CompilerParams(vmem_limit_bytes=VMEM),
        name="dense_attention",
    )(place, q, kv, start)


def dense_backward_kernel(
    place_ref, q_ref, g_ref, kv_ref, start_ref, turned_ref, lse_ref, dq_ref, dkv_ref, acc_ref
):
    group, _, half, _ = q_ref.shape
    ring, _, _, block, _ = kv_ref.shape
    place = place_ref[0]
    span = ring * block
    pieces = []
    for g in range(group):
        pair = kv_ref[:, g, 0].reshape(span, 2 * HDIM)
        pieces.append((pair, pair.T, g * span))
    for g in reversed(range(group)):
        query = unpack_low(q_ref[g, 0]) * jnp.asarray(SCALE, BF)
        packed = g_ref[g, 0]
        grad = unpack_high(packed)
        flat = packed.T
        grad_turned = jnp.concatenate([flat[:HDIM], flat[HDIM:]], axis=1)
        qpos = g * span + place * block + lax.broadcasted_iota(jnp.int32, (1, block), 1)
        grad_query, grads = backward_block(
            query,
            grad,
            grad_turned,
            turned_ref[0, g],
            lse_ref[0, g],
            pieces[: g + 1],
            qpos,
            start_ref[0, g],
            [i == g for i in range(g + 1)],
        )
        dq_ref[g, 0] = pack_turned(grad_query).astype(BF)
        for i, item in enumerate(grads):
            if g == group - 1:
                acc_ref[i] = item
            else:
                acc_ref[i] += item
    for g in range(group):
        dkv_ref[:, g, 0] = acc_ref[g].reshape(ring, block, 2 * HDIM).astype(BF)


def dense_backward(place, q, grad, kv, start, turned, lse):
    group, seqs, half, lanes = q.shape
    ring, _, _, block, _ = kv.shape
    grid = pltpu.PrefetchScalarGridSpec(
        num_scalar_prefetch=1,
        grid=(seqs,),
        in_specs=[
            pl.BlockSpec((group, 1, half, lanes), lambda s, _: (0, s, 0, 0)),
            pl.BlockSpec((group, 1, half, lanes), lambda s, _: (0, s, 0, 0)),
            pl.BlockSpec((ring, group, 1, block, lanes), lambda s, _: (0, 0, s, 0, 0)),
            pl.BlockSpec((1, group, 1, block), lambda s, _: (s, 0, 0, 0)),
            pl.BlockSpec((1, group, HDIM, block), lambda s, _: (s, 0, 0, 0)),
            pl.BlockSpec((1, group, 1, block), lambda s, _: (s, 0, 0, 0)),
        ],
        out_specs=[
            pl.BlockSpec((group, 1, half, lanes), lambda s, _: (0, s, 0, 0)),
            pl.BlockSpec((ring, group, 1, block, lanes), lambda s, _: (0, 0, s, 0, 0)),
        ],
        scratch_shapes=[pltpu.VMEM((group, ring * block, lanes), F32)],
    )
    return pl.pallas_call(
        dense_backward_kernel,
        grid_spec=grid,
        out_shape=[
            jax.ShapeDtypeStruct(q.shape, BF),
            jax.ShapeDtypeStruct(kv.shape, BF),
        ],
        compiler_params=pltpu.CompilerParams(vmem_limit_bytes=VMEM),
        name="dense_attention_grad",
    )(place, q, grad, kv, start, turned, lse)


def routed_parts(place, q_ref, kv_ref, s):
    group, _, block, lanes = q_ref.shape
    ring = kv_ref.shape[0]
    span = ring * block
    query = jnp.concatenate([q_ref[g, s] for g in range(group)], axis=0)
    pair = jnp.concatenate([kv_ref[:, g, s].reshape(span, lanes) for g in range(group)], axis=0)
    index = lax.broadcasted_iota(jnp.int32, (1, group * block), 1)
    slots = (index // block) * span + place * block + lax.rem(index, block)
    return query, pair, slots


def routed_forward_kernel(place_ref, q_ref, kv_ref, start_ref, out_ref, turned_ref, lse_ref):
    group, seqs, block, lanes = q_ref.shape
    for s in range(seqs):
        query, pair, slots = routed_parts(place_ref[0], q_ref, kv_ref, s)
        query = query * jnp.asarray(SCALE, BF)
        mixed, lse = forward_block(query, [(pair, pair.T, 0)], slots, start_ref[s], [True])
        turned_ref[s] = mixed.astype(BF)
        lse_ref[s] = lse
        padded = jnp.concatenate([jnp.zeros_like(mixed), mixed], axis=0).T.astype(BF)
        for g in range(group):
            out_ref[g, s] = padded[g * block : (g + 1) * block]


def routed_forward(place, q, kv, start):
    group, seqs, block, lanes = q.shape
    queries = group * block
    vmem = pl.BlockSpec(memory_space=pltpu.VMEM)
    return pl.pallas_call(
        routed_forward_kernel,
        in_specs=[pl.BlockSpec(memory_space=pltpu.SMEM)] + [vmem] * 3,
        out_specs=[vmem] * 3,
        out_shape=[
            jax.ShapeDtypeStruct(q.shape, BF),
            jax.ShapeDtypeStruct((seqs, HDIM, queries), BF),
            jax.ShapeDtypeStruct((seqs, 1, queries), F32),
        ],
        compiler_params=pltpu.CompilerParams(vmem_limit_bytes=VMEM),
        name="routed_attention",
    )(place, q, kv, start)


def routed_backward_kernel(
    place_ref, q_ref, g_ref, kv_ref, start_ref, turned_ref, lse_ref, dq_ref, dkv_ref
):
    group, seqs, block, lanes = q_ref.shape
    ring = kv_ref.shape[0]
    span = ring * block
    for s in range(seqs):
        query, pair, slots = routed_parts(place_ref[0], q_ref, kv_ref, s)
        query = query * jnp.asarray(SCALE, BF)
        grad = jnp.concatenate([g_ref[g, s] for g in range(group)], axis=0)
        grad_query, grads = backward_block(
            query,
            grad,
            grad.T[HDIM:],
            turned_ref[s],
            lse_ref[s],
            [(pair, pair.T, 0)],
            slots,
            start_ref[s],
            [True],
        )
        padded = jnp.concatenate([grad_query, jnp.zeros_like(grad_query)], axis=0).T.astype(BF)
        for g in range(group):
            dq_ref[g, s] = padded[g * block : (g + 1) * block]
            dkv_ref[:, g, s] = (
                grads[0][g * span : (g + 1) * span].reshape(ring, block, lanes).astype(BF)
            )


def routed_backward(place, q, grad, kv, start, turned, lse):
    vmem = pl.BlockSpec(memory_space=pltpu.VMEM)
    return pl.pallas_call(
        routed_backward_kernel,
        in_specs=[pl.BlockSpec(memory_space=pltpu.SMEM)] + [vmem] * 6,
        out_specs=[vmem] * 2,
        out_shape=[
            jax.ShapeDtypeStruct(q.shape, BF),
            jax.ShapeDtypeStruct(kv.shape, BF),
        ],
        compiler_params=pltpu.CompilerParams(vmem_limit_bytes=VMEM),
        name="routed_attention_grad",
    )(place, q, grad, kv, start, turned, lse)


def inverse_rms(value):
    return lax.rsqrt(jnp.mean(value * value, axis=-1, keepdims=True) + EPS)


def row_scalars(values, width):
    rows = values.reshape(-1, width) if values.shape[0] >= width else jnp.pad(values, (0, width - values.shape[0]))[None]
    high = rows.astype(BF)
    low = (rows - high.astype(F32)).astype(BF)
    both = jnp.concatenate([high, low], axis=0)
    return jnp.pad(both, ((0, -both.shape[0] % 16), (0, 0)))


def read_scalars(rows, count):
    width = rows.shape[1]
    used = max(1, count // width)
    return (rows[:used] + rows[used : 2 * used]).reshape(-1)[:count]


def on_device(
    stream_in,
    segment_ids,
    chosen_rows,
    cotangent,
    dense_prenorm,
    dense_query,
    dense_keys,
    dense_values,
    dense_output,
    dense_midnorm,
    dense_expand,
    dense_shrink,
    routed_prenorm,
    routed_query,
    routed_keys,
    routed_values,
    routed_output,
    routed_midnorm,
    routed_expand,
    routed_shrink,
    router_weight,
):
    sections, dp = lax.axis_size("section"), lax.axis_size("dp")
    section, rank = lax.axis_index("section"), lax.axis_index("dp")
    seqs, rows, width = stream_in.shape
    tokens = seqs * rows
    part = width // sections
    group = HEADS // sections
    ring = dp // group
    total_sel = chosen_rows.shape[1]
    sel = total_sel // dp
    slots = seqs * sel
    place = lax.rem(rank, ring).astype(jnp.int32).reshape(1)
    swap = Exchanger(dp, group)

    def own_columns(value):
        return lax.dynamic_slice_in_dim(value, section * part, part, value.ndim - 1)

    def own_hidden(expand, shrink):
        inner = expand.shape[1] // dp
        share = inner // sections
        cut = expand.reshape(expand.shape[0], dp, sections, share)
        cut = lax.dynamic_index_in_dim(cut, section, 2, keepdims=False).reshape(expand.shape[0], dp * share)
        return cut, lax.dynamic_slice_in_dim(shrink, section * share, share, 0)

    def own_attention(query, keys, values):
        local = query.shape[0]
        pair = jnp.stack(
            [own_columns(keys).reshape(local, group, HDIM), own_columns(values).reshape(local, group, HDIM)],
            axis=2,
        ).reshape(local, 2 * part)
        return jnp.concatenate([pair, own_columns(query)], axis=1)

    def gather(value):
        return lax.all_gather(value, "dp", axis=0, tiled=True)

    def layer_weights(query, keys, values, output, expand, shrink):
        expand_cut, shrink_cut = own_hidden(expand, shrink)
        qkv = gather(own_attention(query, keys, values))
        out = gather(own_columns(output))
        return qkv, out, gather(expand_cut), gather(shrink_cut)

    dense = layer_weights(dense_query, dense_keys, dense_values, dense_output, dense_expand, dense_shrink)
    routed = layer_weights(
        routed_query, routed_keys, routed_values, routed_output, routed_expand, routed_shrink
    )
    gains = jnp.stack([dense_prenorm, dense_midnorm, routed_prenorm, routed_midnorm, router_weight])
    gains = jnp.pad(gains, ((0, 16 - gains.shape[0]), (0, 0)))
    (gains,) = swap("dp", [gains], [((dp,) + gains.shape, BF)], [(0, whole, 0, slot)], "gains")
    gains = jnp.transpose(gains, (1, 0, 2)).reshape(16, width).astype(F32)
    gain_pre, gain_mid, routed_pre, routed_mid, router = [gains[i] for i in range(5)]

    first_of = jnp.sum(
        (segment_ids[:, None, :] < jnp.arange(DOCS, dtype=jnp.int32)[None, :, None]).astype(jnp.int32), axis=2
    )

    def document(positions):
        shape = (seqs,) + (1,) * (positions.ndim - 1)
        found = jnp.zeros(positions.shape, jnp.int32)
        for c in range(1, DOCS):
            found = found + (positions >= first_of[:, c].reshape(shape)).astype(jnp.int32)
        return found

    def pick(table, index):
        shape = (seqs,) + (1,) * (index.ndim - 1)
        out = jnp.zeros(index.shape, jnp.int32)
        for c in range(DOCS):
            out = jnp.where(index == c, table[:, c].reshape(shape), out)
        return out

    blocks = jnp.arange(group, dtype=jnp.int32) * ring + place[0]
    attended_pos = blocks[:, None] * rows + jnp.arange(rows, dtype=jnp.int32)[None, :]
    attended_pos = jnp.broadcast_to(attended_pos[None], (seqs, group, rows))
    start = pick(first_of, document(attended_pos))[:, :, None, :]
    chosen_doc = document(chosen_rows)
    first_slot = jnp.sum(
        (chosen_doc[:, None, :] < jnp.arange(DOCS, dtype=jnp.int32)[None, :, None]).astype(jnp.int32), axis=2
    )
    chosen_start = pick(first_slot, chosen_doc).reshape(seqs, group, ring, sel)
    routed_start = lax.dynamic_index_in_dim(chosen_start, place[0], 2, keepdims=False)
    routed_start = routed_start.reshape(seqs, 1, group * sel)

    def pack(value):
        value = value.reshape(seqs, 2, rows // 2, group, HDIM)
        return jnp.transpose(value, (0, 2, 3, 1, 4)).reshape(tokens // 2, 2 * part)

    def unpack(value):
        value = value.reshape(seqs, rows // 2, group, 2, HDIM)
        return jnp.transpose(value, (0, 3, 1, 2, 4)).reshape(tokens, part)

    lanes = 2 * HDIM

    def to_heads(arrays, name):
        shapes = [((group, a.shape[0], lanes), a.dtype) for a in arrays]
        plan = [(i, columns(lanes), i, slot) for i in range(len(arrays))]
        return swap("z", arrays, shapes, plan, name)

    def from_heads(arrays, name):
        shapes = [((a.shape[1], group * lanes), a.dtype) for a in arrays]
        plan = [(i, slot, i, columns(lanes)) for i in range(len(arrays))]
        return swap("z", arrays, shapes, plan, name)

    def share_pairs(kv, name):
        if ring == 1:
            return kv[None]
        (kv,) = swap("core", [kv], [((ring,) + kv.shape, kv.dtype)], [(0, whole, 0, slot)], name)
        return kv

    def sum_pairs(kv, name):
        if ring == 1:
            return kv[0]
        (kv,) = swap("core", [kv], [(kv.shape, kv.dtype)], [(0, slot, 0, slot)], name)
        return jnp.sum(kv.astype(F32), axis=0).astype(BF)

    value = stream_in.reshape(tokens, width).astype(F32)
    grad_top = cotangent.reshape(tokens, width)
    inv_in = inverse_rms(value)
    normed = (value * inv_in * gain_pre).astype(BF)
    qkv = matmul(normed, dense[0]).astype(BF)
    pairs, queries = qkv[:, : 2 * part], pack(qkv[:, 2 * part :])
    pairs, queries = to_heads([pairs, queries], "dense_to_heads")
    queries = queries.reshape(group, seqs, rows // 2, lanes)
    pairs = share_pairs(pairs, "dense_pairs").reshape(ring, group, seqs, rows, lanes)
    mixed, mixed_turned, lse = dense_forward(place, queries, pairs, start)
    (mixed,) = from_heads([mixed.reshape(group, tokens // 2, lanes)], "dense_mixed")
    mixed = unpack(mixed)
    (mixed,) = gather_columns(swap, [mixed], "dense_mixed_columns")
    attended = matmul(mixed, dense[1]).astype(BF)
    (attended,) = gather_columns(swap, [attended], "dense_attended")
    middle_value = value + attended.astype(F32)
    inv_mid = inverse_rms(middle_value)
    normed_mid = (middle_value * inv_mid * gain_mid).astype(BF)
    hidden_pre = matmul(normed_mid, dense[2])
    hidden = jax.nn.gelu(hidden_pre).astype(BF)
    fed = scatter_columns(swap, matmul(hidden, dense[3]).astype(BF), None, "dense_fed")
    middle_own = own_columns(middle_value)
    after_dense = middle_own + fed

    qpos = rank * rows + jnp.arange(rows, dtype=jnp.int32)
    table = (chosen_rows[:, :, None] == qpos[None, None, :]).astype(BF)

    def take_rows(source, name):
        picked = jnp.einsum(
            "skt,stc->skc", table, source.reshape(seqs, rows, part), preferred_element_type=F32
        ).astype(BF)
        (got,) = swap(
            "dp", [picked], [((dp, seqs, sel, part), BF)], [(0, middle(sel), 0, slot)], name + "_slots"
        )
        got = jnp.sum(got.astype(F32), axis=0).astype(BF).reshape(slots, part)
        (got,) = gather_columns(swap, [got], name + "_columns")
        return got

    grad_sent = take_rows(own_columns(grad_top), "grad_rows").astype(F32)
    picked = take_rows(after_dense.astype(BF), "value_rows").astype(F32)

    def routed_to_heads(arrays, name):
        return [a.reshape(group, seqs, sel, lanes) for a in to_heads(arrays, name)]

    def spread(value, side):
        value = value.reshape(slots, group, HDIM)
        zero = jnp.zeros_like(value)
        both = [value, zero] if side == 0 else [zero, value]
        return jnp.stack(both, axis=2).reshape(slots, 2 * part)

    def narrow(value, side):
        return value.reshape(slots, group, 2, HDIM)[:, :, side].reshape(slots, part)

    r_inv_in = inverse_rms(picked)
    r_normed = (picked * r_inv_in * routed_pre).astype(BF)
    r_qkv = matmul(r_normed, routed[0]).astype(BF)
    r_pairs, r_queries = routed_to_heads(
        [r_qkv[:, : 2 * part], spread(r_qkv[:, 2 * part :], 0)], "routed_to_heads"
    )
    r_pairs = share_pairs(r_pairs, "routed_pairs")
    r_mixed, r_turned, r_lse = routed_forward(place, r_queries, r_pairs, routed_start)
    (r_mixed,) = from_heads([r_mixed.reshape(group, slots, lanes)], "routed_mixed")
    (r_mixed,) = gather_columns(swap, [narrow(r_mixed, 1)], "routed_mixed_columns")
    r_attended_own = matmul(r_mixed, routed[1])
    (r_attended,) = gather_columns(swap, [r_attended_own.astype(BF)], "routed_attended")
    r_middle = picked + r_attended.astype(F32)
    r_inv_mid = inverse_rms(r_middle)
    r_normed_mid = (r_middle * r_inv_mid * routed_mid).astype(BF)
    r_hidden_pre = matmul(r_normed_mid, routed[2])
    r_hidden = jax.nn.gelu(r_hidden_pre).astype(BF)
    gate = jax.nn.sigmoid(jnp.sum(picked * router, axis=1))
    r_fed_part = matmul(r_hidden, routed[3])
    own_attended_part = jnp.sum(own_columns(grad_sent) * r_attended_own, axis=1)
    gate_part = jnp.sum(grad_sent * r_fed_part, axis=1) + own_attended_part
    r_fed, gate_rows = scatter_columns(swap, r_fed_part.astype(BF), row_scalars(gate_part, part), "routed_fed")
    delta_own = r_attended_own + r_fed
    sent_own = (gate[:, None] * delta_own).astype(BF)
    grad_gate = read_scalars(gate_rows, slots)
    grad_logit = grad_gate * gate * (1.0 - gate)
    grad_delta = gate[:, None] * grad_sent
    grad_router = jnp.sum(grad_logit[:, None] * own_columns(picked), axis=0)

    def back_out(kept, weights, gain, grad_fed, extra_middle, extra_attended, names):
        mixed_all, middle_all, inv, normed_all, pre, hid = kept
        count = middle_all.shape[0]
        fed_low = grad_fed.astype(BF)
        grad_shrink = contract(hid, fed_low, 0, 0).astype(BF)
        grad_hidden = contract(fed_low, weights[3], 1, 1)
        _, gelu_pull = jax.vjp(jax.nn.gelu, pre)
        grad_pre = gelu_pull(grad_hidden)[0].astype(BF)
        grad_expand = contract(normed_all, grad_pre, 0, 0).astype(BF)
        grad_normed = contract(grad_pre, weights[2], 1, 1)
        scalar = jnp.sum(grad_normed * middle_all * gain, axis=1)
        grad_normed, scalar = scatter_columns(
            swap, grad_normed.astype(BF), row_scalars(scalar, part), names[0]
        )
        scalar = read_scalars(scalar, count)[:, None] * (1.0 / width)
        own = own_columns(middle_all)
        grad_gain = jnp.sum(grad_normed * own * inv, axis=0)
        grad_middle = inv * (grad_normed * own_columns(gain)) - own * (inv * inv * inv) * scalar
        grad_middle = grad_middle + extra_middle
        grad_attended = (grad_middle + extra_attended).astype(BF)
        grad_output = contract(mixed_all, grad_attended, 0, 0).astype(BF)
        grad_mixed = contract(grad_attended, weights[1], 1, 1).astype(BF)
        grad_mixed = scatter_columns(swap, grad_mixed, None, names[1]).astype(BF)
        return grad_middle, grad_mixed, (grad_output, grad_gain, grad_expand, grad_shrink)

    def back_in(value_all, inv, normed_all, weights, gain, grad_qkv, name):
        count = value_all.shape[0]
        grad_weights = contract(normed_all, grad_qkv, 0, 0).astype(BF)
        grad_normed = contract(grad_qkv, weights[0], 1, 1)
        scalar = jnp.sum(grad_normed * value_all * gain, axis=1)
        grad_normed, scalar = scatter_columns(swap, grad_normed.astype(BF), row_scalars(scalar, part), name)
        scalar = read_scalars(scalar, count)[:, None] * (1.0 / width)
        own = own_columns(value_all)
        grad_gain = jnp.sum(grad_normed * own * inv, axis=0)
        grad_value = inv * (grad_normed * own_columns(gain)) - own * (inv * inv * inv) * scalar
        return grad_value, grad_gain, grad_weights

    def reduce_dp(value):
        return lax.psum_scatter(value, "dp", scatter_dimension=0, tiled=True)

    own_grad_delta = own_columns(grad_delta)
    r_grad_middle, r_grad_mixed, r_outer = back_out(
        (r_mixed, r_middle, r_inv_mid, r_normed_mid, r_hidden_pre, r_hidden),
        routed,
        routed_mid,
        grad_delta,
        0.0,
        own_grad_delta,
        ("routed_back_mid", "routed_back_mixed"),
    )
    (r_grad_heads,) = routed_to_heads([spread(r_grad_mixed, 1)], "routed_grad_to_heads")
    r_dq, r_dkv = routed_backward(
        place, r_queries, r_grad_heads, r_pairs, routed_start, r_turned, r_lse
    )
    r_dkv = sum_pairs(r_dkv, "routed_pair_grads")
    r_dq, r_dkv = from_heads(
        [r_dq.reshape(group, slots, lanes), r_dkv.reshape(group, slots, lanes)], "routed_grad_tokens"
    )
    r_grad_qkv = jnp.concatenate([r_dkv, narrow(r_dq, 0)], axis=1)
    r_grad_in, r_grad_pre, r_grad_qkv_w = back_in(
        picked, r_inv_in, r_normed, routed, routed_pre, r_grad_qkv, "routed_back_in"
    )
    grad_chosen = (r_grad_middle + r_grad_in + grad_logit[:, None] * own_columns(router)).astype(BF)

    def to_positions(value, name):
        cols = value.shape[1]
        (got,) = swap(
            "z",
            [value.reshape(seqs, sel, cols)],
            [((group, seqs, sel, cols), BF)],
            [(0, whole, 0, slot)],
            name + "_z",
        )
        got = share_pairs(got, name + "_core").reshape(ring, group, seqs, sel, cols)
        got = jnp.transpose(got, (2, 1, 0, 3, 4)).reshape(seqs, total_sel, cols)
        return jnp.einsum("skt,skc->stc", table, got, preferred_element_type=F32).reshape(tokens, cols)

    (grad_chosen_all,) = gather_columns(swap, [grad_chosen], "grad_chosen_columns")
    returned = to_positions(grad_chosen_all, "grad_chosen")
    added = to_positions(sent_own, "sent")
    stream_out = (after_dense + added).astype(BF).reshape(seqs, rows, part)

    grad_after = grad_top.astype(F32) + returned
    grad_middle, grad_mixed, outer = back_out(
        (mixed, middle_value, inv_mid, normed_mid, hidden_pre, hidden),
        dense,
        gain_mid,
        grad_after,
        own_columns(grad_after),
        0.0,
        ("dense_back_mid", "dense_back_mixed"),
    )
    (grad_heads,) = to_heads([pack(grad_mixed)], "dense_grad_to_heads")
    dq, dkv = dense_backward(
        place,
        queries,
        grad_heads.reshape(group, seqs, rows // 2, lanes),
        pairs,
        start,
        mixed_turned,
        lse,
    )
    dkv = sum_pairs(dkv, "dense_pair_grads")
    dq, dkv = from_heads(
        [dq.reshape(group, tokens // 2, lanes), dkv.reshape(group, tokens, lanes)], "dense_grad_tokens"
    )
    grad_qkv = jnp.concatenate([dkv, unpack(dq)], axis=1)
    grad_in, grad_pre, grad_qkv_w = back_in(
        value, inv_in, normed, dense, gain_pre, grad_qkv, "dense_back_in"
    )
    stream_grad = (grad_middle + grad_in).astype(BF).reshape(seqs, rows, part)

    def finish(grad_qkv_weight, outer_grads, name):
        grad_output, _, grad_expand, grad_shrink = outer_grads
        shards = [reduce_dp(g) for g in (grad_qkv_weight, grad_output, grad_expand, grad_shrink)]
        got_qkv, got_out, got_expand, got_shrink = swap(
            "section",
            shards,
            [
                ((sections,) + shards[0].shape, BF),
                ((shards[1].shape[0], width), BF),
                ((sections,) + shards[2].shape, BF),
                ((sections,) + shards[3].shape, BF),
            ],
            [(0, whole, 0, slot), (1, whole, 1, columns(part)), (2, whole, 2, slot), (3, whole, 3, slot)],
            name,
        )
        local = got_qkv.shape[1]
        pair = got_qkv[:, :, : 2 * part].reshape(sections, local, group, 2, HDIM)
        keys = jnp.transpose(pair[:, :, :, 0], (1, 0, 2, 3)).reshape(local, width).astype(F32)
        values = jnp.transpose(pair[:, :, :, 1], (1, 0, 2, 3)).reshape(local, width).astype(F32)
        query = jnp.transpose(got_qkv[:, :, 2 * part :], (1, 0, 2)).reshape(local, width).astype(F32)
        share = got_shrink.shape[1]
        expand = got_expand.reshape(sections, local, dp, share)
        expand = jnp.transpose(expand, (1, 2, 0, 3)).reshape(local, sections * dp * share).astype(F32)
        shrink = got_shrink.reshape(sections * share, width).astype(F32)
        return query, keys, values, got_out.astype(F32), expand, shrink

    routed_grads = finish(r_grad_qkv_w, r_outer, "routed_weight_grads")
    dense_grads = finish(grad_qkv_w, outer, "dense_weight_grads")

    vectors = jnp.stack([grad_pre, outer[1], r_grad_pre, r_outer[1], grad_router])
    vectors = jnp.pad(vectors, ((0, 8 - vectors.shape[0]), (0, 0)))
    (vectors,) = gather_columns(swap, [vectors], "vector_columns")
    vectors = jnp.transpose(vectors.reshape(8, dp, width // dp), (1, 0, 2))
    (vectors,) = swap("dp", [vectors], [(vectors.shape, F32)], [(0, slot, 0, slot)], "vector_shards")
    vectors = jnp.sum(vectors, axis=0)
    return (
        stream_out,
        stream_grad,
        vectors[0],
        dense_grads[0],
        dense_grads[1],
        dense_grads[2],
        dense_grads[3],
        vectors[1],
        dense_grads[4],
        dense_grads[5],
        vectors[2],
        routed_grads[0],
        routed_grads[1],
        routed_grads[2],
        routed_grads[3],
        vectors[3],
        routed_grads[4],
        routed_grads[5],
        vectors[4],
    )


def solution(mesh):
    streams, row, vector, copied = P(None, "dp", None), P("dp", None), P("dp"), P()
    layer = (vector, row, row, row, row, vector, row, row)
    outs = (P(None, "dp", "section"),) * 2 + layer + layer + (vector,)
    return jax.shard_map(
        on_device,
        mesh=mesh,
        in_specs=(streams, copied, copied, streams) + layer + layer + (vector,),
        out_specs=outs,
        check_vma=False,
    )
```

```python
import functools

import jax
import jax.numpy as jnp
from jax import lax
from jax.experimental import pallas as pl
from jax.experimental.pallas import tpu as pltpu
from jax.sharding import PartitionSpec as P

HEADS = 16
HDIM = 64
DOCS = 8
EPS = 1e-06
NEG = -1e30
SCALE = HDIM ** (-0.5)
VMEM = 32 * 2**20
MESH = pl.DeviceIdType.MESH
BF = jnp.bfloat16
F32 = jnp.float32


def matmul(left, right):
    return jnp.dot(left, right, preferred_element_type=F32)


def contract(left, right, ldim, rdim):
    return lax.dot_general(left, right, (((ldim,), (rdim,)), ((), ())), preferred_element_type=F32)


class Lines:
    def __init__(self, sections, dp, group):
        self.sizes = {"section": sections, "z": group, "core": dp // group}
        self.ring = dp // group

    def place(self, kind):
        if kind == "section":
            return lax.axis_index("section")
        index = lax.axis_index("dp")
        return index // self.ring if kind == "z" else lax.rem(index, self.ring)

    def device(self, kind, place):
        if kind == "section":
            return {"section": place}
        index = lax.axis_index("dp")
        if kind == "z":
            return {"dp": place * self.ring + lax.rem(index, self.ring)}
        return {"dp": (index // self.ring) * self.ring + place}

    def peers(self, kind):
        size = self.sizes[kind]
        me = self.place(kind)
        return [lax.rem(me + step, size) for step in range(1, size)]


class Copies:
    def __init__(self, lines, send, recv):
        self.lines, self.send, self.recv, self.used = lines, send, recv, 0

    def greet(self, kinds):
        barrier = pltpu.get_barrier_semaphore()
        count = 0
        for kind in kinds:
            for peer in self.lines.peers(kind):
                pl.semaphore_signal(
                    barrier, inc=1, device_id=self.lines.device(kind, peer), device_id_type=MESH
                )
                count += 1
        pl.semaphore_wait(barrier, count)

    def start(self, kind, peer, src, dst):
        copy = pltpu.make_async_remote_copy(
            src_ref=src,
            dst_ref=dst,
            send_sem=self.send.at[self.used],
            recv_sem=self.recv.at[self.used],
            device_id=self.lines.device(kind, peer),
            device_id_type=MESH,
        )
        self.used += 1
        copy.start()
        return copy

    def swap(self, kind, src, dst):
        me = self.lines.place(kind)
        return [self.start(kind, peer, src(peer), dst(me)) for peer in self.lines.peers(kind)]


def wait(copies):
    for copy in copies:
        copy.wait()


def semaphores(count):
    return [pltpu.SemaphoreType.DMA((count,)), pltpu.SemaphoreType.DMA((count,))]


def communicate(kernel, ident, arrays, shapes, scratch, name, limit=24 * 2**20):
    vmem = pl.BlockSpec(memory_space=pltpu.VMEM)
    return pl.pallas_call(
        kernel,
        out_shape=[jax.ShapeDtypeStruct(s, d) for s, d in shapes],
        in_specs=[vmem] * len(arrays),
        out_specs=[vmem] * len(shapes),
        scratch_shapes=scratch,
        compiler_params=pltpu.CompilerParams(
            collective_id=ident, has_side_effects=True, vmem_limit_bytes=limit
        ),
        name=name,
    )(*arrays)


def span(place, width):
    return pl.ds(pl.multiple_of(place * width, width), width)


def square(lines):
    me = lines.place("section")
    low, high = lax.rem(me, 2), me // 2
    return high * 2 + 1 - low, (1 - high) * 2 + low, (1 - high) * 2 + 1 - low


def gather_columns(lines, ident, part, name):
    rows, width = part.shape
    half = rows // 2
    pieces = 2 if half % 32 == 0 else 1
    step = half // pieces

    def kernel(x_ref, o_ref, send, recv):
        copies = Copies(lines, send, recv)
        me = lines.place("section")
        near, far, _ = square(lines)
        copies.greet(["section"])
        first, rest = [], []
        for j in range(pieces):
            for h, (one, two) in enumerate(((near, far), (far, near))):
                at = pl.ds(h * half + j * step, step)
                first.append(copies.start("section", one, x_ref.at[at], o_ref.at[at, span(me, width)]))
        for j in range(pieces):
            for h, (one, two) in enumerate(((near, far), (far, near))):
                at = pl.ds(h * half + j * step, step)
                rest.append(copies.start("section", two, x_ref.at[at], o_ref.at[at, span(me, width)]))
        o_ref[:, span(me, width)] = x_ref[...]
        for j in range(pieces):
            for h, (one, two) in enumerate(((near, far), (far, near))):
                at = pl.ds(h * half + j * step, step)
                first[2 * j + h].wait_recv()
                place = o_ref.at[at, span(one, width)]
                rest.append(copies.start("section", two, place, place))
        for copy in first:
            copy.wait_send()
        wait(rest)

    (out,) = communicate(
        kernel, ident, [part], [((rows, lines.sizes["section"] * width), part.dtype)], semaphores(6 * pieces), name
    )
    return out


def scatter_columns(lines, ident, part, scalars, name):
    rows, full = part.shape
    sections = lines.sizes["section"]
    width = full // sections
    half = rows // 2
    pieces = 2 if half % 32 == 0 else 1
    step = half // pieces
    extra = scalars is not None
    arrays = [part]
    shapes = [((rows, width), F32)]
    scratch = semaphores(6 * pieces + 3) + [
        pltpu.VMEM((2, rows, width), part.dtype),
        pltpu.VMEM((rows, width), part.dtype),
        pltpu.VMEM((rows, width), part.dtype),
    ]
    if extra:
        lines_of = -(-rows // 128)
        padded = lines_of + -lines_of % 8
        block = jnp.pad(scalars, (0, padded * 128 - rows)).reshape(padded, 128)
        arrays.append(block)
        shapes.append((block.shape, F32))
        scratch.append(pltpu.VMEM((sections,) + block.shape, F32))

    def kernel(*refs):
        x_ref, refs = refs[0], refs[1:]
        if extra:
            e_ref, o_ref, eo_ref, send, recv, got, turn, last, e_got = refs
        else:
            o_ref, send, recv, got, turn, last = refs
        copies = Copies(lines, send, recv)
        me = lines.place("section")
        near, far, across = square(lines)
        copies.greet(["section"])
        first, second, others = [], [], []
        ways = ((near, far), (far, near))
        for j in range(pieces):
            for h, (one, two) in enumerate(ways):
                at = pl.ds(h * half + j * step, step)
                first.append(copies.start("section", one, x_ref.at[at, span(across, width)], got.at[0, at]))
                first.append(copies.start("section", one, x_ref.at[at, span(one, width)], got.at[1, at]))
        if extra:
            others = copies.swap("section", lambda peer: e_ref, lambda place: e_got.at[place])
        for j in range(pieces):
            for h, (one, two) in enumerate(ways):
                at = pl.ds(h * half + j * step, step)
                first[4 * j + 2 * h].wait_recv()
                turn[at] = (x_ref[at, span(two, width)].astype(F32) + got[0, at].astype(F32)).astype(part.dtype)
                second.append(copies.start("section", two, turn.at[at], last.at[at]))
        for j in range(pieces):
            for h in range(2):
                at = pl.ds(h * half + j * step, step)
                first[4 * j + 2 * h + 1].wait_recv()
                second[2 * j + h].wait_recv()
                o_ref[at] = (
                    x_ref[at, span(me, width)].astype(F32) + got[1, at].astype(F32) + last[at].astype(F32)
                )
        for copy in first + second:
            copy.wait_send()
        if extra:
            wait(others)
            e_got[me] = e_ref[...]
            total = e_got[0]
            for i in range(1, sections):
                total = total + e_got[i]
            eo_ref[...] = total

    got = communicate(kernel, ident, arrays, shapes, scratch, name)
    if not extra:
        return got[0]
    return got[0], got[1].reshape(-1)[:rows]


def gather_rows(lines, ident, part, name):
    group, ring = lines.sizes["z"], lines.sizes["core"]
    dp = group * ring

    def kernel(x_ref, o_ref, send, recv):
        copies = Copies(lines, send, recv)
        rank = lax.axis_index("dp")
        copies.greet(["z", "core"])
        along = copies.swap("z", lambda peer: x_ref, lambda place: o_ref.at[rank])
        handed = copies.swap("core", lambda peer: x_ref, lambda place: o_ref.at[rank])
        o_ref[rank] = x_ref[...]
        zplace, place = lines.place("z"), lines.place("core")
        for step in range(group - 1, 0, -1):
            along[group - 1 - step].wait_recv()
            source = lax.rem(zplace + step, group) * ring + place
            handed += copies.swap("core", lambda peer: o_ref.at[source], lambda _: o_ref.at[source])
        for copy in along:
            copy.wait_send()
        wait(handed)

    (out,) = communicate(
        kernel,
        ident,
        [part],
        [((dp,) + part.shape, part.dtype)],
        semaphores(group - 1 + group * (ring - 1)),
        name,
    )
    return out


def swap_blocks(lines, ident, kind, arrays, shapes, plan, name):
    size = lines.sizes[kind]

    def kernel(*refs):
        ins, outs = refs[: len(arrays)], refs[len(arrays) : len(arrays) + len(shapes)]
        copies = Copies(lines, *refs[len(arrays) + len(shapes) :])
        me = lines.place(kind)
        copies.greet([kind])
        pending = []
        for i, src, o, dst in plan:
            pending += copies.swap(
                kind, lambda peer: src(ins[i], peer), lambda place: dst(outs[o], place)
            )
        for i, src, o, dst in plan:
            view = dst(outs[o], me)
            view[...] = src(ins[i], me)[...]
        wait(pending)

    return communicate(kernel, ident, arrays, shapes, semaphores((size - 1) * len(plan)), name)


def dense_to_heads(lines, ident, pairs, queries, name):
    group, ring = lines.sizes["z"], lines.sizes["core"]
    lanes = 2 * HDIM

    def kernel(p_ref, q_ref, po_ref, qo_ref, send, recv):
        copies = Copies(lines, send, recv)
        zplace, place = lines.place("z"), lines.place("core")
        copies.greet(["z", "core"])
        along, pending = [], []
        for peer in lines.peers("z"):
            along.append(copies.start("z", peer, p_ref.at[:, span(peer, lanes)], po_ref.at[place, zplace]))
        for peer in lines.peers("z"):
            pending.append(copies.start("z", peer, q_ref.at[:, span(peer, lanes)], qo_ref.at[zplace]))
        own = p_ref.at[:, span(zplace, lanes)]
        pending += copies.swap("core", lambda peer: own, lambda _: po_ref.at[place, zplace])
        po_ref[place, zplace] = own[...]
        qo_ref[zplace] = q_ref[:, span(zplace, lanes)]
        for step in range(group - 1, 0, -1):
            along[group - 1 - step].wait_recv()
            block = po_ref.at[place, lax.rem(zplace + step, group)]
            pending += copies.swap("core", lambda peer: block, lambda _: block)
        for copy in along:
            copy.wait_send()
        wait(pending)

    return communicate(
        kernel,
        ident,
        [pairs, queries],
        [((ring, group, pairs.shape[0], lanes), BF), ((group, queries.shape[0], lanes), BF)],
        semaphores(2 * (group - 1) + group * (ring - 1)),
        name,
    )


def dense_from_heads(lines, ident, pairs, queries, name):
    group, ring = lines.sizes["z"], lines.sizes["core"]
    _, _, rows, lanes = pairs.shape

    def kernel(p_ref, q_ref, po_ref, qo_ref, send, recv, got, turn):
        copies = Copies(lines, send, recv)
        zplace, place = lines.place("z"), lines.place("core")
        copies.greet(["z", "core"])
        order = lines.peers("z") + [zplace]
        around, pending = [], []
        for g in order:
            around.append(copies.swap("core", lambda peer: p_ref.at[peer, g], lambda me: got.at[me, g]))
        for g in order[:-1]:
            pending.append(copies.start("z", g, q_ref.at[g], qo_ref.at[:, span(zplace, lanes)]))
        qo_ref[:, span(zplace, lanes)] = q_ref[zplace]
        for g, arrived in zip(order, around):
            for copy in arrived:
                copy.wait_recv()
            total = p_ref[place, g].astype(F32)
            for peer in lines.peers("core"):
                total = total + got[peer, g].astype(F32)
            if g is zplace:
                po_ref[:, span(zplace, lanes)] = total.astype(BF)
            else:
                turn[g] = total.astype(BF)
                pending.append(copies.start("z", g, turn.at[g], po_ref.at[:, span(zplace, lanes)]))
        for arrived in around:
            for copy in arrived:
                copy.wait_send()
        wait(pending)

    return communicate(
        kernel,
        ident,
        [pairs, queries],
        [((rows, group * lanes), BF), ((queries.shape[1], group * lanes), BF)],
        semaphores(2 * (group - 1) + group * (ring - 1))
        + [pltpu.VMEM((ring, group, rows, lanes), BF), pltpu.VMEM((group, rows, lanes), BF)],
        name,
    )


def whole(ref, place):
    return ref


def slot(ref, place):
    return ref.at[place]


def columns(width):
    def view(ref, place):
        return ref.at[:, span(place, width)]

    return view


def unpack_low(packed):
    lane = lax.broadcasted_iota(jnp.int32, packed.shape, 1)
    zero = jnp.zeros_like(packed)
    low = jnp.where(lane < HDIM, packed, zero)
    turned = jnp.concatenate([packed[:, HDIM:], packed[:, :HDIM]], axis=1)
    high = jnp.where(lane < HDIM, turned, zero)
    return jnp.concatenate([low, high], axis=0)


def unpack_high(packed):
    lane = lax.broadcasted_iota(jnp.int32, packed.shape, 1)
    zero = jnp.zeros_like(packed)
    turned = jnp.concatenate([packed[:, HDIM:], packed[:, :HDIM]], axis=1)
    low = jnp.where(lane >= HDIM, turned, zero)
    high = jnp.where(lane >= HDIM, packed, zero)
    return jnp.concatenate([low, high], axis=0)


def pack_turned(turned):
    half = turned.shape[1] // 2
    return jnp.concatenate([turned[:, :half], turned[:, half:]], axis=0).T


def forward_block(query, pieces, qpos, start, causal):
    scores = []
    peak = None
    for index, (pair, _, first) in enumerate(pieces):
        item = contract(pair, query, 1, 1)
        kpos = first + lax.broadcasted_iota(jnp.int32, item.shape, 0)
        allowed = kpos >= start
        if causal[index]:
            allowed = allowed & (kpos <= qpos)
        item = jnp.where(allowed, item, NEG)
        top = jnp.max(item, axis=0, keepdims=True)
        peak = top if peak is None else jnp.maximum(peak, top)
        scores.append(item)
    total = jnp.zeros_like(peak)
    mixed = None
    for item, (_, turned, _) in zip(scores, pieces):
        weight = jnp.exp(item - peak)
        total = total + jnp.sum(weight, axis=0, keepdims=True)
        part = matmul(turned[HDIM:], weight.astype(BF))
        mixed = part if mixed is None else mixed + part
    return mixed / total, peak + jnp.log(total)


def backward_block(query, grad, grad_turned, mixed_turned, lse, pieces, qpos, start, causal):
    row_sum = jnp.sum(grad_turned.astype(F32) * mixed_turned.astype(F32), axis=0, keepdims=True)
    grad_query = None
    grads = []
    for index, (pair, turned, first) in enumerate(pieces):
        scores = contract(pair, query, 1, 1)
        kpos = first + lax.broadcasted_iota(jnp.int32, scores.shape, 0)
        allowed = kpos >= start
        if causal[index]:
            allowed = allowed & (kpos <= qpos)
        probs = jnp.where(allowed, jnp.exp(scores - lse), 0.0)
        grad_probs = contract(pair, grad, 1, 1)
        grad_scores = (probs * (grad_probs - row_sum)).astype(BF)
        grads.append(matmul(grad_scores, query) + matmul(probs.astype(BF), grad))
        part = matmul(turned[:HDIM], grad_scores)
        grad_query = part if grad_query is None else grad_query + part
    return grad_query * SCALE, grads


def dense_forward_kernel(place_ref, q_ref, kv_ref, start_ref, out_ref, turned_ref, lse_ref):
    group, _, half, _ = q_ref.shape
    ring, _, _, block, _ = kv_ref.shape
    place = place_ref[0]
    span = ring * block
    pieces = []
    for g in range(group):
        pair = kv_ref[:, g, 0].reshape(span, 2 * HDIM)
        pieces.append((pair, pair.T, g * span))
    for g in range(group):
        query = unpack_low(q_ref[g, 0]) * jnp.asarray(SCALE, BF)
        qpos = g * span + place * block + lax.broadcasted_iota(jnp.int32, (1, block), 1)
        mixed, lse = forward_block(
            query, pieces[: g + 1], qpos, start_ref[0, g], [i == g for i in range(g + 1)]
        )
        turned_ref[0, g] = mixed.astype(BF)
        lse_ref[0, g] = lse
        out_ref[g, 0] = pack_turned(mixed).astype(BF)


def dense_forward(place, q, kv, start):
    group, seqs, half, lanes = q.shape
    ring, _, _, block, _ = kv.shape
    grid = pltpu.PrefetchScalarGridSpec(
        num_scalar_prefetch=1,
        grid=(seqs,),
        in_specs=[
            pl.BlockSpec((group, 1, half, lanes), lambda s, _: (0, s, 0, 0)),
            pl.BlockSpec((ring, group, 1, block, lanes), lambda s, _: (0, 0, s, 0, 0)),
            pl.BlockSpec((1, group, 1, block), lambda s, _: (s, 0, 0, 0)),
        ],
        out_specs=[
            pl.BlockSpec((group, 1, half, lanes), lambda s, _: (0, s, 0, 0)),
            pl.BlockSpec((1, group, HDIM, block), lambda s, _: (s, 0, 0, 0)),
            pl.BlockSpec((1, group, 1, block), lambda s, _: (s, 0, 0, 0)),
        ],
    )
    return pl.pallas_call(
        dense_forward_kernel,
        grid_spec=grid,
        out_shape=[
            jax.ShapeDtypeStruct(q.shape, BF),
            jax.ShapeDtypeStruct((seqs, group, HDIM, block), BF),
            jax.ShapeDtypeStruct((seqs, group, 1, block), F32),
        ],
        compiler_params=pltpu.CompilerParams(vmem_limit_bytes=VMEM),
        name="dense_attention",
    )(place, q, kv, start)


def dense_backward_kernel(
    place_ref, q_ref, g_ref, kv_ref, start_ref, turned_ref, lse_ref, dq_ref, dkv_ref, acc_ref
):
    group, _, half, _ = q_ref.shape
    ring, _, _, block, _ = kv_ref.shape
    place = place_ref[0]
    span = ring * block
    pieces = []
    for g in range(group):
        pair = kv_ref[:, g, 0].reshape(span, 2 * HDIM)
        pieces.append((pair, pair.T, g * span))
    for g in reversed(range(group)):
        query = unpack_low(q_ref[g, 0]) * jnp.asarray(SCALE, BF)
        packed = g_ref[g, 0]
        grad = unpack_high(packed)
        flat = packed.T
        grad_turned = jnp.concatenate([flat[:HDIM], flat[HDIM:]], axis=1)
        qpos = g * span + place * block + lax.broadcasted_iota(jnp.int32, (1, block), 1)
        grad_query, grads = backward_block(
            query,
            grad,
            grad_turned,
            turned_ref[0, g],
            lse_ref[0, g],
            pieces[: g + 1],
            qpos,
            start_ref[0, g],
            [i == g for i in range(g + 1)],
        )
        dq_ref[g, 0] = pack_turned(grad_query).astype(BF)
        for i, item in enumerate(grads):
            if g == group - 1:
                acc_ref[i] = item
            else:
                acc_ref[i] += item
    for g in range(group):
        dkv_ref[:, g, 0] = acc_ref[g].reshape(ring, block, 2 * HDIM).astype(BF)


def dense_backward(place, q, grad, kv, start, turned, lse):
    group, seqs, half, lanes = q.shape
    ring, _, _, block, _ = kv.shape
    grid = pltpu.PrefetchScalarGridSpec(
        num_scalar_prefetch=1,
        grid=(seqs,),
        in_specs=[
            pl.BlockSpec((group, 1, half, lanes), lambda s, _: (0, s, 0, 0)),
            pl.BlockSpec((group, 1, half, lanes), lambda s, _: (0, s, 0, 0)),
            pl.BlockSpec((ring, group, 1, block, lanes), lambda s, _: (0, 0, s, 0, 0)),
            pl.BlockSpec((1, group, 1, block), lambda s, _: (s, 0, 0, 0)),
            pl.BlockSpec((1, group, HDIM, block), lambda s, _: (s, 0, 0, 0)),
            pl.BlockSpec((1, group, 1, block), lambda s, _: (s, 0, 0, 0)),
        ],
        out_specs=[
            pl.BlockSpec((group, 1, half, lanes), lambda s, _: (0, s, 0, 0)),
            pl.BlockSpec((ring, group, 1, block, lanes), lambda s, _: (0, 0, s, 0, 0)),
        ],
        scratch_shapes=[pltpu.VMEM((group, ring * block, lanes), F32)],
    )
    return pl.pallas_call(
        dense_backward_kernel,
        grid_spec=grid,
        out_shape=[
            jax.ShapeDtypeStruct(q.shape, BF),
            jax.ShapeDtypeStruct(kv.shape, BF),
        ],
        compiler_params=pltpu.CompilerParams(vmem_limit_bytes=VMEM),
        name="dense_attention_grad",
    )(place, q, grad, kv, start, turned, lse)


def inverse_rms(value):
    return lax.rsqrt(jnp.mean(value * value, axis=-1, keepdims=True) + EPS)


def gelu_terms(value):
    scale = 0.7978845608028654
    square = value * value
    bend = jnp.tanh(scale * (value + 0.044715 * square * value))
    half = 0.5 * (1.0 + bend)
    slope = half + 0.5 * value * (1.0 - bend * bend) * scale * (1.0 + 0.134145 * square)
    return value * half, slope


def side_by_side(blocks):
    return jnp.concatenate(blocks, axis=1)


def routed_kernel(
    lines,
    shape,
    source_ref,
    column_ref,
    row_ref,
    start_ref,
    gains_ref,
    main_ref,
    shrink_ref,
    returned_ref,
    added_ref,
    normed_ref,
    dqkv_ref,
    mixed_ref,
    attended_ref,
    normed_mid_ref,
    dpre_ref,
    hidden_ref,
    fed_ref,
    vectors_ref,
    send,
    recv,
    picked_buf,
    picked_got,
    slots_buf,
    slots_got,
    rows_buf,
    rows_got,
    heads_buf,
    heads_got,
    pairs_all,
    out_buf,
    out_got,
    mixed_all,
    own_buf,
    attended_all,
    fed_buf,
    fed_got,
    gate_buf,
    gate_got,
    wide_buf,
    mid_got,
    scalar_buf,
    scalar_got,
    do_buf,
    do_got,
    grad_buf,
    grad_got,
    turn_buf,
    turn_got,
    back_buf,
    back_got,
    in_buf,
    in_got,
    in_scalar,
    in_scalar_got,
    keep_ref,
    final_buf,
    final_all,
):
    seqs, sel, rows, width, part = shape
    sections, group, ring = (lines.sizes[k] for k in ("section", "z", "core"))
    dp = group * ring
    lanes = 2 * HDIM
    slots = seqs * sel
    copies = Copies(lines, send, recv)
    section, zplace, place = (lines.place(k) for k in ("section", "z", "core"))
    rank = lax.axis_index("dp")
    copies.greet(["section", "z", "core"])
    own = span(section, part)
    gain_pre, gain_mid, router = (gains_ref[i : i + 1, :] for i in range(3))
    own_pre, own_mid, own_router = (gains_ref[i : i + 1, own] for i in range(3))
    qkv_w = main_ref.at[:, : 3 * part]
    out_w = main_ref.at[:, 3 * part : 4 * part]
    expand_w = main_ref.at[:, 4 * part :]

    def sum_columns(value, buf, got, scalars, sbuf, sgot):
        buf[...] = value.astype(BF)
        pending = copies.swap("section", lambda peer: buf.at[:, span(peer, part)], lambda me: got.at[me])
        if scalars is not None:
            sbuf[...] = jnp.broadcast_to(scalars, sbuf.shape)
            pending += copies.swap("section", lambda peer: sbuf, lambda me: sgot.at[me])
        return pending

    def summed(pending, buf, got, sbuf, sgot):
        wait(pending)
        got[section] = buf[:, own]
        total = got[0].astype(F32)
        for i in range(1, sections):
            total = total + got[i].astype(F32)
        if sbuf is None:
            return total
        sgot[section] = sbuf[...]
        scalar = sgot[0]
        for i in range(1, sections):
            scalar = scalar + sgot[i]
        return total, scalar[:, :1]

    def all_columns(value, dst):
        dst[section] = value
        wait(copies.swap("section", lambda peer: dst.at[section], lambda me: dst.at[me]))
        return side_by_side([dst[i] for i in range(sections)])

    position = rank * rows + lax.broadcasted_iota(jnp.int32, (1, rows), 1)
    for q in range(seqs):
        table = (column_ref[q] == position).astype(F32).astype(BF)
        found = matmul(table, source_ref[q]).astype(BF)
        for d in range(dp):
            picked_buf[d % ring, d // ring, q * sel : (q + 1) * sel] = found[d * sel : (d + 1) * sel]
    wait(copies.swap("core", lambda peer: picked_buf.at[peer], lambda me: picked_got.at[me]))
    total = picked_buf[place].astype(F32)
    for peer in lines.peers("core"):
        total = total + picked_got[peer].astype(F32)
    slots_buf[...] = total.astype(BF)
    wait(copies.swap("z", lambda peer: slots_buf.at[peer], lambda me: slots_got.at[me]))
    total = slots_buf[zplace].astype(F32)
    for peer in lines.peers("z"):
        total = total + slots_got[peer].astype(F32)
    rows_got[section] = total.astype(BF)
    wait(copies.swap("section", lambda peer: rows_got.at[section], lambda me: rows_got.at[me]))
    picked = side_by_side([rows_got[i, :, :part] for i in range(sections)]).astype(F32)
    grad_sent = side_by_side([rows_got[i, :, part:] for i in range(sections)]).astype(F32)

    inv_in = inverse_rms(picked)
    normed = (picked * inv_in * gain_pre).astype(BF)
    normed_ref[...] = normed
    qkv = matmul(normed, qkv_w[...]).astype(BF)
    blank = jnp.zeros((slots, HDIM), BF)
    for g in range(group):
        heads_buf[g, :, :lanes] = side_by_side([qkv[:, 2 * part + g * HDIM : 2 * part + (g + 1) * HDIM], blank])
        heads_buf[g, :, lanes:] = qkv[:, g * lanes : (g + 1) * lanes]
    pending = copies.swap("z", lambda peer: heads_buf.at[peer], lambda me: heads_got.at[me])
    heads_got[zplace] = heads_buf[zplace]
    wait(pending)
    pairs_all[place] = heads_got[:, :, lanes:]
    wait(copies.swap("core", lambda peer: pairs_all.at[place], lambda me: pairs_all.at[me]))

    index = lax.broadcasted_iota(jnp.int32, (1, group * sel), 1)
    place_of = (index // sel) * (ring * sel) + place * sel + lax.rem(index, sel)

    def sequence(q):
        at = slice(q * sel, (q + 1) * sel)
        query = jnp.concatenate([heads_got[g, at, :lanes] for g in range(group)], axis=0)
        pair = jnp.concatenate([pairs_all[r, g, at] for g in range(group) for r in range(ring)], axis=0)
        return query * jnp.asarray(SCALE, BF), pair

    kept = []
    for q in range(seqs):
        query, pair = sequence(q)
        turned, lse = forward_block(query, [(pair, pair.T, 0)], place_of, start_ref[q], [True])
        kept.append((turned.astype(BF), lse))
        upright = jnp.concatenate([turned, jnp.zeros_like(turned)], axis=0).T.astype(BF)
        for g in range(group):
            out_buf[g, q * sel : (q + 1) * sel] = upright[g * sel : (g + 1) * sel]
    pending = copies.swap("z", lambda peer: out_buf.at[peer], lambda me: out_got.at[me])
    out_got[zplace] = out_buf[zplace]
    wait(pending)
    mixed = all_columns(side_by_side([out_got[g, :, :HDIM] for g in range(group)]), mixed_all)
    mixed_ref[...] = mixed
    attended_own = matmul(mixed, out_w[...]).astype(BF)
    attended = all_columns(attended_own, attended_all).astype(F32)

    middle = picked + attended
    inv_mid = inverse_rms(middle)
    normed_mid = (middle * inv_mid * gain_mid).astype(BF)
    normed_mid_ref[...] = normed_mid
    hidden_pre = matmul(normed_mid, expand_w[...])
    hidden, slope = gelu_terms(hidden_pre)
    hidden = hidden.astype(BF)
    hidden_ref[...] = hidden
    gate = jax.nn.sigmoid(jnp.sum(picked * router, axis=1, keepdims=True))
    grad_delta = gate * grad_sent
    fed_low = grad_delta.astype(BF)
    fed_ref[...] = fed_low

    grad_hidden = contract(fed_low, shrink_ref[...], 1, 1)
    grad_pre = (grad_hidden * slope).astype(BF)
    dpre_ref[...] = grad_pre
    grad_normed = contract(grad_pre, expand_w[...], 1, 1)
    scalar = jnp.sum(grad_normed * middle * gain_mid, axis=1, keepdims=True)
    pending = sum_columns(grad_normed, wide_buf, mid_got, scalar, scalar_buf, scalar_got)
    fed_part = matmul(hidden, shrink_ref[...])
    keep_ref[0] = middle
    keep_ref[1] = picked
    keep_ref[2] = grad_delta
    keep_ref[3] = grad_sent
    own_attended = attended_own.astype(F32)
    gate_part = jnp.sum(grad_sent * fed_part, axis=1, keepdims=True) + jnp.sum(
        keep_ref[3, :, own] * own_attended, axis=1, keepdims=True
    )
    middle_own, picked_own, grad_delta_own = keep_ref[0, :, own], keep_ref[1, :, own], keep_ref[2, :, own]
    grad_normed, scalar = summed(pending, wide_buf, mid_got, scalar_buf, scalar_got)
    fed_pending = sum_columns(fed_part, fed_buf, fed_got, gate_part, gate_buf, gate_got)
    vectors_ref[...] = jnp.zeros_like(vectors_ref)
    vectors_ref[1:2, :] = jnp.sum(grad_normed * middle_own * inv_mid, axis=0, keepdims=True)
    grad_middle = inv_mid * (grad_normed * own_mid) - middle_own * (inv_mid * inv_mid * inv_mid) * (
        scalar * (1.0 / width)
    )
    grad_attended = (grad_middle + grad_delta_own).astype(BF)
    attended_ref[...] = grad_attended

    pending = sum_columns(contract(grad_attended, out_w[...], 1, 1), own_buf, do_got, None, None, None)
    grad_mixed = summed(pending, own_buf, do_got, None, None).astype(BF)
    for g in range(group):
        grad_buf[g] = side_by_side([blank, grad_mixed[:, g * HDIM : (g + 1) * HDIM]])
    pending = copies.swap("z", lambda peer: grad_buf.at[peer], lambda me: grad_got.at[me])
    grad_got[zplace] = grad_buf[zplace]
    wait(pending)
    for q in range(seqs):
        at = slice(q * sel, (q + 1) * sel)
        query, pair = sequence(q)
        grad = jnp.concatenate([grad_got[g, at] for g in range(group)], axis=0)
        turned, lse = kept[q]
        grad_query, grad_pairs = backward_block(
            query, grad, grad.T[HDIM:], turned, lse, [(pair, pair.T, 0)], place_of, start_ref[q], [True]
        )
        upright = jnp.concatenate([grad_query, jnp.zeros_like(grad_query)], axis=0).T.astype(BF)
        low = grad_pairs[0].astype(BF)
        for g in range(group):
            back_buf[g, at, :lanes] = upright[g * sel : (g + 1) * sel]
            for r in range(ring):
                first = (g * ring + r) * sel
                turn_buf[r, g, at] = low[first : first + sel]
    wait(copies.swap("core", lambda peer: turn_buf.at[peer], lambda me: turn_got.at[me]))
    total = turn_buf[place].astype(F32)
    for peer in lines.peers("core"):
        total = total + turn_got[peer].astype(F32)
    back_buf[:, :, lanes:] = total.astype(BF)
    pending = copies.swap("z", lambda peer: back_buf.at[peer], lambda me: back_got.at[me])
    back_got[zplace] = back_buf[zplace]
    wait(pending)
    grad_qkv = side_by_side(
        [back_got[g, :, lanes:] for g in range(group)] + [back_got[g, :, :HDIM] for g in range(group)]
    )
    dqkv_ref[...] = grad_qkv
    grad_normed = contract(grad_qkv, qkv_w[...], 1, 1)
    scalar = jnp.sum(grad_normed * picked * gain_pre, axis=1, keepdims=True)
    pending = sum_columns(grad_normed, in_buf, in_got, scalar, in_scalar, in_scalar_got)

    fed, grad_gate = summed(fed_pending, fed_buf, fed_got, gate_buf, gate_got)
    sent = (gate * (own_attended + fed)).astype(BF)
    grad_logit = grad_gate * gate * (1.0 - gate)
    vectors_ref[2:3, :] = jnp.sum(grad_logit * picked_own, axis=0, keepdims=True)

    grad_normed, scalar = summed(pending, in_buf, in_got, in_scalar, in_scalar_got)
    vectors_ref[0:1, :] = jnp.sum(grad_normed * picked_own * inv_in, axis=0, keepdims=True)
    grad_in = inv_in * (grad_normed * own_pre) - picked_own * (inv_in * inv_in * inv_in) * (scalar * (1.0 / width))
    grad_chosen = (grad_middle + grad_in + grad_logit * own_router).astype(BF)

    final_buf[:, :part] = grad_chosen
    final_buf[:, part:] = sent
    along = copies.swap("z", lambda peer: final_buf, lambda me: rows_buf.at[me])
    rows_buf[zplace] = final_buf[...]
    spread = []

    def hand_on(i):
        view = rows_buf.at[i, :, pl.ds(0, part)]
        dst = final_all.at[place, i, :, own]
        dst[...] = view[...]
        final_all[place, i, :, width:] = rows_buf[i, :, part:]
        return copies.swap("section", lambda peer: view, lambda me: dst)

    spread += hand_on(zplace)
    for step in range(group - 1, 0, -1):
        along[group - 1 - step].wait_recv()
        spread += hand_on(lax.rem(zplace + step, group))
    for copy in along:
        copy.wait_send()
    wait(spread)
    wait(copies.swap("core", lambda peer: final_all.at[place], lambda me: final_all.at[me]))
    slot_of = rank * rows + lax.broadcasted_iota(jnp.int32, (rows, 1), 0)
    for q in range(seqs):
        at = slice(q * sel, (q + 1) * sel)
        table = (row_ref[q] == slot_of).astype(F32).astype(BF)
        found = jnp.concatenate([final_all[r, g, at] for g in range(group) for r in range(ring)], axis=0)
        placed = matmul(table, found).astype(BF)
        returned_ref[q] = placed[:, :width]
        added_ref[q] = placed[:, width:]


def routed_layer(lines, ident, source, chosen, start, gains, main, shrink, shape):
    seqs, sel, rows, width, part = shape
    sections, group, ring = (lines.sizes[k] for k in ("section", "z", "core"))
    slots = seqs * sel
    lanes = 2 * HDIM
    hidden = shrink.shape[0]
    outs = [
        ((seqs, rows, width), BF),
        ((seqs, rows, part), BF),
        ((slots, width), BF),
        ((slots, 3 * part), BF),
        ((slots, width), BF),
        ((slots, part), BF),
        ((slots, width), BF),
        ((slots, hidden), BF),
        ((slots, hidden), BF),
        ((slots, width), BF),
        ((8, part), F32),
    ]
    z = group - 1
    s = sections - 1
    c = ring - 1
    count = 4 * c + (1 + 1 + 1 + 1 + 1 + 1) * z + (1 + 1 + 1 + 2 + 2 + 1 + 2) * s + group * s
    vmem = pltpu.VMEM
    scratch = semaphores(count) + [
        vmem((ring, group, slots, 2 * part), BF),
        vmem((ring, group, slots, 2 * part), BF),
        vmem((group, slots, 2 * part), BF),
        vmem((group, slots, 2 * part), BF),
        vmem((group, slots, 2 * part), BF),
        vmem((sections, slots, 2 * part), BF),
        vmem((group, slots, 2 * lanes), BF),
        vmem((group, slots, 2 * lanes), BF),
        vmem((ring, group, slots, lanes), BF),
        vmem((group, slots, lanes), BF),
        vmem((group, slots, lanes), BF),
        vmem((sections, slots, part), BF),
        vmem((slots, width), BF),
        vmem((sections, slots, part), BF),
        vmem((slots, width), BF),
        vmem((sections, slots, part), BF),
        vmem((slots, 128), F32),
        vmem((sections, slots, 128), F32),
        vmem((slots, width), BF),
        vmem((sections, slots, part), BF),
        vmem((slots, 128), F32),
        vmem((sections, slots, 128), F32),
        vmem((slots, width), BF),
        vmem((sections, slots, part), BF),
        vmem((group, slots, lanes), BF),
        vmem((group, slots, lanes), BF),
        vmem((ring, group, slots, lanes), BF),
        vmem((ring, group, slots, lanes), BF),
        vmem((group, slots, 2 * lanes), BF),
        vmem((group, slots, 2 * lanes), BF),
        vmem((slots, width), BF),
        vmem((sections, slots, part), BF),
        vmem((slots, 128), F32),
        vmem((sections, slots, 128), F32),
        vmem((4, slots, width), F32),
        vmem((slots, 2 * part), BF),
        vmem((ring, group, slots, width + part), BF),
    ]
    return communicate(
        functools.partial(routed_kernel, lines, shape),
        ident,
        [source, chosen[:, :, None], chosen[:, None, :], start, gains, main, shrink],
        outs,
        scratch,
        "routed_layer",
        limit=48 * 2**20,
    )


def on_device(
    stream_in,
    segment_ids,
    chosen_rows,
    cotangent,
    dense_prenorm,
    dense_query,
    dense_keys,
    dense_values,
    dense_output,
    dense_midnorm,
    dense_expand,
    dense_shrink,
    routed_prenorm,
    routed_query,
    routed_keys,
    routed_values,
    routed_output,
    routed_midnorm,
    routed_expand,
    routed_shrink,
    router_weight,
):
    sections, dp = lax.axis_size("section"), lax.axis_size("dp")
    section, rank = lax.axis_index("section"), lax.axis_index("dp")
    seqs, rows, width = stream_in.shape
    tokens = seqs * rows
    part = width // sections
    group = HEADS // sections
    ring = dp // group
    total_sel = chosen_rows.shape[1]
    sel = total_sel // dp
    place = lax.rem(rank, ring).astype(jnp.int32).reshape(1)
    lines = Lines(sections, dp, group)
    lanes = 2 * HDIM

    def own_columns(value):
        return lax.dynamic_slice_in_dim(value, section * part, part, value.ndim - 1)

    def own_hidden(expand, shrink):
        inner = expand.shape[1] // dp
        share = inner // sections
        cut = expand.reshape(expand.shape[0], dp, sections, share)
        cut = lax.dynamic_index_in_dim(cut, section, 2, keepdims=False).reshape(expand.shape[0], dp * share)
        return cut, lax.dynamic_slice_in_dim(shrink, section * share, share, 0)

    def own_attention(query, keys, values):
        local = query.shape[0]
        pair = jnp.stack(
            [own_columns(keys).reshape(local, group, HDIM), own_columns(values).reshape(local, group, HDIM)],
            axis=2,
        ).reshape(local, 2 * part)
        return jnp.concatenate([pair, own_columns(query)], axis=1)

    gains = jnp.stack([dense_prenorm, dense_midnorm, routed_prenorm, routed_midnorm, router_weight])
    gains = jnp.pad(gains, ((0, 16 - gains.shape[0]), (0, 0)))
    local = dense_query.shape[0]
    first = own_attention(dense_query, dense_keys, dense_values)
    gains = jnp.pad(gains, ((0, 0), (0, first.shape[1] - local)))
    first = gather_rows(lines, 1, jnp.concatenate([first, gains], axis=0), "first_weights")
    dense_qkv = first[:, :local].reshape(width, 3 * part)
    gains = jnp.transpose(first[:, local:, :local], (1, 0, 2)).reshape(16, width).astype(F32)
    gain_pre, gain_mid = gains[0], gains[1]

    def gather(value):
        value, _ = lax.optimization_barrier((value, first))
        return lax.all_gather(value, "dp", axis=0, tiled=True)

    expand_cut, shrink_cut = own_hidden(dense_expand, dense_shrink)
    rest = gather(jnp.concatenate([own_columns(dense_output), expand_cut, shrink_cut], axis=1))
    hidden_size = expand_cut.shape[1]
    dense_out, dense_exp, dense_shr = (
        rest[:, :part],
        rest[:, part : part + hidden_size],
        rest[:, part + hidden_size :],
    )
    expand_cut, shrink_cut = own_hidden(routed_expand, routed_shrink)
    routed_main = gather(
        jnp.concatenate(
            [own_attention(routed_query, routed_keys, routed_values), own_columns(routed_output), expand_cut],
            axis=1,
        )
    )
    routed_shr = gather(shrink_cut)

    first_of = jnp.sum(
        (segment_ids[:, None, :] < jnp.arange(DOCS, dtype=jnp.int32)[None, :, None]).astype(jnp.int32), axis=2
    )

    def document(positions):
        shape = (seqs,) + (1,) * (positions.ndim - 1)
        found = jnp.zeros(positions.shape, jnp.int32)
        for c in range(1, DOCS):
            found = found + (positions >= first_of[:, c].reshape(shape)).astype(jnp.int32)
        return found

    def pick(table, index):
        shape = (seqs,) + (1,) * (index.ndim - 1)
        out = jnp.zeros(index.shape, jnp.int32)
        for c in range(DOCS):
            out = jnp.where(index == c, table[:, c].reshape(shape), out)
        return out

    blocks = jnp.arange(group, dtype=jnp.int32) * ring + place[0]
    attended_pos = blocks[:, None] * rows + jnp.arange(rows, dtype=jnp.int32)[None, :]
    attended_pos = jnp.broadcast_to(attended_pos[None], (seqs, group, rows))
    start = pick(first_of, document(attended_pos))[:, :, None, :]
    chosen_doc = document(chosen_rows)
    first_slot = jnp.sum(
        (chosen_doc[:, None, :] < jnp.arange(DOCS, dtype=jnp.int32)[None, :, None]).astype(jnp.int32), axis=2
    )
    chosen_start = pick(first_slot, chosen_doc).reshape(seqs, group, ring, sel)
    routed_start = lax.dynamic_index_in_dim(chosen_start, place[0], 2, keepdims=False)
    routed_start = routed_start.reshape(seqs, 1, group * sel)

    def pack(value):
        value = value.reshape(seqs, 2, rows // 2, group, HDIM)
        return jnp.transpose(value, (0, 2, 3, 1, 4)).reshape(tokens // 2, 2 * part)

    def unpack(value):
        value = value.reshape(seqs, rows // 2, group, 2, HDIM)
        return jnp.transpose(value, (0, 3, 1, 2, 4)).reshape(tokens, part)

    value = stream_in.reshape(tokens, width).astype(F32)
    grad_top = cotangent.reshape(tokens, width)
    inv_in = inverse_rms(value)
    normed = (value * inv_in * gain_pre).astype(BF)
    qkv = matmul(normed, dense_qkv).astype(BF)
    pairs, queries = dense_to_heads(
        lines, 2, qkv[:, : 2 * part], pack(qkv[:, 2 * part :]), "dense_to_heads"
    )
    queries = queries.reshape(group, seqs, rows // 2, lanes)
    pairs = pairs.reshape(ring, group, seqs, rows, lanes)
    mixed, mixed_turned, lse = dense_forward(place, queries, pairs, start)
    packed = (tokens // 2, group * lanes)
    (mixed,) = swap_blocks(
        lines, 3, "z", [mixed.reshape(group, tokens // 2, lanes)], [(packed, BF)], [(0, slot, 0, columns(lanes))],
        "dense_mixed",
    )
    mixed = gather_columns(lines, 4, unpack(mixed), "dense_mixed_columns")
    attended = gather_columns(lines, 5, matmul(mixed, dense_out).astype(BF), "dense_attended")
    middle_value = value + attended.astype(F32)
    inv_mid = inverse_rms(middle_value)
    normed_mid = (middle_value * inv_mid * gain_mid).astype(BF)
    hidden_pre = matmul(normed_mid, dense_exp)
    hidden = jax.nn.gelu(hidden_pre).astype(BF)
    fed = scatter_columns(lines, 6, matmul(hidden, dense_shr).astype(BF), None, "dense_fed")
    after_dense = own_columns(middle_value) + fed

    source = jnp.concatenate([after_dense.astype(BF), own_columns(grad_top)], axis=1)
    (
        returned,
        added,
        r_normed,
        r_grad_qkv,
        r_mixed,
        r_grad_attended,
        r_normed_mid,
        r_grad_pre,
        r_hidden,
        r_fed_low,
        r_vectors,
    ) = routed_layer(
        lines,
        7,
        source.reshape(seqs, rows, 2 * part),
        chosen_rows,
        routed_start,
        gains[2:5],
        routed_main,
        routed_shr,
        (seqs, sel, rows, width, part),
    )
    stream_out = (after_dense + added.reshape(tokens, part).astype(F32)).astype(BF).reshape(seqs, rows, part)

    def outer(left, right):
        return contract(left, right, 0, 0).astype(BF)

    def column(vector):
        wide = lax.dynamic_update_slice(jnp.zeros((width,), F32), vector, (section * part,))
        return wide[:, None]

    def reduce_dp(parts, vectors):
        last = jnp.concatenate([column(v) for v in vectors], axis=1)
        last = jnp.pad(last, ((0, 0), (0, 128 - last.shape[1]))).astype(BF)
        return lax.psum_scatter(jnp.concatenate(parts + [last], axis=1), "dp", scatter_dimension=0, tiled=True)

    routed_shard = reduce_dp(
        [
            outer(r_normed, r_grad_qkv),
            outer(r_mixed, r_grad_attended),
            outer(r_normed_mid, r_grad_pre),
            outer(r_hidden, r_fed_low),
        ],
        [r_vectors[0], r_vectors[1], r_vectors[2]],
    )

    grad_after = grad_top.astype(F32) + returned.reshape(tokens, width).astype(F32)
    fed_low = grad_after.astype(BF)
    _, gelu_pull = jax.vjp(jax.nn.gelu, hidden_pre)
    grad_pre = gelu_pull(contract(fed_low, dense_shr, 1, 1))[0].astype(BF)
    grad_normed = contract(grad_pre, dense_exp, 1, 1)
    scalar = jnp.sum(grad_normed * middle_value * gain_mid, axis=1)
    grad_normed, scalar = scatter_columns(lines, 8, grad_normed.astype(BF), scalar, "dense_back_mid")
    middle_own = own_columns(middle_value)
    grad_gain_mid = jnp.sum(grad_normed * middle_own * inv_mid, axis=0)
    grad_middle = (
        inv_mid * (grad_normed * own_columns(gain_mid))
        - middle_own * (inv_mid * inv_mid * inv_mid) * (scalar * (1.0 / width))[:, None]
        + own_columns(grad_after)
    )
    grad_attended = grad_middle.astype(BF)
    grad_mixed = scatter_columns(
        lines, 9, contract(grad_attended, dense_out, 1, 1).astype(BF), None, "dense_back_mixed"
    ).astype(BF)
    (grad_heads,) = swap_blocks(
        lines, 10, "z", [pack(grad_mixed)], [((group, tokens // 2, lanes), BF)], [(0, columns(lanes), 0, slot)],
        "dense_grad_to_heads",
    )
    dq, dkv = dense_backward(
        place,
        queries,
        grad_heads.reshape(group, seqs, rows // 2, lanes),
        pairs,
        start,
        mixed_turned,
        lse,
    )
    dkv, dq = dense_from_heads(
        lines, 11, dkv.reshape(ring, group, tokens, lanes), dq.reshape(group, tokens // 2, lanes), "dense_from_heads"
    )
    grad_qkv = jnp.concatenate([dkv, unpack(dq)], axis=1)
    grad_normed = contract(grad_qkv, dense_qkv, 1, 1)
    scalar = jnp.sum(grad_normed * value * gain_pre, axis=1)
    grad_normed, scalar = scatter_columns(lines, 12, grad_normed.astype(BF), scalar, "dense_back_in")
    value_own = own_columns(value)
    grad_gain_pre = jnp.sum(grad_normed * value_own * inv_in, axis=0)
    grad_in = (
        inv_in * (grad_normed * own_columns(gain_pre))
        - value_own * (inv_in * inv_in * inv_in) * (scalar * (1.0 / width))[:, None]
    )
    stream_grad = (grad_middle + grad_in).astype(BF).reshape(seqs, rows, part)
    dense_shard = reduce_dp(
        [outer(normed, grad_qkv), outer(mixed, grad_attended), outer(normed_mid, grad_pre), outer(hidden, fed_low)],
        [grad_gain_pre, grad_gain_mid],
    )

    def finish(ident, shard, count, name):
        local, wide = shard.shape
        got = gather_columns(lines, ident, shard, name).reshape(local, sections, wide)
        got = jnp.transpose(got, (1, 0, 2))
        pair = got[:, :, : 2 * part].reshape(sections, local, group, 2, HDIM)
        keys = jnp.transpose(pair[:, :, :, 0], (1, 0, 2, 3)).reshape(local, width).astype(F32)
        values = jnp.transpose(pair[:, :, :, 1], (1, 0, 2, 3)).reshape(local, width).astype(F32)
        query = jnp.transpose(got[:, :, 2 * part : 3 * part], (1, 0, 2)).reshape(local, width).astype(F32)
        output = jnp.transpose(got[:, :, 3 * part : 4 * part], (1, 0, 2)).reshape(local, width).astype(F32)
        share = hidden_size // dp
        expand = got[:, :, 4 * part : 4 * part + hidden_size].reshape(sections, local, dp, share)
        expand = jnp.transpose(expand, (1, 2, 0, 3)).reshape(local, sections * hidden_size).astype(F32)
        shrink = got[:, :, 4 * part + hidden_size : 4 * part + hidden_size + width]
        shrink = shrink.reshape(sections * local, width).astype(F32)
        vectors = jnp.sum(got[:, :, 4 * part + hidden_size + width :].astype(F32), axis=0)
        return [vectors[:, i] for i in range(count)], [query, keys, values, output, expand, shrink]

    r_vector, r_grads = finish(13, routed_shard, 3, "routed_weight_grads")
    d_vector, d_grads = finish(14, dense_shard, 2, "dense_weight_grads")
    return (
        (stream_out, stream_grad)
        + (d_vector[0], *d_grads[:4], d_vector[1], *d_grads[4:])
        + (r_vector[0], *r_grads[:4], r_vector[1], *r_grads[4:])
        + (r_vector[2],)
    )


def solution(mesh):
    streams, row, vector, copied = P(None, "dp", None), P("dp", None), P("dp"), P()
    layer = (vector, row, row, row, row, vector, row, row)
    outs = (P(None, "dp", "section"),) * 2 + layer + layer + (vector,)
    return jax.shard_map(
        on_device,
        mesh=mesh,
        in_specs=(streams, copied, copied, streams) + layer + layer + (vector,),
        out_specs=outs,
        check_vma=False,
    )
```

```python
import functools

import jax
import jax.numpy as jnp
from jax import lax
from jax.experimental import pallas as pl
from jax.experimental.pallas import tpu as pltpu
from jax.sharding import PartitionSpec as P

HEADS = 16
HDIM = 64
DOCS = 8
EPS = 1e-06
NEG = -1e30
SCALE = HDIM ** (-0.5)
VMEM = 32 * 2**20
MESH = pl.DeviceIdType.MESH
BF = jnp.bfloat16
F32 = jnp.float32


def matmul(left, right):
    return jnp.dot(left, right, preferred_element_type=F32)


def contract(left, right, ldim, rdim):
    return lax.dot_general(left, right, (((ldim,), (rdim,)), ((), ())), preferred_element_type=F32)


class Lines:
    def __init__(self, sections, dp, group):
        self.sizes = {"section": sections, "z": group, "core": dp // group}
        self.ring = dp // group

    def place(self, kind):
        if kind == "section":
            return lax.axis_index("section")
        index = lax.axis_index("dp")
        return index // self.ring if kind == "z" else lax.rem(index, self.ring)

    def device(self, kind, place):
        if kind == "section":
            return {"section": place}
        index = lax.axis_index("dp")
        if kind == "z":
            return {"dp": place * self.ring + lax.rem(index, self.ring)}
        return {"dp": (index // self.ring) * self.ring + place}

    def peers(self, kind):
        size = self.sizes[kind]
        me = self.place(kind)
        return [lax.rem(me + step, size) for step in range(1, size)]


class Copies:
    def __init__(self, lines, send, recv):
        self.lines, self.send, self.recv, self.used = lines, send, recv, 0

    def greet(self, kinds):
        barrier = pltpu.get_barrier_semaphore()
        count = 0
        for kind in kinds:
            for peer in self.lines.peers(kind):
                pl.semaphore_signal(
                    barrier, inc=1, device_id=self.lines.device(kind, peer), device_id_type=MESH
                )
                count += 1
        pl.semaphore_wait(barrier, count)

    def start(self, kind, peer, src, dst):
        copy = pltpu.make_async_remote_copy(
            src_ref=src,
            dst_ref=dst,
            send_sem=self.send.at[self.used],
            recv_sem=self.recv.at[self.used],
            device_id=self.lines.device(kind, peer),
            device_id_type=MESH,
        )
        self.used += 1
        copy.start()
        return copy

    def swap(self, kind, src, dst):
        me = self.lines.place(kind)
        return [self.start(kind, peer, src(peer), dst(me)) for peer in self.lines.peers(kind)]


def wait(copies):
    for copy in copies:
        copy.wait()


def semaphores(count):
    return [pltpu.SemaphoreType.DMA((count,)), pltpu.SemaphoreType.DMA((count,))]


def communicate(kernel, ident, arrays, shapes, scratch, name, limit=24 * 2**20):
    vmem = pl.BlockSpec(memory_space=pltpu.VMEM)
    return pl.pallas_call(
        kernel,
        out_shape=[jax.ShapeDtypeStruct(s, d) for s, d in shapes],
        in_specs=[vmem] * len(arrays),
        out_specs=[vmem] * len(shapes),
        scratch_shapes=scratch,
        compiler_params=pltpu.CompilerParams(
            collective_id=ident, has_side_effects=True, vmem_limit_bytes=limit
        ),
        name=name,
    )(*arrays)


def span(place, width):
    return pl.ds(pl.multiple_of(place * width, width), width)


def square(lines):
    me = lines.place("section")
    low, high = lax.rem(me, 2), me // 2
    return high * 2 + 1 - low, (1 - high) * 2 + low, (1 - high) * 2 + 1 - low


def pieces_of(rows):
    half = rows // 2
    return (2, half // 2) if half % 32 == 0 else (1, half)


class SquareGather:
    @staticmethod
    def count(rows):
        return 6 * pieces_of(rows)[0]

    def __init__(self, copies, x_ref, o_ref):
        self.copies, self.x_ref, self.o_ref = copies, x_ref, o_ref
        self.width = x_ref.shape[1]
        self.me = copies.lines.place("section")
        near, far, _ = square(copies.lines)
        pieces, step = pieces_of(x_ref.shape[0])
        half = x_ref.shape[0] // 2
        self.parts = [
            (pl.ds(h * half + j * step, step), one, two)
            for j in range(pieces)
            for h, (one, two) in enumerate(((near, far), (far, near)))
        ]

    def send(self, at, to):
        dst = self.o_ref.at[at, span(self.me, self.width)]
        return self.copies.start("section", to, self.x_ref.at[at], dst)

    def start(self):
        self.first = [self.send(at, one) for at, one, _ in self.parts]
        self.rest = [self.send(at, two) for at, _, two in self.parts]
        self.o_ref[:, span(self.me, self.width)] = self.x_ref[...]

    def forward(self):
        for (at, one, two), copy in zip(self.parts, self.first):
            copy.wait_recv()
            place = self.o_ref.at[at, span(one, self.width)]
            self.rest.append(self.copies.start("section", two, place, place))

    def finish(self):
        for copy in self.first:
            copy.wait_send()
        wait(self.rest)


class SquareScatter:
    @staticmethod
    def count(rows):
        return 6 * pieces_of(rows)[0]

    @staticmethod
    def scratch(rows, width):
        return [pltpu.VMEM((2, rows, width), BF), pltpu.VMEM((rows, width), BF), pltpu.VMEM((rows, width), BF)]

    def __init__(self, copies, x_ref, got, turn, last):
        self.copies, self.x_ref, self.got, self.turn, self.last = copies, x_ref, got, turn, last
        self.width = turn.shape[1]
        self.me = copies.lines.place("section")
        near, far, self.across = square(copies.lines)
        pieces, step = pieces_of(x_ref.shape[0])
        half = x_ref.shape[0] // 2
        self.parts = [
            (pl.ds(h * half + j * step, step), one, two)
            for j in range(pieces)
            for h, (one, two) in enumerate(((near, far), (far, near)))
        ]

    def read(self, at, place):
        return self.x_ref[at, span(place, self.width)].astype(F32)

    def start(self):
        self.passed, self.kept = [], []
        for at, one, _ in self.parts:
            for place, k, out in ((self.across, 0, self.passed), (one, 1, self.kept)):
                src = self.x_ref.at[at, span(place, self.width)]
                out.append(self.copies.start("section", one, src, self.got.at[k, at]))

    def forward(self):
        self.second = []
        for (at, _, two), copy in zip(self.parts, self.passed):
            copy.wait_recv()
            self.turn[at] = (self.read(at, two) + self.got[0, at].astype(F32)).astype(BF)
            self.second.append(self.copies.start("section", two, self.turn.at[at], self.last.at[at]))

    def finish(self, o_ref):
        for i, (at, _, _) in enumerate(self.parts):
            self.kept[i].wait_recv()
            self.second[i].wait_recv()
            o_ref[at] = self.read(at, self.me) + self.got[1, at].astype(F32) + self.last[at].astype(F32)
        for copy in self.passed + self.kept + self.second:
            copy.wait_send()


def gather_columns(lines, ident, part, name):
    rows, width = part.shape

    def kernel(x_ref, o_ref, send, recv):
        copies = Copies(lines, send, recv)
        copies.greet(["section"])
        gather = SquareGather(copies, x_ref, o_ref)
        gather.start()
        gather.forward()
        gather.finish()

    shape = ((rows, lines.sizes["section"] * width), part.dtype)
    (out,) = communicate(kernel, ident, [part], [shape], semaphores(SquareGather.count(rows)), name)
    return out


def scalar_block(scalars):
    count = -(-scalars.shape[0] // 128)
    count += -count % 8
    return jnp.pad(scalars, (0, count * 128 - scalars.shape[0])).reshape(count, 128)


def sum_places(ref):
    total = ref[0].astype(F32)
    for i in range(1, ref.shape[0]):
        total = total + ref[i].astype(F32)
    return total


def scatter_columns(lines, ident, part, scalars, name):
    rows, full = part.shape
    sections = lines.sizes["section"]
    width = full // sections
    extra = scalars is not None
    arrays = [part]
    shapes = [((rows, width), F32)]
    scratch = semaphores(SquareScatter.count(rows) + sections - 1) + SquareScatter.scratch(rows, width)
    if extra:
        arrays.append(scalar_block(scalars))
        shapes.append((arrays[1].shape, F32))
        scratch.append(pltpu.VMEM((sections,) + arrays[1].shape, F32))

    def kernel(*refs):
        x_ref, refs = refs[0], refs[1:]
        if extra:
            e_ref, o_ref, eo_ref, send, recv, got, turn, last, e_got = refs
        else:
            o_ref, send, recv, got, turn, last = refs
        copies = Copies(lines, send, recv)
        copies.greet(["section"])
        scatter = SquareScatter(copies, x_ref, got, turn, last)
        scatter.start()
        if extra:
            others = copies.swap("section", lambda peer: e_ref, lambda place: e_got.at[place])
            e_got[lines.place("section")] = e_ref[...]
        scatter.forward()
        scatter.finish(o_ref)
        if extra:
            wait(others)
            eo_ref[...] = sum_places(e_got)

    got = communicate(kernel, ident, arrays, shapes, scratch, name)
    if not extra:
        return got[0]
    return got[0], got[1].reshape(-1)[:rows]


def gather_rows(lines, ident, parts, name):
    group, ring = lines.sizes["z"], lines.sizes["core"]
    dp = group * ring
    many = len(parts)

    def kernel(*refs):
        ins, outs, (send, recv) = refs[:many], refs[many : 2 * many], refs[2 * many :]
        copies = Copies(lines, send, recv)
        rank = lax.axis_index("dp")
        zplace, place = lines.place("z"), lines.place("core")
        copies.greet(["z", "core"])
        along, handed = [], []
        for x_ref, o_ref in zip(ins, outs):
            along.append(copies.swap("z", lambda peer: x_ref, lambda _: o_ref.at[rank]))
        for x_ref, o_ref in zip(ins, outs):
            handed += copies.swap("core", lambda peer: x_ref, lambda _: o_ref.at[rank])
            o_ref[rank] = x_ref[...]
        for step in range(group - 1, 0, -1):
            source = lax.rem(zplace + step, group) * ring + place
            for arrived, o_ref in zip(along, outs):
                arrived[group - 1 - step].wait_recv()
                handed += copies.swap("core", lambda peer: o_ref.at[source], lambda _: o_ref.at[source])
        for arrived in along:
            for copy in arrived:
                copy.wait_send()
        wait(handed)

    return communicate(
        kernel,
        ident,
        parts,
        [((dp,) + part.shape, part.dtype) for part in parts],
        semaphores(many * (group - 1 + group * (ring - 1))),
        name,
    )


def swap_blocks(lines, ident, kind, arrays, shapes, plan, name):
    size = lines.sizes[kind]

    def kernel(*refs):
        ins, outs = refs[: len(arrays)], refs[len(arrays) : len(arrays) + len(shapes)]
        copies = Copies(lines, *refs[len(arrays) + len(shapes) :])
        me = lines.place(kind)
        copies.greet([kind])
        pending = []
        for i, src, o, dst in plan:
            pending += copies.swap(
                kind, lambda peer: src(ins[i], peer), lambda place: dst(outs[o], place)
            )
        for i, src, o, dst in plan:
            view = dst(outs[o], me)
            view[...] = src(ins[i], me)[...]
        wait(pending)

    return communicate(kernel, ident, arrays, shapes, semaphores((size - 1) * len(plan)), name)


def slot(ref, place):
    return ref.at[place]


def columns(width):
    def view(ref, place):
        return ref.at[:, span(place, width)]

    return view


def dense_to_heads(lines, ident, pairs, queries, name):
    group, ring = lines.sizes["z"], lines.sizes["core"]
    lanes = 2 * HDIM

    def kernel(p_ref, q_ref, po_ref, qo_ref, send, recv):
        copies = Copies(lines, send, recv)
        zplace, place = lines.place("z"), lines.place("core")
        copies.greet(["z", "core"])
        along, pending = [], []
        for peer in lines.peers("z"):
            along.append(copies.start("z", peer, p_ref.at[:, span(peer, lanes)], po_ref.at[place, zplace]))
        for peer in lines.peers("z"):
            pending.append(copies.start("z", peer, q_ref.at[:, span(peer, lanes)], qo_ref.at[zplace]))
        own = p_ref.at[:, span(zplace, lanes)]
        pending += copies.swap("core", lambda peer: own, lambda _: po_ref.at[place, zplace])
        po_ref[place, zplace] = own[...]
        qo_ref[zplace] = q_ref[:, span(zplace, lanes)]
        for step in range(group - 1, 0, -1):
            along[group - 1 - step].wait_recv()
            block = po_ref.at[place, lax.rem(zplace + step, group)]
            pending += copies.swap("core", lambda peer: block, lambda _: block)
        for copy in along:
            copy.wait_send()
        wait(pending)

    return communicate(
        kernel,
        ident,
        [pairs, queries],
        [((ring, group, pairs.shape[0], lanes), BF), ((group, queries.shape[0], lanes), BF)],
        semaphores(2 * (group - 1) + group * (ring - 1)),
        name,
    )


def dense_from_heads(lines, ident, pairs, queries, shards, name):
    group, ring = lines.sizes["z"], lines.sizes["core"]
    _, _, rows, lanes = pairs.shape
    many = len(shards)

    def kernel(p_ref, q_ref, *refs):
        s_refs, refs = refs[:many], refs[many:]
        po_ref, qo_ref, refs = refs[0], refs[1], refs[2:]
        so_refs, (send, recv, got, turn) = refs[:many], refs[many:]
        copies = Copies(lines, send, recv)
        zplace, place = lines.place("z"), lines.place("core")
        copies.greet(["z", "core", "section"])
        order = lines.peers("z") + [zplace]
        around, pending = [], []
        for g in order:
            around.append(copies.swap("core", lambda peer: p_ref.at[peer, g], lambda me: got.at[me, g]))
        for g in order[:-1]:
            pending.append(copies.start("z", g, q_ref.at[g], qo_ref.at[:, span(zplace, lanes)]))
        gathers = [SquareGather(copies, x, o) for x, o in zip(s_refs, so_refs)]
        for gather in gathers:
            gather.start()
        qo_ref[:, span(zplace, lanes)] = q_ref[zplace]
        for i, (g, arrived) in enumerate(zip(order, around)):
            for copy in arrived:
                copy.wait_recv()
            total = p_ref[place, g].astype(F32)
            for peer in lines.peers("core"):
                total = total + got[peer, g].astype(F32)
            if i == len(order) - 1:
                po_ref[:, span(zplace, lanes)] = total.astype(BF)
            else:
                turn[g] = total.astype(BF)
                pending.append(copies.start("z", g, turn.at[g], po_ref.at[:, span(zplace, lanes)]))
        for gather in gathers:
            gather.forward()
        for arrived in around:
            for copy in arrived:
                copy.wait_send()
        wait(pending)
        for gather in gathers:
            gather.finish()

    sections = lines.sizes["section"]
    got = communicate(
        kernel,
        ident,
        [pairs, queries] + shards,
        [((rows, group * lanes), BF), ((queries.shape[1], group * lanes), BF)]
        + [((x.shape[0], sections * x.shape[1]), x.dtype) for x in shards],
        semaphores(
            2 * (group - 1) + group * (ring - 1) + sum(SquareGather.count(x.shape[0]) for x in shards)
        )
        + [pltpu.VMEM((ring, group, rows, lanes), BF), pltpu.VMEM((group, rows, lanes), BF)],
        name,
    )
    return got[0], got[1], got[2:]


def dense_finish(lines, ident, part, scalars, scaled, weight, shards, name):
    group, ring, sections = (lines.sizes[k] for k in ("z", "core", "section"))
    dp = group * ring
    rows, full = part.shape
    width = full // sections
    many = len(shards)
    local = weight.shape[0] // dp
    wide = weight.shape[1]
    block = scalar_block(scalars)
    weight = weight.reshape(dp, local, wide)

    def kernel(x_ref, e_ref, scaled_ref, w_ref, *refs):
        s_refs, refs = refs[:many], refs[many:]
        o_ref, eo_ref, v_ref, wo_ref, refs = refs[0], refs[1], refs[2], refs[3], refs[4:]
        so_refs, refs = refs[:many], refs[many:]
        send, recv, got, turn, last, e_got, w_got, w_turn, w_all, w_own, v_buf, v_z, v_core, v_all = refs
        copies = Copies(lines, send, recv)
        zplace, place, section = (lines.place(k) for k in ("z", "core", "section"))
        copies.greet(["z", "core", "section"])
        order = lines.peers("z") + [zplace]
        scatter = SquareScatter(copies, x_ref, got, turn, last)
        scatter.start()
        around = [
            copies.swap("core", lambda peer: w_ref.at[g * ring + peer], lambda me: w_got.at[me, g]) for g in order
        ]
        others = copies.swap("section", lambda peer: e_ref, lambda me: e_got.at[me])
        e_got[section] = e_ref[...]
        along = []
        for i, (g, arrived) in enumerate(zip(order, around)):
            for copy in arrived:
                copy.wait_recv()
            total = w_ref[g * ring + place].astype(F32)
            for peer in lines.peers("core"):
                total = total + w_got[peer, g].astype(F32)
            w_turn[g] = total.astype(BF)
            if i < len(order) - 1:
                along.append(copies.start("z", g, w_turn.at[g], w_all.at[zplace]))
        scatter.forward()
        gathers = [SquareGather(copies, x, o) for x, o in zip(s_refs, so_refs)]
        for gather in gathers:
            gather.start()
        scatter.finish(o_ref)
        wait(others)
        eo_ref[...] = sum_places(e_got)
        v_buf[...] = jnp.broadcast_to(jnp.sum(o_ref[...] * scaled_ref[...], axis=0, keepdims=True), v_buf.shape)
        pending = copies.swap("z", lambda peer: v_buf, lambda me: v_z.at[me])
        v_z[zplace] = v_buf[...]
        for gather in gathers:
            gather.forward()
        wait(along)
        w_all[zplace] = w_turn[zplace]
        w_own[...] = sum_places(w_all).astype(BF)
        last_gather = SquareGather(copies, w_own, wo_ref)
        last_gather.start()
        wait(pending)
        v_core[place] = sum_places(v_z)
        wait(copies.swap("core", lambda peer: v_core.at[place], lambda me: v_core.at[me]))
        v_all[section] = sum_places(v_core)
        pending = copies.swap("section", lambda peer: v_all.at[section], lambda me: v_all.at[me])
        last_gather.forward()
        wait(pending)
        for i in range(sections):
            v_ref[:, i * width : (i + 1) * width] = v_all[i]
        for arrived in around:
            for copy in arrived:
                copy.wait_send()
        for gather in gathers:
            gather.finish()
        last_gather.finish()

    z, c, s = group - 1, ring - 1, sections - 1
    vector = (8, width)
    result = communicate(
        kernel,
        ident,
        [part, block, scaled, weight] + shards,
        [((rows, width), F32), (block.shape, F32), ((8, full), F32), ((local, sections * wide), BF)]
        + [((x.shape[0], sections * x.shape[1]), x.dtype) for x in shards],
        semaphores(
            SquareScatter.count(rows)
            + group * c
            + s
            + z
            + sum(SquareGather.count(x.shape[0]) for x in shards)
            + SquareGather.count(local)
            + z
            + c
            + s
        )
        + SquareScatter.scratch(rows, width)
        + [
            pltpu.VMEM((sections,) + block.shape, F32),
            pltpu.VMEM((ring, group, local, wide), BF),
            pltpu.VMEM((group, local, wide), BF),
            pltpu.VMEM((group, local, wide), BF),
            pltpu.VMEM((local, wide), BF),
            pltpu.VMEM(vector, F32),
            pltpu.VMEM((group,) + vector, F32),
            pltpu.VMEM((ring,) + vector, F32),
            pltpu.VMEM((sections,) + vector, F32),
        ],
        name,
        limit=32 * 2**20,
    )
    summed, scalar, vector, gathered = result[0], result[1].reshape(-1)[:rows], result[2][0], result[3]
    return summed, scalar, vector, gathered, result[4:]


def assemble(pieces, share, name):
    arrays = []
    for _, array, _, _ in pieces:
        if not any(array is other for other in arrays):
            arrays.append(array)
    where = [next(i for i, other in enumerate(arrays) if other is array) for _, array, _, _ in pieces]
    local = arrays[0].shape[0]
    steps = local // 32 if local % 32 == 0 else 1
    rows = local // steps
    sections = lax.axis_size("section")
    shapes, specs = [], []
    for kind, _, _, width in pieces:
        many = 2 if kind == "pair" else 1
        for _ in range(many):
            if kind == "stack":
                shapes.append(jax.ShapeDtypeStruct((sections, local, width), F32))
                specs.append(pl.BlockSpec((sections, rows, width), lambda i: (0, i, 0)))
            else:
                total = width if kind == "sum" else sections * width // many
                shapes.append(jax.ShapeDtypeStruct((local, total), F32))
                specs.append(pl.BlockSpec((rows, total), lambda i: (i, 0)))

    def kernel(*refs):
        ins, outs = refs[: len(arrays)], list(refs[len(arrays) :])
        for (kind, array, first, width), i in zip(pieces, where):
            wide = array.shape[1] // sections
            blocks = [ins[i][:, s * wide + first : s * wide + first + width].astype(F32) for s in range(sections)]
            out = outs.pop(0)
            if kind == "columns":
                for s, item in enumerate(blocks):
                    out[:, s * width : (s + 1) * width] = item
            elif kind == "stack":
                for s, item in enumerate(blocks):
                    out[s] = item
            elif kind == "sum":
                total = blocks[0]
                for item in blocks[1:]:
                    total = total + item
                out[...] = total
            elif kind == "hidden":
                for d in range(width // share):
                    out[:, d * share * sections : (d + 1) * share * sections] = jnp.concatenate(
                        [item[:, d * share : (d + 1) * share] for item in blocks], axis=1
                    )
            else:
                other = outs.pop(0)
                half = width // 2
                for s, item in enumerate(blocks):
                    for side, dst in ((0, out), (1, other)):
                        heads = [
                            item[:, (2 * g + side) * HDIM : (2 * g + side + 1) * HDIM]
                            for g in range(width // (2 * HDIM))
                        ]
                        dst[:, s * half : (s + 1) * half] = jnp.concatenate(heads, axis=1)

    return pl.pallas_call(
        kernel,
        grid=(steps,),
        in_specs=[pl.BlockSpec((rows, a.shape[1]), lambda i: (i, 0)) for a in arrays],
        out_specs=specs,
        out_shape=shapes,
        compiler_params=pltpu.CompilerParams(vmem_limit_bytes=24 * 2**20),
        name=name,
    )(*arrays)


def unpack_low(packed):
    lane = lax.broadcasted_iota(jnp.int32, packed.shape, 1)
    zero = jnp.zeros_like(packed)
    low = jnp.where(lane < HDIM, packed, zero)
    turned = jnp.concatenate([packed[:, HDIM:], packed[:, :HDIM]], axis=1)
    high = jnp.where(lane < HDIM, turned, zero)
    return jnp.concatenate([low, high], axis=0)


def unpack_high(packed):
    lane = lax.broadcasted_iota(jnp.int32, packed.shape, 1)
    zero = jnp.zeros_like(packed)
    turned = jnp.concatenate([packed[:, HDIM:], packed[:, :HDIM]], axis=1)
    low = jnp.where(lane >= HDIM, turned, zero)
    high = jnp.where(lane >= HDIM, packed, zero)
    return jnp.concatenate([low, high], axis=0)


def pack_turned(turned):
    half = turned.shape[1] // 2
    return jnp.concatenate([turned[:, :half], turned[:, half:]], axis=0).T


def forward_block(query, pieces, qpos, start, causal):
    scores = []
    peak = None
    for index, (pair, _, first) in enumerate(pieces):
        item = contract(pair, query, 1, 1)
        kpos = first + lax.broadcasted_iota(jnp.int32, item.shape, 0)
        allowed = kpos >= start
        if causal[index]:
            allowed = allowed & (kpos <= qpos)
        item = jnp.where(allowed, item, NEG)
        top = jnp.max(item, axis=0, keepdims=True)
        peak = top if peak is None else jnp.maximum(peak, top)
        scores.append(item)
    total = jnp.zeros_like(peak)
    mixed = None
    for item, (_, turned, _) in zip(scores, pieces):
        weight = jnp.exp(item - peak)
        total = total + jnp.sum(weight, axis=0, keepdims=True)
        part = matmul(turned[HDIM:], weight.astype(BF))
        mixed = part if mixed is None else mixed + part
    return mixed / total, peak + jnp.log(total)


def backward_block(query, grad, grad_turned, mixed_turned, lse, pieces, qpos, start, causal):
    row_sum = jnp.sum(grad_turned.astype(F32) * mixed_turned.astype(F32), axis=0, keepdims=True)
    grad_query = None
    grads = []
    for index, (pair, turned, first) in enumerate(pieces):
        scores = contract(pair, query, 1, 1)
        kpos = first + lax.broadcasted_iota(jnp.int32, scores.shape, 0)
        allowed = kpos >= start
        if causal[index]:
            allowed = allowed & (kpos <= qpos)
        probs = jnp.where(allowed, jnp.exp(scores - lse), 0.0)
        grad_probs = contract(pair, grad, 1, 1)
        grad_scores = (probs * (grad_probs - row_sum)).astype(BF)
        grads.append(matmul(grad_scores, query) + matmul(probs.astype(BF), grad))
        part = matmul(turned[:HDIM], grad_scores)
        grad_query = part if grad_query is None else grad_query + part
    return grad_query * SCALE, grads


def dense_forward_kernel(place_ref, q_ref, kv_ref, start_ref, out_ref, turned_ref, lse_ref):
    group, _, half, _ = q_ref.shape
    ring, _, _, block, _ = kv_ref.shape
    place = place_ref[0]
    span = ring * block
    pieces = []
    for g in range(group):
        pair = kv_ref[:, g, 0].reshape(span, 2 * HDIM)
        pieces.append((pair, pair.T, g * span))
    for g in range(group):
        query = unpack_low(q_ref[g, 0]) * jnp.asarray(SCALE, BF)
        qpos = g * span + place * block + lax.broadcasted_iota(jnp.int32, (1, block), 1)
        mixed, lse = forward_block(
            query, pieces[: g + 1], qpos, start_ref[0, g], [i == g for i in range(g + 1)]
        )
        turned_ref[0, g] = mixed.astype(BF)
        lse_ref[0, g] = lse
        out_ref[g, 0] = pack_turned(mixed).astype(BF)


def dense_forward(place, q, kv, start):
    group, seqs, half, lanes = q.shape
    ring, _, _, block, _ = kv.shape
    grid = pltpu.PrefetchScalarGridSpec(
        num_scalar_prefetch=1,
        grid=(seqs,),
        in_specs=[
            pl.BlockSpec((group, 1, half, lanes), lambda s, _: (0, s, 0, 0)),
            pl.BlockSpec((ring, group, 1, block, lanes), lambda s, _: (0, 0, s, 0, 0)),
            pl.BlockSpec((1, group, 1, block), lambda s, _: (s, 0, 0, 0)),
        ],
        out_specs=[
            pl.BlockSpec((group, 1, half, lanes), lambda s, _: (0, s, 0, 0)),
            pl.BlockSpec((1, group, HDIM, block), lambda s, _: (s, 0, 0, 0)),
            pl.BlockSpec((1, group, 1, block), lambda s, _: (s, 0, 0, 0)),
        ],
    )
    return pl.pallas_call(
        dense_forward_kernel,
        grid_spec=grid,
        out_shape=[
            jax.ShapeDtypeStruct(q.shape, BF),
            jax.ShapeDtypeStruct((seqs, group, HDIM, block), BF),
            jax.ShapeDtypeStruct((seqs, group, 1, block), F32),
        ],
        compiler_params=pltpu.CompilerParams(vmem_limit_bytes=VMEM),
        name="dense_attention",
    )(place, q, kv, start)


def dense_backward_kernel(
    place_ref, q_ref, g_ref, kv_ref, start_ref, turned_ref, lse_ref, dq_ref, dkv_ref, acc_ref
):
    group, _, half, _ = q_ref.shape
    ring, _, _, block, _ = kv_ref.shape
    place = place_ref[0]
    span = ring * block
    pieces = []
    for g in range(group):
        pair = kv_ref[:, g, 0].reshape(span, 2 * HDIM)
        pieces.append((pair, pair.T, g * span))
    for g in reversed(range(group)):
        query = unpack_low(q_ref[g, 0]) * jnp.asarray(SCALE, BF)
        packed = g_ref[g, 0]
        grad = unpack_high(packed)
        flat = packed.T
        grad_turned = jnp.concatenate([flat[:HDIM], flat[HDIM:]], axis=1)
        qpos = g * span + place * block + lax.broadcasted_iota(jnp.int32, (1, block), 1)
        grad_query, grads = backward_block(
            query,
            grad,
            grad_turned,
            turned_ref[0, g],
            lse_ref[0, g],
            pieces[: g + 1],
            qpos,
            start_ref[0, g],
            [i == g for i in range(g + 1)],
        )
        dq_ref[g, 0] = pack_turned(grad_query).astype(BF)
        for i, item in enumerate(grads):
            if g == group - 1:
                acc_ref[i] = item
            else:
                acc_ref[i] += item
    for g in range(group):
        dkv_ref[:, g, 0] = acc_ref[g].reshape(ring, block, 2 * HDIM).astype(BF)


def dense_backward(place, q, grad, kv, start, turned, lse):
    group, seqs, half, lanes = q.shape
    ring, _, _, block, _ = kv.shape
    grid = pltpu.PrefetchScalarGridSpec(
        num_scalar_prefetch=1,
        grid=(seqs,),
        in_specs=[
            pl.BlockSpec((group, 1, half, lanes), lambda s, _: (0, s, 0, 0)),
            pl.BlockSpec((group, 1, half, lanes), lambda s, _: (0, s, 0, 0)),
            pl.BlockSpec((ring, group, 1, block, lanes), lambda s, _: (0, 0, s, 0, 0)),
            pl.BlockSpec((1, group, 1, block), lambda s, _: (s, 0, 0, 0)),
            pl.BlockSpec((1, group, HDIM, block), lambda s, _: (s, 0, 0, 0)),
            pl.BlockSpec((1, group, 1, block), lambda s, _: (s, 0, 0, 0)),
        ],
        out_specs=[
            pl.BlockSpec((group, 1, half, lanes), lambda s, _: (0, s, 0, 0)),
            pl.BlockSpec((ring, group, 1, block, lanes), lambda s, _: (0, 0, s, 0, 0)),
        ],
        scratch_shapes=[pltpu.VMEM((group, ring * block, lanes), F32)],
    )
    return pl.pallas_call(
        dense_backward_kernel,
        grid_spec=grid,
        out_shape=[
            jax.ShapeDtypeStruct(q.shape, BF),
            jax.ShapeDtypeStruct(kv.shape, BF),
        ],
        compiler_params=pltpu.CompilerParams(vmem_limit_bytes=VMEM),
        name="dense_attention_grad",
    )(place, q, grad, kv, start, turned, lse)


def inverse_rms(value):
    return lax.rsqrt(jnp.mean(value * value, axis=-1, keepdims=True) + EPS)


def gelu_terms(value):
    scale = 0.7978845608028654
    square = value * value
    bend = jnp.tanh(scale * (value + 0.044715 * square * value))
    half = 0.5 * (1.0 + bend)
    slope = half + 0.5 * value * (1.0 - bend * bend) * scale * (1.0 + 0.134145 * square)
    return value * half, slope


def side_by_side(blocks):
    return jnp.concatenate(blocks, axis=1)


def all_columns(copies, value, dst):
    section = copies.lines.place("section")
    dst[section] = value
    wait(copies.swap("section", lambda peer: dst.at[section], lambda me: dst.at[me]))
    return side_by_side([dst[i] for i in range(dst.shape[0])])


class ColumnSum:
    @staticmethod
    def count(sections, scalars):
        return (sections - 1) * (2 if scalars else 1)

    @staticmethod
    def scratch(sections, rows, width, scalars):
        buffers = [pltpu.VMEM((rows, sections * width), BF), pltpu.VMEM((sections, rows, width), BF)]
        if scalars:
            buffers += [pltpu.VMEM((rows, 128), F32), pltpu.VMEM((sections, rows, 128), F32)]
        return buffers

    def __init__(self, copies, buffers):
        self.copies, self.buffers = copies, buffers

    def start(self, value, scalars=None):
        buf, got = self.buffers[:2]
        width = got.shape[2]
        section = self.copies.lines.place("section")
        buf[...] = value.astype(BF)
        self.pending = self.copies.swap(
            "section", lambda peer: buf.at[:, span(peer, width)], lambda me: got.at[me]
        )
        got[section] = buf[:, span(section, width)]
        if scalars is not None:
            sbuf, sgot = self.buffers[2:]
            sbuf[...] = jnp.broadcast_to(scalars, sbuf.shape)
            self.pending += self.copies.swap("section", lambda peer: sbuf, lambda me: sgot.at[me])
            sgot[section] = sbuf[...]

    def finish(self):
        wait(self.pending)
        total = sum_places(self.buffers[1])
        if len(self.buffers) == 2:
            return total
        return total, sum_places(self.buffers[3])[:, :1]


def routed_slots(lines, sel):
    group, ring = lines.sizes["z"], lines.sizes["core"]
    index = lax.broadcasted_iota(jnp.int32, (1, group * sel), 1)
    return (index // sel) * (ring * sel) + lines.place("core") * sel + lax.rem(index, sel)


def routed_sequence(lines, heads_ref, pairs_ref, q, sel):
    group, ring = lines.sizes["z"], lines.sizes["core"]
    lanes = 2 * HDIM
    at = slice(q * sel, (q + 1) * sel)
    query = jnp.concatenate([heads_ref[g, at, :lanes] for g in range(group)], axis=0)
    pair = jnp.concatenate([pairs_ref[r, g, at] for g in range(group) for r in range(ring)], axis=0)
    return query * jnp.asarray(SCALE, BF), pair


def routed_enter(lines, ident, source, chosen, start, gain, qkv_w, sel):
    seqs, rows, wide = source.shape
    sections, group, ring = (lines.sizes[k] for k in ("section", "z", "core"))
    dp = group * ring
    part = wide // 2
    width = sections * part
    slots = seqs * sel
    lanes = 2 * HDIM

    def kernel(
        source_ref,
        column_ref,
        start_ref,
        gain_ref,
        qkv_ref,
        value_ref,
        grad_ref,
        normed_ref,
        heads_got,
        pairs_all,
        turned_ref,
        lse_ref,
        mixed_ref,
        send,
        recv,
        picked_buf,
        picked_got,
        slots_buf,
        slots_got,
        rows_got,
        heads_buf,
        out_buf,
        out_got,
        mixed_all,
    ):
        copies = Copies(lines, send, recv)
        section, zplace, place = (lines.place(k) for k in ("section", "z", "core"))
        rank = lax.axis_index("dp")
        copies.greet(["section", "z", "core"])
        position = rank * rows + lax.broadcasted_iota(jnp.int32, (1, rows), 1)
        for q in range(seqs):
            table = (column_ref[q] == position).astype(F32).astype(BF)
            found = matmul(table, source_ref[q]).astype(BF)
            for d in range(dp):
                picked_buf[d % ring, d // ring, q * sel : (q + 1) * sel] = found[d * sel : (d + 1) * sel]
        wait(copies.swap("core", lambda peer: picked_buf.at[peer], lambda me: picked_got.at[me]))
        total = picked_buf[place].astype(F32)
        for peer in lines.peers("core"):
            total = total + picked_got[peer].astype(F32)
        slots_buf[...] = total.astype(BF)
        pending = copies.swap("z", lambda peer: slots_buf.at[peer], lambda me: slots_got.at[me])
        slots_got[zplace] = slots_buf[zplace]
        wait(pending)
        rows_got[section] = sum_places(slots_got).astype(BF)
        wait(copies.swap("section", lambda peer: rows_got.at[section], lambda me: rows_got.at[me]))
        low = side_by_side([rows_got[i, :, :part] for i in range(sections)])
        value_ref[...] = low
        grad_ref[...] = side_by_side([rows_got[i, :, part:] for i in range(sections)])
        picked = low.astype(F32)

        normed = (picked * inverse_rms(picked) * gain_ref[...]).astype(BF)
        normed_ref[...] = normed
        qkv = matmul(normed, qkv_ref[...]).astype(BF)
        blank = jnp.zeros((slots, HDIM), BF)
        for g in range(group):
            query = qkv[:, 2 * part + g * HDIM : 2 * part + (g + 1) * HDIM]
            heads_buf[g, :, :lanes] = side_by_side([query, blank])
            heads_buf[g, :, lanes:] = qkv[:, g * lanes : (g + 1) * lanes]
        pending = copies.swap("z", lambda peer: heads_buf.at[peer], lambda me: heads_got.at[me])
        heads_got[zplace] = heads_buf[zplace]
        wait(pending)
        pairs_all[place] = heads_got[:, :, lanes:]
        wait(copies.swap("core", lambda peer: pairs_all.at[place], lambda me: pairs_all.at[me]))
        for q in range(seqs):
            query, pair = routed_sequence(lines, heads_got, pairs_all, q, sel)
            turned, lse = forward_block(
                query, [(pair, pair.T, 0)], routed_slots(lines, sel), start_ref[q], [True]
            )
            turned_ref[q] = turned.astype(BF)
            lse_ref[q] = lse
            upright = jnp.concatenate([turned, jnp.zeros_like(turned)], axis=0).T.astype(BF)
            for g in range(group):
                out_buf[g, q * sel : (q + 1) * sel] = upright[g * sel : (g + 1) * sel]
        pending = copies.swap("z", lambda peer: out_buf.at[peer], lambda me: out_got.at[me])
        out_got[zplace] = out_buf[zplace]
        wait(pending)
        own = side_by_side([out_got[g, :, :HDIM] for g in range(group)])
        mixed_ref[...] = all_columns(copies, own, mixed_all)

    vmem = pltpu.VMEM
    queries = group * sel
    return communicate(
        kernel,
        ident,
        [source, chosen[:, :, None], start, gain, qkv_w],
        [
            ((slots, width), BF),
            ((slots, width), BF),
            ((slots, width), BF),
            ((group, slots, 2 * lanes), BF),
            ((ring, group, slots, lanes), BF),
            ((seqs, HDIM, queries), BF),
            ((seqs, 1, queries), F32),
            ((slots, width), BF),
        ],
        semaphores(2 * (ring - 1) + 3 * (group - 1) + 2 * (sections - 1))
        + [
            vmem((ring, group, slots, wide), BF),
            vmem((ring, group, slots, wide), BF),
            vmem((group, slots, wide), BF),
            vmem((group, slots, wide), BF),
            vmem((sections, slots, wide), BF),
            vmem((group, slots, 2 * lanes), BF),
            vmem((group, slots, lanes), BF),
            vmem((group, slots, lanes), BF),
            vmem((sections, slots, part), BF),
        ],
        "routed_enter",
    )


def routed_feed(lines, ident, picked, grad_sent, mixed, gains, weights, part):
    sections = lines.sizes["section"]
    slots, width = picked.shape
    hidden_size = weights.shape[1] - part - width

    def kernel(
        value_ref,
        grad_ref,
        mixed_ref,
        gains_ref,
        weights_ref,
        normed_ref,
        dpre_ref,
        hidden_ref,
        fed_ref,
        middle_ref,
        attended_ref,
        sent_ref,
        logit_ref,
        vectors_ref,
        send,
        recv,
        keep_ref,
        attended_all,
        *buffers,
    ):
        copies = Copies(lines, send, recv)
        copies.greet(["section"])
        own = span(lines.place("section"), part)
        out_w = weights_ref.at[:, :part]
        expand_w = weights_ref.at[:, part : part + hidden_size]
        shrink_w = weights_ref.at[:, part + hidden_size :]
        gain, router = gains_ref[0:1, :], gains_ref[1:2, :]
        attended_own = matmul(mixed_ref[...], out_w[...]).astype(BF)
        attended = all_columns(copies, attended_own, attended_all).astype(F32)
        picked = value_ref[...].astype(F32)
        grad_sent = grad_ref[...].astype(F32)
        middle = picked + attended
        inv = inverse_rms(middle)
        normed = (middle * inv * gain).astype(BF)
        normed_ref[...] = normed
        hidden, slope = gelu_terms(matmul(normed, expand_w[...]))
        hidden = hidden.astype(BF)
        hidden_ref[...] = hidden
        gate = jax.nn.sigmoid(jnp.sum(picked * router, axis=1, keepdims=True))
        grad_delta = gate * grad_sent
        fed_low = grad_delta.astype(BF)
        fed_ref[...] = fed_low
        grad_pre = (contract(fed_low, shrink_w[...], 1, 1) * slope).astype(BF)
        dpre_ref[...] = grad_pre
        grad_normed = contract(grad_pre, expand_w[...], 1, 1)
        scalar = jnp.sum(grad_normed * middle * gain, axis=1, keepdims=True)
        back = ColumnSum(copies, buffers[:4])
        back.start(grad_normed, scalar)
        fed_part = matmul(hidden, shrink_w[...])
        keep_ref[0] = middle
        keep_ref[1] = grad_delta
        keep_ref[2] = grad_sent
        own_attended = attended_own.astype(F32)
        gate_part = jnp.sum(grad_sent * fed_part, axis=1, keepdims=True) + jnp.sum(
            keep_ref[2, :, own] * own_attended, axis=1, keepdims=True
        )
        forth = ColumnSum(copies, buffers[4:])
        forth.start(fed_part, gate_part)
        middle_own, picked_own = keep_ref[0, :, own], value_ref[:, own].astype(F32)
        grad_normed, scalar = back.finish()
        vectors_ref[...] = jnp.zeros_like(vectors_ref)
        vectors_ref[0:1, :] = jnp.sum(grad_normed * middle_own * inv, axis=0, keepdims=True)
        grad_middle = inv * (grad_normed * gains_ref[0:1, own]) - middle_own * (inv * inv * inv) * (
            scalar * (1.0 / width)
        )
        middle_ref[...] = grad_middle
        attended_ref[...] = (grad_middle + keep_ref[1, :, own]).astype(BF)
        fed, grad_gate = forth.finish()
        sent_ref[...] = (gate * (own_attended + fed)).astype(BF)
        grad_logit = grad_gate * gate * (1.0 - gate)
        logit_ref[...] = jnp.broadcast_to(grad_logit, logit_ref.shape)
        vectors_ref[1:2, :] = jnp.sum(grad_logit * picked_own, axis=0, keepdims=True)

    return communicate(
        kernel,
        ident,
        [picked, grad_sent, mixed, gains, weights],
        [
            ((slots, width), BF),
            ((slots, hidden_size), BF),
            ((slots, hidden_size), BF),
            ((slots, width), BF),
            ((slots, part), F32),
            ((slots, part), BF),
            ((slots, part), BF),
            ((slots, 128), F32),
            ((8, part), F32),
        ],
        semaphores(sections - 1 + 2 * ColumnSum.count(sections, True))
        + [pltpu.VMEM((3, slots, width), F32), pltpu.VMEM((sections, slots, part), BF)]
        + 2 * ColumnSum.scratch(sections, slots, part, True),
        "routed_feed",
    )


def routed_leave(lines, ident, grad_attended, out_w, qkv_w, kept, start, picked, partial, gains, chosen, sel, rows):
    heads, pairs, turned, lse = kept
    grad_middle, grad_logit, sent = partial
    sections, group, ring = (lines.sizes[k] for k in ("section", "z", "core"))
    slots, width = picked.shape
    part = width // sections
    seqs = chosen.shape[0]
    lanes = 2 * HDIM

    def kernel(
        attended_ref,
        out_ref,
        qkv_ref,
        heads_ref,
        pairs_ref,
        turned_ref,
        lse_ref,
        start_ref,
        value_ref,
        middle_ref,
        logit_ref,
        sent_ref,
        gains_ref,
        row_ref,
        returned_ref,
        added_ref,
        dqkv_ref,
        vectors_ref,
        send,
        recv,
        grad_buf,
        grad_got,
        turn_buf,
        turn_got,
        back_buf,
        back_got,
        final_buf,
        final_got,
        final_all,
        *buffers,
    ):
        copies = Copies(lines, send, recv)
        section, zplace, place = (lines.place(k) for k in ("section", "z", "core"))
        rank = lax.axis_index("dp")
        copies.greet(["section", "z", "core"])
        own = span(section, part)
        outer = ColumnSum(copies, buffers[:2])
        outer.start(contract(attended_ref[...], out_ref[...], 1, 1))
        grad_mixed = outer.finish().astype(BF)
        blank = jnp.zeros((slots, HDIM), BF)
        for g in range(group):
            grad_buf[g] = side_by_side([blank, grad_mixed[:, g * HDIM : (g + 1) * HDIM]])
        pending = copies.swap("z", lambda peer: grad_buf.at[peer], lambda me: grad_got.at[me])
        grad_got[zplace] = grad_buf[zplace]
        wait(pending)
        for q in range(seqs):
            at = slice(q * sel, (q + 1) * sel)
            query, pair = routed_sequence(lines, heads_ref, pairs_ref, q, sel)
            grad = jnp.concatenate([grad_got[g, at] for g in range(group)], axis=0)
            grad_query, grad_pairs = backward_block(
                query,
                grad,
                grad.T[HDIM:],
                turned_ref[q],
                lse_ref[q],
                [(pair, pair.T, 0)],
                routed_slots(lines, sel),
                start_ref[q],
                [True],
            )
            upright = jnp.concatenate([grad_query, jnp.zeros_like(grad_query)], axis=0).T.astype(BF)
            low = grad_pairs[0].astype(BF)
            for g in range(group):
                back_buf[g, at, :lanes] = upright[g * sel : (g + 1) * sel]
                for r in range(ring):
                    first = (g * ring + r) * sel
                    turn_buf[r, g, at] = low[first : first + sel]
        wait(copies.swap("core", lambda peer: turn_buf.at[peer], lambda me: turn_got.at[me]))
        total = turn_buf[place].astype(F32)
        for peer in lines.peers("core"):
            total = total + turn_got[peer].astype(F32)
        back_buf[:, :, lanes:] = total.astype(BF)
        pending = copies.swap("z", lambda peer: back_buf.at[peer], lambda me: back_got.at[me])
        back_got[zplace] = back_buf[zplace]
        wait(pending)
        grad_qkv = side_by_side(
            [back_got[g, :, lanes:] for g in range(group)] + [back_got[g, :, :HDIM] for g in range(group)]
        )
        dqkv_ref[...] = grad_qkv
        grad_normed = contract(grad_qkv, qkv_ref[...], 1, 1)
        picked = value_ref[...].astype(F32)
        inv = inverse_rms(picked)
        inner = ColumnSum(copies, buffers[2:])
        inner.start(grad_normed, jnp.sum(grad_normed * picked * gains_ref[0:1, :], axis=1, keepdims=True))
        picked_own = value_ref[:, own].astype(F32)
        grad_normed, scalar = inner.finish()
        vectors_ref[...] = jnp.zeros_like(vectors_ref)
        vectors_ref[0:1, :] = jnp.sum(grad_normed * picked_own * inv, axis=0, keepdims=True)
        grad_in = inv * (grad_normed * gains_ref[0:1, own]) - picked_own * (inv * inv * inv) * (scalar * (1.0 / width))
        grad_in = middle_ref[...] + grad_in + logit_ref[:, :1] * gains_ref[1:2, own]

        final_buf[:, :part] = grad_in.astype(BF)
        final_buf[:, part:] = sent_ref[...]
        along = copies.swap("z", lambda peer: final_buf, lambda me: final_got.at[me])
        final_got[zplace] = final_buf[...]

        def hand_on(i):
            view = final_got.at[i, :, pl.ds(0, part)]
            dst = final_all.at[place, i, :, own]
            dst[...] = view[...]
            final_all[place, i, :, width:] = final_got[i, :, part:]
            return copies.swap("section", lambda peer: view, lambda me: dst)

        spread = hand_on(zplace)
        for step in range(group - 1, 0, -1):
            along[group - 1 - step].wait_recv()
            spread += hand_on(lax.rem(zplace + step, group))
        for copy in along:
            copy.wait_send()
        wait(spread)
        wait(copies.swap("core", lambda peer: final_all.at[place], lambda me: final_all.at[me]))
        slot_of = rank * rows + lax.broadcasted_iota(jnp.int32, (rows, 1), 0)
        for q in range(seqs):
            at = slice(q * sel, (q + 1) * sel)
            table = (row_ref[q] == slot_of).astype(F32).astype(BF)
            found = jnp.concatenate([final_all[r, g, at] for g in range(group) for r in range(ring)], axis=0)
            placed = matmul(table, found).astype(BF)
            returned_ref[q] = placed[:, :width]
            added_ref[q] = placed[:, width:]

    vmem = pltpu.VMEM
    return communicate(
        kernel,
        ident,
        [
            grad_attended,
            out_w,
            qkv_w,
            heads,
            pairs,
            turned,
            lse,
            start,
            picked,
            grad_middle,
            grad_logit,
            sent,
            gains,
            chosen[:, None, :],
        ],
        [
            ((seqs, rows, width), BF),
            ((seqs, rows, part), BF),
            ((slots, 3 * part), BF),
            ((8, part), F32),
        ],
        semaphores(
            2 * (ring - 1)
            + 3 * (group - 1)
            + ColumnSum.count(sections, False)
            + ColumnSum.count(sections, True)
            + group * (sections - 1)
        )
        + [
            vmem((group, slots, lanes), BF),
            vmem((group, slots, lanes), BF),
            vmem((ring, group, slots, lanes), BF),
            vmem((ring, group, slots, lanes), BF),
            vmem((group, slots, 2 * lanes), BF),
            vmem((group, slots, 2 * lanes), BF),
            vmem((slots, 2 * part), BF),
            vmem((group, slots, 2 * part), BF),
            vmem((ring, group, slots, width + part), BF),
        ]
        + ColumnSum.scratch(sections, slots, part, False)
        + ColumnSum.scratch(sections, slots, part, True),
        "routed_leave",
    )


def on_device(
    stream_in,
    segment_ids,
    chosen_rows,
    cotangent,
    dense_prenorm,
    dense_query,
    dense_keys,
    dense_values,
    dense_output,
    dense_midnorm,
    dense_expand,
    dense_shrink,
    routed_prenorm,
    routed_query,
    routed_keys,
    routed_values,
    routed_output,
    routed_midnorm,
    routed_expand,
    routed_shrink,
    router_weight,
):
    sections, dp = lax.axis_size("section"), lax.axis_size("dp")
    section, rank = lax.axis_index("section"), lax.axis_index("dp")
    seqs, rows, width = stream_in.shape
    tokens = seqs * rows
    part = width // sections
    group = HEADS // sections
    ring = dp // group
    total_sel = chosen_rows.shape[1]
    sel = total_sel // dp
    place = lax.rem(rank, ring).astype(jnp.int32).reshape(1)
    lines = Lines(sections, dp, group)
    lanes = 2 * HDIM

    def own_columns(value):
        return lax.dynamic_slice_in_dim(value, section * part, part, value.ndim - 1)

    def own_hidden(expand, shrink):
        inner = expand.shape[1] // dp
        share = inner // sections
        cut = expand.reshape(expand.shape[0], dp, sections, share)
        cut = lax.dynamic_index_in_dim(cut, section, 2, keepdims=False).reshape(expand.shape[0], dp * share)
        return cut, lax.dynamic_slice_in_dim(shrink, section * share, share, 0)

    def own_attention(query, keys, values):
        local = query.shape[0]
        pair = jnp.stack(
            [own_columns(keys).reshape(local, group, HDIM), own_columns(values).reshape(local, group, HDIM)],
            axis=2,
        ).reshape(local, 2 * part)
        return jnp.concatenate([pair, own_columns(query)], axis=1)

    gains = jnp.stack([dense_prenorm, dense_midnorm, routed_prenorm, routed_midnorm, router_weight])
    gains = jnp.pad(gains, ((0, 16 - gains.shape[0]), (0, 0)))
    first = own_attention(dense_query, dense_keys, dense_values)
    dense_qkv, gains = gather_rows(lines, 1, [first, gains], "first_weights")
    dense_qkv = dense_qkv.reshape(width, 3 * part)
    gains = jnp.transpose(gains, (1, 0, 2)).reshape(16, width).astype(F32)
    gain_pre, gain_mid = gains[0], gains[1]

    def gather(value):
        return lax.all_gather(value, "dp", axis=0, tiled=True)

    def after(value, other):
        return lax.optimization_barrier((value, other))[0]

    expand_cut, shrink_cut = own_hidden(dense_expand, dense_shrink)
    hidden_size = expand_cut.shape[1]
    rest = gather(jnp.concatenate([own_columns(dense_output), expand_cut, shrink_cut], axis=1))
    dense_out, dense_exp, dense_shr = (
        rest[:, :part],
        rest[:, part : part + hidden_size],
        rest[:, part + hidden_size :],
    )
    routed_qkv = gather(after(own_attention(routed_query, routed_keys, routed_values), dense_qkv))
    expand_cut, shrink_cut = own_hidden(routed_expand, routed_shrink)
    routed_rest = jnp.concatenate([own_columns(routed_output), expand_cut, shrink_cut], axis=1)

    first_of = jnp.sum(
        (segment_ids[:, None, :] < jnp.arange(DOCS, dtype=jnp.int32)[None, :, None]).astype(jnp.int32), axis=2
    )

    def document(positions):
        shape = (seqs,) + (1,) * (positions.ndim - 1)
        found = jnp.zeros(positions.shape, jnp.int32)
        for c in range(1, DOCS):
            found = found + (positions >= first_of[:, c].reshape(shape)).astype(jnp.int32)
        return found

    def pick(table, index):
        shape = (seqs,) + (1,) * (index.ndim - 1)
        out = jnp.zeros(index.shape, jnp.int32)
        for c in range(DOCS):
            out = jnp.where(index == c, table[:, c].reshape(shape), out)
        return out

    blocks = jnp.arange(group, dtype=jnp.int32) * ring + place[0]
    attended_pos = blocks[:, None] * rows + jnp.arange(rows, dtype=jnp.int32)[None, :]
    attended_pos = jnp.broadcast_to(attended_pos[None], (seqs, group, rows))
    start = pick(first_of, document(attended_pos))[:, :, None, :]
    chosen_doc = document(chosen_rows)
    first_slot = jnp.sum(
        (chosen_doc[:, None, :] < jnp.arange(DOCS, dtype=jnp.int32)[None, :, None]).astype(jnp.int32), axis=2
    )
    chosen_start = pick(first_slot, chosen_doc).reshape(seqs, group, ring, sel)
    routed_start = lax.dynamic_index_in_dim(chosen_start, place[0], 2, keepdims=False)
    routed_start = routed_start.reshape(seqs, 1, group * sel)

    def pack(value):
        value = value.reshape(seqs, 2, rows // 2, group, HDIM)
        return jnp.transpose(value, (0, 2, 3, 1, 4)).reshape(tokens // 2, 2 * part)

    def unpack(value):
        value = value.reshape(seqs, rows // 2, group, 2, HDIM)
        return jnp.transpose(value, (0, 3, 1, 2, 4)).reshape(tokens, part)

    value = stream_in.reshape(tokens, width).astype(F32)
    grad_top = cotangent.reshape(tokens, width)
    inv_in = inverse_rms(value)
    normed = (value * inv_in * gain_pre).astype(BF)
    qkv = matmul(normed, dense_qkv).astype(BF)
    pairs, queries = dense_to_heads(
        lines, 2, qkv[:, : 2 * part], pack(qkv[:, 2 * part :]), "dense_to_heads"
    )
    routed_rest = gather(after(routed_rest, queries))
    queries = queries.reshape(group, seqs, rows // 2, lanes)
    pairs = pairs.reshape(ring, group, seqs, rows, lanes)
    mixed, mixed_turned, lse = dense_forward(place, queries, pairs, start)
    packed = (tokens // 2, group * lanes)
    (mixed,) = swap_blocks(
        lines, 3, "z", [mixed.reshape(group, tokens // 2, lanes)], [(packed, BF)], [(0, slot, 0, columns(lanes))],
        "dense_mixed",
    )
    mixed = gather_columns(lines, 4, unpack(mixed), "dense_mixed_columns")
    attended = gather_columns(lines, 5, matmul(mixed, dense_out).astype(BF), "dense_attended")
    middle_value = value + attended.astype(F32)
    inv_mid = inverse_rms(middle_value)
    normed_mid = (middle_value * inv_mid * gain_mid).astype(BF)
    hidden_pre = matmul(normed_mid, dense_exp)
    hidden = jax.nn.gelu(hidden_pre).astype(BF)
    fed = scatter_columns(lines, 6, matmul(hidden, dense_shr).astype(BF), None, "dense_fed")
    after_dense = own_columns(middle_value) + fed

    def outer(left, right):
        return contract(left, right, 0, 0).astype(BF)

    def vector_columns(vectors):
        wide = jnp.zeros((width, 128), F32)
        stacked = jnp.pad(jnp.stack(vectors, axis=1), ((0, 0), (0, 128 - len(vectors))))
        return lax.dynamic_update_slice(wide, stacked, (section * part, 0)).astype(BF)

    def reduce_dp(value):
        return lax.psum_scatter(value, "dp", scatter_dimension=0, tiled=True)

    source = jnp.concatenate([after_dense.astype(BF), own_columns(grad_top)], axis=1)
    r_picked, r_grad_sent, r_normed, r_heads, r_pairs, r_turned, r_lse, r_mixed = routed_enter(
        lines, 7, source.reshape(seqs, rows, 2 * part), chosen_rows, routed_start, gains[2:3], routed_qkv, sel
    )
    (
        r_normed_mid,
        r_grad_pre,
        r_hidden,
        r_fed_low,
        r_grad_middle,
        r_grad_attended,
        r_sent,
        r_logit,
        r_vectors,
    ) = routed_feed(lines, 13, r_picked, r_grad_sent, r_mixed, gains[3:5], routed_rest, part)
    routed_grads = jnp.concatenate(
        [
            outer(r_normed_mid, r_grad_pre),
            outer(r_hidden, r_fed_low),
            vector_columns([r_vectors[0], r_vectors[1]]),
        ],
        axis=1,
    )
    routed_shard = reduce_dp(routed_grads)
    r_grad_attended = after(r_grad_attended, routed_grads)
    returned, added, r_grad_qkv, r_vectors = routed_leave(
        lines,
        14,
        r_grad_attended,
        routed_rest[:, :part],
        routed_qkv,
        (r_heads, r_pairs, r_turned, r_lse),
        routed_start,
        r_picked,
        (r_grad_middle, r_logit, r_sent),
        jnp.concatenate([gains[2:3], gains[4:5]], axis=0),
        chosen_rows,
        sel,
        rows,
    )
    routed_shard_in = reduce_dp(
        jnp.concatenate(
            [outer(r_normed, r_grad_qkv), outer(r_mixed, r_grad_attended), vector_columns([r_vectors[0]])], axis=1
        )
    )
    stream_out = (after_dense + added.reshape(tokens, part).astype(F32)).astype(BF).reshape(seqs, rows, part)

    grad_after = grad_top.astype(F32) + returned.reshape(tokens, width).astype(F32)
    fed_low = grad_after.astype(BF)
    _, gelu_pull = jax.vjp(jax.nn.gelu, hidden_pre)
    grad_pre = gelu_pull(contract(fed_low, dense_shr, 1, 1))[0].astype(BF)
    grad_normed = contract(grad_pre, dense_exp, 1, 1)
    scalar = jnp.sum(grad_normed * middle_value * gain_mid, axis=1)
    grad_normed, scalar = scatter_columns(lines, 8, grad_normed.astype(BF), scalar, "dense_back_mid")
    middle_own = own_columns(middle_value)
    grad_gain_mid = jnp.sum(grad_normed * middle_own * inv_mid, axis=0)
    grad_middle = (
        inv_mid * (grad_normed * own_columns(gain_mid))
        - middle_own * (inv_mid * inv_mid * inv_mid) * (scalar * (1.0 / width))[:, None]
        + own_columns(grad_after)
    )
    grad_attended = grad_middle.astype(BF)
    dense_grads = jnp.concatenate(
        [outer(normed_mid, grad_pre), outer(hidden, fed_low), vector_columns([grad_gain_mid])], axis=1
    )
    dense_shard = reduce_dp(dense_grads)
    grad_mixed = scatter_columns(
        lines, 9, contract(grad_attended, dense_out, 1, 1).astype(BF), None, "dense_back_mixed"
    ).astype(BF)
    dense_shard_out = reduce_dp(outer(mixed, grad_attended))
    (grad_heads,) = swap_blocks(
        lines, 10, "z", [pack(grad_mixed)], [((group, tokens // 2, lanes), BF)], [(0, columns(lanes), 0, slot)],
        "dense_grad_to_heads",
    )
    dq, dkv = dense_backward(
        place,
        queries,
        grad_heads.reshape(group, seqs, rows // 2, lanes),
        pairs,
        start,
        mixed_turned,
        lse,
    )
    dkv, dq, (routed_all, routed_all_in) = dense_from_heads(
        lines,
        11,
        dkv.reshape(ring, group, tokens, lanes),
        dq.reshape(group, tokens // 2, lanes),
        [routed_shard, routed_shard_in],
        "dense_from_heads",
    )
    grad_qkv = jnp.concatenate([dkv, unpack(dq)], axis=1)
    grad_normed = contract(grad_qkv, dense_qkv, 1, 1)
    scalar = jnp.sum(grad_normed * value * gain_pre, axis=1)
    value_own = own_columns(value)
    grad_normed, scalar, grad_gain_pre, dense_all_in, (dense_all, dense_all_out) = dense_finish(
        lines,
        12,
        grad_normed.astype(BF),
        scalar,
        value_own * inv_in,
        outer(normed, grad_qkv),
        [dense_shard, dense_shard_out],
        "dense_finish",
    )
    grad_in = (
        inv_in * (grad_normed * own_columns(gain_pre))
        - value_own * (inv_in * inv_in * inv_in) * (scalar * (1.0 / width))[:, None]
    )
    stream_grad = (grad_middle + grad_in).astype(BF).reshape(seqs, rows, part)

    share = hidden_size // dp
    local = width // dp
    middle_at = hidden_size + width
    r_exp, r_shr, r_mid, r_keys, r_values, r_query, r_out, r_pre = assemble(
        [
            ("hidden", routed_all, 0, hidden_size),
            ("stack", routed_all, hidden_size, width),
            ("sum", routed_all, middle_at, 128),
            ("pair", routed_all_in, 0, 2 * part),
            ("columns", routed_all_in, 2 * part, part),
            ("columns", routed_all_in, 3 * part, part),
            ("sum", routed_all_in, 4 * part, 128),
        ],
        share,
        "routed_places",
    )
    d_exp, d_shr, d_mid, d_keys, d_values, d_query, d_out = assemble(
        [
            ("hidden", dense_all, 0, hidden_size),
            ("stack", dense_all, hidden_size, width),
            ("sum", dense_all, middle_at, 128),
            ("pair", dense_all_in, 0, 2 * part),
            ("columns", dense_all_in, 2 * part, part),
            ("columns", dense_all_out, 0, part),
        ],
        share,
        "dense_places",
    )
    d_pre = lax.dynamic_slice_in_dim(grad_gain_pre, rank * local, local)
    d_shr = d_shr.reshape(sections * share, width)
    r_shr = r_shr.reshape(sections * share, width)
    return (
        (stream_out, stream_grad)
        + (d_pre, d_query, d_keys, d_values, d_out, d_mid[:, 0], d_exp, d_shr)
        + (r_pre[:, 0], r_query, r_keys, r_values, r_out, r_mid[:, 0], r_exp, r_shr)
        + (r_mid[:, 1],)
    )


def solution(mesh):
    streams, row, vector, copied = P(None, "dp", None), P("dp", None), P("dp"), P()
    layer = (vector, row, row, row, row, vector, row, row)
    outs = (P(None, "dp", "section"),) * 2 + layer + layer + (vector,)
    return jax.shard_map(
        on_device,
        mesh=mesh,
        in_specs=(streams, copied, copied, streams) + layer + layer + (vector,),
        out_specs=outs,
        check_vma=False,
    )
```

```python
import functools

import jax
import jax.numpy as jnp
from jax import lax
from jax.experimental import pallas as pl
from jax.experimental.pallas import tpu as pltpu
from jax.sharding import PartitionSpec as P

HEADS = 16
HDIM = 64
DOCS = 8
EPS = 1e-06
NEG = -1e30
SCALE = HDIM ** (-0.5)
VMEM = 32 * 2**20
MESH = pl.DeviceIdType.MESH
BF = jnp.bfloat16
F32 = jnp.float32


def matmul(left, right):
    return jnp.dot(left, right, preferred_element_type=F32)


def contract(left, right, ldim, rdim):
    return lax.dot_general(left, right, (((ldim,), (rdim,)), ((), ())), preferred_element_type=F32)


class Lines:
    def __init__(self, sections, dp, group):
        self.sizes = {"section": sections, "z": group, "core": dp // group}
        self.ring = dp // group

    def place(self, kind):
        if kind == "section":
            return lax.axis_index("section")
        index = lax.axis_index("dp")
        return index // self.ring if kind == "z" else lax.rem(index, self.ring)

    def device(self, kind, place):
        if kind == "section":
            return {"section": place}
        index = lax.axis_index("dp")
        if kind == "z":
            return {"dp": place * self.ring + lax.rem(index, self.ring)}
        return {"dp": (index // self.ring) * self.ring + place}

    def peers(self, kind):
        size = self.sizes[kind]
        me = self.place(kind)
        return [lax.rem(me + step, size) for step in range(1, size)]


class Copies:
    def __init__(self, lines, send, recv):
        self.lines, self.send, self.recv, self.used = lines, send, recv, 0

    def greet(self, kinds):
        barrier = pltpu.get_barrier_semaphore()
        count = 0
        for kind in kinds:
            for peer in self.lines.peers(kind):
                pl.semaphore_signal(
                    barrier, inc=1, device_id=self.lines.device(kind, peer), device_id_type=MESH
                )
                count += 1
        pl.semaphore_wait(barrier, count)

    def start(self, kind, peer, src, dst):
        assert self.used < self.send.shape[0]
        copy = pltpu.make_async_remote_copy(
            src_ref=src,
            dst_ref=dst,
            send_sem=self.send.at[self.used],
            recv_sem=self.recv.at[self.used],
            device_id=self.lines.device(kind, peer),
            device_id_type=MESH,
        )
        self.used += 1
        copy.start()
        return copy

    def swap(self, kind, src, dst):
        me = self.lines.place(kind)
        return [self.start(kind, peer, src(peer), dst(me)) for peer in self.lines.peers(kind)]


def wait(copies):
    for copy in copies:
        copy.wait()


def semaphores(count):
    return [pltpu.SemaphoreType.DMA((count,)), pltpu.SemaphoreType.DMA((count,))]


def communicate(kernel, ident, arrays, shapes, scratch, name, limit=24 * 2**20, far=()):
    vmem = pl.BlockSpec(memory_space=pltpu.VMEM)
    place = pl.BlockSpec(memory_space=pl.ANY)
    return pl.pallas_call(
        kernel,
        out_shape=[jax.ShapeDtypeStruct(s, d) for s, d in shapes],
        in_specs=[place if i in far else vmem for i in range(len(arrays))],
        out_specs=[vmem] * len(shapes),
        scratch_shapes=scratch,
        compiler_params=pltpu.CompilerParams(
            collective_id=ident, has_side_effects=True, vmem_limit_bytes=limit
        ),
        name=name,
    )(*arrays)


def span(place, width):
    return pl.ds(pl.multiple_of(place * width, width), width)


def square(lines):
    me = lines.place("section")
    low, high = lax.rem(me, 2), me // 2
    return high * 2 + 1 - low, (1 - high) * 2 + low, (1 - high) * 2 + 1 - low


def pieces_of(rows):
    half = rows // 2
    return (2, half // 2) if half % 32 == 0 else (1, half)


class SquareGather:
    @staticmethod
    def count(rows):
        return 6 * pieces_of(rows)[0]

    def __init__(self, copies, x_ref, o_ref):
        self.copies, self.x_ref, self.o_ref = copies, x_ref, o_ref
        self.width = x_ref.shape[1]
        self.me = copies.lines.place("section")
        near, far, _ = square(copies.lines)
        pieces, step = pieces_of(x_ref.shape[0])
        half = x_ref.shape[0] // 2
        self.parts = [
            (pl.ds(h * half + j * step, step), one, two)
            for j in range(pieces)
            for h, (one, two) in enumerate(((near, far), (far, near)))
        ]

    def send(self, at, to):
        dst = self.o_ref.at[at, span(self.me, self.width)]
        return self.copies.start("section", to, self.x_ref.at[at], dst)

    def start(self):
        self.first = [self.send(at, one) for at, one, _ in self.parts]
        self.rest = [self.send(at, two) for at, _, two in self.parts]
        self.o_ref[:, span(self.me, self.width)] = self.x_ref[...]

    def forward(self):
        for (at, one, two), copy in zip(self.parts, self.first):
            copy.wait_recv()
            place = self.o_ref.at[at, span(one, self.width)]
            self.rest.append(self.copies.start("section", two, place, place))

    def finish(self):
        for copy in self.first:
            copy.wait_send()
        wait(self.rest)


class SquareScatter:
    @staticmethod
    def count(rows):
        return 6 * pieces_of(rows)[0]

    @staticmethod
    def scratch(rows, width):
        return [pltpu.VMEM((2, rows, width), BF), pltpu.VMEM((rows, width), BF), pltpu.VMEM((rows, width), BF)]

    def __init__(self, copies, x_ref, got, turn, last, pieces=None):
        self.copies, self.x_ref, self.got, self.turn, self.last = copies, x_ref, got, turn, last
        self.width = turn.shape[1]
        self.me = copies.lines.place("section")
        near, far, self.across = square(copies.lines)
        half = x_ref.shape[0] // 2
        pieces, step = pieces_of(x_ref.shape[0]) if pieces is None else (pieces, half // pieces)
        self.parts = [
            (pl.ds(h * half + j * step, step), one, two)
            for j in range(pieces)
            for h, (one, two) in enumerate(((near, far), (far, near)))
        ]

    def read(self, at, place):
        return self.x_ref[at, span(place, self.width)].astype(F32)

    def start(self):
        self.passed, self.kept = [], []
        for at, one, _ in self.parts:
            for place, k, out in ((self.across, 0, self.passed), (one, 1, self.kept)):
                src = self.x_ref.at[at, span(place, self.width)]
                out.append(self.copies.start("section", one, src, self.got.at[k, at]))

    def forward(self):
        self.second = []
        for (at, _, two), copy in zip(self.parts, self.passed):
            copy.wait_recv()
            self.turn[at] = (self.read(at, two) + self.got[0, at].astype(F32)).astype(BF)
            self.second.append(self.copies.start("section", two, self.turn.at[at], self.last.at[at]))

    def finish(self, o_ref):
        for i, (at, _, _) in enumerate(self.parts):
            self.kept[i].wait_recv()
            self.second[i].wait_recv()
            o_ref[at] = self.read(at, self.me) + self.got[1, at].astype(F32) + self.last[at].astype(F32)
        for copy in self.passed + self.kept + self.second:
            copy.wait_send()


def gather_columns(lines, ident, part, name):
    rows, width = part.shape

    def kernel(x_ref, o_ref, send, recv):
        copies = Copies(lines, send, recv)
        copies.greet(["section"])
        gather = SquareGather(copies, x_ref, o_ref)
        gather.start()
        gather.forward()
        gather.finish()

    shape = ((rows, lines.sizes["section"] * width), part.dtype)
    (out,) = communicate(kernel, ident, [part], [shape], semaphores(SquareGather.count(rows)), name)
    return out


def scalar_block(scalars):
    count = -(-scalars.shape[0] // 128)
    count += -count % 8
    return jnp.pad(scalars, (0, count * 128 - scalars.shape[0])).reshape(count, 128)


def sum_places(ref):
    total = ref[0].astype(F32)
    for i in range(1, ref.shape[0]):
        total = total + ref[i].astype(F32)
    return total


def scatter_columns(lines, ident, part, scalars, name):
    rows, full = part.shape
    sections = lines.sizes["section"]
    width = full // sections
    extra = scalars is not None
    arrays = [part]
    shapes = [((rows, width), F32)]
    scratch = semaphores(SquareScatter.count(rows) + sections - 1) + SquareScatter.scratch(rows, width)
    if extra:
        arrays.append(scalar_block(scalars))
        shapes.append((arrays[1].shape, F32))
        scratch.append(pltpu.VMEM((sections,) + arrays[1].shape, F32))

    def kernel(*refs):
        x_ref, refs = refs[0], refs[1:]
        if extra:
            e_ref, o_ref, eo_ref, send, recv, got, turn, last, e_got = refs
        else:
            o_ref, send, recv, got, turn, last = refs
        copies = Copies(lines, send, recv)
        copies.greet(["section"])
        scatter = SquareScatter(copies, x_ref, got, turn, last)
        scatter.start()
        if extra:
            others = copies.swap("section", lambda peer: e_ref, lambda place: e_got.at[place])
            e_got[lines.place("section")] = e_ref[...]
        scatter.forward()
        scatter.finish(o_ref)
        if extra:
            wait(others)
            eo_ref[...] = sum_places(e_got)

    got = communicate(kernel, ident, arrays, shapes, scratch, name)
    if not extra:
        return got[0]
    return got[0], got[1].reshape(-1)[:rows]


def gather_rows(lines, ident, parts, name):
    group, ring = lines.sizes["z"], lines.sizes["core"]
    dp = group * ring
    many = len(parts)

    def kernel(*refs):
        ins, outs, (send, recv) = refs[:many], refs[many : 2 * many], refs[2 * many :]
        copies = Copies(lines, send, recv)
        rank = lax.axis_index("dp")
        zplace, place = lines.place("z"), lines.place("core")
        copies.greet(["z", "core"])
        along, handed = [], []
        for x_ref, o_ref in zip(ins, outs):
            along.append(copies.swap("z", lambda peer: x_ref, lambda _: o_ref.at[rank]))
        for x_ref, o_ref in zip(ins, outs):
            handed += copies.swap("core", lambda peer: x_ref, lambda _: o_ref.at[rank])
            o_ref[rank] = x_ref[...]
        for step in range(group - 1, 0, -1):
            source = lax.rem(zplace + step, group) * ring + place
            for arrived, o_ref in zip(along, outs):
                arrived[group - 1 - step].wait_recv()
                handed += copies.swap("core", lambda peer: o_ref.at[source], lambda _: o_ref.at[source])
        for arrived in along:
            for copy in arrived:
                copy.wait_send()
        wait(handed)

    return communicate(
        kernel,
        ident,
        parts,
        [((dp,) + part.shape, part.dtype) for part in parts],
        semaphores(many * (group - 1 + group * (ring - 1))),
        name,
    )


def swap_blocks(lines, ident, kind, arrays, shapes, plan, name):
    size = lines.sizes[kind]

    def kernel(*refs):
        ins, outs = refs[: len(arrays)], refs[len(arrays) : len(arrays) + len(shapes)]
        copies = Copies(lines, *refs[len(arrays) + len(shapes) :])
        me = lines.place(kind)
        copies.greet([kind])
        pending = []
        for i, src, o, dst in plan:
            pending += copies.swap(
                kind, lambda peer: src(ins[i], peer), lambda place: dst(outs[o], place)
            )
        for i, src, o, dst in plan:
            view = dst(outs[o], me)
            view[...] = src(ins[i], me)[...]
        wait(pending)

    return communicate(kernel, ident, arrays, shapes, semaphores((size - 1) * len(plan)), name)


def slot(ref, place):
    return ref.at[place]


def columns(width):
    def view(ref, place):
        return ref.at[:, span(place, width)]

    return view


def dense_to_heads(lines, ident, pairs, queries, name):
    group, ring = lines.sizes["z"], lines.sizes["core"]
    lanes = 2 * HDIM

    def kernel(p_ref, q_ref, po_ref, qo_ref, send, recv):
        copies = Copies(lines, send, recv)
        zplace, place = lines.place("z"), lines.place("core")
        copies.greet(["z", "core"])
        along, pending = [], []
        for peer in lines.peers("z"):
            along.append(copies.start("z", peer, p_ref.at[:, span(peer, lanes)], po_ref.at[place, zplace]))
        for peer in lines.peers("z"):
            pending.append(copies.start("z", peer, q_ref.at[:, span(peer, lanes)], qo_ref.at[zplace]))
        own = p_ref.at[:, span(zplace, lanes)]
        pending += copies.swap("core", lambda peer: own, lambda _: po_ref.at[place, zplace])
        po_ref[place, zplace] = own[...]
        qo_ref[zplace] = q_ref[:, span(zplace, lanes)]
        for step in range(group - 1, 0, -1):
            along[group - 1 - step].wait_recv()
            block = po_ref.at[place, lax.rem(zplace + step, group)]
            pending += copies.swap("core", lambda peer: block, lambda _: block)
        for copy in along:
            copy.wait_send()
        wait(pending)

    return communicate(
        kernel,
        ident,
        [pairs, queries],
        [((ring, group, pairs.shape[0], lanes), BF), ((group, queries.shape[0], lanes), BF)],
        semaphores(2 * (group - 1) + group * (ring - 1)),
        name,
    )


def dense_finish(lines, ident, vectors, weight, shards, name):
    group, ring, sections = (lines.sizes[k] for k in ("z", "core", "section"))
    dp = group * ring
    many = len(shards)
    local = weight.shape[0] // dp
    wide = weight.shape[1]
    weight = weight.reshape(dp, local, wide)
    width = vectors.shape[1]

    def kernel(x_ref, w_ref, *refs):
        s_refs, refs = refs[:many], refs[many:]
        v_ref, wo_ref, refs = refs[0], refs[1], refs[2:]
        so_refs, refs = refs[:many], refs[many:]
        send, recv, w_got, w_turn, w_all, w_own, v_z, v_core, v_all = refs
        copies = Copies(lines, send, recv)
        zplace, place, section = (lines.place(k) for k in ("z", "core", "section"))
        copies.greet(["z", "core", "section"])
        order = lines.peers("z") + [zplace]
        around = [
            copies.swap("core", lambda peer: w_ref.at[g * ring + peer], lambda me: w_got.at[me, g]) for g in order
        ]
        pending = copies.swap("z", lambda peer: x_ref, lambda me: v_z.at[me])
        v_z[zplace] = x_ref[...]
        gathers = [SquareGather(copies, x, o) for x, o in zip(s_refs, so_refs)]
        for gather in gathers:
            gather.start()
        along = []
        for i, (g, arrived) in enumerate(zip(order, around)):
            for copy in arrived:
                copy.wait_recv()
            total = w_ref[g * ring + place].astype(F32)
            for peer in lines.peers("core"):
                total = total + w_got[peer, g].astype(F32)
            w_turn[g] = total.astype(BF)
            if i < len(order) - 1:
                along.append(copies.start("z", g, w_turn.at[g], w_all.at[zplace]))
        wait(pending)
        v_core[place] = sum_places(v_z)
        wait(copies.swap("core", lambda peer: v_core.at[place], lambda me: v_core.at[me]))
        v_all[section] = sum_places(v_core)
        pending = copies.swap("section", lambda peer: v_all.at[section], lambda me: v_all.at[me])
        for gather in gathers:
            gather.forward()
        wait(along)
        w_all[zplace] = w_turn[zplace]
        w_own[...] = sum_places(w_all).astype(BF)
        last_gather = SquareGather(copies, w_own, wo_ref)
        last_gather.start()
        wait(pending)
        for i in range(sections):
            v_ref[:, i * width : (i + 1) * width] = v_all[i]
        last_gather.forward()
        for arrived in around:
            for copy in arrived:
                copy.wait_send()
        for gather in gathers:
            gather.finish()
        last_gather.finish()

    z, c, s = group - 1, ring - 1, sections - 1
    result = communicate(
        kernel,
        ident,
        [vectors, weight] + shards,
        [((8, sections * width), F32), ((local, sections * wide), BF)]
        + [((x.shape[0], sections * x.shape[1]), x.dtype) for x in shards],
        semaphores(
            group * c
            + z
            + sum(SquareGather.count(x.shape[0]) for x in shards)
            + SquareGather.count(local)
            + z
            + c
            + s
        )
        + [
            pltpu.VMEM((ring, group, local, wide), BF),
            pltpu.VMEM((group, local, wide), BF),
            pltpu.VMEM((group, local, wide), BF),
            pltpu.VMEM((local, wide), BF),
            pltpu.VMEM((group, 8, width), F32),
            pltpu.VMEM((ring, 8, width), F32),
            pltpu.VMEM((sections, 8, width), F32),
        ],
        name,
        limit=32 * 2**20,
    )
    return result[0], result[1], result[2:]


def assemble(pieces, share, name):
    arrays = []
    for _, array, _, _ in pieces:
        if not any(array is other for other in arrays):
            arrays.append(array)
    where = [next(i for i, other in enumerate(arrays) if other is array) for _, array, _, _ in pieces]
    local = arrays[0].shape[0]
    steps = local // 32 if local % 32 == 0 else 1
    rows = local // steps
    sections = lax.axis_size("section")
    shapes, specs = [], []
    for kind, _, _, width in pieces:
        many = 2 if kind == "pair" else 1
        for _ in range(many):
            if kind == "stack":
                shapes.append(jax.ShapeDtypeStruct((sections, local, width), F32))
                specs.append(pl.BlockSpec((sections, rows, width), lambda i: (0, i, 0)))
            else:
                total = width if kind == "sum" else sections * width // many
                shapes.append(jax.ShapeDtypeStruct((local, total), F32))
                specs.append(pl.BlockSpec((rows, total), lambda i: (i, 0)))

    def kernel(*refs):
        ins, outs = refs[: len(arrays)], list(refs[len(arrays) :])
        for (kind, array, first, width), i in zip(pieces, where):
            wide = array.shape[1] // sections
            blocks = [ins[i][:, s * wide + first : s * wide + first + width].astype(F32) for s in range(sections)]
            out = outs.pop(0)
            if kind == "columns":
                for s, item in enumerate(blocks):
                    out[:, s * width : (s + 1) * width] = item
            elif kind == "stack":
                for s, item in enumerate(blocks):
                    out[s] = item
            elif kind == "sum":
                total = blocks[0]
                for item in blocks[1:]:
                    total = total + item
                out[...] = total
            elif kind == "hidden":
                for d in range(width // share):
                    out[:, d * share * sections : (d + 1) * share * sections] = jnp.concatenate(
                        [item[:, d * share : (d + 1) * share] for item in blocks], axis=1
                    )
            else:
                other = outs.pop(0)
                half = width // 2
                for s, item in enumerate(blocks):
                    for side, dst in ((0, out), (1, other)):
                        heads = [
                            item[:, (2 * g + side) * HDIM : (2 * g + side + 1) * HDIM]
                            for g in range(width // (2 * HDIM))
                        ]
                        dst[:, s * half : (s + 1) * half] = jnp.concatenate(heads, axis=1)

    return pl.pallas_call(
        kernel,
        grid=(steps,),
        in_specs=[pl.BlockSpec((rows, a.shape[1]), lambda i: (i, 0)) for a in arrays],
        out_specs=specs,
        out_shape=shapes,
        compiler_params=pltpu.CompilerParams(vmem_limit_bytes=24 * 2**20),
        name=name,
    )(*arrays)


def column_to_rows(column):
    return jnp.broadcast_to(column, (column.shape[0], 128)).T[:8]


def row_to_column(row):
    return jnp.broadcast_to(row, (128, row.shape[1])).T[:, :1]


def outer_product(left_ref, right_ref, out_ref, first):
    step = 256
    wide = right_ref.shape[1]
    for i in range(left_ref.shape[1] // step):
        block = contract(left_ref[:, i * step : (i + 1) * step], right_ref[...], 0, 0)
        out_ref[i * step : (i + 1) * step, first : first + wide] = block.astype(BF)


def unpack_low(packed):
    lane = lax.broadcasted_iota(jnp.int32, packed.shape, 1)
    zero = jnp.zeros_like(packed)
    low = jnp.where(lane < HDIM, packed, zero)
    turned = jnp.concatenate([packed[:, HDIM:], packed[:, :HDIM]], axis=1)
    high = jnp.where(lane < HDIM, turned, zero)
    return jnp.concatenate([low, high], axis=0)


def unpack_high(packed):
    lane = lax.broadcasted_iota(jnp.int32, packed.shape, 1)
    zero = jnp.zeros_like(packed)
    turned = jnp.concatenate([packed[:, HDIM:], packed[:, :HDIM]], axis=1)
    low = jnp.where(lane >= HDIM, turned, zero)
    high = jnp.where(lane >= HDIM, packed, zero)
    return jnp.concatenate([low, high], axis=0)


def pack_turned(turned):
    half = turned.shape[1] // 2
    return jnp.concatenate([turned[:, :half], turned[:, half:]], axis=0).T


def forward_block(query, pieces, qpos, start, causal):
    scores = []
    peak = None
    for index, (pair, _, first) in enumerate(pieces):
        item = contract(pair, query, 1, 1)
        kpos = first + lax.broadcasted_iota(jnp.int32, item.shape, 0)
        allowed = kpos >= start
        if causal[index]:
            allowed = allowed & (kpos <= qpos)
        item = jnp.where(allowed, item, NEG)
        top = jnp.max(item, axis=0, keepdims=True)
        peak = top if peak is None else jnp.maximum(peak, top)
        scores.append(item)
    total = jnp.zeros_like(peak)
    mixed = None
    for item, (_, turned, _) in zip(scores, pieces):
        weight = jnp.exp(item - peak)
        total = total + jnp.sum(weight, axis=0, keepdims=True)
        part = matmul(turned[HDIM:], weight.astype(BF))
        mixed = part if mixed is None else mixed + part
    return mixed / total, peak + jnp.log(total)


def backward_block(query, grad, grad_turned, mixed_turned, lse, pieces, qpos, start, causal):
    row_sum = jnp.sum(grad_turned.astype(F32) * mixed_turned.astype(F32), axis=0, keepdims=True)
    grad_query = None
    grads = []
    for index, (pair, turned, first) in enumerate(pieces):
        scores = contract(pair, query, 1, 1)
        kpos = first + lax.broadcasted_iota(jnp.int32, scores.shape, 0)
        allowed = kpos >= start
        if causal[index]:
            allowed = allowed & (kpos <= qpos)
        probs = jnp.where(allowed, jnp.exp(scores - lse), 0.0)
        grad_probs = contract(pair, grad, 1, 1)
        grad_scores = (probs * (grad_probs - row_sum)).astype(BF)
        grads.append(matmul(grad_scores, query) + matmul(probs.astype(BF), grad))
        part = matmul(turned[:HDIM], grad_scores)
        grad_query = part if grad_query is None else grad_query + part
    return grad_query * SCALE, grads


def dense_forward_kernel(place_ref, q_ref, kv_ref, start_ref, out_ref, turned_ref, lse_ref):
    group, _, half, _ = q_ref.shape
    ring, _, _, block, _ = kv_ref.shape
    place = place_ref[0]
    span = ring * block
    pieces = []
    for g in range(group):
        pair = kv_ref[:, g, 0].reshape(span, 2 * HDIM)
        pieces.append((pair, pair.T, g * span))
    for g in range(group):
        query = unpack_low(q_ref[g, 0]) * jnp.asarray(SCALE, BF)
        qpos = g * span + place * block + lax.broadcasted_iota(jnp.int32, (1, block), 1)
        mixed, lse = forward_block(
            query, pieces[: g + 1], qpos, start_ref[0, g], [i == g for i in range(g + 1)]
        )
        turned_ref[0, g] = mixed.astype(BF)
        lse_ref[0, g] = lse
        out_ref[g, 0] = pack_turned(mixed).astype(BF)


def dense_forward(place, q, kv, start):
    group, seqs, half, lanes = q.shape
    ring, _, _, block, _ = kv.shape
    grid = pltpu.PrefetchScalarGridSpec(
        num_scalar_prefetch=1,
        grid=(seqs,),
        in_specs=[
            pl.BlockSpec((group, 1, half, lanes), lambda s, _: (0, s, 0, 0)),
            pl.BlockSpec((ring, group, 1, block, lanes), lambda s, _: (0, 0, s, 0, 0)),
            pl.BlockSpec((1, group, 1, block), lambda s, _: (s, 0, 0, 0)),
        ],
        out_specs=[
            pl.BlockSpec((group, 1, half, lanes), lambda s, _: (0, s, 0, 0)),
            pl.BlockSpec((1, group, HDIM, block), lambda s, _: (s, 0, 0, 0)),
            pl.BlockSpec((1, group, 1, block), lambda s, _: (s, 0, 0, 0)),
        ],
    )
    return pl.pallas_call(
        dense_forward_kernel,
        grid_spec=grid,
        out_shape=[
            jax.ShapeDtypeStruct(q.shape, BF),
            jax.ShapeDtypeStruct((seqs, group, HDIM, block), BF),
            jax.ShapeDtypeStruct((seqs, group, 1, block), F32),
        ],
        compiler_params=pltpu.CompilerParams(vmem_limit_bytes=VMEM),
        name="dense_attention",
    )(place, q, kv, start)


def dense_return(lines, ident, arrays, shape, name):
    seqs, rows, width, hidden_size = shape
    sections, group, ring = (lines.sizes[k] for k in ("section", "z", "core"))
    part = width // sections
    half = rows // 2
    lanes = 2 * HDIM
    block = ring * rows

    def kernel(
        fed_ref,
        own_ref,
        value_ref,
        attended_ref,
        slope_ref,
        hidden_ref,
        mixed_ref,
        rest_ref,
        qkv_w,
        q_ref,
        kv_ref,
        start_ref,
        turned_ref,
        lse_ref,
        gains_ref,
        grads_ref,
        dqkv_w_ref,
        stream_ref,
        vectors_ref,
        send,
        recv,
        normed,
        dpre,
        dattended,
        dqkv,
        wide,
        got,
        turn,
        last,
        scalar,
        scalar_got,
        middle,
        total,
        heads,
        heads_got,
        acc,
        pairs,
        pairs_got,
        queries,
        queries_got,
        sums,
        sums_got,
        kv,
        local,
    ):
        copies = Copies(lines, send, recv)
        section, zplace, place = (lines.place(k) for k in ("section", "z", "core"))
        own = span(section, part)
        copies.greet(["section", "z", "core"])
        out_w = rest_ref.at[:, :part]
        expand_w = rest_ref.at[:, part : part + hidden_size]
        shrink_w = rest_ref.at[:, part + hidden_size :]
        scatters = {}

        def begin(stage, q, value, scalars):
            wide[stage, q] = value.astype(BF)
            item = SquareScatter(
                copies, wide.at[stage, q], got.at[stage, q], turn.at[stage, q], last.at[stage, q], 1
            )
            item.start()
            others = []
            if scalars is not None:
                side = min(stage, 1)
                scalar[side, q] = column_to_rows(scalars)
                others = copies.swap(
                    "section", lambda peer: scalar.at[side, q], lambda me: scalar_got.at[side, q, me]
                )
                scalar_got[side, q, section] = scalar[side, q]
            scatters[stage, q] = (item, others)

        def forward(stage, q):
            scatters[stage, q][0].forward()

        def finish(stage, q):
            item, others = scatters[stage, q]
            item.finish(total)
            if not others:
                return total[...], None
            wait(others)
            return total[...], row_to_column(sum_places(scalar_got.at[min(stage, 1), q])[:1])

        def middle_of(q):
            at = pl.ds(q * rows, rows)
            return value_ref[at].astype(F32) + attended_ref[at].astype(F32)

        def feed(q):
            at = pl.ds(q * rows, rows)
            grad_pre = (contract(fed_ref[at], shrink_w[...], 1, 1) * slope_ref[at].astype(F32)).astype(BF)
            dpre[at] = grad_pre
            grad_normed = contract(grad_pre, expand_w[...], 1, 1)
            weighted = middle_of(q) * gains_ref[1:2]
            begin(0, q, grad_normed, jnp.sum(grad_normed * weighted, axis=1, keepdims=True))

        def project(q):
            at = pl.ds(q * rows, rows)
            grad_normed, scalars = finish(0, q)
            mid = middle_of(q)
            inv = inverse_rms(mid)
            normed[at] = (mid * inv * gains_ref[1:2]).astype(BF)
            mid = value_ref[at, own].astype(F32) + attended_ref[at, own].astype(F32)
            vectors_ref[0:1] += jnp.sum(grad_normed * mid * inv, axis=0, keepdims=True)
            grad = (
                inv * (grad_normed * gains_ref[1:2, own])
                - mid * (inv * inv * inv) * (scalars * (1.0 / width))
                + own_ref[at]
            )
            middle[q] = grad
            low = grad.astype(BF)
            dattended[at] = low
            begin(1, q, contract(low, out_w[...], 1, 1), None)

        def to_heads(q):
            grad, _ = finish(1, q)
            grad = grad.astype(BF)
            for g in range(group):
                columns = slice(g * HDIM, (g + 1) * HDIM)
                heads[g, q] = side_by_side([grad[:half, columns], grad[half:, columns]])
            heads_got[zplace, q] = heads[zplace, q]
            return copies.swap("z", lambda peer: heads.at[peer, q], lambda me: heads_got.at[me, q])

        def fetch(q):
            return pltpu.make_async_copy(kv_ref.at[:, :, q], kv, local.at[q])

        def load(src, index):
            copy = pltpu.make_async_copy(src, dpre, local.at[index])
            copy.start()
            copy.wait()

        def attend(q):
            fetch(q).wait()
            pieces = []
            for g in range(group):
                pair = kv[:, g].reshape(block, lanes)
                pieces.append((pair, pair.T, g * block))
            for g in reversed(range(group)):
                query = unpack_low(q_ref[g, q]) * jnp.asarray(SCALE, BF)
                packed = heads_got[g, q]
                flat = packed.T
                qpos = g * block + place * rows + lax.broadcasted_iota(jnp.int32, (1, rows), 1)
                grad_query, grads = backward_block(
                    query,
                    unpack_high(packed),
                    side_by_side([flat[:HDIM], flat[HDIM:]]),
                    turned_ref[q, g],
                    lse_ref[q, g],
                    pieces[: g + 1],
                    qpos,
                    start_ref[q, g],
                    [i == g for i in range(g + 1)],
                )
                queries[g, q] = pack_turned(grad_query).astype(BF)
                for i, item in enumerate(grads):
                    if g == group - 1:
                        acc[i] = item
                    else:
                        acc[i] += item
            for g in range(group):
                for r in range(ring):
                    pairs[r, g] = acc[g, r * rows : (r + 1) * rows].astype(BF)
            if q + 1 < seqs:
                fetch(q + 1).start()
            queries_got[zplace, q] = queries[zplace, q]
            around = copies.swap("core", lambda peer: pairs.at[peer], lambda me: pairs_got.at[me, :, q])
            along = copies.swap("z", lambda peer: queries.at[peer, q], lambda me: queries_got.at[me, q])
            return around, along

        def to_tokens(q, around):
            wait(around)
            for g in range(group):
                item = pairs[place, g].astype(F32)
                for peer in lines.peers("core"):
                    item = item + pairs_got[peer, g, q].astype(F32)
                sums[g, q] = item.astype(BF)
            sums_got[zplace, q] = sums[zplace, q]
            return copies.swap("z", lambda peer: sums.at[peer, q], lambda me: sums_got.at[me, q])

        def enter(q, pending):
            wait(pending)
            at = pl.ds(q * rows, rows)
            packed = [queries_got[g, q] for g in range(group)]
            upright = [jnp.concatenate([p[:, :HDIM], p[:, HDIM:]], axis=0) for p in packed]
            grad = side_by_side([sums_got[g, q] for g in range(group)] + upright)
            dqkv[at] = grad
            grad_normed = contract(grad, qkv_w[...], 1, 1)
            value = value_ref[at].astype(F32)
            normed[at] = (value * inverse_rms(value) * gains_ref[0:1]).astype(BF)
            begin(2, q, grad_normed, jnp.sum(grad_normed * value * gains_ref[0:1], axis=1, keepdims=True))

        def leave(q):
            at = pl.ds(q * rows, rows)
            grad_normed, scalars = finish(2, q)
            inv = inverse_rms(value_ref[at].astype(F32))
            value = value_ref[at, own].astype(F32)
            vectors_ref[1:2] += jnp.sum(grad_normed * value * inv, axis=0, keepdims=True)
            grad = (
                inv * (grad_normed * gains_ref[0:1, own])
                - value * (inv * inv * inv) * (scalars * (1.0 / width))
                + middle[q]
            )
            stream_ref[at] = grad.astype(BF)

        vectors_ref[...] = jnp.zeros_like(vectors_ref)
        arriving, around, along, leaving = {}, {}, {}, {}
        fetch(0).start()

        def turn_back(q):
            wait(arriving[q])
            around[q], along[q] = attend(q)

        def hand_back(q):
            leaving[q] = to_tokens(q, around[q]) + along[q]

        def step(name, q):
            if q < 0 or q >= seqs:
                return
            if name == "heads":
                arriving[q] = to_heads(q)
            elif name == "enter":
                enter(q, leaving[q])
            elif name in ("mid", "out", "in"):
                forward(("mid", "out", "in").index(name), q)
            else:
                {"feed": feed, "project": project, "attend": turn_back, "back": hand_back, "leave": leave}[name](q)

        last_of = seqs - 1
        for q in range(seqs):
            step("feed", q)
            step("mid", q - 1)
            step("project", q - 2)
        step("mid", last_of)
        step("project", last_of - 1)
        step("out", 0)
        step("heads", 0)
        step("project", last_of)
        for q in range(1, seqs):
            step("out", q)
            step("heads", q)
            step("attend", q - 1)
            step("back", q - 1)
        outer_product(normed, dpre, grads_ref, 0)
        step("attend", last_of)
        step("back", last_of)
        load(hidden_ref, seqs)
        outer_product(dpre, fed_ref, grads_ref, hidden_size)
        load(mixed_ref, seqs + 1)
        outer_product(dpre, dattended, grads_ref, hidden_size + width)
        for q in range(seqs):
            step("enter", q)
            step("in", q - 1)
            step("leave", q - 2)
        outer_product(normed, dqkv, dqkv_w_ref, 0)
        step("in", last_of)
        step("leave", last_of - 1)
        step("leave", last_of)

    tokens = seqs * rows
    z, c, s = group - 1, ring - 1, sections - 1
    vmem = pltpu.VMEM
    return communicate(
        kernel,
        ident,
        arrays,
        [
            ((width, hidden_size + width + part), BF),
            ((width, 3 * part), BF),
            ((tokens, part), BF),
            ((8, part), F32),
        ],
        semaphores(seqs * (3 * 6 + 2 * s + 3 * z + c))
        + [
            vmem((tokens, width), BF),
            vmem((tokens, hidden_size), BF),
            vmem((tokens, part), BF),
            vmem((tokens, 3 * part), BF),
            vmem((3, seqs, rows, width), BF),
            vmem((3, seqs, 2, rows, part), BF),
            vmem((3, seqs, rows, part), BF),
            vmem((3, seqs, rows, part), BF),
            vmem((2, seqs, 8, rows), F32),
            vmem((2, seqs, sections, 8, rows), F32),
            vmem((seqs, rows, part), F32),
            vmem((rows, part), F32),
            vmem((group, seqs, half, lanes), BF),
            vmem((group, seqs, half, lanes), BF),
            vmem((group, block, lanes), F32),
            vmem((ring, group, rows, lanes), BF),
            vmem((ring, group, seqs, rows, lanes), BF),
            vmem((group, seqs, half, lanes), BF),
            vmem((group, seqs, half, lanes), BF),
            vmem((group, seqs, rows, lanes), BF),
            vmem((group, seqs, rows, lanes), BF),
            vmem((ring, group, rows, lanes), BF),
            pltpu.SemaphoreType.DMA((seqs + 2,)),
        ],
        name,
        limit=62 * 2**20,
        far=(5, 6, 10),
    )


def inverse_rms(value):
    return lax.rsqrt(jnp.mean(value * value, axis=-1, keepdims=True) + EPS)


def gelu_terms(value):
    scale = 0.7978845608028654
    square = value * value
    bend = jnp.tanh(scale * (value + 0.044715 * square * value))
    half = 0.5 * (1.0 + bend)
    slope = half + 0.5 * value * (1.0 - bend * bend) * scale * (1.0 + 0.134145 * square)
    return value * half, slope


def side_by_side(blocks):
    return jnp.concatenate(blocks, axis=1)


class ColumnSum:
    @staticmethod
    def count(sections, scalars):
        return (sections - 1) * (2 if scalars else 1)

    @staticmethod
    def scratch(sections, rows, width, scalars):
        buffers = [pltpu.VMEM((rows, sections * width), BF), pltpu.VMEM((sections, rows, width), BF)]
        if scalars:
            wide = rows + -rows % 128
            buffers += [pltpu.VMEM((8, wide), F32), pltpu.VMEM((sections, 8, wide), F32)]
        return buffers

    def __init__(self, copies, buffers):
        self.copies, self.buffers = copies, buffers

    def start(self, value, scalars=None):
        buf, got = self.buffers[:2]
        width = got.shape[2]
        section = self.copies.lines.place("section")
        buf[...] = value.astype(BF)
        self.pending = self.copies.swap(
            "section", lambda peer: buf.at[:, span(peer, width)], lambda me: got.at[me]
        )
        got[section] = buf[:, span(section, width)]
        if scalars is not None:
            sbuf, sgot = self.buffers[2:]
            sbuf[...] = jnp.zeros_like(sbuf)
            sbuf[:, : scalars.shape[0]] = column_to_rows(scalars)
            self.pending += self.copies.swap("section", lambda peer: sbuf, lambda me: sgot.at[me])
            sgot[section] = sbuf[...]

    def finish(self):
        wait(self.pending)
        total = sum_places(self.buffers[1])
        if len(self.buffers) == 2:
            return total
        rows = total.shape[0]
        return total, row_to_column(sum_places(self.buffers[3])[:1, :rows])


def routed_layer(lines, ident, arrays, shape, name):
    seqs, sel, rows, width, part = shape
    sections, group, ring = (lines.sizes[k] for k in ("section", "z", "core"))
    dp = group * ring
    slots = seqs * sel
    lanes = 2 * HDIM
    rest_w = arrays[-1]
    hidden_size = rest_w.shape[1] - part - width
    qkv_at = hidden_size + width
    vector_at = qkv_at + 4 * part

    def kernel(
        source_ref,
        top_ref,
        column_ref,
        row_ref,
        start_ref,
        gains_ref,
        qkv_w,
        rest_ref,
        fed_out,
        own_out,
        added_ref,
        grads_ref,
        send,
        recv,
        value_core,
        value_core_got,
        value_z,
        value_z_got,
        value_all,
        grad_core,
        grad_core_got,
        grad_z,
        grad_z_got,
        grad_all,
        heads_buf,
        heads_got,
        pairs_all,
        out_buf,
        out_got,
        mixed_all,
        attended_all,
        grad_buf,
        grad_got,
        turn_buf,
        turn_got,
        back_buf,
        back_got,
        keep,
        normed_keep,
        mixed_keep,
        mid_keep,
        dpre_keep,
        hidden_keep,
        fed_keep,
        attended_keep,
        dqkv_keep,
        sent_buf,
        sent_got,
        sent_all,
        final_buf,
        final_got,
        final_all,
        *buffers,
    ):
        copies = Copies(lines, send, recv)
        section, zplace, place = (lines.place(k) for k in ("section", "z", "core"))
        rank = lax.axis_index("dp")
        copies.greet(["section", "z", "core"])
        own = span(section, part)
        gain_pre, gain_mid, router = (gains_ref[i : i + 1, :] for i in range(3))
        own_pre, own_mid, own_router = (gains_ref[i : i + 1, own] for i in range(3))
        out_w = rest_ref.at[:, :part]
        expand_w = rest_ref.at[:, part : part + hidden_size]
        shrink_w = rest_ref.at[:, part + hidden_size :]
        sums = [ColumnSum(copies, buffers[4 * i : 4 * i + 4]) for i in range(3)]
        sums.append(ColumnSum(copies, buffers[12:14]))

        def ring_swap(buf, got):
            return copies.swap("core", lambda peer: buf.at[peer], lambda me: got.at[me])

        def ring_sum(buf, got):
            total = buf[place].astype(F32)
            for peer in lines.peers("core"):
                total = total + got[peer].astype(F32)
            return total.astype(BF)

        def z_swap(buf, got):
            pending = copies.swap("z", lambda peer: buf.at[peer], lambda me: got.at[me])
            got[zplace] = buf[zplace]
            return pending

        def share(kind, all_ref):
            me = lines.place(kind)
            return copies.swap(kind, lambda peer: all_ref.at[me], lambda _: all_ref.at[me])

        def together(all_ref):
            return side_by_side([all_ref[i] for i in range(sections)])

        position = rank * rows + lax.broadcasted_iota(jnp.int32, (1, rows), 1)
        for q in range(seqs):
            table = (column_ref[q] == position).astype(F32).astype(BF)
            found = matmul(table, source_ref[q]).astype(BF)
            for d in range(dp):
                at = slice(q * sel, (q + 1) * sel)
                value_core[d % ring, d // ring, at] = found[d * sel : (d + 1) * sel, :part]
                grad_core[d % ring, d // ring, at] = found[d * sel : (d + 1) * sel, part:]
        pending = ring_swap(value_core, value_core_got)
        grad_pending = ring_swap(grad_core, grad_core_got)
        wait(pending)
        value_z[...] = ring_sum(value_core, value_core_got)
        pending = z_swap(value_z, value_z_got)
        wait(grad_pending)
        grad_z[...] = ring_sum(grad_core, grad_core_got)
        wait(pending)
        value_all[section] = sum_places(value_z_got).astype(BF)
        pending = share("section", value_all)
        grad_pending = z_swap(grad_z, grad_z_got)
        wait(pending)
        picked = together(value_all).astype(F32)

        inv_in = inverse_rms(picked)
        normed = (picked * inv_in * gain_pre).astype(BF)
        normed_keep[...] = normed
        qkv = matmul(normed, qkv_w[...]).astype(BF)
        blank = jnp.zeros((slots, HDIM), BF)
        for g in range(group):
            query = qkv[:, 2 * part + g * HDIM : 2 * part + (g + 1) * HDIM]
            heads_buf[g, :, :lanes] = side_by_side([query, blank])
            heads_buf[g, :, lanes:] = qkv[:, g * lanes : (g + 1) * lanes]
        pending = z_swap(heads_buf, heads_got)
        wait(grad_pending)
        grad_all[section] = sum_places(grad_z_got).astype(BF)
        grad_pending = share("section", grad_all)
        wait(pending)
        pairs_all[place] = heads_got[:, :, lanes:]
        wait(share("core", pairs_all))

        index = lax.broadcasted_iota(jnp.int32, (1, group * sel), 1)
        place_of = (index // sel) * (ring * sel) + place * sel + lax.rem(index, sel)

        def sequence(q):
            at = slice(q * sel, (q + 1) * sel)
            query = jnp.concatenate([heads_got[g, at, :lanes] for g in range(group)], axis=0)
            pair = jnp.concatenate([pairs_all[r, g, at] for g in range(group) for r in range(ring)], axis=0)
            return query * jnp.asarray(SCALE, BF), pair

        kept = []
        for q in range(seqs):
            query, pair = sequence(q)
            turned, lse = forward_block(query, [(pair, pair.T, 0)], place_of, start_ref[q], [True])
            kept.append((turned.astype(BF), lse))
            upright = jnp.concatenate([turned, jnp.zeros_like(turned)], axis=0).T.astype(BF)
            for g in range(group):
                out_buf[g, q * sel : (q + 1) * sel] = upright[g * sel : (g + 1) * sel]
        wait(z_swap(out_buf, out_got))
        mixed_all[section] = side_by_side([out_got[g, :, :HDIM] for g in range(group)])
        wait(share("section", mixed_all))
        mixed_keep[...] = together(mixed_all)
        attended_own = matmul(mixed_keep[...], out_w[...]).astype(BF)
        attended_all[section] = attended_own
        pending = share("section", attended_all)
        wait(grad_pending)
        grad_sent = together(grad_all).astype(F32)
        gate = jax.nn.sigmoid(jnp.sum(picked * router, axis=1, keepdims=True))
        grad_delta = gate * grad_sent
        fed_low = grad_delta.astype(BF)
        fed_keep[...] = fed_low
        grad_hidden = contract(fed_low, shrink_w[...], 1, 1)
        wait(pending)

        middle = picked + together(attended_all).astype(F32)
        inv_mid = inverse_rms(middle)
        normed_mid = (middle * inv_mid * gain_mid).astype(BF)
        hidden, slope = gelu_terms(matmul(normed_mid, expand_w[...]))
        hidden = hidden.astype(BF)
        grad_pre = (grad_hidden * slope).astype(BF)
        grad_normed = contract(grad_pre, expand_w[...], 1, 1)
        sums[0].start(grad_normed, jnp.sum(grad_normed * middle * gain_mid, axis=1, keepdims=True))
        mid_keep[...] = normed_mid
        hidden_keep[...] = hidden
        dpre_keep[...] = grad_pre
        fed_part = matmul(hidden, shrink_w[...])
        keep[0] = middle
        keep[1] = grad_delta
        keep[2] = grad_sent
        own_attended = attended_own.astype(F32)
        gate_part = jnp.sum(grad_sent * fed_part, axis=1, keepdims=True) + jnp.sum(
            keep[2, :, own] * own_attended, axis=1, keepdims=True
        )
        middle_own, grad_delta_own = keep[0, :, own], keep[1, :, own]
        picked_own = value_all[section].astype(F32)
        grad_normed, scalar = sums[0].finish()
        vector_mid = jnp.sum(grad_normed * middle_own * inv_mid, axis=0, keepdims=True)
        grad_middle = inv_mid * (grad_normed * own_mid) - middle_own * (inv_mid * inv_mid * inv_mid) * (
            scalar * (1.0 / width)
        )
        grad_attended = (grad_middle + grad_delta_own).astype(BF)
        attended_keep[...] = grad_attended

        sums[3].start(contract(grad_attended, out_w[...], 1, 1))
        sums[1].start(fed_part, gate_part)
        outer_product(mid_keep, dpre_keep, grads_ref, 0)
        grad_mixed = sums[3].finish().astype(BF)
        for g in range(group):
            grad_buf[g] = side_by_side([blank, grad_mixed[:, g * HDIM : (g + 1) * HDIM]])
        pending = z_swap(grad_buf, grad_got)
        fed, grad_gate = sums[1].finish()
        sent_buf[...] = (gate * (own_attended + fed)).astype(BF)
        grad_logit = grad_gate * gate * (1.0 - gate)
        vector_router = jnp.sum(grad_logit * picked_own, axis=0, keepdims=True)
        wait(pending)
        sent_pending = copies.swap("z", lambda peer: sent_buf, lambda me: sent_got.at[me])
        sent_got[zplace] = sent_buf[...]
        for q in range(seqs):
            at = slice(q * sel, (q + 1) * sel)
            query, pair = sequence(q)
            grad = jnp.concatenate([grad_got[g, at] for g in range(group)], axis=0)
            turned, lse = kept[q]
            grad_query, grad_pairs = backward_block(
                query, grad, grad.T[HDIM:], turned, lse, [(pair, pair.T, 0)], place_of, start_ref[q], [True]
            )
            upright = jnp.concatenate([grad_query, jnp.zeros_like(grad_query)], axis=0).T.astype(BF)
            low = grad_pairs[0].astype(BF)
            for g in range(group):
                back_buf[g, at, :lanes] = upright[g * sel : (g + 1) * sel]
                for r in range(ring):
                    first = (g * ring + r) * sel
                    turn_buf[r, g, at] = low[first : first + sel]
        wait(ring_swap(turn_buf, turn_got))
        back_buf[:, :, lanes:] = ring_sum(turn_buf, turn_got)
        pending = z_swap(back_buf, back_got)
        wait(sent_pending)
        sent_all[place] = sent_got[...]
        sent_pending = share("core", sent_all)
        outer_product(hidden_keep, fed_keep, grads_ref, hidden_size)
        wait(pending)
        dqkv_keep[...] = side_by_side(
            [back_got[g, :, lanes:] for g in range(group)] + [back_got[g, :, :HDIM] for g in range(group)]
        )
        grad_normed = contract(dqkv_keep[...], qkv_w[...], 1, 1)
        sums[2].start(grad_normed, jnp.sum(grad_normed * picked * gain_pre, axis=1, keepdims=True))
        outer_product(normed_keep, dqkv_keep, grads_ref, qkv_at)
        grad_normed, scalar = sums[2].finish()
        vector_pre = jnp.sum(grad_normed * picked_own * inv_in, axis=0, keepdims=True)
        grad_in = inv_in * (grad_normed * own_pre) - picked_own * (inv_in * inv_in * inv_in) * (
            scalar * (1.0 / width)
        )
        final_buf[...] = (grad_middle + grad_in + grad_logit * own_router).astype(BF)

        along = copies.swap("z", lambda peer: final_buf, lambda me: final_got.at[me])
        final_got[zplace] = final_buf[...]

        def hand_on(i):
            dst = final_all.at[place, i, :, own]
            dst[...] = final_got[i]
            return copies.swap("section", lambda peer: final_got.at[i], lambda me: dst)

        spread = hand_on(zplace)
        outer_product(mixed_keep, attended_keep, grads_ref, qkv_at + 3 * part)
        lane = lax.broadcasted_iota(jnp.int32, (part, 128), 1)
        vectors = jnp.zeros((part, 128), F32)
        for i, vector in enumerate((vector_pre, vector_mid, vector_router)):
            vectors = jnp.where(lane == i, row_to_column(vector), vectors)
        grads_ref[:, vector_at:] = jnp.zeros((width, 128), BF)
        grads_ref[pl.ds(pl.multiple_of(section * part, part), part), vector_at:] = vectors.astype(BF)
        wait(sent_pending)
        slot_of = rank * rows + lax.broadcasted_iota(jnp.int32, (rows, 1), 0)
        tables = [(row_ref[q] == slot_of).astype(F32).astype(BF) for q in range(seqs)]

        def at_positions(q, all_ref):
            at = slice(q * sel, (q + 1) * sel)
            found = jnp.concatenate([all_ref[r, g, at] for g in range(group) for r in range(ring)], axis=0)
            return matmul(tables[q], found)

        for q in range(seqs):
            added_ref[q] = at_positions(q, sent_all).astype(BF)
        for step in range(group - 1, 0, -1):
            along[group - 1 - step].wait_recv()
            spread += hand_on(lax.rem(zplace + step, group))
        for copy in along:
            copy.wait_send()
        wait(spread)
        wait(share("core", final_all))
        for q in range(seqs):
            grad = top_ref[q].astype(F32) + at_positions(q, final_all)
            fed_out[q] = grad.astype(BF)
            returned = jnp.concatenate(
                [final_all[r, g, q * sel : (q + 1) * sel, own] for g in range(group) for r in range(ring)], axis=0
            )
            own_out[q] = top_ref[q, :, own].astype(F32) + matmul(tables[q], returned)

    vmem = pltpu.VMEM
    z, s, c = group - 1, sections - 1, ring - 1
    short = ((group, slots, part), BF)
    lane_block = ((group, slots, lanes), BF)
    ring_block = ((ring, group, slots, lanes), BF)
    row = ((slots, width), BF)
    scratch = [
        ((ring,) + short[0], BF),
        ((ring,) + short[0], BF),
        short,
        short,
        ((sections, slots, part), BF),
        ((ring,) + short[0], BF),
        ((ring,) + short[0], BF),
        short,
        short,
        ((sections, slots, part), BF),
        ((group, slots, 2 * lanes), BF),
        ((group, slots, 2 * lanes), BF),
        ring_block,
        lane_block,
        lane_block,
        ((sections, slots, part), BF),
        ((sections, slots, part), BF),
        lane_block,
        lane_block,
        ring_block,
        ring_block,
        ((group, slots, 2 * lanes), BF),
        ((group, slots, 2 * lanes), BF),
        ((3, slots, width), F32),
        row,
        row,
        row,
        ((slots, hidden_size), BF),
        ((slots, hidden_size), BF),
        row,
        ((slots, part), BF),
        ((slots, 3 * part), BF),
        ((slots, part), BF),
        short,
        ((ring,) + short[0], BF),
        ((slots, part), BF),
        short,
        ((ring, group, slots, width), BF),
    ]
    return communicate(
        kernel,
        ident,
        arrays,
        [
            ((seqs, rows, width), BF),
            ((seqs, rows, part), F32),
            ((seqs, rows, part), BF),
            ((width, vector_at + 128), BF),
        ],
        semaphores(
            6 * c
            + 8 * z
            + 4 * s
            + 3 * ColumnSum.count(sections, True)
            + ColumnSum.count(sections, False)
            + group * s
        )
        + [vmem(a, b) for a, b in scratch]
        + 3 * ColumnSum.scratch(sections, slots, part, True)
        + ColumnSum.scratch(sections, slots, part, False),
        name,
        limit=56 * 2**20,
    )


def on_device(
    stream_in,
    segment_ids,
    chosen_rows,
    cotangent,
    dense_prenorm,
    dense_query,
    dense_keys,
    dense_values,
    dense_output,
    dense_midnorm,
    dense_expand,
    dense_shrink,
    routed_prenorm,
    routed_query,
    routed_keys,
    routed_values,
    routed_output,
    routed_midnorm,
    routed_expand,
    routed_shrink,
    router_weight,
):
    sections, dp = lax.axis_size("section"), lax.axis_size("dp")
    section, rank = lax.axis_index("section"), lax.axis_index("dp")
    seqs, rows, width = stream_in.shape
    tokens = seqs * rows
    part = width // sections
    group = HEADS // sections
    ring = dp // group
    total_sel = chosen_rows.shape[1]
    sel = total_sel // dp
    place = lax.rem(rank, ring).astype(jnp.int32).reshape(1)
    lines = Lines(sections, dp, group)
    lanes = 2 * HDIM

    def own_columns(value):
        return lax.dynamic_slice_in_dim(value, section * part, part, value.ndim - 1)

    def own_hidden(expand, shrink):
        inner = expand.shape[1] // dp
        share = inner // sections
        cut = expand.reshape(expand.shape[0], dp, sections, share)
        cut = lax.dynamic_index_in_dim(cut, section, 2, keepdims=False).reshape(expand.shape[0], dp * share)
        return cut, lax.dynamic_slice_in_dim(shrink, section * share, share, 0)

    def own_attention(query, keys, values):
        local = query.shape[0]
        pair = jnp.stack(
            [own_columns(keys).reshape(local, group, HDIM), own_columns(values).reshape(local, group, HDIM)],
            axis=2,
        ).reshape(local, 2 * part)
        return jnp.concatenate([pair, own_columns(query)], axis=1)

    gains = jnp.stack([dense_prenorm, dense_midnorm, routed_prenorm, routed_midnorm, router_weight])
    gains = jnp.pad(gains, ((0, 16 - gains.shape[0]), (0, 0)))
    first = own_attention(dense_query, dense_keys, dense_values)
    dense_qkv, gains = gather_rows(lines, 1, [first, gains], "first_weights")
    dense_qkv = dense_qkv.reshape(width, 3 * part)
    gains = jnp.transpose(gains, (1, 0, 2)).reshape(16, width).astype(F32)
    gain_pre, gain_mid = gains[0], gains[1]

    def gather(value):
        return lax.all_gather(value, "dp", axis=0, tiled=True)

    def after(value, other):
        return lax.optimization_barrier((value, other))[0]

    expand_cut, shrink_cut = own_hidden(dense_expand, dense_shrink)
    hidden_size = expand_cut.shape[1]
    rest = gather(jnp.concatenate([own_columns(dense_output), expand_cut, shrink_cut], axis=1))
    dense_out, dense_exp, dense_shr = (
        rest[:, :part],
        rest[:, part : part + hidden_size],
        rest[:, part + hidden_size :],
    )
    routed_qkv = gather(after(own_attention(routed_query, routed_keys, routed_values), dense_qkv))
    expand_cut, shrink_cut = own_hidden(routed_expand, routed_shrink)
    routed_rest = jnp.concatenate([own_columns(routed_output), expand_cut, shrink_cut], axis=1)

    first_of = jnp.sum(
        (segment_ids[:, None, :] < jnp.arange(DOCS, dtype=jnp.int32)[None, :, None]).astype(jnp.int32), axis=2
    )

    def document(positions):
        shape = (seqs,) + (1,) * (positions.ndim - 1)
        found = jnp.zeros(positions.shape, jnp.int32)
        for c in range(1, DOCS):
            found = found + (positions >= first_of[:, c].reshape(shape)).astype(jnp.int32)
        return found

    def pick(table, index):
        shape = (seqs,) + (1,) * (index.ndim - 1)
        out = jnp.zeros(index.shape, jnp.int32)
        for c in range(DOCS):
            out = jnp.where(index == c, table[:, c].reshape(shape), out)
        return out

    blocks = jnp.arange(group, dtype=jnp.int32) * ring + place[0]
    attended_pos = blocks[:, None] * rows + jnp.arange(rows, dtype=jnp.int32)[None, :]
    attended_pos = jnp.broadcast_to(attended_pos[None], (seqs, group, rows))
    start = pick(first_of, document(attended_pos))[:, :, None, :]
    chosen_doc = document(chosen_rows)
    first_slot = jnp.sum(
        (chosen_doc[:, None, :] < jnp.arange(DOCS, dtype=jnp.int32)[None, :, None]).astype(jnp.int32), axis=2
    )
    chosen_start = pick(first_slot, chosen_doc).reshape(seqs, group, ring, sel)
    routed_start = lax.dynamic_index_in_dim(chosen_start, place[0], 2, keepdims=False)
    routed_start = routed_start.reshape(seqs, 1, group * sel)

    def pack(value):
        value = value.reshape(seqs, 2, rows // 2, group, HDIM)
        return jnp.transpose(value, (0, 2, 3, 1, 4)).reshape(tokens // 2, 2 * part)

    def unpack(value):
        value = value.reshape(seqs, rows // 2, group, 2, HDIM)
        return jnp.transpose(value, (0, 3, 1, 2, 4)).reshape(tokens, part)

    value = stream_in.reshape(tokens, width).astype(F32)
    grad_top = cotangent.reshape(tokens, width)
    inv_in = inverse_rms(value)
    normed = (value * inv_in * gain_pre).astype(BF)
    qkv = matmul(normed, dense_qkv).astype(BF)
    pairs, queries = dense_to_heads(
        lines, 2, qkv[:, : 2 * part], pack(qkv[:, 2 * part :]), "dense_to_heads"
    )
    routed_rest = gather(after(routed_rest, queries))
    queries = queries.reshape(group, seqs, rows // 2, lanes)
    pairs = pairs.reshape(ring, group, seqs, rows, lanes)
    mixed, mixed_turned, lse = dense_forward(place, queries, pairs, start)
    packed = (tokens // 2, group * lanes)
    (mixed,) = swap_blocks(
        lines, 3, "z", [mixed.reshape(group, tokens // 2, lanes)], [(packed, BF)], [(0, slot, 0, columns(lanes))],
        "dense_mixed",
    )
    mixed = gather_columns(lines, 4, unpack(mixed), "dense_mixed_columns")
    attended = gather_columns(lines, 5, matmul(mixed, dense_out).astype(BF), "dense_attended")
    middle_value = value + attended.astype(F32)
    inv_mid = inverse_rms(middle_value)
    normed_mid = (middle_value * inv_mid * gain_mid).astype(BF)
    hidden_pre = matmul(normed_mid, dense_exp)
    hidden, slope = gelu_terms(hidden_pre)
    hidden, slope = hidden.astype(BF), slope.astype(BF)
    fed = scatter_columns(lines, 6, matmul(hidden, dense_shr).astype(BF), None, "dense_fed")
    after_dense = own_columns(middle_value) + fed

    def reduce_dp(value):
        return lax.psum_scatter(value, "dp", scatter_dimension=0, tiled=True)

    source = jnp.concatenate([after_dense.astype(BF), own_columns(grad_top)], axis=1)
    fed_low, grad_own, added, routed_grads = routed_layer(
        lines,
        7,
        [
            source.reshape(seqs, rows, 2 * part),
            cotangent,
            chosen_rows[:, :, None],
            chosen_rows[:, None, :],
            routed_start,
            gains[2:5],
            routed_qkv,
            routed_rest,
        ],
        (seqs, sel, rows, width, part),
        "routed_layer",
    )
    stream_out = (after_dense + added.reshape(tokens, part).astype(F32)).astype(BF).reshape(seqs, rows, part)
    routed_shard = reduce_dp(routed_grads)

    dense_grads, dense_qkv_grad, stream_grad, d_vectors = dense_return(
        lines,
        8,
        [
            fed_low.reshape(tokens, width),
            grad_own.reshape(tokens, part),
            stream_in.reshape(tokens, width),
            attended,
            slope,
            hidden,
            mixed,
            rest,
            dense_qkv,
            queries,
            pairs,
            start,
            mixed_turned,
            lse,
            gains[:2],
        ],
        (seqs, rows, width, hidden_size),
        "dense_return",
    )
    stream_grad = stream_grad.reshape(seqs, rows, part)
    dense_shard = reduce_dp(dense_grads)
    vectors, dense_all_in, (routed_all,) = dense_finish(
        lines, 9, d_vectors, dense_qkv_grad, [routed_shard], "dense_finish"
    )
    dense_all = gather_columns(lines, 10, after(dense_shard, dense_all_in), "dense_shards")

    share = hidden_size // dp
    local = width // dp
    inner_at = hidden_size + width
    r_exp, r_shr, r_keys, r_values, r_query, r_out, r_vector = assemble(
        [
            ("hidden", routed_all, 0, hidden_size),
            ("stack", routed_all, hidden_size, width),
            ("pair", routed_all, inner_at, 2 * part),
            ("columns", routed_all, inner_at + 2 * part, part),
            ("columns", routed_all, inner_at + 3 * part, part),
            ("sum", routed_all, inner_at + 4 * part, 128),
        ],
        share,
        "routed_places",
    )
    d_exp, d_shr, d_out, d_keys, d_values, d_query = assemble(
        [
            ("hidden", dense_all, 0, hidden_size),
            ("stack", dense_all, hidden_size, width),
            ("columns", dense_all, hidden_size + width, part),
            ("pair", dense_all_in, 0, 2 * part),
            ("columns", dense_all_in, 2 * part, part),
        ],
        share,
        "dense_places",
    )
    vectors = lax.dynamic_slice_in_dim(vectors, rank * local, local, 1)
    d_shr = d_shr.reshape(sections * share, width)
    r_shr = r_shr.reshape(sections * share, width)
    return (
        (stream_out, stream_grad)
        + (vectors[1], d_query, d_keys, d_values, d_out, vectors[0], d_exp, d_shr)
        + (r_vector[:, 0], r_query, r_keys, r_values, r_out, r_vector[:, 1], r_exp, r_shr)
        + (r_vector[:, 2],)
    )


def solution(mesh):
    streams, row, vector, copied = P(None, "dp", None), P("dp", None), P("dp"), P()
    layer = (vector, row, row, row, row, vector, row, row)
    outs = (P(None, "dp", "section"),) * 2 + layer + layer + (vector,)
    return jax.shard_map(
        on_device,
        mesh=mesh,
        in_specs=(streams, copied, copied, streams) + layer + layer + (vector,),
        out_specs=outs,
        check_vma=False,
    )
```

```python
import functools

import jax
import jax.numpy as jnp
from jax import lax
from jax.experimental import pallas as pl
from jax.experimental.pallas import tpu as pltpu
from jax.sharding import PartitionSpec as P

HEADS = 16
HDIM = 64
DOCS = 8
EPS = 1e-06
NEG = -1e30
SCALE = HDIM ** (-0.5)
VMEM = 32 * 2**20
MESH = pl.DeviceIdType.MESH
BF = jnp.bfloat16
F32 = jnp.float32


def matmul(left, right):
    return jnp.dot(left, right, preferred_element_type=F32)


def contract(left, right, ldim, rdim):
    return lax.dot_general(left, right, (((ldim,), (rdim,)), ((), ())), preferred_element_type=F32)


class Lines:
    def __init__(self, sections, dp, group):
        self.sizes = {"section": sections, "z": group, "core": dp // group}
        self.ring = dp // group

    def place(self, kind):
        if kind == "section":
            return lax.axis_index("section")
        index = lax.axis_index("dp")
        return index // self.ring if kind == "z" else lax.rem(index, self.ring)

    def device(self, kind, place):
        if kind == "section":
            return {"section": place}
        index = lax.axis_index("dp")
        if kind == "z":
            return {"dp": place * self.ring + lax.rem(index, self.ring)}
        return {"dp": (index // self.ring) * self.ring + place}

    def peers(self, kind):
        size = self.sizes[kind]
        me = self.place(kind)
        return [lax.rem(me + step, size) for step in range(1, size)]


class Copies:
    loads, flush = (), None

    def __init__(self, lines, send, recv):
        self.lines, self.send, self.recv, self.used = lines, send, recv, 0

    def greet(self, kinds):
        barrier = pltpu.get_barrier_semaphore()
        count = 0
        for kind in kinds:
            for peer in self.lines.peers(kind):
                pl.semaphore_signal(
                    barrier, inc=1, device_id=self.lines.device(kind, peer), device_id_type=MESH
                )
                count += 1
        for load in Copies.loads:
            load.wait()
        pl.semaphore_wait(barrier, count)

    def start(self, kind, peer, src, dst):
        assert self.used < self.send.shape[0]
        copy = pltpu.make_async_remote_copy(
            src_ref=src,
            dst_ref=dst,
            send_sem=self.send.at[self.used],
            recv_sem=self.recv.at[self.used],
            device_id=self.lines.device(kind, peer),
            device_id_type=MESH,
        )
        self.used += 1
        copy.start()
        return copy

    def swap(self, kind, src, dst):
        me = self.lines.place(kind)
        return [self.start(kind, peer, src(peer), dst(me)) for peer in self.lines.peers(kind)]


def wait(copies):
    for copy in copies:
        copy.wait()


def semaphores(count):
    return [pltpu.SemaphoreType.DMA((count,)), pltpu.SemaphoreType.DMA((count,))]


def communicate(kernel, ident, arrays, shapes, scratch, name, limit=60 * 2**20, far=()):
    place = pl.BlockSpec(memory_space=pl.ANY)
    near = [i for i in range(len(arrays)) if i not in far]
    many, outs = len(arrays), len(shapes)

    def body(*refs):
        ins, results, refs = list(refs[:many]), refs[many : many + outs], refs[many + outs :]
        inner, refs = refs[: len(scratch)], refs[len(scratch) :]
        in_bufs, out_bufs, (in_sems, out_sems) = refs[: len(near)], refs[len(near) : len(near) + outs], refs[-2:]
        loads = []
        for k, i in enumerate(near):
            loads.append(pltpu.make_async_copy(ins[i], in_bufs[k], in_sems.at[k]))
            loads[-1].start()
            ins[i] = in_bufs[k]
        stores = [pltpu.make_async_copy(out_bufs[k], results[k], out_sems.at[k]) for k in range(outs)]
        started = set()

        def flush(ref):
            k = next(k for k in range(outs) if out_bufs[k] is ref)
            stores[k].start()
            started.add(k)

        Copies.loads, Copies.flush = loads, staticmethod(flush)
        kernel(*ins, *out_bufs, *inner)
        for k in range(outs):
            if k not in started:
                stores[k].start()
        for store in stores:
            store.wait()

    return pl.pallas_call(
        body,
        out_shape=[jax.ShapeDtypeStruct(s, d) for s, d in shapes],
        in_specs=[place] * many,
        out_specs=[place] * outs,
        scratch_shapes=list(scratch)
        + [pltpu.VMEM(arrays[i].shape, arrays[i].dtype) for i in near]
        + [pltpu.VMEM(s, d) for s, d in shapes]
        + [pltpu.SemaphoreType.DMA((max(1, len(near)),)), pltpu.SemaphoreType.DMA((outs,))],
        compiler_params=pltpu.CompilerParams(
            collective_id=ident, has_side_effects=True, vmem_limit_bytes=limit
        ),
        name=name,
    )(*arrays)


def span(place, width):
    return pl.ds(pl.multiple_of(place * width, width), width)


def square(lines):
    me = lines.place("section")
    low, high = lax.rem(me, 2), me // 2
    return high * 2 + 1 - low, (1 - high) * 2 + low, (1 - high) * 2 + 1 - low


def pieces_of(rows):
    half = rows // 2
    return (2, half // 2) if half % 32 == 0 else (1, half)


class SquareGather:
    @staticmethod
    def count(rows):
        return 6 * pieces_of(rows)[0]

    def __init__(self, copies, x_ref, o_ref, pieces=None):
        self.copies, self.x_ref, self.o_ref = copies, x_ref, o_ref
        self.width = x_ref.shape[1]
        self.me = copies.lines.place("section")
        near, far, _ = square(copies.lines)
        half = x_ref.shape[0] // 2
        pieces, step = pieces_of(x_ref.shape[0]) if pieces is None else (pieces, half // pieces)
        self.parts = [
            (pl.ds(h * half + j * step, step), one, two)
            for j in range(pieces)
            for h, (one, two) in enumerate(((near, far), (far, near)))
        ]

    def send(self, at, to):
        dst = self.o_ref.at[at, span(self.me, self.width)]
        return self.copies.start("section", to, self.x_ref.at[at], dst)

    def start(self):
        self.first = [self.send(at, one) for at, one, _ in self.parts]
        self.rest = [self.send(at, two) for at, _, two in self.parts]
        self.o_ref[:, span(self.me, self.width)] = self.x_ref[...]

    def forward(self):
        for (at, one, two), copy in zip(self.parts, self.first):
            copy.wait_recv()
            place = self.o_ref.at[at, span(one, self.width)]
            self.rest.append(self.copies.start("section", two, place, place))

    def finish(self):
        for copy in self.first:
            copy.wait_send()
        wait(self.rest)


class SquareScatter:
    @staticmethod
    def count(rows):
        return 6 * pieces_of(rows)[0]

    @staticmethod
    def scratch(rows, width):
        return [pltpu.VMEM((2, rows, width), BF), pltpu.VMEM((rows, width), BF), pltpu.VMEM((rows, width), BF)]

    def __init__(self, copies, x_ref, got, turn, last, pieces=None):
        self.copies, self.x_ref, self.got, self.turn, self.last = copies, x_ref, got, turn, last
        self.width = turn.shape[1]
        self.me = copies.lines.place("section")
        near, far, self.across = square(copies.lines)
        half = x_ref.shape[0] // 2
        pieces, step = pieces_of(x_ref.shape[0]) if pieces is None else (pieces, half // pieces)
        self.parts = [
            (pl.ds(h * half + j * step, step), one, two)
            for j in range(pieces)
            for h, (one, two) in enumerate(((near, far), (far, near)))
        ]

    def read(self, at, place):
        return self.x_ref[at, span(place, self.width)].astype(F32)

    def start(self):
        self.passed, self.kept = [], []
        for at, one, _ in self.parts:
            for place, k, out in ((self.across, 0, self.passed), (one, 1, self.kept)):
                src = self.x_ref.at[at, span(place, self.width)]
                out.append(self.copies.start("section", one, src, self.got.at[k, at]))

    def forward(self):
        self.second = []
        for (at, _, two), copy in zip(self.parts, self.passed):
            copy.wait_recv()
            self.turn[at] = (self.read(at, two) + self.got[0, at].astype(F32)).astype(BF)
            self.second.append(self.copies.start("section", two, self.turn.at[at], self.last.at[at]))

    def finish(self, o_ref):
        for i, (at, _, _) in enumerate(self.parts):
            self.kept[i].wait_recv()
            self.second[i].wait_recv()
            o_ref[at] = self.read(at, self.me) + self.got[1, at].astype(F32) + self.last[at].astype(F32)
        for copy in self.passed + self.kept + self.second:
            copy.wait_send()


def gather_columns(lines, ident, part, name):
    rows, width = part.shape

    def kernel(x_ref, o_ref, send, recv):
        copies = Copies(lines, send, recv)
        copies.greet(["section"])
        gather = SquareGather(copies, x_ref, o_ref)
        gather.start()
        gather.forward()
        gather.finish()

    shape = ((rows, lines.sizes["section"] * width), part.dtype)
    (out,) = communicate(kernel, ident, [part], [shape], semaphores(SquareGather.count(rows)), name)
    return out


def scalar_block(scalars):
    count = -(-scalars.shape[0] // 128)
    count += -count % 8
    return jnp.pad(scalars, (0, count * 128 - scalars.shape[0])).reshape(count, 128)


def sum_places(ref):
    total = ref[0].astype(F32)
    for i in range(1, ref.shape[0]):
        total = total + ref[i].astype(F32)
    return total


def scatter_columns(lines, ident, part, scalars, name):
    rows, full = part.shape
    sections = lines.sizes["section"]
    width = full // sections
    extra = scalars is not None
    arrays = [part]
    shapes = [((rows, width), F32)]
    scratch = semaphores(SquareScatter.count(rows) + sections - 1) + SquareScatter.scratch(rows, width)
    if extra:
        arrays.append(scalar_block(scalars))
        shapes.append((arrays[1].shape, F32))
        scratch.append(pltpu.VMEM((sections,) + arrays[1].shape, F32))

    def kernel(*refs):
        x_ref, refs = refs[0], refs[1:]
        if extra:
            e_ref, o_ref, eo_ref, send, recv, got, turn, last, e_got = refs
        else:
            o_ref, send, recv, got, turn, last = refs
        copies = Copies(lines, send, recv)
        copies.greet(["section"])
        scatter = SquareScatter(copies, x_ref, got, turn, last)
        scatter.start()
        if extra:
            others = copies.swap("section", lambda peer: e_ref, lambda place: e_got.at[place])
            e_got[lines.place("section")] = e_ref[...]
        scatter.forward()
        scatter.finish(o_ref)
        if extra:
            wait(others)
            eo_ref[...] = sum_places(e_got)

    got = communicate(kernel, ident, arrays, shapes, scratch, name)
    if not extra:
        return got[0]
    return got[0], got[1].reshape(-1)[:rows]


def dense_finish(lines, ident, vectors, weight, shards, name):
    group, ring, sections = (lines.sizes[k] for k in ("z", "core", "section"))
    dp = group * ring
    many = len(shards)
    local = weight.shape[0] // dp
    wide = weight.shape[1]
    weight = weight.reshape(dp, local, wide)
    width = vectors.shape[1]

    def kernel(x_ref, w_ref, *refs):
        s_refs, refs = refs[:many], refs[many:]
        v_ref, wo_ref, refs = refs[0], refs[1], refs[2:]
        so_refs, refs = refs[:many], refs[many:]
        send, recv, w_got, w_turn, w_all, w_own, v_z, v_core, v_all = refs
        copies = Copies(lines, send, recv)
        zplace, place, section = (lines.place(k) for k in ("z", "core", "section"))
        copies.greet(["z", "core", "section"])
        order = lines.peers("z") + [zplace]
        around = [
            copies.swap("core", lambda peer: w_ref.at[g * ring + peer], lambda me: w_got.at[me, g]) for g in order
        ]
        pending = copies.swap("z", lambda peer: x_ref, lambda me: v_z.at[me])
        v_z[zplace] = x_ref[...]
        gathers = [SquareGather(copies, x, o) for x, o in zip(s_refs, so_refs)]
        for gather in gathers:
            gather.start()
        along = []
        for i, (g, arrived) in enumerate(zip(order, around)):
            for copy in arrived:
                copy.wait_recv()
            total = w_ref[g * ring + place].astype(F32)
            for peer in lines.peers("core"):
                total = total + w_got[peer, g].astype(F32)
            w_turn[g] = total.astype(BF)
            if i < len(order) - 1:
                along.append(copies.start("z", g, w_turn.at[g], w_all.at[zplace]))
        wait(pending)
        v_core[place] = sum_places(v_z)
        wait(copies.swap("core", lambda peer: v_core.at[place], lambda me: v_core.at[me]))
        v_all[section] = sum_places(v_core)
        pending = copies.swap("section", lambda peer: v_all.at[section], lambda me: v_all.at[me])
        for gather in gathers:
            gather.forward()
        wait(along)
        w_all[zplace] = w_turn[zplace]
        w_own[...] = sum_places(w_all).astype(BF)
        last_gather = SquareGather(copies, w_own, wo_ref)
        last_gather.start()
        wait(pending)
        for i in range(sections):
            v_ref[:, i * width : (i + 1) * width] = v_all[i]
        last_gather.forward()
        for arrived in around:
            for copy in arrived:
                copy.wait_send()
        for gather in gathers:
            gather.finish()
        last_gather.finish()

    z, c, s = group - 1, ring - 1, sections - 1
    result = communicate(
        kernel,
        ident,
        [vectors, weight] + shards,
        [((8, sections * width), F32), ((local, sections * wide), BF)]
        + [((x.shape[0], sections * x.shape[1]), x.dtype) for x in shards],
        semaphores(
            group * c
            + z
            + sum(SquareGather.count(x.shape[0]) for x in shards)
            + SquareGather.count(local)
            + z
            + c
            + s
        )
        + [
            pltpu.VMEM((ring, group, local, wide), BF),
            pltpu.VMEM((group, local, wide), BF),
            pltpu.VMEM((group, local, wide), BF),
            pltpu.VMEM((local, wide), BF),
            pltpu.VMEM((group, 8, width), F32),
            pltpu.VMEM((ring, 8, width), F32),
            pltpu.VMEM((sections, 8, width), F32),
        ],
        name,
        limit=60 * 2**20,
    )
    return result[0], result[1], result[2:]


def assemble(pieces, share, name):
    arrays = []
    for _, array, _, _ in pieces:
        if not any(array is other for other in arrays):
            arrays.append(array)
    where = [next(i for i, other in enumerate(arrays) if other is array) for _, array, _, _ in pieces]
    local = arrays[0].shape[0]
    steps = local // 32 if local % 32 == 0 else 1
    rows = local // steps
    sections = lax.axis_size("section")
    shapes, specs = [], []
    for kind, _, _, width in pieces:
        many = 2 if kind == "pair" else 1
        for _ in range(many):
            if kind == "stack":
                shapes.append(jax.ShapeDtypeStruct((sections, local, width), F32))
                specs.append(pl.BlockSpec((sections, rows, width), lambda i: (0, i, 0)))
            else:
                total = width if kind == "sum" else sections * width // many
                shapes.append(jax.ShapeDtypeStruct((local, total), F32))
                specs.append(pl.BlockSpec((rows, total), lambda i: (i, 0)))

    def kernel(*refs):
        ins, outs = refs[: len(arrays)], list(refs[len(arrays) :])
        for (kind, array, first, width), i in zip(pieces, where):
            wide = array.shape[1] // sections
            blocks = [ins[i][:, s * wide + first : s * wide + first + width].astype(F32) for s in range(sections)]
            out = outs.pop(0)
            if kind == "columns":
                for s, item in enumerate(blocks):
                    out[:, s * width : (s + 1) * width] = item
            elif kind == "stack":
                for s, item in enumerate(blocks):
                    out[s] = item
            elif kind == "sum":
                total = blocks[0]
                for item in blocks[1:]:
                    total = total + item
                out[...] = total
            elif kind == "hidden":
                for d in range(width // share):
                    out[:, d * share * sections : (d + 1) * share * sections] = jnp.concatenate(
                        [item[:, d * share : (d + 1) * share] for item in blocks], axis=1
                    )
            else:
                other = outs.pop(0)
                half = width // 2
                for s, item in enumerate(blocks):
                    for side, dst in ((0, out), (1, other)):
                        heads = [
                            item[:, (2 * g + side) * HDIM : (2 * g + side + 1) * HDIM]
                            for g in range(width // (2 * HDIM))
                        ]
                        dst[:, s * half : (s + 1) * half] = jnp.concatenate(heads, axis=1)

    return pl.pallas_call(
        kernel,
        grid=(steps,),
        in_specs=[pl.BlockSpec((rows, a.shape[1]), lambda i: (i, 0)) for a in arrays],
        out_specs=specs,
        out_shape=shapes,
        compiler_params=pltpu.CompilerParams(vmem_limit_bytes=60 * 2**20),
        name=name,
    )(*arrays)


def column_to_rows(column):
    return jnp.broadcast_to(column, (column.shape[0], 128)).T[:8]


def row_to_column(row):
    return jnp.broadcast_to(row, (128, row.shape[1])).T[:, :1]


def outer_product(left_ref, right_ref, out_ref, first):
    step = 256
    wide = right_ref.shape[1]
    for i in range(left_ref.shape[1] // step):
        block = contract(left_ref[:, i * step : (i + 1) * step], right_ref[...], 0, 0)
        out_ref[i * step : (i + 1) * step, first : first + wide] = block.astype(BF)


def unpack_low(packed):
    lane = lax.broadcasted_iota(jnp.int32, packed.shape, 1)
    zero = jnp.zeros_like(packed)
    low = jnp.where(lane < HDIM, packed, zero)
    turned = jnp.concatenate([packed[:, HDIM:], packed[:, :HDIM]], axis=1)
    high = jnp.where(lane < HDIM, turned, zero)
    return jnp.concatenate([low, high], axis=0)


def unpack_high(packed):
    lane = lax.broadcasted_iota(jnp.int32, packed.shape, 1)
    zero = jnp.zeros_like(packed)
    turned = jnp.concatenate([packed[:, HDIM:], packed[:, :HDIM]], axis=1)
    low = jnp.where(lane >= HDIM, turned, zero)
    high = jnp.where(lane >= HDIM, packed, zero)
    return jnp.concatenate([low, high], axis=0)


def pack_turned(turned):
    half = turned.shape[1] // 2
    return jnp.concatenate([turned[:, :half], turned[:, half:]], axis=0).T


def forward_block(query, pieces, qpos, start, causal):
    scores = []
    peak = None
    for index, (pair, _, first) in enumerate(pieces):
        item = contract(pair, query, 1, 1)
        kpos = first + lax.broadcasted_iota(jnp.int32, item.shape, 0)
        allowed = kpos >= start
        if causal[index]:
            allowed = allowed & (kpos <= qpos)
        item = jnp.where(allowed, item, NEG)
        top = jnp.max(item, axis=0, keepdims=True)
        peak = top if peak is None else jnp.maximum(peak, top)
        scores.append(item)
    total = jnp.zeros_like(peak)
    mixed = None
    for item, (_, turned, _) in zip(scores, pieces):
        weight = jnp.exp(item - peak)
        total = total + jnp.sum(weight, axis=0, keepdims=True)
        part = matmul(turned[HDIM:], weight.astype(BF))
        mixed = part if mixed is None else mixed + part
    return mixed / total, peak + jnp.log(total)


def backward_block(query, grad, grad_turned, mixed_turned, lse, pieces, qpos, start, causal):
    row_sum = jnp.sum(grad_turned.astype(F32) * mixed_turned.astype(F32), axis=0, keepdims=True)
    grad_query = None
    grads = []
    for index, (pair, turned, first) in enumerate(pieces):
        scores = contract(pair, query, 1, 1)
        kpos = first + lax.broadcasted_iota(jnp.int32, scores.shape, 0)
        allowed = kpos >= start
        if causal[index]:
            allowed = allowed & (kpos <= qpos)
        probs = jnp.where(allowed, jnp.exp(scores - lse), 0.0)
        grad_probs = contract(pair, grad, 1, 1)
        grad_scores = (probs * (grad_probs - row_sum)).astype(BF)
        grads.append(matmul(grad_scores, query) + matmul(probs.astype(BF), grad))
        part = matmul(turned[:HDIM], grad_scores)
        grad_query = part if grad_query is None else grad_query + part
    return grad_query * SCALE, grads


def document_starts(ids):
    return [
        jnp.sum((ids < c).astype(F32), axis=1, keepdims=True) if c else jnp.zeros((1, 1), F32) for c in range(DOCS)
    ]


def start_of(documents, firsts):
    start = jnp.zeros(documents.shape, F32)
    for c in range(1, DOCS):
        start = jnp.where(documents >= c, firsts[c], start)
    return start.astype(jnp.int32)


def dense_enter(lines, ident, arrays, shape, name):
    seqs, rows, width = shape
    sections, group, ring = (lines.sizes[k] for k in ("section", "z", "core"))
    dp = group * ring
    part = width // sections
    half = rows // 2
    lanes = 2 * HDIM
    block = ring * rows
    local = width // dp

    def kernel(
        value_ref,
        weights_ref,
        cut_ref,
        ids_ref,
        weights_all,
        gains_ref,
        q_got,
        kv_all,
        start_ref,
        turned_ref,
        lse_ref,
        mixed_ref,
        send,
        recv,
        cut_all,
        kv_buf,
        q_buf,
        o_buf,
        o_got,
        o_own,
    ):
        copies = Copies(lines, send, recv)
        zplace, place = lines.place("z"), lines.place("core")
        rank = lax.axis_index("dp")
        copies.greet(["section", "z", "core"])
        pairs = [(weights_ref, weights_all), (cut_ref, cut_all)]
        along, handed = [], []
        for x_ref, o_ref in pairs:
            along.append(copies.swap("z", lambda peer: x_ref, lambda _: o_ref.at[rank]))
        for x_ref, o_ref in pairs:
            handed += copies.swap("core", lambda peer: x_ref, lambda _: o_ref.at[rank])
            o_ref[rank] = x_ref[...]
        for q in range(seqs):
            firsts = document_starts(ids_ref[q])
            for g in range(group):
                at = pl.ds(pl.multiple_of((g * ring + place) * rows, rows), rows)
                start_ref[q, g] = start_of(ids_ref[q, :, at], firsts)
        for step in range(group - 1, 0, -1):
            source = lax.rem(zplace + step, group) * ring + place
            for arrived, (_, o_ref) in zip(along, pairs):
                arrived[group - 1 - step].wait_recv()
                handed += copies.swap("core", lambda peer: o_ref.at[source], lambda _: o_ref.at[source])
        for arrived in along:
            for copy in arrived:
                copy.wait_send()
        wait(handed)
        for d in range(dp):
            gains_ref[:, d * local : (d + 1) * local] = cut_all[d].astype(F32)

        arriving, queries, around, outward, gathers = {}, {}, {}, {}, {}

        def project(q):
            value = value_ref[pl.ds(q * rows, rows)].astype(F32)
            normed = (value * inverse_rms(value) * gains_ref[0:1]).astype(BF)
            qkv = matmul(normed, weights_all[...].reshape(width, 3 * part)).astype(BF)
            for g in range(group):
                kv_buf[g, q] = qkv[:, g * lanes : (g + 1) * lanes]
                at = slice(2 * part + g * HDIM, 2 * part + (g + 1) * HDIM)
                q_buf[g, q] = side_by_side([qkv[:half, at], qkv[half:, at]])
            arriving[q] = copies.swap("z", lambda peer: kv_buf.at[peer, q], lambda me: kv_all.at[place, me, q])
            queries[q] = copies.swap("z", lambda peer: q_buf.at[peer, q], lambda me: q_got.at[me, q])
            q_got[zplace, q] = q_buf[zplace, q]
            kv_all[place, zplace, q] = kv_buf[zplace, q]
            own = kv_all.at[place, zplace, q]
            around[q] = copies.swap("core", lambda peer: own, lambda _: own)

        def hand(q):
            for step in range(group - 1, 0, -1):
                arriving[q][group - 1 - step].wait_recv()
                item = kv_all.at[place, lax.rem(zplace + step, group), q]
                around[q] += copies.swap("core", lambda peer: item, lambda _: item)

        def attend(q):
            for copy in arriving[q]:
                copy.wait_send()
            wait(queries[q])
            wait(around[q])
            pieces = []
            for g in range(group):
                pair = kv_all[:, g, q].reshape(block, lanes)
                pieces.append((pair, pair.T, g * block))
            for g in range(group):
                query = unpack_low(q_got[g, q]) * jnp.asarray(SCALE, BF)
                qpos = g * block + place * rows + lax.broadcasted_iota(jnp.int32, (1, rows), 1)
                mixed, lse = forward_block(
                    query, pieces[: g + 1], qpos, start_ref[q, g], [i == g for i in range(g + 1)]
                )
                turned_ref[q, g] = mixed.astype(BF)
                lse_ref[q, g] = lse
                o_buf[g, q] = pack_turned(mixed).astype(BF)
            outward[q] = copies.swap("z", lambda peer: o_buf.at[peer, q], lambda me: o_got.at[me, q])
            o_got[zplace, q] = o_buf[zplace, q]

        def merge(q):
            wait(outward[q])
            packed = [o_got[g, q] for g in range(group)]
            o_own[q] = side_by_side([jnp.concatenate([p[:, :HDIM], p[:, HDIM:]], axis=0) for p in packed])
            gathers[q] = SquareGather(copies, o_own.at[q], mixed_ref.at[q], 1)
            gathers[q].start()

        for q in range(seqs):
            project(q)
        for q in range(seqs):
            hand(q)
            attend(q)
            if q > 0:
                merge(q - 1)
            if q > 1:
                gathers[q - 2].forward()
        merge(seqs - 1)
        for q in range(max(0, seqs - 2), seqs):
            gathers[q].forward()
        for q in range(seqs):
            gathers[q].finish()

    z, c = group - 1, ring - 1
    vmem = pltpu.VMEM
    packed = ((group, seqs, half, lanes), BF)
    return communicate(
        kernel,
        ident,
        arrays,
        [
            ((dp, local, 3 * part), BF),
            ((16, width), F32),
            packed,
            ((ring, group, seqs, rows, lanes), BF),
            ((seqs, group, 1, rows), jnp.int32),
            ((seqs, group, HDIM, rows), BF),
            ((seqs, group, 1, rows), F32),
            ((seqs, rows, width), BF),
        ],
        semaphores(2 * (z + group * c) + seqs * (3 * z + group * c + 6))
        + [
            vmem((dp, 16, local), BF),
            vmem((group, seqs, rows, lanes), BF),
            vmem(*packed),
            vmem(*packed),
            vmem(*packed),
            vmem((seqs, rows, part), BF),
        ],
        name,
        limit=60 * 2**20,
    )


def dense_feed(lines, ident, arrays, shape, name):
    seqs, rows, width, hidden_size = shape
    sections = lines.sizes["section"]
    part = width // sections

    def kernel(
        value_ref,
        mixed_ref,
        gains_ref,
        rest_ref,
        attended_ref,
        slope_ref,
        hidden_ref,
        out_ref,
        send,
        recv,
        sems,
        out_w,
        expand_w,
        shrink_w,
        own_buf,
        wide,
        got,
        turn,
        last,
    ):
        loads = Loads(sems)
        out_load = loads.start(rest_ref.at[:, :part], out_w)
        expand_load = loads.start(rest_ref.at[:, part : part + hidden_size], expand_w)
        shrink_load = loads.start(rest_ref.at[:, part + hidden_size :], shrink_w)
        copies = Copies(lines, send, recv)
        own = span(lines.place("section"), part)
        copies.greet(["section"])
        out_load.wait()
        gathers, scatters = {}, {}

        def project(q):
            own_buf[q] = matmul(mixed_ref[q], out_w[...]).astype(BF)
            gathers[q] = SquareGather(copies, own_buf.at[q], attended_ref.at[q], 1)
            gathers[q].start()

        def feed(q):
            gathers[q].finish()
            middle = value_ref[q].astype(F32) + attended_ref[q].astype(F32)
            normed = (middle * inverse_rms(middle) * gains_ref[1:2]).astype(BF)
            hidden, slope = gelu_terms(matmul(normed, expand_w[...]))
            hidden = hidden.astype(BF)
            hidden_ref[q] = hidden
            slope_ref[q] = slope.astype(BF)
            wide[q] = matmul(hidden, shrink_w[...]).astype(BF)
            scatters[q] = SquareScatter(copies, wide.at[q], got.at[q], turn.at[q], last.at[q], 1)
            scatters[q].start()

        def leave(q):
            scatters[q].finish(out_ref.at[q])
            out_ref[q] = out_ref[q] + value_ref[q, :, own].astype(F32) + attended_ref[q, :, own].astype(F32)

        for q in range(seqs):
            project(q)
            if q > 0:
                gathers[q - 1].forward()
        gathers[seqs - 1].forward()
        expand_load.wait()
        shrink_load.wait()
        for q in range(seqs):
            feed(q)
            if q > 0:
                scatters[q - 1].forward()
            if q > 1:
                leave(q - 2)
        scatters[seqs - 1].forward()
        for q in range(max(0, seqs - 2), seqs):
            leave(q)

    vmem = pltpu.VMEM
    return communicate(
        kernel,
        ident,
        arrays,
        [
            ((seqs, rows, width), BF),
            ((seqs, rows, hidden_size), BF),
            ((seqs, rows, hidden_size), BF),
            ((seqs, rows, part), F32),
        ],
        semaphores(seqs * 12)
        + [
            pltpu.SemaphoreType.DMA((3,)),
            vmem((width, part), BF),
            vmem((width, hidden_size), BF),
            vmem((hidden_size, width), BF),
            vmem((seqs, rows, part), BF),
            vmem((seqs, rows, width), BF),
            vmem((seqs, 2, rows, part), BF),
            vmem((seqs, rows, part), BF),
            vmem((seqs, rows, part), BF),
        ],
        name,
        limit=60 * 2**20,
        far=(3,),
    )


class SequenceSums:
    @staticmethod
    def count(sections, seqs, scalars):
        return seqs * (6 + (sections - 1 if scalars else 0))

    @staticmethod
    def scratch(sections, seqs, rows, part, scalars):
        vmem = pltpu.VMEM
        buffers = [
            vmem((seqs, rows, sections * part), BF),
            vmem((seqs, 2, rows, part), BF),
            vmem((seqs, rows, part), BF),
            vmem((seqs, rows, part), BF),
            vmem((rows, part), F32),
        ]
        if scalars:
            buffers += [vmem((seqs, 8, rows), F32), vmem((seqs, sections, 8, rows), F32)]
        return buffers

    def __init__(self, copies, buffers):
        self.copies, self.buffers, self.items = copies, buffers, {}

    def start(self, q, value, scalars=None):
        wide, got, turn, last = self.buffers[:4]
        wide[q] = value.astype(BF)
        item = SquareScatter(self.copies, wide.at[q], got.at[q], turn.at[q], last.at[q], 1)
        item.start()
        others = []
        if scalars is not None:
            buf, arrived = self.buffers[5:]
            section = self.copies.lines.place("section")
            buf[q] = column_to_rows(scalars)
            others = self.copies.swap("section", lambda peer: buf.at[q], lambda me: arrived.at[q, me])
            arrived[q, section] = buf[q]
        self.items[q] = (item, others)

    def forward(self, q):
        self.items[q][0].forward()

    def finish(self, q):
        item, others = self.items[q]
        total = self.buffers[4]
        item.finish(total)
        if not others:
            return total[...]
        wait(others)
        return total[...], row_to_column(sum_places(self.buffers[6].at[q])[:1])


class Loads:
    def __init__(self, sems):
        self.sems, self.used = sems, 0

    def start(self, src, dst):
        copy = pltpu.make_async_copy(src, dst, self.sems.at[self.used])
        self.used += 1
        copy.start()
        return copy


def dense_return(lines, ident, arrays, shape, name):
    seqs, rows, width, hidden_size = shape
    sections, group = lines.sizes["section"], lines.sizes["z"]
    part = width // sections
    half = rows // 2

    def kernel(
        fed_ref,
        own_ref,
        value_ref,
        attended_ref,
        slope_ref,
        hidden_ref,
        rest_ref,
        gains_ref,
        grads_ref,
        dattended,
        middle,
        heads,
        vectors_ref,
        send,
        recv,
        sems,
        out_w,
        expand_w,
        shrink_w,
        hidden,
        normed,
        dpre,
        *buffers,
    ):
        loads = Loads(sems)
        shrink_load = loads.start(rest_ref.at[:, part + hidden_size :], shrink_w)
        expand_load = loads.start(rest_ref.at[:, part : part + hidden_size], expand_w)
        out_load = loads.start(rest_ref.at[:, :part], out_w)
        hidden_load = loads.start(hidden_ref, hidden)
        copies = Copies(lines, send, recv)
        own = span(lines.place("section"), part)
        copies.greet(["section"])
        mids = SequenceSums(copies, buffers[:7])
        outs = SequenceSums(copies, buffers[7:])

        def middle_of(at):
            return value_ref[at].astype(F32) + attended_ref[at].astype(F32)

        def feed(q):
            at = pl.ds(q * rows, rows)
            grad_hidden = contract(fed_ref[at], shrink_w[...], 1, 1)
            grad_pre = (grad_hidden * slope_ref[at].astype(F32)).astype(BF)
            dpre[at] = grad_pre
            grad_normed = contract(grad_pre, expand_w[...], 1, 1)
            mid = middle_of(at)
            mids.start(q, grad_normed, jnp.sum(grad_normed * mid * gains_ref[1:2], axis=1, keepdims=True))
            normed[at] = (mid * inverse_rms(mid) * gains_ref[1:2]).astype(BF)

        def project(q):
            at = pl.ds(q * rows, rows)
            grad_normed, scalars = mids.finish(q)
            inv = inverse_rms(middle_of(at))
            mid = value_ref[at, own].astype(F32) + attended_ref[at, own].astype(F32)
            vectors_ref[0:1] += jnp.sum(grad_normed * mid * inv, axis=0, keepdims=True)
            grad = (
                inv * (grad_normed * gains_ref[1:2, own])
                - mid * (inv * inv * inv) * (scalars * (1.0 / width))
                + own_ref[at]
            )
            middle[at] = grad
            low = grad.astype(BF)
            dattended[at] = low
            outs.start(q, contract(low, out_w[...], 1, 1))

        def leave(q):
            grad = outs.finish(q).astype(BF)
            for g in range(group):
                columns = slice(g * HDIM, (g + 1) * HDIM)
                heads[g, q] = side_by_side([grad[:half, columns], grad[half:, columns]])

        vectors_ref[...] = jnp.zeros_like(vectors_ref)
        shrink_load.wait()
        expand_load.wait()
        out_load.wait()
        last = seqs - 1
        for q in range(seqs):
            feed(q)
            if q > 0:
                mids.forward(q - 1)
            if q > 1:
                project(q - 2)
        mids.forward(last)
        hidden_load.wait()
        outer_product(hidden, fed_ref, grads_ref, hidden_size)
        for q in range(max(0, last - 1), seqs):
            project(q)
            outs.forward(q - 1)
        outer_product(normed, dpre, grads_ref, 0)
        Copies.flush(grads_ref)
        outs.forward(last)
        for q in range(seqs):
            leave(q)

    tokens = seqs * rows
    vmem = pltpu.VMEM
    return communicate(
        kernel,
        ident,
        arrays,
        [
            ((width, hidden_size + width), BF),
            ((tokens, part), BF),
            ((tokens, part), F32),
            ((group, seqs, half, 2 * HDIM), BF),
            ((8, part), F32),
        ],
        semaphores(SequenceSums.count(sections, seqs, True) + SequenceSums.count(sections, seqs, False))
        + [
            pltpu.SemaphoreType.DMA((4,)),
            vmem((width, part), BF),
            vmem((width, hidden_size), BF),
            vmem((hidden_size, width), BF),
            vmem((tokens, hidden_size), BF),
            vmem((tokens, width), BF),
            vmem((tokens, hidden_size), BF),
        ]
        + SequenceSums.scratch(sections, seqs, rows, part, True)
        + SequenceSums.scratch(sections, seqs, rows, part, False),
        name,
        limit=60 * 2**20,
        far=(5, 6),
    )


def dense_leave(lines, ident, arrays, shards, shape, name):
    seqs, rows, width = shape
    sections, group, ring = (lines.sizes[k] for k in ("section", "z", "core"))
    part = width // sections
    half = rows // 2
    lanes = 2 * HDIM
    block = ring * rows
    many = len(shards)
    tokens = seqs * rows

    def kernel(
        heads,
        value_ref,
        q_ref,
        kv_ref,
        start_ref,
        turned_ref,
        lse_ref,
        qkv_w,
        mixed_ref,
        dattended,
        middle,
        gains_ref,
        mid_vectors_ref,
        *refs,
    ):
        s_refs, refs = refs[:many], refs[many:]
        (grads_ref, stream_ref, vectors_ref), refs = refs[:3], refs[3:]
        so_refs, refs = refs[:many], refs[many:]
        (
            send,
            recv,
            sems,
            kv,
            mixed,
            normed,
            dqkv,
            heads_got,
            acc,
            pairs,
            pairs_got,
            queries,
            queries_got,
            sums,
            sums_got,
            *buffers,
        ) = refs
        loads = Loads(sems)
        mixed_load = loads.start(mixed_ref, mixed)
        kv_loads = {0: loads.start(kv_ref.at[:, :, 0], kv)}
        copies = Copies(lines, send, recv)
        section, zplace, place = (lines.place(k) for k in ("section", "z", "core"))
        own = span(section, part)
        copies.greet(["section", "z", "core"])
        inner = SequenceSums(copies, buffers)
        arriving, around, along, back = {}, {}, {}, {}
        for q in range(seqs):
            heads_got[zplace, q] = heads[zplace, q]
            arriving[q] = copies.swap("z", lambda peer: heads.at[peer, q], lambda me: heads_got.at[me, q])
        gathers = [SquareGather(copies, x, o) for x, o in zip(s_refs, so_refs)]
        for gather in gathers:
            gather.start()

        def attend(q):
            wait(arriving[q])
            kv_loads[q].wait()
            pieces = []
            for g in range(group):
                pair = kv[:, g].reshape(block, lanes)
                pieces.append((pair, pair.T, g * block))
            for g in reversed(range(group)):
                query = unpack_low(q_ref[g, q]) * jnp.asarray(SCALE, BF)
                packed = heads_got[g, q]
                flat = packed.T
                qpos = g * block + place * rows + lax.broadcasted_iota(jnp.int32, (1, rows), 1)
                grad_query, grads = backward_block(
                    query,
                    unpack_high(packed),
                    side_by_side([flat[:HDIM], flat[HDIM:]]),
                    turned_ref[q, g],
                    lse_ref[q, g],
                    pieces[: g + 1],
                    qpos,
                    start_ref[q, g],
                    [i == g for i in range(g + 1)],
                )
                queries[g, q] = pack_turned(grad_query).astype(BF)
                for i, item in enumerate(grads):
                    if g == group - 1:
                        acc[i] = item
                    else:
                        acc[i] += item
            if q > 0:
                wait(around[q - 1])
            for g in range(group):
                for r in range(ring):
                    pairs[r, g] = acc[g, r * rows : (r + 1) * rows].astype(BF)
            if q + 1 < seqs:
                kv_loads[q + 1] = loads.start(kv_ref.at[:, :, q + 1], kv)
            queries_got[zplace, q] = queries[zplace, q]
            around[q] = copies.swap("core", lambda peer: pairs.at[peer], lambda me: pairs_got.at[me, :, q])
            along[q] = copies.swap("z", lambda peer: queries.at[peer, q], lambda me: queries_got.at[me, q])

        def to_tokens(q):
            wait(around[q])
            around[q] = []
            for g in range(group):
                item = pairs[place, g].astype(F32)
                for peer in lines.peers("core"):
                    item = item + pairs_got[peer, g, q].astype(F32)
                sums[g, q] = item.astype(BF)
            sums_got[zplace, q] = sums[zplace, q]
            back[q] = copies.swap("z", lambda peer: sums.at[peer, q], lambda me: sums_got.at[me, q])

        def enter(q):
            wait(back[q] + along[q])
            at = pl.ds(q * rows, rows)
            packed = [queries_got[g, q] for g in range(group)]
            upright = [jnp.concatenate([p[:, :HDIM], p[:, HDIM:]], axis=0) for p in packed]
            grad = side_by_side([sums_got[g, q] for g in range(group)] + upright)
            dqkv[at] = grad
            grad_normed = contract(grad, qkv_w[...], 1, 1)
            value = value_ref[at].astype(F32)
            inner.start(q, grad_normed, jnp.sum(grad_normed * value * gains_ref[0:1], axis=1, keepdims=True))

        def leave(q):
            at = pl.ds(q * rows, rows)
            grad_normed, scalars = inner.finish(q)
            inv = inverse_rms(value_ref[at].astype(F32))
            value = value_ref[at, own].astype(F32)
            vectors_ref[1:2] += jnp.sum(grad_normed * value * inv, axis=0, keepdims=True)
            grad = (
                inv * (grad_normed * gains_ref[0:1, own])
                - value * (inv * inv * inv) * (scalars * (1.0 / width))
                + middle[at]
            )
            stream_ref[at] = grad.astype(BF)

        vectors_ref[...] = mid_vectors_ref[...]
        last = seqs - 1
        for q in range(seqs):
            attend(q)
            to_tokens(q)
            if q == 0:
                for gather in gathers:
                    gather.forward()
        for q in range(seqs):
            at = pl.ds(q * rows, rows)
            value = value_ref[at].astype(F32)
            normed[at] = (value * inverse_rms(value) * gains_ref[0:1]).astype(BF)
        mixed_load.wait()
        outer_product(mixed, dattended, grads_ref, 3 * part)
        for q in range(seqs):
            enter(q)
            if q > 0:
                inner.forward(q - 1)
            if q > 1:
                leave(q - 2)
        inner.forward(last)
        outer_product(normed, dqkv, grads_ref, 0)
        Copies.flush(grads_ref)
        for q in range(max(0, last - 1), seqs):
            leave(q)
        for gather in gathers:
            gather.finish()

    z, c = group - 1, ring - 1
    vmem = pltpu.VMEM
    result = communicate(
        kernel,
        ident,
        arrays + shards,
        [
            ((width, 3 * part + part), BF),
            ((tokens, part), BF),
            ((8, part), F32),
        ]
        + [((x.shape[0], sections * x.shape[1]), x.dtype) for x in shards],
        semaphores(
            seqs * (3 * z + c)
            + SequenceSums.count(sections, seqs, True)
            + sum(SquareGather.count(x.shape[0]) for x in shards)
        )
        + [
            pltpu.SemaphoreType.DMA((seqs + 1,)),
            vmem((ring, group, rows, lanes), BF),
            vmem((tokens, width), BF),
            vmem((tokens, width), BF),
            vmem((tokens, 3 * part), BF),
            vmem((group, seqs, half, lanes), BF),
            vmem((group, block, lanes), F32),
            vmem((ring, group, rows, lanes), BF),
            vmem((ring, group, seqs, rows, lanes), BF),
            vmem((group, seqs, half, lanes), BF),
            vmem((group, seqs, half, lanes), BF),
            vmem((group, seqs, rows, lanes), BF),
            vmem((group, seqs, rows, lanes), BF),
        ]
        + SequenceSums.scratch(sections, seqs, rows, part, True),
        name,
        limit=60 * 2**20,
        far=(3, 8),
    )
    return result[0], result[1], result[2], result[3:]


def inverse_rms(value):
    return lax.rsqrt(jnp.mean(value * value, axis=-1, keepdims=True) + EPS)


def gelu_terms(value):
    scale = 0.7978845608028654
    square = value * value
    bend = jnp.tanh(scale * (value + 0.044715 * square * value))
    half = 0.5 * (1.0 + bend)
    slope = half + 0.5 * value * (1.0 - bend * bend) * scale * (1.0 + 0.134145 * square)
    return value * half, slope


def side_by_side(blocks):
    return jnp.concatenate(blocks, axis=1)


class ColumnSum:
    @staticmethod
    def count(sections, scalars):
        return (sections - 1) * (2 if scalars else 1)

    @staticmethod
    def scratch(sections, rows, width, scalars):
        buffers = [pltpu.VMEM((rows, sections * width), BF), pltpu.VMEM((sections, rows, width), BF)]
        if scalars:
            wide = rows + -rows % 128
            buffers += [pltpu.VMEM((8, wide), F32), pltpu.VMEM((sections, 8, wide), F32)]
        return buffers

    def __init__(self, copies, buffers):
        self.copies, self.buffers = copies, buffers

    def start(self, value, scalars=None):
        buf, got = self.buffers[:2]
        width = got.shape[2]
        section = self.copies.lines.place("section")
        buf[...] = value.astype(BF)
        self.pending = self.copies.swap(
            "section", lambda peer: buf.at[:, span(peer, width)], lambda me: got.at[me]
        )
        got[section] = buf[:, span(section, width)]
        if scalars is not None:
            sbuf, sgot = self.buffers[2:]
            sbuf[...] = jnp.zeros_like(sbuf)
            sbuf[:, : scalars.shape[0]] = column_to_rows(scalars)
            self.pending += self.copies.swap("section", lambda peer: sbuf, lambda me: sgot.at[me])
            sgot[section] = sbuf[...]

    def finish(self):
        wait(self.pending)
        total = sum_places(self.buffers[1])
        if len(self.buffers) == 2:
            return total
        rows = total.shape[0]
        return total, row_to_column(sum_places(self.buffers[3])[:1, :rows])


class Swaps:
    def __init__(self, copies):
        self.copies, self.lines = copies, copies.lines

    def ring(self, buf, got):
        return self.copies.swap("core", lambda peer: buf.at[peer], lambda me: got.at[me])

    def ring_sum(self, buf, got):
        total = buf[self.lines.place("core")].astype(F32)
        for peer in self.lines.peers("core"):
            total = total + got[peer].astype(F32)
        return total.astype(BF)

    def z(self, buf, got):
        place = self.lines.place("z")
        pending = self.copies.swap("z", lambda peer: buf.at[peer], lambda me: got.at[me])
        got[place] = buf[place]
        return pending

    def share(self, kind, all_ref):
        me = self.lines.place(kind)
        return self.copies.swap(kind, lambda peer: all_ref.at[me], lambda _: all_ref.at[me])


def together(all_ref):
    return side_by_side([all_ref[i] for i in range(all_ref.shape[0])])


def slots_of(lines, sel):
    group, ring = lines.sizes["z"], lines.sizes["core"]
    index = lax.broadcasted_iota(jnp.int32, (1, group * sel), 1)
    return (index // sel) * (ring * sel) + lines.place("core") * sel + lax.rem(index, sel)


def slot_sequence(lines, heads_ref, pairs_ref, q, sel):
    group, ring = lines.sizes["z"], lines.sizes["core"]
    at = slice(q * sel, (q + 1) * sel)
    query = jnp.concatenate([heads_ref[g, at, : 2 * HDIM] for g in range(group)], axis=0)
    pair = jnp.concatenate([pairs_ref[r, g, at] for g in range(group) for r in range(ring)], axis=0)
    return query * jnp.asarray(SCALE, BF), pair


def routed_enter(lines, ident, arrays, shape, name):
    seqs, sel, rows, width, part = shape
    sections, group, ring = (lines.sizes[k] for k in ("section", "z", "core"))
    dp = group * ring
    slots = seqs * sel
    lanes = 2 * HDIM
    queries = group * sel

    def kernel(
        source_ref,
        top_ref,
        column_ref,
        row_ref,
        ids_ref,
        gains_ref,
        qkv_w,
        value_ref,
        grad_ref,
        normed_ref,
        heads_got,
        pairs_all,
        start_ref,
        turned_ref,
        lse_ref,
        mixed_ref,
        send,
        recv,
        value_core,
        value_core_got,
        value_z,
        value_z_got,
        value_all,
        grad_core,
        grad_core_got,
        grad_z,
        grad_z_got,
        grad_all,
        heads_buf,
        out_buf,
        out_got,
        mixed_all,
    ):
        copies = Copies(lines, send, recv)
        swaps = Swaps(copies)
        section, place = lines.place("section"), lines.place("core")
        rank = lax.axis_index("dp")
        own = span(section, part)
        copies.greet(["section", "z", "core"])
        position = rank * rows + lax.broadcasted_iota(jnp.int32, (1, rows), 1)
        tables = [(column_ref[q] == position).astype(F32).astype(BF) for q in range(seqs)]

        def pick(q, source, buf):
            found = matmul(tables[q], source).astype(BF)
            for d in range(dp):
                buf[d % ring, d // ring, q * sel : (q + 1) * sel] = found[d * sel : (d + 1) * sel]

        for q in range(seqs):
            pick(q, source_ref[q].astype(BF), value_core)
        pending = swaps.ring(value_core, value_core_got)
        for q in range(seqs):
            pick(q, top_ref[q, :, own], grad_core)
        wait(pending)
        value_z[...] = swaps.ring_sum(value_core, value_core_got)
        pending = swaps.z(value_z, value_z_got)
        grad_pending = swaps.ring(grad_core, grad_core_got)

        def slot_starts(q):
            firsts = document_starts(ids_ref[q])
            chosen = row_ref[q].astype(F32)
            documents = sum((chosen >= firsts[c]).astype(F32) for c in range(1, DOCS))
            column = jnp.broadcast_to(column_ref[q].astype(F32), (dp * sel, queries))
            slot = lax.broadcasted_iota(jnp.int32, column.shape, 0)
            mine = jnp.sum(jnp.where(slot == slots_of(lines, sel), column, 0.0), axis=0, keepdims=True)
            mine = sum((mine >= firsts[c]).astype(F32) for c in range(1, DOCS))
            return start_of(mine, document_starts(documents))

        for q in range(seqs):
            start_ref[q] = slot_starts(q)
        wait(grad_pending)
        grad_z[...] = swaps.ring_sum(grad_core, grad_core_got)
        wait(pending)
        value_all[section] = sum_places(value_z_got).astype(BF)
        pending = swaps.share("section", value_all)
        grad_pending = swaps.z(grad_z, grad_z_got)
        wait(pending)
        low = together(value_all)
        value_ref[...] = low
        picked = low.astype(F32)
        normed = (picked * inverse_rms(picked) * gains_ref[0:1]).astype(BF)
        normed_ref[...] = normed
        qkv = matmul(normed, qkv_w[...]).astype(BF)
        blank = jnp.zeros((slots, HDIM), BF)
        for g in range(group):
            query = qkv[:, 2 * part + g * HDIM : 2 * part + (g + 1) * HDIM]
            heads_buf[g, :, :lanes] = side_by_side([query, blank])
            heads_buf[g, :, lanes:] = qkv[:, g * lanes : (g + 1) * lanes]
        pending = swaps.z(heads_buf, heads_got)
        wait(grad_pending)
        grad_all[section] = sum_places(grad_z_got).astype(BF)
        grad_pending = swaps.share("section", grad_all)
        wait(pending)
        pairs_all[place] = heads_got[:, :, lanes:]
        wait(swaps.share("core", pairs_all))
        for q in range(seqs):
            query, pair = slot_sequence(lines, heads_got, pairs_all, q, sel)
            turned, lse = forward_block(
                query, [(pair, pair.T, 0)], slots_of(lines, sel), start_ref[q], [True]
            )
            turned_ref[q] = turned.astype(BF)
            lse_ref[q] = lse
            upright = jnp.concatenate([turned, jnp.zeros_like(turned)], axis=0).T.astype(BF)
            for g in range(group):
                out_buf[g, q * sel : (q + 1) * sel] = upright[g * sel : (g + 1) * sel]
        pending = swaps.z(out_buf, out_got)
        wait(grad_pending)
        grad_ref[...] = together(grad_all)
        wait(pending)
        mixed_all[section] = side_by_side([out_got[g, :, :HDIM] for g in range(group)])
        wait(swaps.share("section", mixed_all))
        mixed_ref[...] = together(mixed_all)

    vmem = pltpu.VMEM
    z, s, c = group - 1, sections - 1, ring - 1
    short = ((group, slots, part), BF)
    lane_block = ((group, slots, lanes), BF)
    across = ((sections, slots, part), BF)
    scratch = [
        ((ring,) + short[0], BF),
        ((ring,) + short[0], BF),
        short,
        short,
        across,
        ((ring,) + short[0], BF),
        ((ring,) + short[0], BF),
        short,
        short,
        across,
        ((group, slots, 2 * lanes), BF),
        lane_block,
        lane_block,
        across,
    ]
    return communicate(
        kernel,
        ident,
        arrays,
        [
            ((slots, width), BF),
            ((slots, width), BF),
            ((slots, width), BF),
            ((group, slots, 2 * lanes), BF),
            ((ring, group, slots, lanes), BF),
            ((seqs, 1, queries), jnp.int32),
            ((seqs, HDIM, queries), BF),
            ((seqs, 1, queries), F32),
            ((slots, width), BF),
        ],
        semaphores(3 * c + 4 * z + 3 * s) + [vmem(a, b) for a, b in scratch],
        name,
        limit=60 * 2**20,
    )


def routed_feed(lines, ident, arrays, shape, name):
    slots, width, part, hidden_size = shape
    sections = lines.sizes["section"]

    def kernel(
        value_ref,
        grad_ref,
        mixed_ref,
        gains_ref,
        rest_ref,
        grads_ref,
        middle_ref,
        attended_ref,
        sent_ref,
        logit_ref,
        vectors_ref,
        send,
        recv,
        sems,
        out_w,
        expand_w,
        shrink_w,
        keep,
        mid_keep,
        dpre_keep,
        hidden_keep,
        fed_keep,
        attended_all,
        *buffers,
    ):
        loads = Loads(sems)
        out_load = loads.start(rest_ref.at[:, :part], out_w)
        shrink_load = loads.start(rest_ref.at[:, part + hidden_size :], shrink_w)
        expand_load = loads.start(rest_ref.at[:, part : part + hidden_size], expand_w)
        copies = Copies(lines, send, recv)
        swaps = Swaps(copies)
        section = lines.place("section")
        own = span(section, part)
        copies.greet(["section"])
        back, forth = ColumnSum(copies, buffers[:4]), ColumnSum(copies, buffers[4:])
        gain, router = gains_ref[1:2, :], gains_ref[2:3, :]
        out_load.wait()
        attended_own = matmul(mixed_ref[...], out_w[...]).astype(BF)
        attended_all[section] = attended_own
        pending = swaps.share("section", attended_all)
        picked = value_ref[...].astype(F32)
        grad_sent = grad_ref[...].astype(F32)
        gate = jax.nn.sigmoid(jnp.sum(picked * router, axis=1, keepdims=True))
        grad_delta = gate * grad_sent
        fed_low = grad_delta.astype(BF)
        fed_keep[...] = fed_low
        shrink_load.wait()
        grad_hidden = contract(fed_low, shrink_w[...], 1, 1)
        expand_load.wait()
        wait(pending)
        middle = picked + together(attended_all).astype(F32)
        inv = inverse_rms(middle)
        normed = (middle * inv * gain).astype(BF)
        hidden, slope = gelu_terms(matmul(normed, expand_w[...]))
        hidden = hidden.astype(BF)
        grad_pre = (grad_hidden * slope).astype(BF)
        grad_normed = contract(grad_pre, expand_w[...], 1, 1)
        back.start(grad_normed, jnp.sum(grad_normed * middle * gain, axis=1, keepdims=True))
        mid_keep[...] = normed
        hidden_keep[...] = hidden
        dpre_keep[...] = grad_pre
        fed_part = matmul(hidden, shrink_w[...])
        keep[0] = middle
        keep[1] = grad_delta
        keep[2] = grad_sent
        own_attended = attended_own.astype(F32)
        gate_part = jnp.sum(grad_sent * fed_part, axis=1, keepdims=True) + jnp.sum(
            keep[2, :, own] * own_attended, axis=1, keepdims=True
        )
        forth.start(fed_part, gate_part)
        outer_product(mid_keep, dpre_keep, grads_ref, 0)
        grad_normed, scalar = back.finish()
        middle_own = keep[0, :, own]
        vectors_ref[...] = jnp.zeros_like(vectors_ref)
        vectors_ref[1:2] = jnp.sum(grad_normed * middle_own * inv, axis=0, keepdims=True)
        grad_middle = inv * (grad_normed * gains_ref[1:2, own]) - middle_own * (inv * inv * inv) * (
            scalar * (1.0 / width)
        )
        middle_ref[...] = grad_middle
        attended_ref[...] = (grad_middle + keep[1, :, own]).astype(BF)
        outer_product(hidden_keep, fed_keep, grads_ref, hidden_size)
        Copies.flush(grads_ref)
        fed, grad_gate = forth.finish()
        sent_ref[...] = (gate * (own_attended + fed)).astype(BF)
        grad_logit = grad_gate * gate * (1.0 - gate)
        logit_ref[...] = jnp.broadcast_to(grad_logit, logit_ref.shape)
        vectors_ref[2:3] = jnp.sum(grad_logit * value_ref[:, own].astype(F32), axis=0, keepdims=True)

    vmem = pltpu.VMEM
    return communicate(
        kernel,
        ident,
        arrays,
        [
            ((width, hidden_size + width), BF),
            ((slots, part), F32),
            ((slots, part), BF),
            ((slots, part), BF),
            ((slots, 128), F32),
            ((8, part), F32),
        ],
        semaphores(sections - 1 + 2 * ColumnSum.count(sections, True))
        + [
            pltpu.SemaphoreType.DMA((3,)),
            vmem((width, part), BF),
            vmem((width, hidden_size), BF),
            vmem((hidden_size, width), BF),
            vmem((3, slots, width), F32),
            vmem((slots, width), BF),
            vmem((slots, hidden_size), BF),
            vmem((slots, hidden_size), BF),
            vmem((slots, width), BF),
            vmem((sections, slots, part), BF),
        ]
        + 2 * ColumnSum.scratch(sections, slots, part, True),
        name,
        limit=60 * 2**20,
        far=(4,),
    )


def routed_leave(lines, ident, arrays, shape, name):
    seqs, sel, rows, width, part = shape
    sections, group, ring = (lines.sizes[k] for k in ("section", "z", "core"))
    slots = seqs * sel
    lanes = 2 * HDIM

    def kernel(
        attended_ref,
        rest_ref,
        qkv_w,
        heads_ref,
        pairs_ref,
        start_ref,
        turned_ref,
        lse_ref,
        value_ref,
        normed_ref,
        mixed_ref,
        middle_ref,
        logit_ref,
        sent_ref,
        feed_vectors_ref,
        gains_ref,
        row_ref,
        top_ref,
        fed_out,
        own_out,
        added_ref,
        grads_ref,
        send,
        recv,
        sems,
        out_w,
        grad_buf,
        grad_got,
        turn_buf,
        turn_got,
        back_buf,
        back_got,
        dqkv_keep,
        sent_got,
        sent_all,
        final_buf,
        final_got,
        final_all,
        *buffers,
    ):
        loads = Loads(sems)
        out_load = loads.start(rest_ref.at[:, :part], out_w)
        copies = Copies(lines, send, recv)
        swaps = Swaps(copies)
        section, zplace, place = (lines.place(k) for k in ("section", "z", "core"))
        rank = lax.axis_index("dp")
        own = span(section, part)
        copies.greet(["section", "z", "core"])
        outer, inner = ColumnSum(copies, buffers[:2]), ColumnSum(copies, buffers[2:])
        out_load.wait()
        outer.start(contract(attended_ref[...], out_w[...], 1, 1))
        sent_pending = copies.swap("z", lambda peer: sent_ref, lambda me: sent_got.at[me])
        sent_got[zplace] = sent_ref[...]
        outer_product(mixed_ref, attended_ref, grads_ref, 3 * part)
        slot_of = rank * rows + lax.broadcasted_iota(jnp.int32, (rows, 1), 0)
        tables = [(row_ref[q] == slot_of).astype(F32).astype(BF) for q in range(seqs)]
        blank = jnp.zeros((slots, HDIM), BF)
        grad_mixed = outer.finish().astype(BF)
        for g in range(group):
            grad_buf[g] = side_by_side([blank, grad_mixed[:, g * HDIM : (g + 1) * HDIM]])
        pending = swaps.z(grad_buf, grad_got)
        wait(sent_pending)
        sent_all[place] = sent_got[...]
        sent_pending = swaps.share("core", sent_all)
        wait(pending)
        for q in range(seqs):
            at = slice(q * sel, (q + 1) * sel)
            query, pair = slot_sequence(lines, heads_ref, pairs_ref, q, sel)
            grad = jnp.concatenate([grad_got[g, at] for g in range(group)], axis=0)
            grad_query, grad_pairs = backward_block(
                query,
                grad,
                grad.T[HDIM:],
                turned_ref[q],
                lse_ref[q],
                [(pair, pair.T, 0)],
                slots_of(lines, sel),
                start_ref[q],
                [True],
            )
            upright = jnp.concatenate([grad_query, jnp.zeros_like(grad_query)], axis=0).T.astype(BF)
            low = grad_pairs[0].astype(BF)
            for g in range(group):
                back_buf[g, at, :lanes] = upright[g * sel : (g + 1) * sel]
                for r in range(ring):
                    first = (g * ring + r) * sel
                    turn_buf[r, g, at] = low[first : first + sel]
        wait(swaps.ring(turn_buf, turn_got))
        back_buf[:, :, lanes:] = swaps.ring_sum(turn_buf, turn_got)
        pending = swaps.z(back_buf, back_got)
        wait(sent_pending)

        def at_positions(q, all_ref):
            at = slice(q * sel, (q + 1) * sel)
            found = jnp.concatenate([all_ref[r, g, at] for g in range(group) for r in range(ring)], axis=0)
            return matmul(tables[q], found)

        for q in range(seqs):
            added_ref[q] = at_positions(q, sent_all).astype(BF)
        wait(pending)
        dqkv_keep[...] = side_by_side(
            [back_got[g, :, lanes:] for g in range(group)] + [back_got[g, :, :HDIM] for g in range(group)]
        )
        grad_normed = contract(dqkv_keep[...], qkv_w[...], 1, 1)
        picked = value_ref[...].astype(F32)
        inv = inverse_rms(picked)
        inner.start(grad_normed, jnp.sum(grad_normed * picked * gains_ref[0:1], axis=1, keepdims=True))
        outer_product(normed_ref, dqkv_keep, grads_ref, 0)
        picked = value_ref[:, own].astype(F32)
        grad_normed, scalar = inner.finish()
        vector_pre = jnp.sum(grad_normed * picked * inv, axis=0, keepdims=True)
        grad_in = inv * (grad_normed * gains_ref[0:1, own]) - picked * (inv * inv * inv) * (scalar * (1.0 / width))
        final_buf[...] = (middle_ref[...] + grad_in + logit_ref[:, :1] * gains_ref[2:3, own]).astype(BF)

        along = copies.swap("z", lambda peer: final_buf, lambda me: final_got.at[me])
        final_got[zplace] = final_buf[...]

        def hand_on(i):
            dst = final_all.at[place, i, :, own]
            dst[...] = final_got[i]
            return copies.swap("section", lambda peer: final_got.at[i], lambda me: dst)

        spread = hand_on(zplace)
        lane = lax.broadcasted_iota(jnp.int32, (part, 128), 1)
        vectors = jnp.zeros((part, 128), F32)
        for i, vector in enumerate((vector_pre, feed_vectors_ref[1:2], feed_vectors_ref[2:3])):
            vectors = jnp.where(lane == i, row_to_column(vector), vectors)
        grads_ref[:, 4 * part :] = jnp.zeros((width, 128), BF)
        grads_ref[pl.ds(pl.multiple_of(section * part, part), part), 4 * part :] = vectors.astype(BF)
        Copies.flush(grads_ref)
        for step in range(group - 1, 0, -1):
            along[group - 1 - step].wait_recv()
            spread += hand_on(lax.rem(zplace + step, group))
        for copy in along:
            copy.wait_send()
        wait(spread)
        wait(swaps.share("core", final_all))
        for q in range(seqs):
            fed_out[q] = (top_ref[q].astype(F32) + at_positions(q, final_all)).astype(BF)
            returned = jnp.concatenate(
                [final_all[r, g, q * sel : (q + 1) * sel, own] for g in range(group) for r in range(ring)], axis=0
            )
            own_out[q] = top_ref[q, :, own].astype(F32) + matmul(tables[q], returned)

    vmem = pltpu.VMEM
    z, s, c = group - 1, sections - 1, ring - 1
    lane_block = ((group, slots, lanes), BF)
    ring_block = ((ring, group, slots, lanes), BF)
    short = ((group, slots, part), BF)
    scratch = [
        ((width, part), BF),
        lane_block,
        lane_block,
        ring_block,
        ring_block,
        ((group, slots, 2 * lanes), BF),
        ((group, slots, 2 * lanes), BF),
        ((slots, 3 * part), BF),
        short,
        ((ring,) + short[0], BF),
        ((slots, part), BF),
        short,
        ((ring, group, slots, width), BF),
    ]
    return communicate(
        kernel,
        ident,
        arrays,
        [
            ((seqs, rows, width), BF),
            ((seqs, rows, part), F32),
            ((seqs, rows, part), BF),
            ((width, 4 * part + 128), BF),
        ],
        semaphores(
            3 * c
            + 4 * z
            + ColumnSum.count(sections, True)
            + ColumnSum.count(sections, False)
            + group * s
        )
        + [pltpu.SemaphoreType.DMA((1,))]
        + [vmem(a, b) for a, b in scratch]
        + ColumnSum.scratch(sections, slots, part, False)
        + ColumnSum.scratch(sections, slots, part, True),
        name,
        limit=60 * 2**20,
        far=(1,),
    )


def cut_weights(arrays, sections, dp, group, name):
    local, width = arrays[0].shape
    part = width // sections
    inner = arrays[4].shape[1] // dp
    share = inner // sections
    hidden_size = dp * share

    def kernel(q_ref, k_ref, v_ref, o_ref, e_ref, s_ref, first_ref, rest_ref, k_buf, v_buf, sems):
        section = lax.axis_index("section")
        own = span(section, part)
        moves = [
            (k_ref.at[:, own], k_buf),
            (v_ref.at[:, own], v_buf),
            (q_ref.at[:, own], first_ref.at[:, 2 * part :]),
            (o_ref.at[:, own], rest_ref.at[:, :part]),
            (
                s_ref.at[pl.ds(pl.multiple_of(section * share, share), share)],
                rest_ref.at[:, part + hidden_size :],
            ),
        ]
        for d in range(dp):
            at = pl.ds(pl.multiple_of(d * inner + section * share, 128), share)
            moves.append((e_ref.at[:, at], rest_ref.at[:, part + d * share : part + (d + 1) * share]))
        copies = [pltpu.make_async_copy(src, dst, sems.at[i]) for i, (src, dst) in enumerate(moves)]
        for copy in copies:
            copy.start()
        for copy in copies:
            copy.wait()
        for g in range(group):
            at = slice(g * HDIM, (g + 1) * HDIM)
            first_ref[:, 2 * g * HDIM : 2 * (g + 1) * HDIM] = side_by_side([k_buf[:, at], v_buf[:, at]])

    anywhere, vmem = pl.BlockSpec(memory_space=pl.ANY), pl.BlockSpec(memory_space=pltpu.VMEM)
    return pl.pallas_call(
        kernel,
        in_specs=[anywhere] * 6,
        out_specs=[vmem] * 2,
        out_shape=[
            jax.ShapeDtypeStruct((local, 3 * part), BF),
            jax.ShapeDtypeStruct((local, part + hidden_size + width), BF),
        ],
        scratch_shapes=[
            pltpu.VMEM((local, part), BF),
            pltpu.VMEM((local, part), BF),
            pltpu.SemaphoreType.DMA((5 + dp,)),
        ],
        compiler_params=pltpu.CompilerParams(vmem_limit_bytes=60 * 2**20),
        name=name,
    )(*arrays)


def on_device(
    stream_in,
    segment_ids,
    chosen_rows,
    cotangent,
    dense_prenorm,
    dense_query,
    dense_keys,
    dense_values,
    dense_output,
    dense_midnorm,
    dense_expand,
    dense_shrink,
    routed_prenorm,
    routed_query,
    routed_keys,
    routed_values,
    routed_output,
    routed_midnorm,
    routed_expand,
    routed_shrink,
    router_weight,
):
    sections, dp = lax.axis_size("section"), lax.axis_size("dp")
    section, rank = lax.axis_index("section"), lax.axis_index("dp")
    seqs, rows, width = stream_in.shape
    tokens = seqs * rows
    part = width // sections
    group = HEADS // sections
    ring = dp // group
    total_sel = chosen_rows.shape[1]
    sel = total_sel // dp
    lines = Lines(sections, dp, group)

    def own_columns(value):
        return lax.dynamic_slice_in_dim(value, section * part, part, value.ndim - 1)

    def own_hidden(expand, shrink):
        inner = expand.shape[1] // dp
        share = inner // sections
        cut = expand.reshape(expand.shape[0], dp, sections, share)
        cut = lax.dynamic_index_in_dim(cut, section, 2, keepdims=False).reshape(expand.shape[0], dp * share)
        return cut, lax.dynamic_slice_in_dim(shrink, section * share, share, 0)

    def own_attention(query, keys, values):
        local = query.shape[0]
        pair = jnp.stack(
            [own_columns(keys).reshape(local, group, HDIM), own_columns(values).reshape(local, group, HDIM)],
            axis=2,
        ).reshape(local, 2 * part)
        return jnp.concatenate([pair, own_columns(query)], axis=1)

    def cut(query, keys, values, output, expand, shrink, name):
        if expand.shape[1] // (dp * sections) % 128 == 0:
            return cut_weights([query, keys, values, output, expand, shrink], sections, dp, group, name)
        expand_cut, shrink_cut = own_hidden(expand, shrink)
        rest = jnp.concatenate([own_columns(output), expand_cut, shrink_cut], axis=1)
        return own_attention(query, keys, values), rest

    def gather(value):
        return lax.all_gather(value, "dp", axis=0, tiled=True)

    def after(value, other):
        return lax.optimization_barrier((value, other))[0]

    hidden_size = dense_expand.shape[1] // sections
    gains = jnp.stack([dense_prenorm, dense_midnorm, routed_prenorm, routed_midnorm, router_weight])
    gains = jnp.pad(gains, ((0, 16 - gains.shape[0]), (0, 0)))
    dense_first, dense_rest = cut(
        dense_query, dense_keys, dense_values, dense_output, dense_expand, dense_shrink, "cut_dense"
    )
    routed_first, routed_rest = cut(
        routed_query, routed_keys, routed_values, routed_output, routed_expand, routed_shrink, "cut_routed"
    )
    rest = gather(dense_rest)
    routed_qkv = gather(routed_first)
    routed_rest = gather(routed_rest)

    ids = segment_ids[:, None, :]
    grad_top = cotangent.reshape(tokens, width)
    dense_qkv, gains, queries, pairs, start, mixed_turned, lse, mixed = dense_enter(
        lines,
        1,
        [stream_in.reshape(tokens, width), dense_first, gains, ids],
        (seqs, rows, width),
        "dense_enter",
    )
    dense_qkv = dense_qkv.reshape(width, 3 * part)
    attended, slope, hidden, after_dense = dense_feed(
        lines, 2, [stream_in, mixed, gains[:2], rest], (seqs, rows, width, hidden_size), "dense_feed"
    )
    after_dense = after_dense.reshape(tokens, part)
    attended, slope, hidden, mixed = (x.reshape(tokens, -1) for x in (attended, slope, hidden, mixed))

    def reduce_dp(value):
        return lax.psum_scatter(value, "dp", scatter_dimension=0, tiled=True)

    shape = (seqs, sel, rows, width, part)
    columns, chosen = chosen_rows[:, :, None], chosen_rows[:, None, :]
    r_value, r_grad, r_normed, r_heads, r_pairs, r_start, r_turned, r_lse, r_mixed = routed_enter(
        lines,
        3,
        [after_dense.reshape(seqs, rows, part), cotangent, columns, chosen, ids, gains[2:5], routed_qkv],
        shape,
        "routed_enter",
    )
    routed_grads, r_middle, r_grad_attended, r_sent, r_logit, r_vectors = routed_feed(
        lines,
        4,
        [r_value, r_grad, r_mixed, gains[2:5], routed_rest],
        (seqs * sel, width, part, hidden_size),
        "routed_feed",
    )
    routed_shard = reduce_dp(routed_grads)
    fed_low, grad_own, added, routed_grads = routed_leave(
        lines,
        5,
        [
            r_grad_attended,
            routed_rest,
            routed_qkv,
            r_heads,
            r_pairs,
            r_start,
            r_turned,
            r_lse,
            r_value,
            r_normed,
            r_mixed,
            r_middle,
            r_logit,
            r_sent,
            r_vectors,
            gains[2:5],
            chosen,
            cotangent,
        ],
        shape,
        "routed_leave",
    )
    routed_shard_in = reduce_dp(after(routed_grads, routed_shard))
    stream_out = (after_dense + added.reshape(tokens, part).astype(F32)).astype(BF).reshape(seqs, rows, part)

    dense_grads, grad_attended, grad_middle, grad_heads, d_vectors = dense_return(
        lines,
        6,
        [
            fed_low.reshape(tokens, width),
            grad_own.reshape(tokens, part),
            stream_in.reshape(tokens, width),
            attended,
            slope,
            hidden,
            rest,
            gains[:2],
        ],
        (seqs, rows, width, hidden_size),
        "dense_return",
    )
    dense_shard = reduce_dp(after(dense_grads, routed_shard_in))
    dense_grads, stream_grad, d_vectors, (routed_all, routed_all_in) = dense_leave(
        lines,
        7,
        [
            grad_heads,
            stream_in.reshape(tokens, width),
            queries,
            pairs,
            start,
            mixed_turned,
            lse,
            dense_qkv,
            mixed,
            grad_attended,
            grad_middle,
            gains[:2],
            d_vectors,
        ],
        [routed_shard, routed_shard_in],
        (seqs, rows, width),
        "dense_leave",
    )
    stream_grad = stream_grad.reshape(seqs, rows, part)
    vectors, dense_all_in, (dense_all,) = dense_finish(
        lines, 8, d_vectors, dense_grads, [dense_shard], "dense_finish"
    )

    share = hidden_size // dp
    local = width // dp
    r_exp, r_shr, r_keys, r_values, r_query, r_out, r_vector = assemble(
        [
            ("hidden", routed_all, 0, hidden_size),
            ("stack", routed_all, hidden_size, width),
            ("pair", routed_all_in, 0, 2 * part),
            ("columns", routed_all_in, 2 * part, part),
            ("columns", routed_all_in, 3 * part, part),
            ("sum", routed_all_in, 4 * part, 128),
        ],
        share,
        "routed_places",
    )
    d_exp, d_shr, d_keys, d_values, d_query, d_out = assemble(
        [
            ("hidden", dense_all, 0, hidden_size),
            ("stack", dense_all, hidden_size, width),
            ("pair", dense_all_in, 0, 2 * part),
            ("columns", dense_all_in, 2 * part, part),
            ("columns", dense_all_in, 3 * part, part),
        ],
        share,
        "dense_places",
    )
    vectors = lax.dynamic_slice_in_dim(vectors, rank * local, local, 1)
    d_shr = d_shr.reshape(sections * share, width)
    r_shr = r_shr.reshape(sections * share, width)
    return (
        (stream_out, stream_grad)
        + (vectors[1], d_query, d_keys, d_values, d_out, vectors[0], d_exp, d_shr)
        + (r_vector[:, 0], r_query, r_keys, r_values, r_out, r_vector[:, 1], r_exp, r_shr)
        + (r_vector[:, 2],)
    )


def solution(mesh):
    streams, row, vector, copied = P(None, "dp", None), P("dp", None), P("dp"), P()
    layer = (vector, row, row, row, row, vector, row, row)
    outs = (P(None, "dp", "section"),) * 2 + layer + layer + (vector,)
    return jax.shard_map(
        on_device,
        mesh=mesh,
        in_specs=(streams, copied, copied, streams) + layer + layer + (vector,),
        out_specs=outs,
        check_vma=False,
    )
```

```python
import functools

import jax
import jax.numpy as jnp
from jax import lax
from jax.experimental import pallas as pl
from jax.experimental.pallas import tpu as pltpu
from jax.sharding import PartitionSpec as P

HEADS = 16
HDIM = 64
DOCS = 8
EPS = 1e-06
NEG = -1e30
SCALE = HDIM ** (-0.5)
VMEM = 32 * 2**20
MESH = pl.DeviceIdType.MESH
BF = jnp.bfloat16
F32 = jnp.float32


def matmul(left, right):
    return jnp.dot(left, right, preferred_element_type=F32)


def contract(left, right, ldim, rdim):
    return lax.dot_general(left, right, (((ldim,), (rdim,)), ((), ())), preferred_element_type=F32)


class Lines:
    def __init__(self, sections, dp, group):
        self.sizes = {"section": sections, "z": group, "core": dp // group}
        self.ring = dp // group

    def place(self, kind):
        if kind == "section":
            return lax.axis_index("section")
        index = lax.axis_index("dp")
        return index // self.ring if kind == "z" else lax.rem(index, self.ring)

    def device(self, kind, place):
        if kind == "section":
            return {"section": place}
        index = lax.axis_index("dp")
        if kind == "z":
            return {"dp": place * self.ring + lax.rem(index, self.ring)}
        return {"dp": (index // self.ring) * self.ring + place}

    def peers(self, kind):
        size = self.sizes[kind]
        me = self.place(kind)
        return [lax.rem(me + step, size) for step in range(1, size)]


class Copies:
    loads, flush = (), None

    def __init__(self, lines, send, recv):
        self.lines, self.send, self.recv, self.used = lines, send, recv, 0

    def greet(self, kinds):
        barrier = pltpu.get_barrier_semaphore()
        count = 0
        for kind in kinds:
            for peer in self.lines.peers(kind):
                pl.semaphore_signal(
                    barrier, inc=1, device_id=self.lines.device(kind, peer), device_id_type=MESH
                )
                count += 1
        for load in Copies.loads:
            load.wait()
        pl.semaphore_wait(barrier, count)

    def start(self, kind, peer, src, dst):
        assert self.used < self.send.shape[0]
        copy = pltpu.make_async_remote_copy(
            src_ref=src,
            dst_ref=dst,
            send_sem=self.send.at[self.used],
            recv_sem=self.recv.at[self.used],
            device_id=self.lines.device(kind, peer),
            device_id_type=MESH,
        )
        self.used += 1
        copy.start()
        return copy

    def swap(self, kind, src, dst):
        me = self.lines.place(kind)
        return [self.start(kind, peer, src(peer), dst(me)) for peer in self.lines.peers(kind)]


def wait(copies):
    for copy in copies:
        copy.wait()


def semaphores(count):
    return [pltpu.SemaphoreType.DMA((count,)), pltpu.SemaphoreType.DMA((count,))]


def communicate(kernel, ident, arrays, shapes, scratch, name, limit=60 * 2**20, far=()):
    place = pl.BlockSpec(memory_space=pl.ANY)
    near = [i for i in range(len(arrays)) if i not in far]
    many, outs = len(arrays), len(shapes)

    def body(*refs):
        ins, results, refs = list(refs[:many]), refs[many : many + outs], refs[many + outs :]
        inner, refs = refs[: len(scratch)], refs[len(scratch) :]
        in_bufs, out_bufs, (in_sems, out_sems) = refs[: len(near)], refs[len(near) : len(near) + outs], refs[-2:]
        loads = []
        for k, i in enumerate(near):
            loads.append(pltpu.make_async_copy(ins[i], in_bufs[k], in_sems.at[k]))
            loads[-1].start()
            ins[i] = in_bufs[k]
        stores = [pltpu.make_async_copy(out_bufs[k], results[k], out_sems.at[k]) for k in range(outs)]
        started = set()

        def flush(ref):
            k = next(k for k in range(outs) if out_bufs[k] is ref)
            stores[k].start()
            started.add(k)

        Copies.loads, Copies.flush = loads, staticmethod(flush)
        kernel(*ins, *out_bufs, *inner)
        for k in range(outs):
            if k not in started:
                stores[k].start()
        for store in stores:
            store.wait()

    return pl.pallas_call(
        body,
        out_shape=[jax.ShapeDtypeStruct(s, d) for s, d in shapes],
        in_specs=[place] * many,
        out_specs=[place] * outs,
        scratch_shapes=list(scratch)
        + [pltpu.VMEM(arrays[i].shape, arrays[i].dtype) for i in near]
        + [pltpu.VMEM(s, d) for s, d in shapes]
        + [pltpu.SemaphoreType.DMA((max(1, len(near)),)), pltpu.SemaphoreType.DMA((outs,))],
        compiler_params=pltpu.CompilerParams(
            collective_id=ident, has_side_effects=True, vmem_limit_bytes=limit
        ),
        name=name,
    )(*arrays)


def span(place, width):
    return pl.ds(pl.multiple_of(place * width, width), width)


def square(lines):
    me = lines.place("section")
    low, high = lax.rem(me, 2), me // 2
    return high * 2 + 1 - low, (1 - high) * 2 + low, (1 - high) * 2 + 1 - low


def pieces_of(rows):
    half = rows // 2
    return (2, half // 2) if half % 32 == 0 else (1, half)


class SquareGather:
    @staticmethod
    def count(rows):
        return 6 * pieces_of(rows)[0]

    def __init__(self, copies, x_ref, o_ref, pieces=None):
        self.copies, self.x_ref, self.o_ref = copies, x_ref, o_ref
        self.width = x_ref.shape[1]
        self.me = copies.lines.place("section")
        near, far, _ = square(copies.lines)
        half = x_ref.shape[0] // 2
        pieces, step = pieces_of(x_ref.shape[0]) if pieces is None else (pieces, half // pieces)
        self.parts = [
            (pl.ds(h * half + j * step, step), one, two)
            for j in range(pieces)
            for h, (one, two) in enumerate(((near, far), (far, near)))
        ]

    def send(self, at, to):
        dst = self.o_ref.at[at, span(self.me, self.width)]
        return self.copies.start("section", to, self.x_ref.at[at], dst)

    def start(self):
        self.first = [self.send(at, one) for at, one, _ in self.parts]
        self.rest = [self.send(at, two) for at, _, two in self.parts]
        self.o_ref[:, span(self.me, self.width)] = self.x_ref[...]

    def forward(self):
        for (at, one, two), copy in zip(self.parts, self.first):
            copy.wait_recv()
            place = self.o_ref.at[at, span(one, self.width)]
            self.rest.append(self.copies.start("section", two, place, place))

    def finish(self):
        for copy in self.first:
            copy.wait_send()
        wait(self.rest)


class SquareScatter:
    @staticmethod
    def count(rows):
        return 6 * pieces_of(rows)[0]

    @staticmethod
    def scratch(rows, width):
        return [pltpu.VMEM((2, rows, width), BF), pltpu.VMEM((rows, width), BF), pltpu.VMEM((rows, width), BF)]

    def __init__(self, copies, x_ref, got, turn, last, pieces=None):
        self.copies, self.x_ref, self.got, self.turn, self.last = copies, x_ref, got, turn, last
        self.width = turn.shape[1]
        self.me = copies.lines.place("section")
        near, far, self.across = square(copies.lines)
        half = x_ref.shape[0] // 2
        pieces, step = pieces_of(x_ref.shape[0]) if pieces is None else (pieces, half // pieces)
        self.parts = [
            (pl.ds(h * half + j * step, step), one, two)
            for j in range(pieces)
            for h, (one, two) in enumerate(((near, far), (far, near)))
        ]

    def read(self, at, place):
        return self.x_ref[at, span(place, self.width)].astype(F32)

    def start(self):
        self.passed, self.kept = [], []
        for at, one, _ in self.parts:
            for place, k, out in ((self.across, 0, self.passed), (one, 1, self.kept)):
                src = self.x_ref.at[at, span(place, self.width)]
                out.append(self.copies.start("section", one, src, self.got.at[k, at]))

    def forward(self):
        self.second = []
        for (at, _, two), copy in zip(self.parts, self.passed):
            copy.wait_recv()
            self.turn[at] = (self.read(at, two) + self.got[0, at].astype(F32)).astype(BF)
            self.second.append(self.copies.start("section", two, self.turn.at[at], self.last.at[at]))

    def finish(self, o_ref):
        for i, (at, _, _) in enumerate(self.parts):
            self.kept[i].wait_recv()
            self.second[i].wait_recv()
            o_ref[at] = self.read(at, self.me) + self.got[1, at].astype(F32) + self.last[at].astype(F32)
        for copy in self.passed + self.kept + self.second:
            copy.wait_send()


def gather_columns(lines, ident, part, name):
    rows, width = part.shape

    def kernel(x_ref, o_ref, send, recv):
        copies = Copies(lines, send, recv)
        copies.greet(["section"])
        gather = SquareGather(copies, x_ref, o_ref)
        gather.start()
        gather.forward()
        gather.finish()

    shape = ((rows, lines.sizes["section"] * width), part.dtype)
    (out,) = communicate(kernel, ident, [part], [shape], semaphores(SquareGather.count(rows)), name)
    return out


def scalar_block(scalars):
    count = -(-scalars.shape[0] // 128)
    count += -count % 8
    return jnp.pad(scalars, (0, count * 128 - scalars.shape[0])).reshape(count, 128)


def sum_places(ref):
    total = ref[0].astype(F32)
    for i in range(1, ref.shape[0]):
        total = total + ref[i].astype(F32)
    return total


def scatter_columns(lines, ident, part, scalars, name):
    rows, full = part.shape
    sections = lines.sizes["section"]
    width = full // sections
    extra = scalars is not None
    arrays = [part]
    shapes = [((rows, width), F32)]
    scratch = semaphores(SquareScatter.count(rows) + sections - 1) + SquareScatter.scratch(rows, width)
    if extra:
        arrays.append(scalar_block(scalars))
        shapes.append((arrays[1].shape, F32))
        scratch.append(pltpu.VMEM((sections,) + arrays[1].shape, F32))

    def kernel(*refs):
        x_ref, refs = refs[0], refs[1:]
        if extra:
            e_ref, o_ref, eo_ref, send, recv, got, turn, last, e_got = refs
        else:
            o_ref, send, recv, got, turn, last = refs
        copies = Copies(lines, send, recv)
        copies.greet(["section"])
        scatter = SquareScatter(copies, x_ref, got, turn, last)
        scatter.start()
        if extra:
            others = copies.swap("section", lambda peer: e_ref, lambda place: e_got.at[place])
            e_got[lines.place("section")] = e_ref[...]
        scatter.forward()
        scatter.finish(o_ref)
        if extra:
            wait(others)
            eo_ref[...] = sum_places(e_got)

    got = communicate(kernel, ident, arrays, shapes, scratch, name)
    if not extra:
        return got[0]
    return got[0], got[1].reshape(-1)[:rows]


def dense_finish(lines, ident, vectors, weight, shards, name):
    group, ring, sections = (lines.sizes[k] for k in ("z", "core", "section"))
    dp = group * ring
    many = len(shards)
    local = weight.shape[0] // dp
    wide = weight.shape[1]
    weight = weight.reshape(dp, local, wide)
    width = vectors.shape[1]

    def kernel(x_ref, w_ref, *refs):
        s_refs, refs = refs[:many], refs[many:]
        v_ref, wo_ref, refs = refs[0], refs[1], refs[2:]
        so_refs, refs = refs[:many], refs[many:]
        send, recv, w_got, w_turn, w_all, w_own, v_z, v_core, v_all = refs
        copies = Copies(lines, send, recv)
        zplace, place, section = (lines.place(k) for k in ("z", "core", "section"))
        copies.greet(["z", "core", "section"])
        order = lines.peers("z") + [zplace]
        around = [
            copies.swap("core", lambda peer: w_ref.at[g * ring + peer], lambda me: w_got.at[me, g]) for g in order
        ]
        pending = copies.swap("z", lambda peer: x_ref, lambda me: v_z.at[me])
        v_z[zplace] = x_ref[...]
        gathers = [SquareGather(copies, x, o) for x, o in zip(s_refs, so_refs)]
        for gather in gathers:
            gather.start()
        along = []
        for i, (g, arrived) in enumerate(zip(order, around)):
            for copy in arrived:
                copy.wait_recv()
            total = w_ref[g * ring + place].astype(F32)
            for peer in lines.peers("core"):
                total = total + w_got[peer, g].astype(F32)
            w_turn[g] = total.astype(BF)
            if i < len(order) - 1:
                along.append(copies.start("z", g, w_turn.at[g], w_all.at[zplace]))
        wait(pending)
        v_core[place] = sum_places(v_z)
        wait(copies.swap("core", lambda peer: v_core.at[place], lambda me: v_core.at[me]))
        v_all[section] = sum_places(v_core)
        pending = copies.swap("section", lambda peer: v_all.at[section], lambda me: v_all.at[me])
        for gather in gathers:
            gather.forward()
        wait(along)
        w_all[zplace] = w_turn[zplace]
        w_own[...] = sum_places(w_all).astype(BF)
        last_gather = SquareGather(copies, w_own, wo_ref)
        last_gather.start()
        wait(pending)
        for i in range(sections):
            v_ref[:, i * width : (i + 1) * width] = v_all[i]
        last_gather.forward()
        for arrived in around:
            for copy in arrived:
                copy.wait_send()
        for gather in gathers:
            gather.finish()
        last_gather.finish()

    z, c, s = group - 1, ring - 1, sections - 1
    result = communicate(
        kernel,
        ident,
        [vectors, weight] + shards,
        [((8, sections * width), F32), ((local, sections * wide), BF)]
        + [((x.shape[0], sections * x.shape[1]), x.dtype) for x in shards],
        semaphores(
            group * c
            + z
            + sum(SquareGather.count(x.shape[0]) for x in shards)
            + SquareGather.count(local)
            + z
            + c
            + s
        )
        + [
            pltpu.VMEM((ring, group, local, wide), BF),
            pltpu.VMEM((group, local, wide), BF),
            pltpu.VMEM((group, local, wide), BF),
            pltpu.VMEM((local, wide), BF),
            pltpu.VMEM((group, 8, width), F32),
            pltpu.VMEM((ring, 8, width), F32),
            pltpu.VMEM((sections, 8, width), F32),
        ],
        name,
        limit=60 * 2**20,
    )
    return result[0], result[1], result[2:]


def assemble(pieces, share, name):
    arrays = []
    for _, array, _, _ in pieces:
        if not any(array is other for other in arrays):
            arrays.append(array)
    where = [next(i for i, other in enumerate(arrays) if other is array) for _, array, _, _ in pieces]
    local = arrays[0].shape[0]
    steps = local // 32 if local % 32 == 0 else 1
    rows = local // steps
    sections = lax.axis_size("section")
    shapes, specs = [], []
    for kind, _, _, width in pieces:
        many = 2 if kind == "pair" else 1
        for _ in range(many):
            if kind == "stack":
                shapes.append(jax.ShapeDtypeStruct((sections, local, width), F32))
                specs.append(pl.BlockSpec((sections, rows, width), lambda i: (0, i, 0)))
            else:
                total = width if kind == "sum" else sections * width // many
                shapes.append(jax.ShapeDtypeStruct((local, total), F32))
                specs.append(pl.BlockSpec((rows, total), lambda i: (i, 0)))

    def kernel(*refs):
        ins, outs = refs[: len(arrays)], list(refs[len(arrays) :])
        for (kind, array, first, width), i in zip(pieces, where):
            wide = array.shape[1] // sections
            blocks = [ins[i][:, s * wide + first : s * wide + first + width].astype(F32) for s in range(sections)]
            out = outs.pop(0)
            if kind == "columns":
                for s, item in enumerate(blocks):
                    out[:, s * width : (s + 1) * width] = item
            elif kind == "stack":
                for s, item in enumerate(blocks):
                    out[s] = item
            elif kind == "sum":
                total = blocks[0]
                for item in blocks[1:]:
                    total = total + item
                out[...] = total
            elif kind == "hidden":
                for d in range(width // share):
                    out[:, d * share * sections : (d + 1) * share * sections] = jnp.concatenate(
                        [item[:, d * share : (d + 1) * share] for item in blocks], axis=1
                    )
            else:
                other = outs.pop(0)
                half = width // 2
                for s, item in enumerate(blocks):
                    for side, dst in ((0, out), (1, other)):
                        heads = [
                            item[:, (2 * g + side) * HDIM : (2 * g + side + 1) * HDIM]
                            for g in range(width // (2 * HDIM))
                        ]
                        dst[:, s * half : (s + 1) * half] = jnp.concatenate(heads, axis=1)

    return pl.pallas_call(
        kernel,
        grid=(steps,),
        in_specs=[pl.BlockSpec((rows, a.shape[1]), lambda i: (i, 0)) for a in arrays],
        out_specs=specs,
        out_shape=shapes,
        compiler_params=pltpu.CompilerParams(vmem_limit_bytes=60 * 2**20),
        name=name,
    )(*arrays)


def column_to_rows(column):
    return jnp.broadcast_to(column, (column.shape[0], 128)).T[:8]


def row_to_column(row):
    return jnp.broadcast_to(row, (128, row.shape[1])).T[:, :1]


def outer_product(left_ref, right_ref, out_ref, first):
    step = 256
    wide = right_ref.shape[1]

    @pl.loop(0, left_ref.shape[1] // step)
    def _(i):
        at = span(i, step)
        block = contract(left_ref[:, at], right_ref[...], 0, 0)
        out_ref[at, first : first + wide] = block.astype(BF)


def unpack_low(packed):
    lane = lax.broadcasted_iota(jnp.int32, packed.shape, 1)
    zero = jnp.zeros_like(packed)
    low = jnp.where(lane < HDIM, packed, zero)
    turned = jnp.concatenate([packed[:, HDIM:], packed[:, :HDIM]], axis=1)
    high = jnp.where(lane < HDIM, turned, zero)
    return jnp.concatenate([low, high], axis=0)


def unpack_high(packed):
    lane = lax.broadcasted_iota(jnp.int32, packed.shape, 1)
    zero = jnp.zeros_like(packed)
    turned = jnp.concatenate([packed[:, HDIM:], packed[:, :HDIM]], axis=1)
    low = jnp.where(lane >= HDIM, turned, zero)
    high = jnp.where(lane >= HDIM, packed, zero)
    return jnp.concatenate([low, high], axis=0)


def pack_turned(turned):
    half = turned.shape[1] // 2
    return jnp.concatenate([turned[:, :half], turned[:, half:]], axis=0).T


def forward_block(query, pieces, qpos, start, causal):
    scores = []
    peak = None
    for index, (pair, _, first) in enumerate(pieces):
        item = contract(pair, query, 1, 1)
        kpos = first + lax.broadcasted_iota(jnp.int32, item.shape, 0)
        allowed = kpos >= start
        if causal[index]:
            allowed = allowed & (kpos <= qpos)
        item = jnp.where(allowed, item, NEG)
        top = jnp.max(item, axis=0, keepdims=True)
        peak = top if peak is None else jnp.maximum(peak, top)
        scores.append(item)
    total = jnp.zeros_like(peak)
    mixed = None
    for item, (_, turned, _) in zip(scores, pieces):
        weight = jnp.exp(item - peak)
        total = total + jnp.sum(weight, axis=0, keepdims=True)
        part = matmul(turned[HDIM:], weight.astype(BF))
        mixed = part if mixed is None else mixed + part
    return mixed / total, peak + jnp.log(total)


def backward_block(query, grad, grad_turned, mixed_turned, lse, pieces, qpos, start, causal):
    row_sum = jnp.sum(grad_turned.astype(F32) * mixed_turned.astype(F32), axis=0, keepdims=True)
    grad_query = None
    grads = []
    for index, (pair, turned, first) in enumerate(pieces):
        scores = contract(pair, query, 1, 1)
        kpos = first + lax.broadcasted_iota(jnp.int32, scores.shape, 0)
        allowed = kpos >= start
        if causal[index]:
            allowed = allowed & (kpos <= qpos)
        probs = jnp.where(allowed, jnp.exp(scores - lse), 0.0)
        grad_probs = contract(pair, grad, 1, 1)
        grad_scores = (probs * (grad_probs - row_sum)).astype(BF)
        grads.append(matmul(grad_scores, query) + matmul(probs.astype(BF), grad))
        part = matmul(turned[:HDIM], grad_scores)
        grad_query = part if grad_query is None else grad_query + part
    return grad_query * SCALE, grads


def document_starts(ids):
    return [
        jnp.sum((ids < c).astype(F32), axis=1, keepdims=True) if c else jnp.zeros((1, 1), F32) for c in range(DOCS)
    ]


def start_of(documents, firsts):
    start = jnp.zeros(documents.shape, F32)
    for c in range(1, DOCS):
        start = jnp.where(documents >= c, firsts[c], start)
    return start.astype(jnp.int32)


def dense_enter(lines, ident, arrays, shape, name):
    seqs, rows, width = shape
    sections, group, ring = (lines.sizes[k] for k in ("section", "z", "core"))
    dp = group * ring
    part = width // sections
    half = rows // 2
    lanes = 2 * HDIM
    block = ring * rows
    local = width // dp

    def kernel(
        value_ref,
        weights_ref,
        cut_ref,
        ids_ref,
        weights_all,
        gains_ref,
        q_got,
        kv_all,
        start_ref,
        turned_ref,
        lse_ref,
        mixed_ref,
        send,
        recv,
        cut_all,
        kv_buf,
        q_buf,
        o_buf,
        o_got,
        o_own,
    ):
        copies = Copies(lines, send, recv)
        zplace, place = lines.place("z"), lines.place("core")
        rank = lax.axis_index("dp")
        copies.greet(["section", "z", "core"])
        pairs = [(weights_ref, weights_all), (cut_ref, cut_all)]
        along, handed = [], []
        for x_ref, o_ref in pairs:
            along.append(copies.swap("z", lambda peer: x_ref, lambda _: o_ref.at[rank]))
        for x_ref, o_ref in pairs:
            handed += copies.swap("core", lambda peer: x_ref, lambda _: o_ref.at[rank])
            o_ref[rank] = x_ref[...]
        for q in range(seqs):
            firsts = document_starts(ids_ref[q : q + 1])
            for g in range(group):
                at = pl.ds(pl.multiple_of((g * ring + place) * rows, rows), rows)
                start_ref[q, g] = start_of(ids_ref[q : q + 1, at], firsts)
        for step in range(group - 1, 0, -1):
            source = lax.rem(zplace + step, group) * ring + place
            for arrived, (_, o_ref) in zip(along, pairs):
                arrived[group - 1 - step].wait_recv()
                handed += copies.swap("core", lambda peer: o_ref.at[source], lambda _: o_ref.at[source])
        for arrived in along:
            for copy in arrived:
                copy.wait_send()
        wait(handed)
        for d in range(dp):
            gains_ref[:, d * local : (d + 1) * local] = cut_all[d].astype(F32)

        arriving, queries, around, outward, gathers = {}, {}, {}, {}, {}

        def project(q):
            value = value_ref[pl.ds(q * rows, rows)].astype(F32)
            normed = (value * inverse_rms(value) * gains_ref[0:1]).astype(BF)
            qkv = matmul(normed, weights_all[...].reshape(width, 3 * part)).astype(BF)
            for g in range(group):
                kv_buf[g, q] = qkv[:, g * lanes : (g + 1) * lanes]
                at = slice(2 * part + g * HDIM, 2 * part + (g + 1) * HDIM)
                q_buf[g, q] = side_by_side([qkv[:half, at], qkv[half:, at]])
            arriving[q] = copies.swap("z", lambda peer: kv_buf.at[peer, q], lambda me: kv_all.at[place, me, q])
            queries[q] = copies.swap("z", lambda peer: q_buf.at[peer, q], lambda me: q_got.at[me, q])
            q_got[zplace, q] = q_buf[zplace, q]
            kv_all[place, zplace, q] = kv_buf[zplace, q]
            own = kv_all.at[place, zplace, q]
            around[q] = copies.swap("core", lambda peer: own, lambda _: own)

        def hand(q):
            for step in range(group - 1, 0, -1):
                arriving[q][group - 1 - step].wait_recv()
                item = kv_all.at[place, lax.rem(zplace + step, group), q]
                around[q] += copies.swap("core", lambda peer: item, lambda _: item)

        def attend(q):
            for copy in arriving[q]:
                copy.wait_send()
            wait(queries[q])
            wait(around[q])
            pieces = []
            for g in range(group):
                pair = kv_all[:, g, q].reshape(block, lanes)
                pieces.append((pair, pair.T, g * block))
            for g in range(group):
                query = unpack_low(q_got[g, q]) * jnp.asarray(SCALE, BF)
                qpos = g * block + place * rows + lax.broadcasted_iota(jnp.int32, (1, rows), 1)
                mixed, lse = forward_block(
                    query, pieces[: g + 1], qpos, start_ref[q, g], [i == g for i in range(g + 1)]
                )
                turned_ref[q, g] = mixed.astype(BF)
                lse_ref[q, g] = lse
                o_buf[g, q] = pack_turned(mixed).astype(BF)
            outward[q] = copies.swap("z", lambda peer: o_buf.at[peer, q], lambda me: o_got.at[me, q])
            o_got[zplace, q] = o_buf[zplace, q]

        def merge(q):
            wait(outward[q])
            packed = [o_got[g, q] for g in range(group)]
            o_own[q] = side_by_side([jnp.concatenate([p[:, :HDIM], p[:, HDIM:]], axis=0) for p in packed])
            gathers[q] = SquareGather(copies, o_own.at[q], mixed_ref.at[q], 1)
            gathers[q].start()

        for q in range(seqs):
            project(q)
        for q in range(seqs):
            hand(q)
            attend(q)
            if q > 0:
                merge(q - 1)
            if q > 1:
                gathers[q - 2].forward()
        merge(seqs - 1)
        for q in range(max(0, seqs - 2), seqs):
            gathers[q].forward()
        for q in range(seqs):
            gathers[q].finish()

    z, c = group - 1, ring - 1
    vmem = pltpu.VMEM
    packed = ((group, seqs, half, lanes), BF)
    return communicate(
        kernel,
        ident,
        arrays,
        [
            ((dp, local, 3 * part), BF),
            ((16, width), F32),
            packed,
            ((ring, group, seqs, rows, lanes), BF),
            ((seqs, group, 1, rows), jnp.int32),
            ((seqs, group, HDIM, rows), BF),
            ((seqs, group, 1, rows), F32),
            ((seqs, rows, width), BF),
        ],
        semaphores(2 * (z + group * c) + seqs * (3 * z + group * c + 6))
        + [
            vmem((dp, 16, local), BF),
            vmem((group, seqs, rows, lanes), BF),
            vmem(*packed),
            vmem(*packed),
            vmem(*packed),
            vmem((seqs, rows, part), BF),
        ],
        name,
        limit=60 * 2**20,
    )


class SequenceSums:
    @staticmethod
    def count(sections, seqs, scalars):
        return seqs * (6 + (sections - 1 if scalars else 0))

    @staticmethod
    def scratch(sections, seqs, rows, part, scalars):
        vmem = pltpu.VMEM
        buffers = [
            vmem((seqs, rows, sections * part), BF),
            vmem((seqs, 2, rows, part), BF),
            vmem((seqs, rows, part), BF),
            vmem((seqs, rows, part), BF),
            vmem((rows, part), F32),
        ]
        if scalars:
            buffers += [vmem((seqs, 8, rows), F32), vmem((seqs, sections, 8, rows), F32)]
        return buffers

    def __init__(self, copies, buffers):
        self.copies, self.buffers, self.items = copies, buffers, {}

    def start(self, q, value, scalars=None):
        wide, got, turn, last = self.buffers[:4]
        wide[q] = value.astype(BF)
        item = SquareScatter(self.copies, wide.at[q], got.at[q], turn.at[q], last.at[q], 1)
        item.start()
        others = []
        if scalars is not None:
            buf, arrived = self.buffers[5:]
            section = self.copies.lines.place("section")
            buf[q] = column_to_rows(scalars)
            others = self.copies.swap("section", lambda peer: buf.at[q], lambda me: arrived.at[q, me])
            arrived[q, section] = buf[q]
        self.items[q] = (item, others)

    def forward(self, q):
        self.items[q][0].forward()

    def finish(self, q):
        item, others = self.items[q]
        total = self.buffers[4]
        item.finish(total)
        if not others:
            return total[...]
        wait(others)
        return total[...], row_to_column(sum_places(self.buffers[6].at[q])[:1])


class Loads:
    def __init__(self, sems):
        self.sems, self.used = sems, 0

    def start(self, src, dst):
        copy = pltpu.make_async_copy(src, dst, self.sems.at[self.used])
        self.used += 1
        copy.start()
        return copy


def dense_return(lines, ident, arrays, shape, name):
    seqs, rows, width, hidden_size = shape
    sections, group = lines.sizes["section"], lines.sizes["z"]
    part = width // sections
    half = rows // 2

    def kernel(
        fed_ref,
        own_ref,
        value_ref,
        attended_ref,
        slope_ref,
        hidden_ref,
        rest_ref,
        gains_ref,
        grads_ref,
        dattended,
        middle,
        heads,
        vectors_ref,
        send,
        recv,
        sems,
        out_w,
        expand_w,
        shrink_w,
        hidden,
        normed,
        dpre,
        *buffers,
    ):
        loads = Loads(sems)
        shrink_load = loads.start(rest_ref.at[:, part + hidden_size :], shrink_w)
        expand_load = loads.start(rest_ref.at[:, part : part + hidden_size], expand_w)
        out_load = loads.start(rest_ref.at[:, :part], out_w)
        hidden_load = loads.start(hidden_ref, hidden)
        copies = Copies(lines, send, recv)
        own = span(lines.place("section"), part)
        copies.greet(["section"])
        mids = SequenceSums(copies, buffers[:7])
        outs = SequenceSums(copies, buffers[7:])

        def middle_of(at):
            return value_ref[at].astype(F32) + attended_ref[at].astype(F32)

        def feed(q):
            at = pl.ds(q * rows, rows)
            grad_hidden = contract(fed_ref[at], shrink_w[...], 1, 1)
            grad_pre = (grad_hidden * slope_ref[at].astype(F32)).astype(BF)
            dpre[at] = grad_pre
            grad_normed = contract(grad_pre, expand_w[...], 1, 1)
            mid = middle_of(at)
            mids.start(q, grad_normed, jnp.sum(grad_normed * mid * gains_ref[1:2], axis=1, keepdims=True))
            normed[at] = (mid * inverse_rms(mid) * gains_ref[1:2]).astype(BF)

        def project(q):
            at = pl.ds(q * rows, rows)
            grad_normed, scalars = mids.finish(q)
            inv = inverse_rms(middle_of(at))
            mid = value_ref[at, own].astype(F32) + attended_ref[at, own].astype(F32)
            vectors_ref[0:1] += jnp.sum(grad_normed * mid * inv, axis=0, keepdims=True)
            grad = (
                inv * (grad_normed * gains_ref[1:2, own])
                - mid * (inv * inv * inv) * (scalars * (1.0 / width))
                + own_ref[at]
            )
            middle[at] = grad
            low = grad.astype(BF)
            dattended[at] = low
            outs.start(q, contract(low, out_w[...], 1, 1))

        def leave(q):
            grad = outs.finish(q).astype(BF)
            for g in range(group):
                columns = slice(g * HDIM, (g + 1) * HDIM)
                heads[g, q] = side_by_side([grad[:half, columns], grad[half:, columns]])

        vectors_ref[...] = jnp.zeros_like(vectors_ref)
        shrink_load.wait()
        expand_load.wait()
        out_load.wait()
        last = seqs - 1
        for q in range(seqs):
            feed(q)
            if q > 0:
                mids.forward(q - 1)
            if q > 1:
                project(q - 2)
        mids.forward(last)
        hidden_load.wait()
        outer_product(hidden, fed_ref, grads_ref, hidden_size)
        for q in range(max(0, last - 1), seqs):
            project(q)
            outs.forward(q - 1)
        outer_product(normed, dpre, grads_ref, 0)
        Copies.flush(grads_ref)
        outs.forward(last)
        for q in range(seqs):
            leave(q)

    tokens = seqs * rows
    vmem = pltpu.VMEM
    return communicate(
        kernel,
        ident,
        arrays,
        [
            ((width, hidden_size + width), BF),
            ((tokens, part), BF),
            ((tokens, part), F32),
            ((group, seqs, half, 2 * HDIM), BF),
            ((8, part), F32),
        ],
        semaphores(SequenceSums.count(sections, seqs, True) + SequenceSums.count(sections, seqs, False))
        + [
            pltpu.SemaphoreType.DMA((4,)),
            vmem((width, part), BF),
            vmem((width, hidden_size), BF),
            vmem((hidden_size, width), BF),
            vmem((tokens, hidden_size), BF),
            vmem((tokens, width), BF),
            vmem((tokens, hidden_size), BF),
        ]
        + SequenceSums.scratch(sections, seqs, rows, part, True)
        + SequenceSums.scratch(sections, seqs, rows, part, False),
        name,
        limit=60 * 2**20,
        far=(5, 6),
    )


def dense_leave(lines, ident, arrays, shards, shape, name):
    seqs, rows, width = shape
    sections, group, ring = (lines.sizes[k] for k in ("section", "z", "core"))
    part = width // sections
    half = rows // 2
    lanes = 2 * HDIM
    block = ring * rows
    many = len(shards)
    tokens = seqs * rows

    def kernel(
        heads,
        value_ref,
        q_ref,
        kv_ref,
        start_ref,
        turned_ref,
        lse_ref,
        qkv_w,
        mixed_ref,
        dattended,
        middle,
        gains_ref,
        mid_vectors_ref,
        *refs,
    ):
        s_refs, refs = refs[:many], refs[many:]
        (grads_ref, stream_ref, vectors_ref), refs = refs[:3], refs[3:]
        so_refs, refs = refs[:many], refs[many:]
        (
            send,
            recv,
            sems,
            kv,
            mixed,
            normed,
            dqkv,
            heads_got,
            acc,
            pairs,
            pairs_got,
            queries,
            queries_got,
            sums,
            sums_got,
            *buffers,
        ) = refs
        loads = Loads(sems)
        mixed_load = loads.start(mixed_ref, mixed)
        kv_loads = {0: loads.start(kv_ref.at[:, :, 0], kv)}
        copies = Copies(lines, send, recv)
        section, zplace, place = (lines.place(k) for k in ("section", "z", "core"))
        own = span(section, part)
        copies.greet(["section", "z", "core"])
        inner = SequenceSums(copies, buffers)
        arriving, around, along, back = {}, {}, {}, {}
        for q in range(seqs):
            heads_got[zplace, q] = heads[zplace, q]
            arriving[q] = copies.swap("z", lambda peer: heads.at[peer, q], lambda me: heads_got.at[me, q])
        gathers = [SquareGather(copies, x, o) for x, o in zip(s_refs, so_refs)]
        for gather in gathers:
            gather.start()

        def attend(q):
            wait(arriving[q])
            kv_loads[q].wait()
            pieces = []
            for g in range(group):
                pair = kv[:, g].reshape(block, lanes)
                pieces.append((pair, pair.T, g * block))
            for g in reversed(range(group)):
                query = unpack_low(q_ref[g, q]) * jnp.asarray(SCALE, BF)
                packed = heads_got[g, q]
                flat = packed.T
                qpos = g * block + place * rows + lax.broadcasted_iota(jnp.int32, (1, rows), 1)
                grad_query, grads = backward_block(
                    query,
                    unpack_high(packed),
                    side_by_side([flat[:HDIM], flat[HDIM:]]),
                    turned_ref[q, g],
                    lse_ref[q, g],
                    pieces[: g + 1],
                    qpos,
                    start_ref[q, g],
                    [i == g for i in range(g + 1)],
                )
                queries[g, q] = pack_turned(grad_query).astype(BF)
                for i, item in enumerate(grads):
                    if g == group - 1:
                        acc[i] = item
                    else:
                        acc[i] += item
            if q > 0:
                wait(around[q - 1])
            for g in range(group):
                for r in range(ring):
                    pairs[r, g] = acc[g, r * rows : (r + 1) * rows].astype(BF)
            if q + 1 < seqs:
                kv_loads[q + 1] = loads.start(kv_ref.at[:, :, q + 1], kv)
            queries_got[zplace, q] = queries[zplace, q]
            around[q] = copies.swap("core", lambda peer: pairs.at[peer], lambda me: pairs_got.at[me, :, q])
            along[q] = copies.swap("z", lambda peer: queries.at[peer, q], lambda me: queries_got.at[me, q])

        def to_tokens(q):
            wait(around[q])
            around[q] = []
            for g in range(group):
                item = pairs[place, g].astype(F32)
                for peer in lines.peers("core"):
                    item = item + pairs_got[peer, g, q].astype(F32)
                sums[g, q] = item.astype(BF)
            sums_got[zplace, q] = sums[zplace, q]
            back[q] = copies.swap("z", lambda peer: sums.at[peer, q], lambda me: sums_got.at[me, q])

        def enter(q):
            wait(back[q] + along[q])
            at = pl.ds(q * rows, rows)
            packed = [queries_got[g, q] for g in range(group)]
            upright = [jnp.concatenate([p[:, :HDIM], p[:, HDIM:]], axis=0) for p in packed]
            grad = side_by_side([sums_got[g, q] for g in range(group)] + upright)
            dqkv[at] = grad
            grad_normed = contract(grad, qkv_w[...], 1, 1)
            value = value_ref[at].astype(F32)
            inner.start(q, grad_normed, jnp.sum(grad_normed * value * gains_ref[0:1], axis=1, keepdims=True))

        def leave(q):
            at = pl.ds(q * rows, rows)
            grad_normed, scalars = inner.finish(q)
            inv = inverse_rms(value_ref[at].astype(F32))
            value = value_ref[at, own].astype(F32)
            vectors_ref[1:2] += jnp.sum(grad_normed * value * inv, axis=0, keepdims=True)
            grad = (
                inv * (grad_normed * gains_ref[0:1, own])
                - value * (inv * inv * inv) * (scalars * (1.0 / width))
                + middle[at]
            )
            stream_ref[at] = grad.astype(BF)

        vectors_ref[...] = mid_vectors_ref[...]
        last = seqs - 1
        for q in range(seqs):
            attend(q)
            to_tokens(q)
            if q == 0:
                for gather in gathers:
                    gather.forward()
        for q in range(seqs):
            at = pl.ds(q * rows, rows)
            value = value_ref[at].astype(F32)
            normed[at] = (value * inverse_rms(value) * gains_ref[0:1]).astype(BF)
        mixed_load.wait()
        outer_product(mixed, dattended, grads_ref, 3 * part)
        for q in range(seqs):
            enter(q)
            if q > 0:
                inner.forward(q - 1)
            if q > 1:
                leave(q - 2)
        inner.forward(last)
        outer_product(normed, dqkv, grads_ref, 0)
        Copies.flush(grads_ref)
        for q in range(max(0, last - 1), seqs):
            leave(q)
        for gather in gathers:
            gather.finish()

    z, c = group - 1, ring - 1
    vmem = pltpu.VMEM
    result = communicate(
        kernel,
        ident,
        arrays + shards,
        [
            ((width, 3 * part + part), BF),
            ((tokens, part), BF),
            ((8, part), F32),
        ]
        + [((x.shape[0], sections * x.shape[1]), x.dtype) for x in shards],
        semaphores(
            seqs * (3 * z + c)
            + SequenceSums.count(sections, seqs, True)
            + sum(SquareGather.count(x.shape[0]) for x in shards)
        )
        + [
            pltpu.SemaphoreType.DMA((seqs + 1,)),
            vmem((ring, group, rows, lanes), BF),
            vmem((tokens, width), BF),
            vmem((tokens, width), BF),
            vmem((tokens, 3 * part), BF),
            vmem((group, seqs, half, lanes), BF),
            vmem((group, block, lanes), F32),
            vmem((ring, group, rows, lanes), BF),
            vmem((ring, group, seqs, rows, lanes), BF),
            vmem((group, seqs, half, lanes), BF),
            vmem((group, seqs, half, lanes), BF),
            vmem((group, seqs, rows, lanes), BF),
            vmem((group, seqs, rows, lanes), BF),
        ]
        + SequenceSums.scratch(sections, seqs, rows, part, True),
        name,
        limit=60 * 2**20,
        far=(3, 8),
    )
    return result[0], result[1], result[2], result[3:]


def inverse_rms(value):
    return lax.rsqrt(jnp.mean(value * value, axis=-1, keepdims=True) + EPS)


def gelu_terms(value):
    scale = 0.7978845608028654
    square = value * value
    bend = jnp.tanh(scale * (value + 0.044715 * square * value))
    half = 0.5 * (1.0 + bend)
    slope = half + 0.5 * value * (1.0 - bend * bend) * scale * (1.0 + 0.134145 * square)
    return value * half, slope


def side_by_side(blocks):
    return jnp.concatenate(blocks, axis=1)


class ColumnSum:
    @staticmethod
    def count(sections, scalars):
        return (sections - 1) * (2 if scalars else 1)

    @staticmethod
    def scratch(sections, rows, width, scalars):
        buffers = [pltpu.VMEM((rows, sections * width), BF), pltpu.VMEM((sections, rows, width), BF)]
        if scalars:
            wide = rows + -rows % 128
            buffers += [pltpu.VMEM((8, wide), F32), pltpu.VMEM((sections, 8, wide), F32)]
        return buffers

    def __init__(self, copies, buffers):
        self.copies, self.buffers = copies, buffers

    def start(self, value, scalars=None):
        buf, got = self.buffers[:2]
        width = got.shape[2]
        section = self.copies.lines.place("section")
        buf[...] = value.astype(BF)
        self.pending = self.copies.swap(
            "section", lambda peer: buf.at[:, span(peer, width)], lambda me: got.at[me]
        )
        got[section] = buf[:, span(section, width)]
        if scalars is not None:
            sbuf, sgot = self.buffers[2:]
            sbuf[...] = jnp.zeros_like(sbuf)
            sbuf[:, : scalars.shape[0]] = column_to_rows(scalars)
            self.pending += self.copies.swap("section", lambda peer: sbuf, lambda me: sgot.at[me])
            sgot[section] = sbuf[...]

    def finish(self):
        wait(self.pending)
        total = sum_places(self.buffers[1])
        if len(self.buffers) == 2:
            return total
        rows = total.shape[0]
        return total, row_to_column(sum_places(self.buffers[3])[:1, :rows])


class Swaps:
    def __init__(self, copies):
        self.copies, self.lines = copies, copies.lines

    def ring(self, buf, got):
        return self.copies.swap("core", lambda peer: buf.at[peer], lambda me: got.at[me])

    def ring_sum(self, buf, got):
        total = buf[self.lines.place("core")].astype(F32)
        for peer in self.lines.peers("core"):
            total = total + got[peer].astype(F32)
        return total.astype(BF)

    def z(self, buf, got):
        place = self.lines.place("z")
        pending = self.copies.swap("z", lambda peer: buf.at[peer], lambda me: got.at[me])
        got[place] = buf[place]
        return pending

    def share(self, kind, all_ref):
        me = self.lines.place(kind)
        return self.copies.swap(kind, lambda peer: all_ref.at[me], lambda _: all_ref.at[me])


def together(all_ref):
    return side_by_side([all_ref[i] for i in range(all_ref.shape[0])])


def halves(value):
    rows = value.shape[0] // 2
    return side_by_side([value[:rows], value[rows:]])


def upright(packed):
    return jnp.concatenate([packed[:, :HDIM], packed[:, HDIM:]], axis=0)


def slots_of(lines, sel):
    group, ring = lines.sizes["z"], lines.sizes["core"]
    index = lax.broadcasted_iota(jnp.int32, (1, group * sel), 1)
    return (index // sel) * (ring * sel) + lines.place("core") * sel + lax.rem(index, sel)


def slot_sequence(lines, queries_ref, pairs_ref, q, sel):
    group, ring = lines.sizes["z"], lines.sizes["core"]
    at = slice(q * sel, (q + 1) * sel)
    query = jnp.concatenate([queries_ref[g, at] for g in range(group)], axis=0)
    pair = jnp.concatenate([pairs_ref[r, g, at] for g in range(group) for r in range(ring)], axis=0)
    return query * jnp.asarray(SCALE, BF), pair


def dense_feed(lines, ident, arrays, shape, name):
    seqs, sel, rows, width, part, hidden_size = shape
    sections, group, ring = (lines.sizes[k] for k in ("section", "z", "core"))
    dp = group * ring
    slots = seqs * sel
    lanes = 2 * HDIM
    queries = group * sel

    def kernel(
        value_ref,
        mixed_ref,
        gains_ref,
        rest_ref,
        top_ref,
        chosen_ref,
        ids_ref,
        qkv_w,
        attended_ref,
        slope_ref,
        hidden_ref,
        out_ref,
        picked_ref,
        grad_ref,
        normed_ref,
        queries_ref,
        pairs_all,
        start_ref,
        turned_ref,
        lse_ref,
        r_mixed_ref,
        send,
        recv,
        sems,
        out_w,
        expand_w,
        shrink_w,
        top,
        own_buf,
        wide,
        got,
        turn,
        last,
        value_core,
        value_core_got,
        value_z,
        value_z_got,
        value_all,
        grad_core,
        grad_core_got,
        grad_z,
        grad_z_got,
        grad_all,
        heads_buf,
        heads_got,
        o_buf,
        o_got,
        mixed_all,
    ):
        loads = Loads(sems)
        section, place = lines.place("section"), lines.place("core")
        rank = lax.axis_index("dp")
        own = span(section, part)
        out_load = loads.start(rest_ref.at[:, :part], out_w)
        top_load = loads.start(top_ref.at[:, :, own], top)
        expand_load = loads.start(rest_ref.at[:, part : part + hidden_size], expand_w)
        shrink_load = loads.start(rest_ref.at[:, part + hidden_size :], shrink_w)
        copies = Copies(lines, send, recv)
        swaps = Swaps(copies)
        copies.greet(["section", "z", "core"])
        out_load.wait()
        gathers, scatters = {}, {}
        position = rank * rows + lax.broadcasted_iota(jnp.int32, (1, rows), 1).astype(F32)

        def table(q):
            chosen = row_to_column(chosen_ref[q : q + 1].astype(F32))
            return (chosen == position).astype(F32).astype(BF)

        def pick(q, source, buf):
            found = matmul(table(q), source).astype(BF)
            for d in range(dp):
                buf[d % ring, d // ring, q * sel : (q + 1) * sel] = found[d * sel : (d + 1) * sel]

        def project(q):
            own_buf[q] = matmul(mixed_ref[q], out_w[...]).astype(BF)
            gathers[q] = SquareGather(copies, own_buf.at[q], attended_ref.at[q], 1)
            gathers[q].start()

        def feed(q):
            gathers[q].finish()
            middle = value_ref[q].astype(F32) + attended_ref[q].astype(F32)
            normed = (middle * inverse_rms(middle) * gains_ref[1:2]).astype(BF)
            hidden, slope = gelu_terms(matmul(normed, expand_w[...]))
            hidden = hidden.astype(BF)
            hidden_ref[q] = hidden
            slope_ref[q] = slope.astype(BF)
            wide[q] = matmul(hidden, shrink_w[...]).astype(BF)
            scatters[q] = SquareScatter(copies, wide.at[q], got.at[q], turn.at[q], last.at[q], 1)
            scatters[q].start()

        def leave(q):
            scatters[q].finish(out_ref.at[q])
            after = out_ref[q] + value_ref[q, :, own].astype(F32) + attended_ref[q, :, own].astype(F32)
            out_ref[q] = after
            pick(q, after.astype(BF), value_core)

        for q in range(seqs):
            project(q)
            if q > 0:
                gathers[q - 1].forward()
        gathers[seqs - 1].forward()
        top_load.wait()
        for q in range(seqs):
            pick(q, top[q], grad_core)
        grad_pending = swaps.ring(grad_core, grad_core_got)
        expand_load.wait()
        shrink_load.wait()
        for q in range(seqs):
            feed(q)
            if q == 0:
                wait(grad_pending)
                grad_z[...] = swaps.ring_sum(grad_core, grad_core_got)
                grad_pending = swaps.z(grad_z, grad_z_got)
            else:
                scatters[q - 1].forward()
            if q > 1:
                leave(q - 2)
        Copies.flush(hidden_ref)
        Copies.flush(slope_ref)
        Copies.flush(attended_ref)
        scatters[seqs - 1].forward()
        for q in range(max(0, seqs - 2), seqs):
            leave(q)
        Copies.flush(out_ref)

        pending = swaps.ring(value_core, value_core_got)
        wait(grad_pending)
        grad_all[section] = sum_places(grad_z_got).astype(BF)
        wait(pending)
        value_z[...] = swaps.ring_sum(value_core, value_core_got)
        pending = swaps.z(value_z, value_z_got)
        grad_pending = swaps.share("section", grad_all)

        def slot_starts(q):
            firsts = document_starts(ids_ref[q : q + 1])
            chosen = chosen_ref[q : q + 1].astype(F32)
            documents = sum((chosen >= firsts[c]).astype(F32) for c in range(1, DOCS))
            column = jnp.broadcast_to(row_to_column(chosen), (dp * sel, queries))
            slot = lax.broadcasted_iota(jnp.int32, column.shape, 0)
            mine = jnp.sum(jnp.where(slot == slots_of(lines, sel), column, 0.0), axis=0, keepdims=True)
            mine = sum((mine >= firsts[c]).astype(F32) for c in range(1, DOCS))
            return start_of(mine, document_starts(documents))

        for q in range(seqs):
            start_ref[q] = slot_starts(q)
        wait(pending)
        value_all[section] = sum_places(value_z_got).astype(BF)
        pending = swaps.share("section", value_all)
        wait(grad_pending)
        grad_ref[...] = together(grad_all)
        wait(pending)
        low = together(value_all)
        picked_ref[...] = low
        picked = low.astype(F32)
        normed = (picked * inverse_rms(picked) * gains_ref[2:3]).astype(BF)
        normed_ref[...] = normed
        qkv = matmul(normed, qkv_w[...]).astype(BF)
        for g in range(group):
            heads_buf[g, :slots] = qkv[:, g * lanes : (g + 1) * lanes]
            heads_buf[g, slots:] = halves(qkv[:, 2 * part + g * HDIM : 2 * part + (g + 1) * HDIM])
        wait(swaps.z(heads_buf, heads_got))
        pairs_all[place] = heads_got[:, :slots]
        pending = swaps.share("core", pairs_all)
        blank = jnp.zeros((slots, HDIM), BF)
        for g in range(group):
            queries_ref[g] = side_by_side([upright(heads_got[g, slots:]), blank])
        wait(pending)
        turned_all = []
        for q in range(seqs):
            query, pair = slot_sequence(lines, queries_ref, pairs_all, q, sel)
            turned, lse = forward_block(
                query, [(pair, pair.T, 0)], slots_of(lines, sel), start_ref[q], [True]
            )
            turned_ref[q] = turned.astype(BF)
            lse_ref[q] = lse
            turned_all.append(jnp.concatenate([turned, jnp.zeros_like(turned)], axis=0).T.astype(BF)[:, :HDIM])
        for g in range(group):
            o_buf[g] = halves(jnp.concatenate([t[g * sel : (g + 1) * sel] for t in turned_all], axis=0))
        wait(swaps.z(o_buf, o_got))
        mixed_all[section] = side_by_side([upright(o_got[g]) for g in range(group)])
        wait(swaps.share("section", mixed_all))
        r_mixed_ref[...] = together(mixed_all)

    vmem = pltpu.VMEM
    z, s, c = group - 1, sections - 1, ring - 1
    short = ((group, slots, part), BF)
    across = ((sections, slots, part), BF)
    packed = ((group, slots // 2, lanes), BF)
    heads = ((group, slots + slots // 2, lanes), BF)
    row = ((slots, width), BF)
    scratch = [
        ((width, part), BF),
        ((width, hidden_size), BF),
        ((hidden_size, width), BF),
        ((seqs, rows, part), BF),
        ((seqs, rows, part), BF),
        ((seqs, rows, width), BF),
        ((seqs, 2, rows, part), BF),
        ((seqs, rows, part), BF),
        ((seqs, rows, part), BF),
        ((ring,) + short[0], BF),
        ((ring,) + short[0], BF),
        short,
        short,
        across,
        ((ring,) + short[0], BF),
        ((ring,) + short[0], BF),
        short,
        short,
        across,
        heads,
        heads,
        packed,
        packed,
        across,
    ]
    return communicate(
        kernel,
        ident,
        arrays,
        [
            ((seqs, rows, width), BF),
            ((seqs, rows, hidden_size), BF),
            ((seqs, rows, hidden_size), BF),
            ((seqs, rows, part), F32),
            row,
            row,
            row,
            ((group, slots, lanes), BF),
            ((ring, group, slots, lanes), BF),
            ((seqs, 1, queries), jnp.int32),
            ((seqs, HDIM, queries), BF),
            ((seqs, 1, queries), F32),
            row,
        ],
        semaphores(seqs * 12 + 3 * c + 4 * z + 3 * s)
        + [pltpu.SemaphoreType.DMA((4,))]
        + [vmem(a, b) for a, b in scratch],
        name,
        limit=60 * 2**20,
        far=(3, 4),
    )


def routed_feed(lines, ident, arrays, shape, name):
    slots, width, part, hidden_size = shape
    sections = lines.sizes["section"]

    def kernel(
        value_ref,
        grad_ref,
        mixed_ref,
        gains_ref,
        rest_ref,
        grads_ref,
        middle_ref,
        attended_ref,
        sent_ref,
        logit_ref,
        vectors_ref,
        send,
        recv,
        sems,
        out_w,
        expand_w,
        shrink_w,
        keep,
        mid_keep,
        dpre_keep,
        hidden_keep,
        fed_keep,
        attended_all,
        *buffers,
    ):
        loads = Loads(sems)
        out_load = loads.start(rest_ref.at[:, :part], out_w)
        shrink_load = loads.start(rest_ref.at[:, part + hidden_size :], shrink_w)
        expand_load = loads.start(rest_ref.at[:, part : part + hidden_size], expand_w)
        copies = Copies(lines, send, recv)
        swaps = Swaps(copies)
        section = lines.place("section")
        own = span(section, part)
        copies.greet(["section"])
        back, forth = ColumnSum(copies, buffers[:4]), ColumnSum(copies, buffers[4:])
        gain, router = gains_ref[3:4, :], gains_ref[4:5, :]
        out_load.wait()
        attended_own = matmul(mixed_ref[...], out_w[...]).astype(BF)
        attended_all[section] = attended_own
        pending = swaps.share("section", attended_all)
        picked = value_ref[...].astype(F32)
        grad_sent = grad_ref[...].astype(F32)
        gate = jax.nn.sigmoid(jnp.sum(picked * router, axis=1, keepdims=True))
        grad_delta = gate * grad_sent
        fed_low = grad_delta.astype(BF)
        fed_keep[...] = fed_low
        shrink_load.wait()
        grad_hidden = contract(fed_low, shrink_w[...], 1, 1)
        expand_load.wait()
        wait(pending)
        middle = picked + together(attended_all).astype(F32)
        inv = inverse_rms(middle)
        normed = (middle * inv * gain).astype(BF)
        hidden, slope = gelu_terms(matmul(normed, expand_w[...]))
        hidden = hidden.astype(BF)
        grad_pre = (grad_hidden * slope).astype(BF)
        grad_normed = contract(grad_pre, expand_w[...], 1, 1)
        back.start(grad_normed, jnp.sum(grad_normed * middle * gain, axis=1, keepdims=True))
        mid_keep[...] = normed
        hidden_keep[...] = hidden
        dpre_keep[...] = grad_pre
        fed_part = matmul(hidden, shrink_w[...])
        keep[0] = middle
        keep[1] = grad_delta
        keep[2] = grad_sent
        own_attended = attended_own.astype(F32)
        gate_part = jnp.sum(grad_sent * fed_part, axis=1, keepdims=True) + jnp.sum(
            keep[2, :, own] * own_attended, axis=1, keepdims=True
        )
        forth.start(fed_part, gate_part)
        outer_product(mid_keep, dpre_keep, grads_ref, 0)
        grad_normed, scalar = back.finish()
        middle_own = keep[0, :, own]
        vectors_ref[...] = jnp.zeros_like(vectors_ref)
        vectors_ref[1:2] = jnp.sum(grad_normed * middle_own * inv, axis=0, keepdims=True)
        grad_middle = inv * (grad_normed * gains_ref[3:4, own]) - middle_own * (inv * inv * inv) * (
            scalar * (1.0 / width)
        )
        middle_ref[...] = grad_middle
        attended_ref[...] = (grad_middle + keep[1, :, own]).astype(BF)
        outer_product(hidden_keep, fed_keep, grads_ref, hidden_size)
        Copies.flush(grads_ref)
        fed, grad_gate = forth.finish()
        sent_ref[...] = (gate * (own_attended + fed)).astype(BF)
        grad_logit = grad_gate * gate * (1.0 - gate)
        logit_ref[...] = jnp.broadcast_to(grad_logit, logit_ref.shape)
        vectors_ref[2:3] = jnp.sum(grad_logit * value_ref[:, own].astype(F32), axis=0, keepdims=True)

    vmem = pltpu.VMEM
    return communicate(
        kernel,
        ident,
        arrays,
        [
            ((width, hidden_size + width), BF),
            ((slots, part), F32),
            ((slots, part), BF),
            ((slots, part), BF),
            ((slots, 128), F32),
            ((8, part), F32),
        ],
        semaphores(sections - 1 + 2 * ColumnSum.count(sections, True))
        + [
            pltpu.SemaphoreType.DMA((3,)),
            vmem((width, part), BF),
            vmem((width, hidden_size), BF),
            vmem((hidden_size, width), BF),
            vmem((3, slots, width), F32),
            vmem((slots, width), BF),
            vmem((slots, hidden_size), BF),
            vmem((slots, hidden_size), BF),
            vmem((slots, width), BF),
            vmem((sections, slots, part), BF),
        ]
        + 2 * ColumnSum.scratch(sections, slots, part, True),
        name,
        limit=60 * 2**20,
        far=(4,),
    )


def routed_leave(lines, ident, arrays, shape, name):
    seqs, sel, rows, width, part = shape
    sections, group, ring = (lines.sizes[k] for k in ("section", "z", "core"))
    slots = seqs * sel
    lanes = 2 * HDIM

    def kernel(
        attended_ref,
        rest_ref,
        qkv_w,
        queries_ref,
        pairs_ref,
        start_ref,
        turned_ref,
        lse_ref,
        value_ref,
        normed_ref,
        mixed_ref,
        middle_ref,
        logit_ref,
        sent_ref,
        feed_vectors_ref,
        gains_ref,
        chosen_ref,
        top_ref,
        fed_out,
        own_out,
        added_ref,
        grads_ref,
        send,
        recv,
        sems,
        out_w,
        grad_buf,
        grad_got,
        grad_high,
        turn_buf,
        turn_got,
        back_buf,
        back_got,
        dqkv_keep,
        sent_got,
        sent_all,
        final_buf,
        final_got,
        final_all,
        *buffers,
    ):
        loads = Loads(sems)
        out_load = loads.start(rest_ref.at[:, :part], out_w)
        copies = Copies(lines, send, recv)
        swaps = Swaps(copies)
        section, zplace, place = (lines.place(k) for k in ("section", "z", "core"))
        rank = lax.axis_index("dp")
        own = span(section, part)
        copies.greet(["section", "z", "core"])
        outer, inner = ColumnSum(copies, buffers[:2]), ColumnSum(copies, buffers[2:])
        out_load.wait()
        outer.start(contract(attended_ref[...], out_w[...], 1, 1))
        sent_pending = copies.swap("z", lambda peer: sent_ref, lambda me: sent_got.at[me])
        sent_got[zplace] = sent_ref[...]
        outer_product(mixed_ref, attended_ref, grads_ref, 3 * part)
        slot_of = rank * rows + lax.broadcasted_iota(jnp.int32, (rows, 1), 0)
        tables = [(chosen_ref[q : q + 1] == slot_of).astype(F32).astype(BF) for q in range(seqs)]
        blank = jnp.zeros((slots, HDIM), BF)
        grad_mixed = outer.finish().astype(BF)
        for g in range(group):
            grad_buf[g] = halves(grad_mixed[:, g * HDIM : (g + 1) * HDIM])
        pending = swaps.z(grad_buf, grad_got)
        wait(sent_pending)
        sent_all[place] = sent_got[...]
        sent_pending = swaps.share("core", sent_all)
        wait(pending)
        for g in range(group):
            grad_high[g] = side_by_side([blank, upright(grad_got[g])])
        query_grads = []
        for q in range(seqs):
            at = slice(q * sel, (q + 1) * sel)
            query, pair = slot_sequence(lines, queries_ref, pairs_ref, q, sel)
            grad = jnp.concatenate([grad_high[g, at] for g in range(group)], axis=0)
            grad_query, grad_pairs = backward_block(
                query,
                grad,
                grad.T[HDIM:],
                turned_ref[q],
                lse_ref[q],
                [(pair, pair.T, 0)],
                slots_of(lines, sel),
                start_ref[q],
                [True],
            )
            turned = jnp.concatenate([grad_query, jnp.zeros_like(grad_query)], axis=0).T.astype(BF)
            query_grads.append(turned[:, :HDIM])
            low = grad_pairs[0].astype(BF)
            for g in range(group):
                for r in range(ring):
                    first = (g * ring + r) * sel
                    turn_buf[r, g, at] = low[first : first + sel]
        pending = swaps.ring(turn_buf, turn_got)
        for g in range(group):
            back_buf[g, slots:] = halves(
                jnp.concatenate([t[g * sel : (g + 1) * sel] for t in query_grads], axis=0)
            )
        wait(pending)
        back_buf[:, :slots] = swaps.ring_sum(turn_buf, turn_got)
        pending = swaps.z(back_buf, back_got)
        wait(sent_pending)

        def at_positions(q, all_ref):
            at = slice(q * sel, (q + 1) * sel)
            found = jnp.concatenate([all_ref[r, g, at] for g in range(group) for r in range(ring)], axis=0)
            return matmul(tables[q], found)

        for q in range(seqs):
            added_ref[q] = at_positions(q, sent_all).astype(BF)
        wait(pending)
        dqkv_keep[...] = side_by_side(
            [back_got[g, :slots] for g in range(group)] + [upright(back_got[g, slots:]) for g in range(group)]
        )
        grad_normed = contract(dqkv_keep[...], qkv_w[...], 1, 1)
        picked = value_ref[...].astype(F32)
        inv = inverse_rms(picked)
        inner.start(grad_normed, jnp.sum(grad_normed * picked * gains_ref[2:3], axis=1, keepdims=True))
        outer_product(normed_ref, dqkv_keep, grads_ref, 0)
        picked = value_ref[:, own].astype(F32)
        grad_normed, scalar = inner.finish()
        vector_pre = jnp.sum(grad_normed * picked * inv, axis=0, keepdims=True)
        grad_in = inv * (grad_normed * gains_ref[2:3, own]) - picked * (inv * inv * inv) * (scalar * (1.0 / width))
        final_buf[...] = (middle_ref[...] + grad_in + logit_ref[:, :1] * gains_ref[4:5, own]).astype(BF)

        along = copies.swap("z", lambda peer: final_buf, lambda me: final_got.at[me])
        final_got[zplace] = final_buf[...]

        def hand_on(i):
            dst = final_all.at[place, i, :, own]
            dst[...] = final_got[i]
            return copies.swap("section", lambda peer: final_got.at[i], lambda me: dst)

        spread = hand_on(zplace)
        lane = lax.broadcasted_iota(jnp.int32, (part, 128), 1)
        vectors = jnp.zeros((part, 128), F32)
        for i, vector in enumerate((vector_pre, feed_vectors_ref[1:2], feed_vectors_ref[2:3])):
            vectors = jnp.where(lane == i, row_to_column(vector), vectors)
        grads_ref[:, 4 * part :] = jnp.zeros((width, 128), BF)
        grads_ref[pl.ds(pl.multiple_of(section * part, part), part), 4 * part :] = vectors.astype(BF)
        Copies.flush(grads_ref)
        for step in range(group - 1, 0, -1):
            along[group - 1 - step].wait_recv()
            spread += hand_on(lax.rem(zplace + step, group))
        for copy in along:
            copy.wait_send()
        wait(spread)
        wait(swaps.share("core", final_all))
        for q in range(seqs):
            fed_out[q] = (top_ref[q].astype(F32) + at_positions(q, final_all)).astype(BF)
            returned = jnp.concatenate(
                [final_all[r, g, q * sel : (q + 1) * sel, own] for g in range(group) for r in range(ring)], axis=0
            )
            own_out[q] = top_ref[q, :, own].astype(F32) + matmul(tables[q], returned)

    vmem = pltpu.VMEM
    z, s, c = group - 1, sections - 1, ring - 1
    lane_block = ((group, slots, lanes), BF)
    packed = ((group, slots // 2, lanes), BF)
    heads = ((group, slots + slots // 2, lanes), BF)
    ring_block = ((ring, group, slots, lanes), BF)
    short = ((group, slots, part), BF)
    scratch = [
        ((width, part), BF),
        packed,
        packed,
        lane_block,
        ring_block,
        ring_block,
        heads,
        heads,
        ((slots, 3 * part), BF),
        short,
        ((ring,) + short[0], BF),
        ((slots, part), BF),
        short,
        ((ring, group, slots, width), BF),
    ]
    return communicate(
        kernel,
        ident,
        arrays,
        [
            ((seqs, rows, width), BF),
            ((seqs, rows, part), F32),
            ((seqs, rows, part), BF),
            ((width, 4 * part + 128), BF),
        ],
        semaphores(
            3 * c
            + 4 * z
            + ColumnSum.count(sections, True)
            + ColumnSum.count(sections, False)
            + group * s
        )
        + [pltpu.SemaphoreType.DMA((1,))]
        + [vmem(a, b) for a, b in scratch]
        + ColumnSum.scratch(sections, slots, part, False)
        + ColumnSum.scratch(sections, slots, part, True),
        name,
        limit=60 * 2**20,
        far=(1,),
    )


def cut_weights(arrays, sections, dp, group, name):
    local, width = arrays[0].shape
    part = width // sections
    inner = arrays[4].shape[1] // dp
    share = inner // sections
    hidden_size = dp * share
    layers = len(arrays) // 6

    def kernel(*refs):
        ins, outs = refs[: 6 * layers], refs[6 * layers : 8 * layers]
        k_buf, v_buf, sems = refs[8 * layers :]
        section = lax.axis_index("section")
        own = span(section, part)
        moves = []
        for i in range(layers):
            q_ref, k_ref, v_ref, o_ref, e_ref, s_ref = ins[6 * i : 6 * i + 6]
            first_ref, rest_ref = outs[2 * i : 2 * i + 2]
            rows = pl.ds(pl.multiple_of(section * share, share), share)
            moves += [
                (k_ref.at[:, own], k_buf.at[i]),
                (v_ref.at[:, own], v_buf.at[i]),
                (q_ref.at[:, own], first_ref.at[:, 2 * part :]),
                (o_ref.at[:, own], rest_ref.at[:, :part]),
                (s_ref.at[rows], rest_ref.at[:, part + hidden_size :]),
            ]
            for d in range(dp):
                at = pl.ds(pl.multiple_of(d * inner + section * share, 128), share)
                moves.append((e_ref.at[:, at], rest_ref.at[:, part + d * share : part + (d + 1) * share]))
        copies = [pltpu.make_async_copy(src, dst, sems.at[i]) for i, (src, dst) in enumerate(moves)]
        for copy in copies:
            copy.start()
        for copy in copies:
            copy.wait()
        for i in range(layers):
            for g in range(group):
                at = slice(g * HDIM, (g + 1) * HDIM)
                pair = side_by_side([k_buf[i, :, at], v_buf[i, :, at]])
                outs[2 * i][:, 2 * g * HDIM : 2 * (g + 1) * HDIM] = pair

    anywhere, vmem = pl.BlockSpec(memory_space=pl.ANY), pl.BlockSpec(memory_space=pltpu.VMEM)
    shapes = [
        jax.ShapeDtypeStruct((local, 3 * part), BF),
        jax.ShapeDtypeStruct((local, part + hidden_size + width), BF),
    ]
    return pl.pallas_call(
        kernel,
        in_specs=[anywhere] * 6 * layers,
        out_specs=[vmem] * 2 * layers,
        out_shape=shapes * layers,
        scratch_shapes=[
            pltpu.VMEM((layers, local, part), BF),
            pltpu.VMEM((layers, local, part), BF),
            pltpu.SemaphoreType.DMA((layers * (5 + dp),)),
        ],
        compiler_params=pltpu.CompilerParams(vmem_limit_bytes=60 * 2**20),
        name=name,
    )(*arrays)


def on_device(
    stream_in,
    segment_ids,
    chosen_rows,
    cotangent,
    dense_prenorm,
    dense_query,
    dense_keys,
    dense_values,
    dense_output,
    dense_midnorm,
    dense_expand,
    dense_shrink,
    routed_prenorm,
    routed_query,
    routed_keys,
    routed_values,
    routed_output,
    routed_midnorm,
    routed_expand,
    routed_shrink,
    router_weight,
):
    sections, dp = lax.axis_size("section"), lax.axis_size("dp")
    section, rank = lax.axis_index("section"), lax.axis_index("dp")
    seqs, rows, width = stream_in.shape
    tokens = seqs * rows
    part = width // sections
    group = HEADS // sections
    ring = dp // group
    total_sel = chosen_rows.shape[1]
    sel = total_sel // dp
    lines = Lines(sections, dp, group)

    def own_columns(value):
        return lax.dynamic_slice_in_dim(value, section * part, part, value.ndim - 1)

    def own_hidden(expand, shrink):
        inner = expand.shape[1] // dp
        share = inner // sections
        cut = expand.reshape(expand.shape[0], dp, sections, share)
        cut = lax.dynamic_index_in_dim(cut, section, 2, keepdims=False).reshape(expand.shape[0], dp * share)
        return cut, lax.dynamic_slice_in_dim(shrink, section * share, share, 0)

    def own_attention(query, keys, values):
        local = query.shape[0]
        pair = jnp.stack(
            [own_columns(keys).reshape(local, group, HDIM), own_columns(values).reshape(local, group, HDIM)],
            axis=2,
        ).reshape(local, 2 * part)
        return jnp.concatenate([pair, own_columns(query)], axis=1)

    def cut(*layers):
        if dense_expand.shape[1] // (dp * sections) % 128 == 0:
            return cut_weights([w for layer in layers for w in layer], sections, dp, group, "cut")
        out = []
        for query, keys, values, output, expand, shrink in layers:
            expand_cut, shrink_cut = own_hidden(expand, shrink)
            rest = jnp.concatenate([own_columns(output), expand_cut, shrink_cut], axis=1)
            out += [own_attention(query, keys, values), rest]
        return out

    def gather(value):
        return lax.all_gather(value, "dp", axis=0, tiled=True)

    def after(value, other):
        return lax.optimization_barrier((value, other))[0]

    hidden_size = dense_expand.shape[1] // sections
    gains = jnp.stack([dense_prenorm, dense_midnorm, routed_prenorm, routed_midnorm, router_weight])
    gains = jnp.pad(gains, ((0, 16 - gains.shape[0]), (0, 0)))
    dense_first, dense_rest, routed_first, routed_rest = cut(
        (dense_query, dense_keys, dense_values, dense_output, dense_expand, dense_shrink),
        (routed_query, routed_keys, routed_values, routed_output, routed_expand, routed_shrink),
    )
    rest = gather(dense_rest)
    routed_qkv = gather(routed_first)
    routed_rest = gather(routed_rest)

    shape = (seqs, sel, rows, width, part)
    grad_top = cotangent.reshape(tokens, width)
    dense_qkv, gains, queries, pairs, start, mixed_turned, lse, mixed = dense_enter(
        lines,
        1,
        [stream_in.reshape(tokens, width), dense_first, gains, segment_ids],
        (seqs, rows, width),
        "dense_enter",
    )
    dense_qkv = dense_qkv.reshape(width, 3 * part)
    (
        attended,
        slope,
        hidden,
        after_dense,
        r_value,
        r_grad,
        r_normed,
        r_queries,
        r_pairs,
        r_start,
        r_turned,
        r_lse,
        r_mixed,
    ) = dense_feed(
        lines,
        2,
        [stream_in, mixed, gains, rest, cotangent, chosen_rows, segment_ids, routed_qkv],
        shape + (hidden_size,),
        "dense_feed",
    )
    after_dense = after_dense.reshape(tokens, part)
    attended, slope, hidden, mixed = (x.reshape(tokens, -1) for x in (attended, slope, hidden, mixed))

    def reduce_dp(value):
        return lax.psum_scatter(value, "dp", scatter_dimension=0, tiled=True)

    routed_grads, r_middle, r_grad_attended, r_sent, r_logit, r_vectors = routed_feed(
        lines,
        4,
        [r_value, r_grad, r_mixed, gains, routed_rest],
        (seqs * sel, width, part, hidden_size),
        "routed_feed",
    )
    routed_shard = reduce_dp(routed_grads)
    fed_low, grad_own, added, routed_grads = routed_leave(
        lines,
        5,
        [
            r_grad_attended,
            routed_rest,
            routed_qkv,
            r_queries,
            r_pairs,
            r_start,
            r_turned,
            r_lse,
            r_value,
            r_normed,
            r_mixed,
            r_middle,
            r_logit,
            r_sent,
            r_vectors,
            gains,
            chosen_rows,
            cotangent,
        ],
        shape,
        "routed_leave",
    )
    routed_shard_in = reduce_dp(after(routed_grads, routed_shard))
    stream_out = (after_dense + added.reshape(tokens, part).astype(F32)).astype(BF).reshape(seqs, rows, part)

    dense_grads, grad_attended, grad_middle, grad_heads, d_vectors = dense_return(
        lines,
        6,
        [
            fed_low.reshape(tokens, width),
            grad_own.reshape(tokens, part),
            stream_in.reshape(tokens, width),
            attended,
            slope,
            hidden,
            rest,
            gains,
        ],
        (seqs, rows, width, hidden_size),
        "dense_return",
    )
    dense_shard = reduce_dp(after(dense_grads, routed_shard_in))
    dense_grads, stream_grad, d_vectors, (routed_all, routed_all_in) = dense_leave(
        lines,
        7,
        [
            grad_heads,
            stream_in.reshape(tokens, width),
            queries,
            pairs,
            start,
            mixed_turned,
            lse,
            dense_qkv,
            mixed,
            grad_attended,
            grad_middle,
            gains,
            d_vectors,
        ],
        [routed_shard, routed_shard_in],
        (seqs, rows, width),
        "dense_leave",
    )
    stream_grad = stream_grad.reshape(seqs, rows, part)
    vectors, dense_all_in, (dense_all,) = dense_finish(
        lines, 8, d_vectors, dense_grads, [dense_shard], "dense_finish"
    )

    share = hidden_size // dp
    local = width // dp
    r_exp, r_shr, r_keys, r_values, r_query, r_out, r_vector = assemble(
        [
            ("hidden", routed_all, 0, hidden_size),
            ("stack", routed_all, hidden_size, width),
            ("pair", routed_all_in, 0, 2 * part),
            ("columns", routed_all_in, 2 * part, part),
            ("columns", routed_all_in, 3 * part, part),
            ("sum", routed_all_in, 4 * part, 128),
        ],
        share,
        "routed_places",
    )
    d_exp, d_shr, d_keys, d_values, d_query, d_out = assemble(
        [
            ("hidden", dense_all, 0, hidden_size),
            ("stack", dense_all, hidden_size, width),
            ("pair", dense_all_in, 0, 2 * part),
            ("columns", dense_all_in, 2 * part, part),
            ("columns", dense_all_in, 3 * part, part),
        ],
        share,
        "dense_places",
    )
    vectors = lax.dynamic_slice_in_dim(vectors, rank * local, local, 1)
    d_shr = d_shr.reshape(sections * share, width)
    r_shr = r_shr.reshape(sections * share, width)
    return (
        (stream_out, stream_grad)
        + (vectors[1], d_query, d_keys, d_values, d_out, vectors[0], d_exp, d_shr)
        + (r_vector[:, 0], r_query, r_keys, r_values, r_out, r_vector[:, 1], r_exp, r_shr)
        + (r_vector[:, 2],)
    )


def solution(mesh):
    streams, row, vector, copied = P(None, "dp", None), P("dp", None), P("dp"), P()
    layer = (vector, row, row, row, row, vector, row, row)
    outs = (P(None, "dp", "section"),) * 2 + layer + layer + (vector,)
    return jax.shard_map(
        on_device,
        mesh=mesh,
        in_specs=(streams, copied, copied, streams) + layer + layer + (vector,),
        out_specs=outs,
        check_vma=False,
    )
```

```python
import functools

import jax
import jax.numpy as jnp
from jax import lax
from jax.experimental import pallas as pl
from jax.experimental.pallas import tpu as pltpu
from jax.sharding import PartitionSpec as P

HEADS = 16
HDIM = 64
DOCS = 8
EPS = 1e-06
NEG = -1e30
SCALE = HDIM ** (-0.5)
VMEM = 32 * 2**20
MESH = pl.DeviceIdType.MESH
BF = jnp.bfloat16
F32 = jnp.float32


def matmul(left, right):
    return jnp.dot(left, right, preferred_element_type=F32)


def contract(left, right, ldim, rdim):
    return lax.dot_general(left, right, (((ldim,), (rdim,)), ((), ())), preferred_element_type=F32)


class Lines:
    def __init__(self, sections, dp, group):
        self.sizes = {"section": sections, "z": group, "core": dp // group}
        self.ring = dp // group

    def place(self, kind):
        if kind == "section":
            return lax.axis_index("section")
        index = lax.axis_index("dp")
        return index // self.ring if kind == "z" else lax.rem(index, self.ring)

    def device(self, kind, place):
        if kind == "section":
            return {"section": place}
        index = lax.axis_index("dp")
        if kind == "z":
            return {"dp": place * self.ring + lax.rem(index, self.ring)}
        return {"dp": (index // self.ring) * self.ring + place}

    def peers(self, kind):
        size = self.sizes[kind]
        me = self.place(kind)
        return [lax.rem(me + step, size) for step in range(1, size)]


class Copies:
    loads, flush = (), None

    def __init__(self, lines, send, recv):
        self.lines, self.send, self.recv, self.used = lines, send, recv, 0

    def greet(self, kinds):
        barrier = pltpu.get_barrier_semaphore()
        count = 0
        for kind in kinds:
            for peer in self.lines.peers(kind):
                pl.semaphore_signal(
                    barrier, inc=1, device_id=self.lines.device(kind, peer), device_id_type=MESH
                )
                count += 1
        for load in Copies.loads:
            load.wait()
        pl.semaphore_wait(barrier, count)

    def start(self, kind, peer, src, dst):
        assert self.used < self.send.shape[0]
        copy = pltpu.make_async_remote_copy(
            src_ref=src,
            dst_ref=dst,
            send_sem=self.send.at[self.used],
            recv_sem=self.recv.at[self.used],
            device_id=self.lines.device(kind, peer),
            device_id_type=MESH,
        )
        self.used += 1
        copy.start()
        return copy

    def swap(self, kind, src, dst):
        me = self.lines.place(kind)
        return [self.start(kind, peer, src(peer), dst(me)) for peer in self.lines.peers(kind)]


def wait(copies):
    for copy in copies:
        copy.wait()


def semaphores(count):
    return [pltpu.SemaphoreType.DMA((count,)), pltpu.SemaphoreType.DMA((count,))]


def communicate(kernel, ident, arrays, shapes, scratch, name, limit=60 * 2**20, far=()):
    place = pl.BlockSpec(memory_space=pl.ANY)
    near = [i for i in range(len(arrays)) if i not in far]
    many, outs = len(arrays), len(shapes)

    def body(*refs):
        ins, results, refs = list(refs[:many]), refs[many : many + outs], refs[many + outs :]
        inner, refs = refs[: len(scratch)], refs[len(scratch) :]
        in_bufs, out_bufs, (in_sems, out_sems) = refs[: len(near)], refs[len(near) : len(near) + outs], refs[-2:]
        loads = []
        for k, i in enumerate(near):
            loads.append(pltpu.make_async_copy(ins[i], in_bufs[k], in_sems.at[k]))
            loads[-1].start()
            ins[i] = in_bufs[k]
        stores = [pltpu.make_async_copy(out_bufs[k], results[k], out_sems.at[k]) for k in range(outs)]
        started = set()

        def flush(ref):
            k = next(k for k in range(outs) if out_bufs[k] is ref)
            stores[k].start()
            started.add(k)

        Copies.loads, Copies.flush = loads, staticmethod(flush)
        kernel(*ins, *out_bufs, *inner)
        for k in range(outs):
            if k not in started:
                stores[k].start()
        for store in stores:
            store.wait()

    return pl.pallas_call(
        body,
        out_shape=[jax.ShapeDtypeStruct(s, d) for s, d in shapes],
        in_specs=[place] * many,
        out_specs=[place] * outs,
        scratch_shapes=list(scratch)
        + [pltpu.VMEM(arrays[i].shape, arrays[i].dtype) for i in near]
        + [pltpu.VMEM(s, d) for s, d in shapes]
        + [pltpu.SemaphoreType.DMA((max(1, len(near)),)), pltpu.SemaphoreType.DMA((outs,))],
        compiler_params=pltpu.CompilerParams(
            collective_id=ident, has_side_effects=True, vmem_limit_bytes=limit
        ),
        name=name,
    )(*arrays)


def span(place, width):
    return pl.ds(pl.multiple_of(place * width, width), width)


def square(lines):
    me = lines.place("section")
    low, high = lax.rem(me, 2), me // 2
    return high * 2 + 1 - low, (1 - high) * 2 + low, (1 - high) * 2 + 1 - low


def pieces_of(rows):
    half = rows // 2
    return (2, half // 2) if half % 32 == 0 else (1, half)


class SquareGather:
    @staticmethod
    def count(rows):
        return 6 * pieces_of(rows)[0]

    def __init__(self, copies, x_ref, o_ref, pieces=None):
        self.copies, self.x_ref, self.o_ref = copies, x_ref, o_ref
        self.width = x_ref.shape[1]
        self.me = copies.lines.place("section")
        near, far, _ = square(copies.lines)
        half = x_ref.shape[0] // 2
        pieces, step = pieces_of(x_ref.shape[0]) if pieces is None else (pieces, half // pieces)
        self.parts = [
            (pl.ds(h * half + j * step, step), one, two)
            for j in range(pieces)
            for h, (one, two) in enumerate(((near, far), (far, near)))
        ]

    def send(self, at, to):
        dst = self.o_ref.at[at, span(self.me, self.width)]
        return self.copies.start("section", to, self.x_ref.at[at], dst)

    def start(self):
        self.first = [self.send(at, one) for at, one, _ in self.parts]
        self.rest = [self.send(at, two) for at, _, two in self.parts]
        self.o_ref[:, span(self.me, self.width)] = self.x_ref[...]

    def forward(self):
        for (at, one, two), copy in zip(self.parts, self.first):
            copy.wait_recv()
            place = self.o_ref.at[at, span(one, self.width)]
            self.rest.append(self.copies.start("section", two, place, place))

    def finish(self):
        for copy in self.first:
            copy.wait_send()
        wait(self.rest)


class SquareScatter:
    @staticmethod
    def count(rows):
        return 6 * pieces_of(rows)[0]

    @staticmethod
    def scratch(rows, width):
        return [pltpu.VMEM((2, rows, width), BF), pltpu.VMEM((rows, width), BF), pltpu.VMEM((rows, width), BF)]

    def __init__(self, copies, x_ref, got, turn, last, pieces=None):
        self.copies, self.x_ref, self.got, self.turn, self.last = copies, x_ref, got, turn, last
        self.width = turn.shape[1]
        self.me = copies.lines.place("section")
        near, far, self.across = square(copies.lines)
        half = x_ref.shape[0] // 2
        pieces, step = pieces_of(x_ref.shape[0]) if pieces is None else (pieces, half // pieces)
        self.parts = [
            (pl.ds(h * half + j * step, step), one, two)
            for j in range(pieces)
            for h, (one, two) in enumerate(((near, far), (far, near)))
        ]

    def read(self, at, place):
        return self.x_ref[at, span(place, self.width)].astype(F32)

    def start(self):
        self.passed, self.kept = [], []
        for at, one, _ in self.parts:
            for place, k, out in ((self.across, 0, self.passed), (one, 1, self.kept)):
                src = self.x_ref.at[at, span(place, self.width)]
                out.append(self.copies.start("section", one, src, self.got.at[k, at]))

    def forward(self):
        self.second = []
        for (at, _, two), copy in zip(self.parts, self.passed):
            copy.wait_recv()
            self.turn[at] = (self.read(at, two) + self.got[0, at].astype(F32)).astype(BF)
            self.second.append(self.copies.start("section", two, self.turn.at[at], self.last.at[at]))

    def finish(self, o_ref):
        for i, (at, _, _) in enumerate(self.parts):
            self.kept[i].wait_recv()
            self.second[i].wait_recv()
            o_ref[at] = self.read(at, self.me) + self.got[1, at].astype(F32) + self.last[at].astype(F32)
        for copy in self.passed + self.kept + self.second:
            copy.wait_send()


def gather_columns(lines, ident, part, name):
    rows, width = part.shape

    def kernel(x_ref, o_ref, send, recv):
        copies = Copies(lines, send, recv)
        copies.greet(["section"])
        gather = SquareGather(copies, x_ref, o_ref)
        gather.start()
        gather.forward()
        gather.finish()

    shape = ((rows, lines.sizes["section"] * width), part.dtype)
    (out,) = communicate(kernel, ident, [part], [shape], semaphores(SquareGather.count(rows)), name)
    return out


def scalar_block(scalars):
    count = -(-scalars.shape[0] // 128)
    count += -count % 8
    return jnp.pad(scalars, (0, count * 128 - scalars.shape[0])).reshape(count, 128)


def sum_places(ref):
    total = ref[0].astype(F32)
    for i in range(1, ref.shape[0]):
        total = total + ref[i].astype(F32)
    return total


def scatter_columns(lines, ident, part, scalars, name):
    rows, full = part.shape
    sections = lines.sizes["section"]
    width = full // sections
    extra = scalars is not None
    arrays = [part]
    shapes = [((rows, width), F32)]
    scratch = semaphores(SquareScatter.count(rows) + sections - 1) + SquareScatter.scratch(rows, width)
    if extra:
        arrays.append(scalar_block(scalars))
        shapes.append((arrays[1].shape, F32))
        scratch.append(pltpu.VMEM((sections,) + arrays[1].shape, F32))

    def kernel(*refs):
        x_ref, refs = refs[0], refs[1:]
        if extra:
            e_ref, o_ref, eo_ref, send, recv, got, turn, last, e_got = refs
        else:
            o_ref, send, recv, got, turn, last = refs
        copies = Copies(lines, send, recv)
        copies.greet(["section"])
        scatter = SquareScatter(copies, x_ref, got, turn, last)
        scatter.start()
        if extra:
            others = copies.swap("section", lambda peer: e_ref, lambda place: e_got.at[place])
            e_got[lines.place("section")] = e_ref[...]
        scatter.forward()
        scatter.finish(o_ref)
        if extra:
            wait(others)
            eo_ref[...] = sum_places(e_got)

    got = communicate(kernel, ident, arrays, shapes, scratch, name)
    if not extra:
        return got[0]
    return got[0], got[1].reshape(-1)[:rows]


class RowScatter:
    @staticmethod
    def count(group, ring):
        return group * (ring - 1) + group - 1

    @staticmethod
    def scratch(group, ring, local, wide):
        vmem = pltpu.VMEM
        return [vmem((ring, group, local, wide), BF), vmem((group, local, wide), BF), vmem((group, local, wide), BF)]

    def __init__(self, copies, w_ref, buffers):
        self.copies, self.w_ref = copies, w_ref
        self.got, self.turn, self.all = buffers
        lines = copies.lines
        self.zplace, self.ring = lines.place("z"), lines.sizes["core"]
        self.order = lines.peers("z") + [self.zplace]

    def start(self):
        self.around = [
            self.copies.swap(
                "core", lambda peer: self.w_ref.at[g * self.ring + peer], lambda me: self.got.at[me, g]
            )
            for g in self.order
        ]

    def forward(self):
        lines = self.copies.lines
        place = lines.place("core")
        self.along = []
        for i, (g, arrived) in enumerate(zip(self.order, self.around)):
            for copy in arrived:
                copy.wait_recv()
            total = self.w_ref[g * self.ring + place].astype(F32)
            for peer in lines.peers("core"):
                total = total + self.got[peer, g].astype(F32)
            self.turn[g] = total.astype(BF)
            if i < len(self.order) - 1:
                self.along.append(self.copies.start("z", g, self.turn.at[g], self.all.at[self.zplace]))
        self.all[self.zplace] = self.turn[self.zplace]

    def finish(self, out_ref):
        wait(self.along)
        out_ref[...] = sum_places(self.all).astype(BF)
        for arrived in self.around:
            for copy in arrived:
                copy.wait_send()


def dense_finish(lines, ident, vectors, weight, shards, cuts, name):
    group, ring, sections = (lines.sizes[k] for k in ("z", "core", "section"))
    dp = group * ring
    many = len(shards)
    local = weight.shape[0] // dp
    wide = weight.shape[1]
    weight = weight.reshape(dp, local, wide)
    width = vectors.shape[1]
    bounds = [sum(cuts[:i]) for i in range(len(cuts) + 1)]
    parts = [pl.ds(bounds[i], cuts[i]) for i in range(len(cuts))]
    count = len(cuts)

    def kernel(x_ref, w_ref, *refs):
        s_refs, refs = refs[:many], refs[many:]
        v_ref, refs = refs[0], refs[1:]
        wo_refs, refs = refs[:count], refs[count:]
        so_refs, refs = refs[:many], refs[many:]
        send, recv, w_got, w_turn, w_all, v_z, v_core, v_all, *w_own = refs
        copies = Copies(lines, send, recv)
        zplace, place, section = (lines.place(k) for k in ("z", "core", "section"))
        copies.greet(["z", "core", "section"])
        order = lines.peers("z") + [zplace]
        around = {}
        for h, at in enumerate(parts):
            for i, g in enumerate(order):
                around[h, i] = copies.swap(
                    "core", lambda peer: w_ref.at[g * ring + peer, :, at], lambda me: w_got.at[me, g, :, at]
                )
        along = {h: [] for h in range(count)}
        for h, at in enumerate(parts):
            for i, g in enumerate(order):
                for copy in around[h, i]:
                    copy.wait_recv()
                total = w_ref[g * ring + place, :, at].astype(F32)
                for peer in lines.peers("core"):
                    total = total + w_got[peer, g, :, at].astype(F32)
                w_turn[g, :, at] = total.astype(BF)
                if i < len(order) - 1:
                    along[h].append(copies.start("z", g, w_turn.at[g, :, at], w_all.at[zplace, :, at]))
        pending = copies.swap("z", lambda peer: x_ref, lambda me: v_z.at[me])
        v_z[zplace] = x_ref[...]
        gathers = [SquareGather(copies, x, o) for x, o in zip(s_refs, so_refs)]
        for gather in gathers:
            gather.start()
        w_all[zplace] = w_turn[zplace]
        for gather in gathers:
            gather.forward()
        for h, at in enumerate(parts):
            wait(along[h])
            total = w_all[0, :, at].astype(F32)
            for i in range(1, group):
                total = total + w_all[i, :, at].astype(F32)
            w_own[h][...] = total.astype(BF)
            gathers.append(SquareGather(copies, w_own[h], wo_refs[h], 1))
            gathers[-1].start()
            if h > 0:
                gathers[-2].forward()
        wait(pending)
        v_core[place] = sum_places(v_z)
        wait(copies.swap("core", lambda peer: v_core.at[place], lambda me: v_core.at[me]))
        v_all[section] = sum_places(v_core)
        pending = copies.swap("section", lambda peer: v_all.at[section], lambda me: v_all.at[me])
        gathers[-1].forward()
        wait(pending)
        for i in range(sections):
            v_ref[:, i * width : (i + 1) * width] = v_all[i]
        for arrived in around.values():
            for copy in arrived:
                copy.wait_send()
        for gather in gathers:
            gather.finish()

    z, c, s = group - 1, ring - 1, sections - 1
    result = communicate(
        kernel,
        ident,
        [vectors, weight] + shards,
        [((8, sections * width), F32)]
        + [((local, sections * cut), BF) for cut in cuts]
        + [((x.shape[0], sections * x.shape[1]), x.dtype) for x in shards],
        semaphores(
            count * (group * c + z + 6)
            + sum(SquareGather.count(x.shape[0]) for x in shards)
            + z
            + c
            + s
        )
        + [
            pltpu.VMEM((ring, group, local, wide), BF),
            pltpu.VMEM((group, local, wide), BF),
            pltpu.VMEM((group, local, wide), BF),
            pltpu.VMEM((group, 8, width), F32),
            pltpu.VMEM((ring, 8, width), F32),
            pltpu.VMEM((sections, 8, width), F32),
        ]
        + [pltpu.VMEM((local, cut), BF) for cut in cuts],
        name,
        limit=60 * 2**20,
    )
    return result[0], result[1 : 1 + count], result[1 + count :]


def assemble(pieces, share, name):
    arrays = []
    for _, array, _, _ in pieces:
        if not any(array is other for other in arrays):
            arrays.append(array)
    where = [next(i for i, other in enumerate(arrays) if other is array) for _, array, _, _ in pieces]
    local = arrays[0].shape[0]
    steps = local // 32 if local % 32 == 0 else 1
    rows = local // steps
    sections = lax.axis_size("section")
    shapes, specs = [], []
    for kind, _, _, width in pieces:
        many = 2 if kind == "pair" else 1
        for _ in range(many):
            if kind == "stack":
                shapes.append(jax.ShapeDtypeStruct((sections, local, width), F32))
                specs.append(pl.BlockSpec((sections, rows, width), lambda i: (0, i, 0)))
            else:
                total = width if kind == "sum" else sections * width // many
                shapes.append(jax.ShapeDtypeStruct((local, total), F32))
                specs.append(pl.BlockSpec((rows, total), lambda i: (i, 0)))

    def kernel(*refs):
        ins, outs = refs[: len(arrays)], list(refs[len(arrays) :])
        for (kind, array, first, width), i in zip(pieces, where):
            wide = array.shape[1] // sections
            blocks = [ins[i][:, s * wide + first : s * wide + first + width].astype(F32) for s in range(sections)]
            out = outs.pop(0)
            if kind == "columns":
                for s, item in enumerate(blocks):
                    out[:, s * width : (s + 1) * width] = item
            elif kind == "stack":
                for s, item in enumerate(blocks):
                    out[s] = item
            elif kind == "sum":
                total = blocks[0]
                for item in blocks[1:]:
                    total = total + item
                out[...] = total
            elif kind == "hidden":
                for d in range(width // share):
                    out[:, d * share * sections : (d + 1) * share * sections] = jnp.concatenate(
                        [item[:, d * share : (d + 1) * share] for item in blocks], axis=1
                    )
            else:
                other = outs.pop(0)
                half = width // 2
                for s, item in enumerate(blocks):
                    for side, dst in ((0, out), (1, other)):
                        heads = [
                            item[:, (2 * g + side) * HDIM : (2 * g + side + 1) * HDIM]
                            for g in range(width // (2 * HDIM))
                        ]
                        dst[:, s * half : (s + 1) * half] = jnp.concatenate(heads, axis=1)

    return pl.pallas_call(
        kernel,
        grid=(steps,),
        in_specs=[pl.BlockSpec((rows, a.shape[1]), lambda i: (i, 0)) for a in arrays],
        out_specs=specs,
        out_shape=shapes,
        compiler_params=pltpu.CompilerParams(vmem_limit_bytes=60 * 2**20),
        name=name,
    )(*arrays)


def column_to_rows(column):
    return jnp.broadcast_to(column, (column.shape[0], 128)).T[:8]


def row_to_column(row):
    return jnp.broadcast_to(row, (128, row.shape[1])).T[:, :1]


def outer_product(left_ref, right_ref, out_ref, first):
    step = 256
    wide = right_ref.shape[1]

    @pl.loop(0, left_ref.shape[1] // step)
    def _(i):
        at = span(i, step)
        block = contract(left_ref[:, at], right_ref[...], 0, 0)
        out_ref[at, first : first + wide] = block.astype(BF)


def unpack_low(packed):
    lane = lax.broadcasted_iota(jnp.int32, packed.shape, 1)
    zero = jnp.zeros_like(packed)
    low = jnp.where(lane < HDIM, packed, zero)
    turned = jnp.concatenate([packed[:, HDIM:], packed[:, :HDIM]], axis=1)
    high = jnp.where(lane < HDIM, turned, zero)
    return jnp.concatenate([low, high], axis=0)


def unpack_high(packed):
    lane = lax.broadcasted_iota(jnp.int32, packed.shape, 1)
    zero = jnp.zeros_like(packed)
    turned = jnp.concatenate([packed[:, HDIM:], packed[:, :HDIM]], axis=1)
    low = jnp.where(lane >= HDIM, turned, zero)
    high = jnp.where(lane >= HDIM, packed, zero)
    return jnp.concatenate([low, high], axis=0)


def pack_turned(turned):
    half = turned.shape[1] // 2
    return jnp.concatenate([turned[:, :half], turned[:, half:]], axis=0).T


def forward_block(query, pieces, qpos, start, causal):
    scores = []
    peak = None
    for index, (pair, _, first) in enumerate(pieces):
        item = contract(pair, query, 1, 1)
        kpos = first + lax.broadcasted_iota(jnp.int32, item.shape, 0)
        allowed = kpos >= start
        if causal[index]:
            allowed = allowed & (kpos <= qpos)
        item = jnp.where(allowed, item, NEG)
        top = jnp.max(item, axis=0, keepdims=True)
        peak = top if peak is None else jnp.maximum(peak, top)
        scores.append(item)
    total = jnp.zeros_like(peak)
    mixed = None
    for item, (_, turned, _) in zip(scores, pieces):
        weight = jnp.exp(item - peak)
        total = total + jnp.sum(weight, axis=0, keepdims=True)
        part = matmul(turned[HDIM:], weight.astype(BF))
        mixed = part if mixed is None else mixed + part
    return mixed / total, peak + jnp.log(total)


def backward_block(query, grad, grad_turned, mixed_turned, lse, pieces, qpos, start, causal):
    row_sum = jnp.sum(grad_turned.astype(F32) * mixed_turned.astype(F32), axis=0, keepdims=True)
    grad_query = None
    grads = []
    for index, (pair, turned, first) in enumerate(pieces):
        scores = contract(pair, query, 1, 1)
        kpos = first + lax.broadcasted_iota(jnp.int32, scores.shape, 0)
        allowed = kpos >= start
        if causal[index]:
            allowed = allowed & (kpos <= qpos)
        probs = jnp.where(allowed, jnp.exp(scores - lse), 0.0)
        grad_probs = contract(pair, grad, 1, 1)
        grad_scores = (probs * (grad_probs - row_sum)).astype(BF)
        grads.append(matmul(grad_scores, query) + matmul(probs.astype(BF), grad))
        part = matmul(turned[:HDIM], grad_scores)
        grad_query = part if grad_query is None else grad_query + part
    return grad_query * SCALE, grads


def document_starts(ids):
    return [
        jnp.sum((ids < c).astype(F32), axis=1, keepdims=True) if c else jnp.zeros((1, 1), F32) for c in range(DOCS)
    ]


def start_of(documents, firsts):
    start = jnp.zeros(documents.shape, F32)
    for c in range(1, DOCS):
        start = jnp.where(documents >= c, firsts[c], start)
    return start.astype(jnp.int32)


def dense_enter(lines, ident, arrays, shape, name):
    seqs, rows, width = shape
    sections, group, ring = (lines.sizes[k] for k in ("section", "z", "core"))
    dp = group * ring
    part = width // sections
    half = rows // 2
    lanes = 2 * HDIM
    block = ring * rows
    local = width // dp

    def kernel(
        value_ref,
        weights_ref,
        cut_ref,
        ids_ref,
        weights_all,
        gains_ref,
        q_got,
        kv_all,
        start_ref,
        turned_ref,
        lse_ref,
        mixed_ref,
        send,
        recv,
        cut_all,
        kv_buf,
        q_buf,
        o_buf,
        o_got,
        o_own,
    ):
        copies = Copies(lines, send, recv)
        zplace, place = lines.place("z"), lines.place("core")
        rank = lax.axis_index("dp")
        copies.greet(["section", "z", "core"])
        pairs = [(weights_ref, weights_all), (cut_ref, cut_all)]
        along, handed = [], []
        for x_ref, o_ref in pairs:
            along.append(copies.swap("z", lambda peer: x_ref, lambda _: o_ref.at[rank]))
        for x_ref, o_ref in pairs:
            handed += copies.swap("core", lambda peer: x_ref, lambda _: o_ref.at[rank])
            o_ref[rank] = x_ref[...]
        for q in range(seqs):
            firsts = document_starts(ids_ref[q : q + 1])
            for g in range(group):
                at = pl.ds(pl.multiple_of((g * ring + place) * rows, rows), rows)
                start_ref[q, g] = start_of(ids_ref[q : q + 1, at], firsts)
        for step in range(group - 1, 0, -1):
            source = lax.rem(zplace + step, group) * ring + place
            for arrived, (_, o_ref) in zip(along, pairs):
                arrived[group - 1 - step].wait_recv()
                handed += copies.swap("core", lambda peer: o_ref.at[source], lambda _: o_ref.at[source])
        for arrived in along:
            for copy in arrived:
                copy.wait_send()
        wait(handed)
        for d in range(dp):
            gains_ref[:, d * local : (d + 1) * local] = cut_all[d].astype(F32)

        arriving, queries, around, outward, gathers = {}, {}, {}, {}, {}

        def project(q):
            value = value_ref[pl.ds(q * rows, rows)].astype(F32)
            normed = (value * inverse_rms(value) * gains_ref[0:1]).astype(BF)
            qkv = matmul(normed, weights_all[...].reshape(width, 3 * part)).astype(BF)
            for g in range(group):
                kv_buf[g, q] = qkv[:, g * lanes : (g + 1) * lanes]
                at = slice(2 * part + g * HDIM, 2 * part + (g + 1) * HDIM)
                q_buf[g, q] = side_by_side([qkv[:half, at], qkv[half:, at]])
            arriving[q] = copies.swap("z", lambda peer: kv_buf.at[peer, q], lambda me: kv_all.at[place, me, q])
            queries[q] = copies.swap("z", lambda peer: q_buf.at[peer, q], lambda me: q_got.at[me, q])
            q_got[zplace, q] = q_buf[zplace, q]
            kv_all[place, zplace, q] = kv_buf[zplace, q]
            own = kv_all.at[place, zplace, q]
            around[q] = copies.swap("core", lambda peer: own, lambda _: own)

        def hand(q):
            for step in range(group - 1, 0, -1):
                arriving[q][group - 1 - step].wait_recv()
                item = kv_all.at[place, lax.rem(zplace + step, group), q]
                around[q] += copies.swap("core", lambda peer: item, lambda _: item)

        def attend(q):
            for copy in arriving[q]:
                copy.wait_send()
            wait(queries[q])
            wait(around[q])
            pieces = []
            for g in range(group):
                pair = kv_all[:, g, q].reshape(block, lanes)
                pieces.append((pair, pair.T, g * block))
            for g in range(group):
                query = unpack_low(q_got[g, q]) * jnp.asarray(SCALE, BF)
                qpos = g * block + place * rows + lax.broadcasted_iota(jnp.int32, (1, rows), 1)
                mixed, lse = forward_block(
                    query, pieces[: g + 1], qpos, start_ref[q, g], [i == g for i in range(g + 1)]
                )
                turned_ref[q, g] = mixed.astype(BF)
                lse_ref[q, g] = lse
                o_buf[g, q] = pack_turned(mixed).astype(BF)
            outward[q] = copies.swap("z", lambda peer: o_buf.at[peer, q], lambda me: o_got.at[me, q])
            o_got[zplace, q] = o_buf[zplace, q]

        def merge(q):
            wait(outward[q])
            packed = [o_got[g, q] for g in range(group)]
            o_own[q] = side_by_side([jnp.concatenate([p[:, :HDIM], p[:, HDIM:]], axis=0) for p in packed])
            gathers[q] = SquareGather(copies, o_own.at[q], mixed_ref.at[q], 1)
            gathers[q].start()

        for q in range(seqs):
            project(q)
        for q in range(seqs):
            hand(q)
            attend(q)
            if q > 0:
                merge(q - 1)
            if q > 1:
                gathers[q - 2].forward()
        merge(seqs - 1)
        for q in range(max(0, seqs - 2), seqs):
            gathers[q].forward()
        for q in range(seqs):
            gathers[q].finish()

    z, c = group - 1, ring - 1
    vmem = pltpu.VMEM
    packed = ((group, seqs, half, lanes), BF)
    return communicate(
        kernel,
        ident,
        arrays,
        [
            ((dp, local, 3 * part), BF),
            ((16, width), F32),
            packed,
            ((ring, group, seqs, rows, lanes), BF),
            ((seqs, group, 1, rows), jnp.int32),
            ((seqs, group, HDIM, rows), BF),
            ((seqs, group, 1, rows), F32),
            ((seqs, rows, width), BF),
        ],
        semaphores(2 * (z + group * c) + seqs * (3 * z + group * c + 6))
        + [
            vmem((dp, 16, local), BF),
            vmem((group, seqs, rows, lanes), BF),
            vmem(*packed),
            vmem(*packed),
            vmem(*packed),
            vmem((seqs, rows, part), BF),
        ],
        name,
        limit=60 * 2**20,
    )


class SequenceSums:
    @staticmethod
    def count(sections, seqs, scalars):
        return seqs * (6 + (sections - 1 if scalars else 0))

    @staticmethod
    def scratch(sections, seqs, rows, part, scalars):
        vmem = pltpu.VMEM
        buffers = [
            vmem((seqs, rows, sections * part), BF),
            vmem((seqs, 2, rows, part), BF),
            vmem((seqs, rows, part), BF),
            vmem((seqs, rows, part), BF),
            vmem((rows, part), F32),
        ]
        if scalars:
            buffers += [vmem((seqs, 8, rows), F32), vmem((seqs, sections, 8, rows), F32)]
        return buffers

    def __init__(self, copies, buffers):
        self.copies, self.buffers, self.items = copies, buffers, {}

    def start(self, q, value, scalars=None):
        wide, got, turn, last = self.buffers[:4]
        wide[q] = value.astype(BF)
        item = SquareScatter(self.copies, wide.at[q], got.at[q], turn.at[q], last.at[q], 1)
        item.start()
        others = []
        if scalars is not None:
            buf, arrived = self.buffers[5:]
            section = self.copies.lines.place("section")
            buf[q] = column_to_rows(scalars)
            others = self.copies.swap("section", lambda peer: buf.at[q], lambda me: arrived.at[q, me])
            arrived[q, section] = buf[q]
        self.items[q] = (item, others)

    def forward(self, q):
        self.items[q][0].forward()

    def finish(self, q):
        item, others = self.items[q]
        total = self.buffers[4]
        item.finish(total)
        if not others:
            return total[...]
        wait(others)
        return total[...], row_to_column(sum_places(self.buffers[6].at[q])[:1])


class Loads:
    def __init__(self, sems):
        self.sems, self.used = sems, 0

    def start(self, src, dst):
        copy = pltpu.make_async_copy(src, dst, self.sems.at[self.used])
        self.used += 1
        copy.start()
        return copy


def dense_return(lines, ident, arrays, shape, name):
    seqs, rows, width, hidden_size = shape
    sections, group, ring = (lines.sizes[k] for k in ("section", "z", "core"))
    part = width // sections
    half = rows // 2

    def kernel(
        fed_ref,
        own_ref,
        value_ref,
        attended_ref,
        slope_ref,
        hidden_ref,
        mixed_ref,
        rest_ref,
        gains_ref,
        r_vectors_ref,
        r_grads_ref,
        grads_ref,
        middle,
        heads,
        vectors_ref,
        r_shard_ref,
        send,
        recv,
        sems,
        dattended,
        out_w,
        expand_w,
        shrink_w,
        late,
        normed,
        dpre,
        *buffers,
    ):
        loads = Loads(sems)
        shrink_load = loads.start(rest_ref.at[:, part + hidden_size :], shrink_w)
        expand_load = loads.start(rest_ref.at[:, part : part + hidden_size], expand_w)
        out_load = loads.start(rest_ref.at[:, :part], out_w)
        hidden_load = loads.start(hidden_ref, late)
        copies = Copies(lines, send, recv)
        own = span(lines.place("section"), part)
        copies.greet(["section", "z", "core"])
        mids = SequenceSums(copies, buffers[:7])
        outs = SequenceSums(copies, buffers[7:-3])
        r_sum = RowScatter(copies, r_grads_ref, buffers[-3:])
        r_sum.start()

        def middle_of(at):
            return value_ref[at].astype(F32) + attended_ref[at].astype(F32)

        def feed(q):
            at = pl.ds(q * rows, rows)
            grad_hidden = contract(fed_ref[at], shrink_w[...], 1, 1)
            grad_pre = (grad_hidden * slope_ref[at].astype(F32)).astype(BF)
            dpre[at] = grad_pre
            grad_normed = contract(grad_pre, expand_w[...], 1, 1)
            mid = middle_of(at)
            mids.start(q, grad_normed, jnp.sum(grad_normed * mid * gains_ref[1:2], axis=1, keepdims=True))
            normed[at] = (mid * inverse_rms(mid) * gains_ref[1:2]).astype(BF)

        def project(q):
            at = pl.ds(q * rows, rows)
            grad_normed, scalars = mids.finish(q)
            inv = inverse_rms(middle_of(at))
            mid = value_ref[at, own].astype(F32) + attended_ref[at, own].astype(F32)
            vectors_ref[1:2] += jnp.sum(grad_normed * mid * inv, axis=0, keepdims=True)
            grad = (
                inv * (grad_normed * gains_ref[1:2, own])
                - mid * (inv * inv * inv) * (scalars * (1.0 / width))
                + own_ref[at]
            )
            middle[at] = grad
            low = grad.astype(BF)
            dattended[at] = low
            outs.start(q, contract(low, out_w[...], 1, 1))

        def leave(q):
            grad = outs.finish(q).astype(BF)
            for g in range(group):
                columns = slice(g * HDIM, (g + 1) * HDIM)
                heads[g, q] = side_by_side([grad[:half, columns], grad[half:, columns]])

        vectors_ref[...] = r_vectors_ref[...]
        vectors_ref[0:2] = jnp.zeros((2, part), F32)
        shrink_load.wait()
        expand_load.wait()
        out_load.wait()
        last = seqs - 1
        for q in range(seqs):
            feed(q)
            if q == 0:
                r_sum.forward()
            if q > 0:
                mids.forward(q - 1)
            if q > 1:
                project(q - 2)
        mids.forward(last)
        hidden_load.wait()
        outer_product(late, fed_ref, grads_ref, hidden_size)
        mixed_load = loads.start(mixed_ref, late)
        for q in range(max(0, last - 1), seqs):
            project(q)
            outs.forward(q - 1)
        outer_product(normed, dpre, grads_ref, 0)
        outs.forward(last)
        mixed_load.wait()
        outer_product(late, dattended, grads_ref, hidden_size + width)
        Copies.flush(grads_ref)
        for q in range(seqs):
            leave(q)
        r_sum.finish(r_shard_ref)

    tokens = seqs * rows
    vmem = pltpu.VMEM
    r_grads = arrays[-1].reshape(group * ring, -1, arrays[-1].shape[1])
    arrays = arrays[:-1] + [r_grads]
    return communicate(
        kernel,
        ident,
        arrays,
        [
            ((width, hidden_size + width + part), BF),
            ((tokens, part), F32),
            ((group, seqs, half, 2 * HDIM), BF),
            ((8, part), F32),
            (r_grads.shape[1:], BF),
        ],
        semaphores(
            SequenceSums.count(sections, seqs, True)
            + SequenceSums.count(sections, seqs, False)
            + RowScatter.count(group, ring)
        )
        + [
            pltpu.SemaphoreType.DMA((5,)),
            vmem((tokens, part), BF),
            vmem((width, part), BF),
            vmem((width, hidden_size), BF),
            vmem((hidden_size, width), BF),
            vmem((tokens, width), BF),
            vmem((tokens, width), BF),
            vmem((tokens, hidden_size), BF),
        ]
        + SequenceSums.scratch(sections, seqs, rows, part, True)
        + SequenceSums.scratch(sections, seqs, rows, part, False)
        + RowScatter.scratch(group, ring, *r_grads.shape[1:]),
        name,
        limit=60 * 2**20,
        far=(5, 6, 7),
    )


def dense_leave(lines, ident, arrays, shards, shape, name):
    seqs, rows, width = shape
    sections, group, ring = (lines.sizes[k] for k in ("section", "z", "core"))
    part = width // sections
    half = rows // 2
    lanes = 2 * HDIM
    block = ring * rows
    many = len(shards)
    tokens = seqs * rows

    def kernel(
        heads,
        value_ref,
        q_ref,
        kv_ref,
        start_ref,
        turned_ref,
        lse_ref,
        qkv_w,
        middle,
        gains_ref,
        mid_vectors_ref,
        *refs,
    ):
        s_refs, refs = refs[:many], refs[many:]
        (grads_ref, stream_ref, vectors_ref), refs = refs[:3], refs[3:]
        so_refs, refs = refs[:many], refs[many:]
        (
            send,
            recv,
            sems,
            kv,
            normed,
            dqkv,
            heads_got,
            acc,
            pairs,
            pairs_got,
            queries,
            queries_got,
            sums,
            sums_got,
            *buffers,
        ) = refs
        loads = Loads(sems)
        kv_loads = {0: loads.start(kv_ref.at[:, :, 0], kv)}
        copies = Copies(lines, send, recv)
        section, zplace, place = (lines.place(k) for k in ("section", "z", "core"))
        own = span(section, part)
        copies.greet(["section", "z", "core"])
        inner = SequenceSums(copies, buffers)
        arriving, around, along, back = {}, {}, {}, {}
        for q in range(seqs):
            heads_got[zplace, q] = heads[zplace, q]
            arriving[q] = copies.swap("z", lambda peer: heads.at[peer, q], lambda me: heads_got.at[me, q])
        gathers = [SquareGather(copies, x, o) for x, o in zip(s_refs, so_refs)]
        for gather in gathers:
            gather.start()

        def attend(q):
            wait(arriving[q])
            kv_loads[q].wait()
            pieces = []
            for g in range(group):
                pair = kv[:, g].reshape(block, lanes)
                pieces.append((pair, pair.T, g * block))
            for g in reversed(range(group)):
                query = unpack_low(q_ref[g, q]) * jnp.asarray(SCALE, BF)
                packed = heads_got[g, q]
                flat = packed.T
                qpos = g * block + place * rows + lax.broadcasted_iota(jnp.int32, (1, rows), 1)
                grad_query, grads = backward_block(
                    query,
                    unpack_high(packed),
                    side_by_side([flat[:HDIM], flat[HDIM:]]),
                    turned_ref[q, g],
                    lse_ref[q, g],
                    pieces[: g + 1],
                    qpos,
                    start_ref[q, g],
                    [i == g for i in range(g + 1)],
                )
                queries[g, q] = pack_turned(grad_query).astype(BF)
                for i, item in enumerate(grads):
                    if g == group - 1:
                        acc[i] = item
                    else:
                        acc[i] += item
            if q > 0:
                wait(around[q - 1])
            for g in range(group):
                for r in range(ring):
                    pairs[r, g] = acc[g, r * rows : (r + 1) * rows].astype(BF)
            if q + 1 < seqs:
                kv_loads[q + 1] = loads.start(kv_ref.at[:, :, q + 1], kv)
            queries_got[zplace, q] = queries[zplace, q]
            around[q] = copies.swap("core", lambda peer: pairs.at[peer], lambda me: pairs_got.at[me, :, q])
            along[q] = copies.swap("z", lambda peer: queries.at[peer, q], lambda me: queries_got.at[me, q])

        def to_tokens(q):
            wait(around[q])
            around[q] = []
            for g in range(group):
                item = pairs[place, g].astype(F32)
                for peer in lines.peers("core"):
                    item = item + pairs_got[peer, g, q].astype(F32)
                sums[g, q] = item.astype(BF)
            sums_got[zplace, q] = sums[zplace, q]
            back[q] = copies.swap("z", lambda peer: sums.at[peer, q], lambda me: sums_got.at[me, q])

        def enter(q):
            wait(back[q] + along[q])
            at = pl.ds(q * rows, rows)
            packed = [queries_got[g, q] for g in range(group)]
            upright = [jnp.concatenate([p[:, :HDIM], p[:, HDIM:]], axis=0) for p in packed]
            grad = side_by_side([sums_got[g, q] for g in range(group)] + upright)
            dqkv[at] = grad
            grad_normed = contract(grad, qkv_w[...], 1, 1)
            value = value_ref[at].astype(F32)
            inner.start(q, grad_normed, jnp.sum(grad_normed * value * gains_ref[0:1], axis=1, keepdims=True))

        def leave(q):
            at = pl.ds(q * rows, rows)
            grad_normed, scalars = inner.finish(q)
            inv = inverse_rms(value_ref[at].astype(F32))
            value = value_ref[at, own].astype(F32)
            vectors_ref[0:1] += jnp.sum(grad_normed * value * inv, axis=0, keepdims=True)
            grad = (
                inv * (grad_normed * gains_ref[0:1, own])
                - value * (inv * inv * inv) * (scalars * (1.0 / width))
                + middle[at]
            )
            stream_ref[at] = grad.astype(BF)

        vectors_ref[...] = mid_vectors_ref[...]
        last = seqs - 1
        for q in range(seqs):
            attend(q)
            to_tokens(q)
            if q == 0:
                for gather in gathers:
                    gather.forward()
        for q in range(seqs):
            at = pl.ds(q * rows, rows)
            value = value_ref[at].astype(F32)
            normed[at] = (value * inverse_rms(value) * gains_ref[0:1]).astype(BF)
        for q in range(seqs):
            enter(q)
            if q > 0:
                inner.forward(q - 1)
            if q > 1:
                leave(q - 2)
        inner.forward(last)
        outer_product(normed, dqkv, grads_ref, 0)
        Copies.flush(grads_ref)
        for q in range(max(0, last - 1), seqs):
            leave(q)
        for gather in gathers:
            gather.finish()

    z, c = group - 1, ring - 1
    vmem = pltpu.VMEM
    result = communicate(
        kernel,
        ident,
        arrays + shards,
        [
            ((width, 3 * part), BF),
            ((tokens, part), BF),
            ((8, part), F32),
        ]
        + [((x.shape[0], sections * x.shape[1]), x.dtype) for x in shards],
        semaphores(
            seqs * (3 * z + c)
            + SequenceSums.count(sections, seqs, True)
            + sum(SquareGather.count(x.shape[0]) for x in shards)
        )
        + [
            pltpu.SemaphoreType.DMA((seqs + 1,)),
            vmem((ring, group, rows, lanes), BF),
            vmem((tokens, width), BF),
            vmem((tokens, 3 * part), BF),
            vmem((group, seqs, half, lanes), BF),
            vmem((group, block, lanes), F32),
            vmem((ring, group, rows, lanes), BF),
            vmem((ring, group, seqs, rows, lanes), BF),
            vmem((group, seqs, half, lanes), BF),
            vmem((group, seqs, half, lanes), BF),
            vmem((group, seqs, rows, lanes), BF),
            vmem((group, seqs, rows, lanes), BF),
        ]
        + SequenceSums.scratch(sections, seqs, rows, part, True),
        name,
        limit=60 * 2**20,
        far=(3,),
    )
    return result[0], result[1], result[2], result[3:]


def inverse_rms(value):
    return lax.rsqrt(jnp.mean(value * value, axis=-1, keepdims=True) + EPS)


def gelu_terms(value):
    scale = 0.7978845608028654
    square = value * value
    bend = jnp.tanh(scale * (value + 0.044715 * square * value))
    half = 0.5 * (1.0 + bend)
    slope = half + 0.5 * value * (1.0 - bend * bend) * scale * (1.0 + 0.134145 * square)
    return value * half, slope


def side_by_side(blocks):
    return jnp.concatenate(blocks, axis=1)


class ColumnSum:
    @staticmethod
    def count(sections, scalars):
        return (sections - 1) * (2 if scalars else 1)

    @staticmethod
    def scratch(sections, rows, width, scalars):
        buffers = [pltpu.VMEM((rows, sections * width), BF), pltpu.VMEM((sections, rows, width), BF)]
        if scalars:
            wide = rows + -rows % 128
            buffers += [pltpu.VMEM((8, wide), F32), pltpu.VMEM((sections, 8, wide), F32)]
        return buffers

    def __init__(self, copies, buffers):
        self.copies, self.buffers = copies, buffers

    def start(self, value, scalars=None):
        buf, got = self.buffers[:2]
        width = got.shape[2]
        section = self.copies.lines.place("section")
        buf[...] = value.astype(BF)
        self.pending = self.copies.swap(
            "section", lambda peer: buf.at[:, span(peer, width)], lambda me: got.at[me]
        )
        got[section] = buf[:, span(section, width)]
        if scalars is not None:
            sbuf, sgot = self.buffers[2:]
            sbuf[...] = jnp.zeros_like(sbuf)
            sbuf[:, : scalars.shape[0]] = column_to_rows(scalars)
            self.pending += self.copies.swap("section", lambda peer: sbuf, lambda me: sgot.at[me])
            sgot[section] = sbuf[...]

    def finish(self):
        wait(self.pending)
        total = sum_places(self.buffers[1])
        if len(self.buffers) == 2:
            return total
        rows = total.shape[0]
        return total, row_to_column(sum_places(self.buffers[3])[:1, :rows])


class Swaps:
    def __init__(self, copies):
        self.copies, self.lines = copies, copies.lines

    def ring(self, buf, got):
        return self.copies.swap("core", lambda peer: buf.at[peer], lambda me: got.at[me])

    def ring_sum(self, buf, got):
        total = buf[self.lines.place("core")].astype(F32)
        for peer in self.lines.peers("core"):
            total = total + got[peer].astype(F32)
        return total.astype(BF)

    def z(self, buf, got):
        place = self.lines.place("z")
        pending = self.copies.swap("z", lambda peer: buf.at[peer], lambda me: got.at[me])
        got[place] = buf[place]
        return pending

    def share(self, kind, all_ref):
        me = self.lines.place(kind)
        return self.copies.swap(kind, lambda peer: all_ref.at[me], lambda _: all_ref.at[me])


def together(all_ref):
    return side_by_side([all_ref[i] for i in range(all_ref.shape[0])])


def halves(value):
    rows = value.shape[0] // 2
    return side_by_side([value[:rows], value[rows:]])


def upright(packed):
    return jnp.concatenate([packed[:, :HDIM], packed[:, HDIM:]], axis=0)


def slots_of(lines, sel):
    group, ring = lines.sizes["z"], lines.sizes["core"]
    index = lax.broadcasted_iota(jnp.int32, (1, group * sel), 1)
    return (index // sel) * (ring * sel) + lines.place("core") * sel + lax.rem(index, sel)


def slot_sequence(lines, queries_ref, pairs_ref, q, sel):
    group, ring = lines.sizes["z"], lines.sizes["core"]
    at = slice(q * sel, (q + 1) * sel)
    query = jnp.concatenate([queries_ref[g, at] for g in range(group)], axis=0)
    pair = jnp.concatenate([pairs_ref[r, g, at] for g in range(group) for r in range(ring)], axis=0)
    return query * jnp.asarray(SCALE, BF), pair


def dense_feed(lines, ident, arrays, shape, name):
    seqs, sel, rows, width, part, hidden_size = shape
    sections, group, ring = (lines.sizes[k] for k in ("section", "z", "core"))
    dp = group * ring
    slots = seqs * sel
    lanes = 2 * HDIM
    queries = group * sel

    def kernel(
        value_ref,
        mixed_ref,
        gains_ref,
        rest_ref,
        top_ref,
        chosen_ref,
        ids_ref,
        first_ref,
        attended_ref,
        slope_ref,
        hidden_ref,
        out_ref,
        picked_ref,
        grad_ref,
        normed_ref,
        queries_ref,
        pairs_all,
        start_ref,
        turned_ref,
        lse_ref,
        r_mixed_ref,
        weights_all,
        send,
        recv,
        sems,
        out_w,
        expand_w,
        shrink_w,
        top,
        own_buf,
        wide,
        got,
        turn,
        last,
        value_core,
        value_core_got,
        value_z,
        value_z_got,
        value_all,
        grad_core,
        grad_core_got,
        grad_z,
        grad_z_got,
        grad_all,
        heads_buf,
        heads_got,
        o_buf,
        o_got,
        mixed_all,
    ):
        loads = Loads(sems)
        section, place = lines.place("section"), lines.place("core")
        rank = lax.axis_index("dp")
        own = span(section, part)
        out_load = loads.start(rest_ref.at[:, :part], out_w)
        top_load = loads.start(top_ref.at[:, :, own], top)
        expand_load = loads.start(rest_ref.at[:, part : part + hidden_size], expand_w)
        shrink_load = loads.start(rest_ref.at[:, part + hidden_size :], shrink_w)
        copies = Copies(lines, send, recv)
        swaps = Swaps(copies)
        copies.greet(["section", "z", "core"])
        weights_along = copies.swap("z", lambda peer: first_ref, lambda _: weights_all.at[rank])
        weights_handed = copies.swap("core", lambda peer: first_ref, lambda _: weights_all.at[rank])
        weights_all[rank] = first_ref[...]
        out_load.wait()
        gathers, scatters = {}, {}
        position = rank * rows + lax.broadcasted_iota(jnp.int32, (1, rows), 1).astype(F32)

        def table(q):
            chosen = row_to_column(chosen_ref[q : q + 1].astype(F32))
            return (chosen == position).astype(F32).astype(BF)

        def pick(q, source, buf):
            found = matmul(table(q), source).astype(BF)
            for d in range(dp):
                buf[d % ring, d // ring, q * sel : (q + 1) * sel] = found[d * sel : (d + 1) * sel]

        def project(q):
            own_buf[q] = matmul(mixed_ref[q], out_w[...]).astype(BF)
            gathers[q] = SquareGather(copies, own_buf.at[q], attended_ref.at[q], 1)
            gathers[q].start()

        def feed(q):
            gathers[q].finish()
            middle = value_ref[q].astype(F32) + attended_ref[q].astype(F32)
            normed = (middle * inverse_rms(middle) * gains_ref[1:2]).astype(BF)
            hidden, slope = gelu_terms(matmul(normed, expand_w[...]))
            hidden = hidden.astype(BF)
            hidden_ref[q] = hidden
            slope_ref[q] = slope.astype(BF)
            wide[q] = matmul(hidden, shrink_w[...]).astype(BF)
            scatters[q] = SquareScatter(copies, wide.at[q], got.at[q], turn.at[q], last.at[q], 1)
            scatters[q].start()

        def leave(q):
            scatters[q].finish(out_ref.at[q])
            after = out_ref[q] + value_ref[q, :, own].astype(F32) + attended_ref[q, :, own].astype(F32)
            out_ref[q] = after
            pick(q, after.astype(BF), value_core)

        for q in range(seqs):
            project(q)
            if q > 0:
                gathers[q - 1].forward()
        gathers[seqs - 1].forward()
        top_load.wait()
        for q in range(seqs):
            pick(q, top[q], grad_core)
        grad_pending = swaps.ring(grad_core, grad_core_got)
        expand_load.wait()
        shrink_load.wait()
        for q in range(seqs):
            feed(q)
            if q == 0:
                wait(grad_pending)
                grad_z[...] = swaps.ring_sum(grad_core, grad_core_got)
                grad_pending = swaps.z(grad_z, grad_z_got)
            else:
                scatters[q - 1].forward()
            if q > 1:
                leave(q - 2)
        Copies.flush(hidden_ref)
        Copies.flush(slope_ref)
        Copies.flush(attended_ref)
        scatters[seqs - 1].forward()
        for q in range(max(0, seqs - 2), seqs):
            leave(q)
        Copies.flush(out_ref)

        pending = swaps.ring(value_core, value_core_got)
        wait(grad_pending)
        grad_all[section] = sum_places(grad_z_got).astype(BF)
        wait(pending)
        value_z[...] = swaps.ring_sum(value_core, value_core_got)
        pending = swaps.z(value_z, value_z_got)
        grad_pending = swaps.share("section", grad_all)

        def slot_starts(q):
            firsts = document_starts(ids_ref[q : q + 1])
            chosen = chosen_ref[q : q + 1].astype(F32)
            documents = sum((chosen >= firsts[c]).astype(F32) for c in range(1, DOCS))
            column = jnp.broadcast_to(row_to_column(chosen), (dp * sel, queries))
            slot = lax.broadcasted_iota(jnp.int32, column.shape, 0)
            mine = jnp.sum(jnp.where(slot == slots_of(lines, sel), column, 0.0), axis=0, keepdims=True)
            mine = sum((mine >= firsts[c]).astype(F32) for c in range(1, DOCS))
            return start_of(mine, document_starts(documents))

        for q in range(seqs):
            start_ref[q] = slot_starts(q)
        for step in range(group - 1, 0, -1):
            weights_along[group - 1 - step].wait_recv()
            source = lax.rem(lines.place("z") + step, group) * ring + place
            weights_handed += copies.swap(
                "core", lambda peer: weights_all.at[source], lambda _: weights_all.at[source]
            )
        wait(pending)
        value_all[section] = sum_places(value_z_got).astype(BF)
        pending = swaps.share("section", value_all)
        wait(grad_pending)
        grad_ref[...] = together(grad_all)
        wait(pending)
        low = together(value_all)
        picked_ref[...] = low
        picked = low.astype(F32)
        normed = (picked * inverse_rms(picked) * gains_ref[2:3]).astype(BF)
        normed_ref[...] = normed
        for copy in weights_along:
            copy.wait_send()
        wait(weights_handed)
        qkv = matmul(normed, weights_all[...].reshape(width, 3 * part)).astype(BF)
        for g in range(group):
            heads_buf[g, :slots] = qkv[:, g * lanes : (g + 1) * lanes]
            heads_buf[g, slots:] = halves(qkv[:, 2 * part + g * HDIM : 2 * part + (g + 1) * HDIM])
        wait(swaps.z(heads_buf, heads_got))
        pairs_all[place] = heads_got[:, :slots]
        pending = swaps.share("core", pairs_all)
        blank = jnp.zeros((slots, HDIM), BF)
        for g in range(group):
            queries_ref[g] = side_by_side([upright(heads_got[g, slots:]), blank])
        wait(pending)
        turned_all = []
        for q in range(seqs):
            query, pair = slot_sequence(lines, queries_ref, pairs_all, q, sel)
            turned, lse = forward_block(
                query, [(pair, pair.T, 0)], slots_of(lines, sel), start_ref[q], [True]
            )
            turned_ref[q] = turned.astype(BF)
            lse_ref[q] = lse
            turned_all.append(jnp.concatenate([turned, jnp.zeros_like(turned)], axis=0).T.astype(BF)[:, :HDIM])
        for g in range(group):
            o_buf[g] = halves(jnp.concatenate([t[g * sel : (g + 1) * sel] for t in turned_all], axis=0))
        wait(swaps.z(o_buf, o_got))
        mixed_all[section] = side_by_side([upright(o_got[g]) for g in range(group)])
        wait(swaps.share("section", mixed_all))
        r_mixed_ref[...] = together(mixed_all)

    vmem = pltpu.VMEM
    z, s, c = group - 1, sections - 1, ring - 1
    short = ((group, slots, part), BF)
    across = ((sections, slots, part), BF)
    packed = ((group, slots // 2, lanes), BF)
    heads = ((group, slots + slots // 2, lanes), BF)
    row = ((slots, width), BF)
    scratch = [
        ((width, part), BF),
        ((width, hidden_size), BF),
        ((hidden_size, width), BF),
        ((seqs, rows, part), BF),
        ((seqs, rows, part), BF),
        ((seqs, rows, width), BF),
        ((seqs, 2, rows, part), BF),
        ((seqs, rows, part), BF),
        ((seqs, rows, part), BF),
        ((ring,) + short[0], BF),
        ((ring,) + short[0], BF),
        short,
        short,
        across,
        ((ring,) + short[0], BF),
        ((ring,) + short[0], BF),
        short,
        short,
        across,
        heads,
        heads,
        packed,
        packed,
        across,
    ]
    return communicate(
        kernel,
        ident,
        arrays,
        [
            ((seqs, rows, width), BF),
            ((seqs, rows, hidden_size), BF),
            ((seqs, rows, hidden_size), BF),
            ((seqs, rows, part), F32),
            row,
            row,
            row,
            ((group, slots, lanes), BF),
            ((ring, group, slots, lanes), BF),
            ((seqs, 1, queries), jnp.int32),
            ((seqs, HDIM, queries), BF),
            ((seqs, 1, queries), F32),
            row,
            ((dp,) + arrays[-1].shape, BF),
        ],
        semaphores(seqs * 12 + 3 * c + 4 * z + 3 * s + z + group * c)
        + [pltpu.SemaphoreType.DMA((4,))]
        + [vmem(a, b) for a, b in scratch],
        name,
        limit=60 * 2**20,
        far=(3, 4),
    )


def routed_feed(lines, ident, arrays, shape, name):
    slots, width, part, hidden_size = shape
    sections = lines.sizes["section"]

    def kernel(
        value_ref,
        grad_ref,
        mixed_ref,
        gains_ref,
        rest_ref,
        grads_ref,
        middle_ref,
        attended_ref,
        sent_ref,
        logit_ref,
        vectors_ref,
        send,
        recv,
        sems,
        out_w,
        expand_w,
        shrink_w,
        keep,
        mid_keep,
        dpre_keep,
        hidden_keep,
        fed_keep,
        attended_all,
        *buffers,
    ):
        loads = Loads(sems)
        out_load = loads.start(rest_ref.at[:, :part], out_w)
        shrink_load = loads.start(rest_ref.at[:, part + hidden_size :], shrink_w)
        expand_load = loads.start(rest_ref.at[:, part : part + hidden_size], expand_w)
        copies = Copies(lines, send, recv)
        swaps = Swaps(copies)
        section = lines.place("section")
        own = span(section, part)
        copies.greet(["section"])
        back, forth = ColumnSum(copies, buffers[:4]), ColumnSum(copies, buffers[4:])
        gain, router = gains_ref[3:4, :], gains_ref[4:5, :]
        out_load.wait()
        attended_own = matmul(mixed_ref[...], out_w[...]).astype(BF)
        attended_all[section] = attended_own
        pending = swaps.share("section", attended_all)
        picked = value_ref[...].astype(F32)
        grad_sent = grad_ref[...].astype(F32)
        gate = jax.nn.sigmoid(jnp.sum(picked * router, axis=1, keepdims=True))
        grad_delta = gate * grad_sent
        fed_low = grad_delta.astype(BF)
        fed_keep[...] = fed_low
        shrink_load.wait()
        grad_hidden = contract(fed_low, shrink_w[...], 1, 1)
        expand_load.wait()
        wait(pending)
        middle = picked + together(attended_all).astype(F32)
        inv = inverse_rms(middle)
        normed = (middle * inv * gain).astype(BF)
        hidden, slope = gelu_terms(matmul(normed, expand_w[...]))
        hidden = hidden.astype(BF)
        grad_pre = (grad_hidden * slope).astype(BF)
        grad_normed = contract(grad_pre, expand_w[...], 1, 1)
        back.start(grad_normed, jnp.sum(grad_normed * middle * gain, axis=1, keepdims=True))
        mid_keep[...] = normed
        hidden_keep[...] = hidden
        dpre_keep[...] = grad_pre
        fed_part = matmul(hidden, shrink_w[...])
        keep[0] = middle
        keep[1] = grad_delta
        keep[2] = grad_sent
        own_attended = attended_own.astype(F32)
        gate_part = jnp.sum(grad_sent * fed_part, axis=1, keepdims=True) + jnp.sum(
            keep[2, :, own] * own_attended, axis=1, keepdims=True
        )
        forth.start(fed_part, gate_part)
        outer_product(mid_keep, dpre_keep, grads_ref, 0)
        grad_normed, scalar = back.finish()
        middle_own = keep[0, :, own]
        vectors_ref[...] = jnp.zeros_like(vectors_ref)
        vectors_ref[3:4] = jnp.sum(grad_normed * middle_own * inv, axis=0, keepdims=True)
        grad_middle = inv * (grad_normed * gains_ref[3:4, own]) - middle_own * (inv * inv * inv) * (
            scalar * (1.0 / width)
        )
        middle_ref[...] = grad_middle
        attended_ref[...] = (grad_middle + keep[1, :, own]).astype(BF)
        outer_product(hidden_keep, fed_keep, grads_ref, hidden_size)
        Copies.flush(grads_ref)
        fed, grad_gate = forth.finish()
        sent_ref[...] = (gate * (own_attended + fed)).astype(BF)
        grad_logit = grad_gate * gate * (1.0 - gate)
        logit_ref[...] = jnp.broadcast_to(grad_logit, logit_ref.shape)
        vectors_ref[4:5] = jnp.sum(grad_logit * value_ref[:, own].astype(F32), axis=0, keepdims=True)

    vmem = pltpu.VMEM
    return communicate(
        kernel,
        ident,
        arrays,
        [
            ((width, hidden_size + width), BF),
            ((slots, part), F32),
            ((slots, part), BF),
            ((slots, part), BF),
            ((slots, 128), F32),
            ((8, part), F32),
        ],
        semaphores(sections - 1 + 2 * ColumnSum.count(sections, True))
        + [
            pltpu.SemaphoreType.DMA((3,)),
            vmem((width, part), BF),
            vmem((width, hidden_size), BF),
            vmem((hidden_size, width), BF),
            vmem((3, slots, width), F32),
            vmem((slots, width), BF),
            vmem((slots, hidden_size), BF),
            vmem((slots, hidden_size), BF),
            vmem((slots, width), BF),
            vmem((sections, slots, part), BF),
        ]
        + 2 * ColumnSum.scratch(sections, slots, part, True),
        name,
        limit=60 * 2**20,
        far=(4,),
    )


def routed_leave(lines, ident, arrays, shape, name):
    seqs, sel, rows, width, part = shape
    sections, group, ring = (lines.sizes[k] for k in ("section", "z", "core"))
    slots = seqs * sel
    lanes = 2 * HDIM

    def kernel(
        attended_ref,
        rest_ref,
        qkv_w,
        queries_ref,
        pairs_ref,
        start_ref,
        turned_ref,
        lse_ref,
        value_ref,
        normed_ref,
        mixed_ref,
        middle_ref,
        logit_ref,
        sent_ref,
        feed_vectors_ref,
        gains_ref,
        chosen_ref,
        top_ref,
        fed_out,
        own_out,
        added_ref,
        grads_ref,
        vectors_ref,
        send,
        recv,
        sems,
        out_w,
        grad_buf,
        grad_got,
        grad_high,
        turn_buf,
        turn_got,
        back_buf,
        back_got,
        dqkv_keep,
        sent_got,
        sent_all,
        final_buf,
        final_got,
        final_all,
        *buffers,
    ):
        loads = Loads(sems)
        out_load = loads.start(rest_ref.at[:, :part], out_w)
        copies = Copies(lines, send, recv)
        swaps = Swaps(copies)
        section, zplace, place = (lines.place(k) for k in ("section", "z", "core"))
        rank = lax.axis_index("dp")
        own = span(section, part)
        copies.greet(["section", "z", "core"])
        outer, inner = ColumnSum(copies, buffers[:2]), ColumnSum(copies, buffers[2:])
        out_load.wait()
        outer.start(contract(attended_ref[...], out_w[...], 1, 1))
        sent_pending = copies.swap("z", lambda peer: sent_ref, lambda me: sent_got.at[me])
        sent_got[zplace] = sent_ref[...]
        outer_product(mixed_ref, attended_ref, grads_ref, 3 * part)
        slot_of = rank * rows + lax.broadcasted_iota(jnp.int32, (rows, 1), 0)
        tables = [(chosen_ref[q : q + 1] == slot_of).astype(F32).astype(BF) for q in range(seqs)]
        blank = jnp.zeros((slots, HDIM), BF)
        grad_mixed = outer.finish().astype(BF)
        for g in range(group):
            grad_buf[g] = halves(grad_mixed[:, g * HDIM : (g + 1) * HDIM])
        pending = swaps.z(grad_buf, grad_got)
        wait(sent_pending)
        sent_all[place] = sent_got[...]
        sent_pending = swaps.share("core", sent_all)
        wait(pending)
        for g in range(group):
            grad_high[g] = side_by_side([blank, upright(grad_got[g])])
        query_grads = []
        for q in range(seqs):
            at = slice(q * sel, (q + 1) * sel)
            query, pair = slot_sequence(lines, queries_ref, pairs_ref, q, sel)
            grad = jnp.concatenate([grad_high[g, at] for g in range(group)], axis=0)
            grad_query, grad_pairs = backward_block(
                query,
                grad,
                grad.T[HDIM:],
                turned_ref[q],
                lse_ref[q],
                [(pair, pair.T, 0)],
                slots_of(lines, sel),
                start_ref[q],
                [True],
            )
            turned = jnp.concatenate([grad_query, jnp.zeros_like(grad_query)], axis=0).T.astype(BF)
            query_grads.append(turned[:, :HDIM])
            low = grad_pairs[0].astype(BF)
            for g in range(group):
                for r in range(ring):
                    first = (g * ring + r) * sel
                    turn_buf[r, g, at] = low[first : first + sel]
        pending = swaps.ring(turn_buf, turn_got)
        for g in range(group):
            back_buf[g, slots:] = halves(
                jnp.concatenate([t[g * sel : (g + 1) * sel] for t in query_grads], axis=0)
            )
        wait(pending)
        back_buf[:, :slots] = swaps.ring_sum(turn_buf, turn_got)
        pending = swaps.z(back_buf, back_got)
        wait(sent_pending)

        def at_positions(q, all_ref):
            at = slice(q * sel, (q + 1) * sel)
            found = jnp.concatenate([all_ref[r, g, at] for g in range(group) for r in range(ring)], axis=0)
            return matmul(tables[q], found)

        for q in range(seqs):
            added_ref[q] = at_positions(q, sent_all).astype(BF)
        wait(pending)
        dqkv_keep[...] = side_by_side(
            [back_got[g, :slots] for g in range(group)] + [upright(back_got[g, slots:]) for g in range(group)]
        )
        grad_normed = contract(dqkv_keep[...], qkv_w[...], 1, 1)
        picked = value_ref[...].astype(F32)
        inv = inverse_rms(picked)
        inner.start(grad_normed, jnp.sum(grad_normed * picked * gains_ref[2:3], axis=1, keepdims=True))
        outer_product(normed_ref, dqkv_keep, grads_ref, 0)
        picked = value_ref[:, own].astype(F32)
        grad_normed, scalar = inner.finish()
        vectors_ref[...] = feed_vectors_ref[...]
        vectors_ref[2:3] = jnp.sum(grad_normed * picked * inv, axis=0, keepdims=True)
        grad_in = inv * (grad_normed * gains_ref[2:3, own]) - picked * (inv * inv * inv) * (scalar * (1.0 / width))
        final_buf[...] = (middle_ref[...] + grad_in + logit_ref[:, :1] * gains_ref[4:5, own]).astype(BF)

        along = copies.swap("z", lambda peer: final_buf, lambda me: final_got.at[me])
        final_got[zplace] = final_buf[...]

        def hand_on(i):
            dst = final_all.at[place, i, :, own]
            dst[...] = final_got[i]
            return copies.swap("section", lambda peer: final_got.at[i], lambda me: dst)

        spread = hand_on(zplace)
        Copies.flush(grads_ref)
        for step in range(group - 1, 0, -1):
            along[group - 1 - step].wait_recv()
            spread += hand_on(lax.rem(zplace + step, group))
        for copy in along:
            copy.wait_send()
        wait(spread)
        wait(swaps.share("core", final_all))
        for q in range(seqs):
            fed_out[q] = (top_ref[q].astype(F32) + at_positions(q, final_all)).astype(BF)
            returned = jnp.concatenate(
                [final_all[r, g, q * sel : (q + 1) * sel, own] for g in range(group) for r in range(ring)], axis=0
            )
            own_out[q] = top_ref[q, :, own].astype(F32) + matmul(tables[q], returned)

    vmem = pltpu.VMEM
    z, s, c = group - 1, sections - 1, ring - 1
    lane_block = ((group, slots, lanes), BF)
    packed = ((group, slots // 2, lanes), BF)
    heads = ((group, slots + slots // 2, lanes), BF)
    ring_block = ((ring, group, slots, lanes), BF)
    short = ((group, slots, part), BF)
    scratch = [
        ((width, part), BF),
        packed,
        packed,
        lane_block,
        ring_block,
        ring_block,
        heads,
        heads,
        ((slots, 3 * part), BF),
        short,
        ((ring,) + short[0], BF),
        ((slots, part), BF),
        short,
        ((ring, group, slots, width), BF),
    ]
    return communicate(
        kernel,
        ident,
        arrays,
        [
            ((seqs, rows, width), BF),
            ((seqs, rows, part), F32),
            ((seqs, rows, part), BF),
            ((width, 4 * part), BF),
            ((8, part), F32),
        ],
        semaphores(
            3 * c
            + 4 * z
            + ColumnSum.count(sections, True)
            + ColumnSum.count(sections, False)
            + group * s
        )
        + [pltpu.SemaphoreType.DMA((1,))]
        + [vmem(a, b) for a, b in scratch]
        + ColumnSum.scratch(sections, slots, part, False)
        + ColumnSum.scratch(sections, slots, part, True),
        name,
        limit=60 * 2**20,
        far=(1,),
    )


def cut_weights(arrays, sections, dp, group, name):
    local, width = arrays[0].shape
    part = width // sections
    inner = arrays[4].shape[1] // dp
    share = inner // sections
    hidden_size = dp * share
    layers = len(arrays) // 6

    def kernel(*refs):
        ins, outs = refs[: 6 * layers], refs[6 * layers : 8 * layers]
        k_buf, v_buf, sems = refs[8 * layers :]
        section = lax.axis_index("section")
        own = span(section, part)
        moves = []
        for i in range(layers):
            q_ref, k_ref, v_ref, o_ref, e_ref, s_ref = ins[6 * i : 6 * i + 6]
            first_ref, rest_ref = outs[2 * i : 2 * i + 2]
            rows = pl.ds(pl.multiple_of(section * share, share), share)
            moves += [
                (k_ref.at[:, own], k_buf.at[i]),
                (v_ref.at[:, own], v_buf.at[i]),
                (q_ref.at[:, own], first_ref.at[:, 2 * part :]),
                (o_ref.at[:, own], rest_ref.at[:, :part]),
                (s_ref.at[rows], rest_ref.at[:, part + hidden_size :]),
            ]
            for d in range(dp):
                at = pl.ds(pl.multiple_of(d * inner + section * share, 128), share)
                moves.append((e_ref.at[:, at], rest_ref.at[:, part + d * share : part + (d + 1) * share]))
        copies = [pltpu.make_async_copy(src, dst, sems.at[i]) for i, (src, dst) in enumerate(moves)]
        for copy in copies:
            copy.start()
        for copy in copies:
            copy.wait()
        for i in range(layers):
            for g in range(group):
                at = slice(g * HDIM, (g + 1) * HDIM)
                pair = side_by_side([k_buf[i, :, at], v_buf[i, :, at]])
                outs[2 * i][:, 2 * g * HDIM : 2 * (g + 1) * HDIM] = pair

    anywhere, vmem = pl.BlockSpec(memory_space=pl.ANY), pl.BlockSpec(memory_space=pltpu.VMEM)
    shapes = [
        jax.ShapeDtypeStruct((local, 3 * part), BF),
        jax.ShapeDtypeStruct((local, part + hidden_size + width), BF),
    ]
    return pl.pallas_call(
        kernel,
        in_specs=[anywhere] * 6 * layers,
        out_specs=[vmem] * 2 * layers,
        out_shape=shapes * layers,
        scratch_shapes=[
            pltpu.VMEM((layers, local, part), BF),
            pltpu.VMEM((layers, local, part), BF),
            pltpu.SemaphoreType.DMA((layers * (5 + dp),)),
        ],
        compiler_params=pltpu.CompilerParams(vmem_limit_bytes=60 * 2**20),
        name=name,
    )(*arrays)


def on_device(
    stream_in,
    segment_ids,
    chosen_rows,
    cotangent,
    dense_prenorm,
    dense_query,
    dense_keys,
    dense_values,
    dense_output,
    dense_midnorm,
    dense_expand,
    dense_shrink,
    routed_prenorm,
    routed_query,
    routed_keys,
    routed_values,
    routed_output,
    routed_midnorm,
    routed_expand,
    routed_shrink,
    router_weight,
):
    sections, dp = lax.axis_size("section"), lax.axis_size("dp")
    section, rank = lax.axis_index("section"), lax.axis_index("dp")
    seqs, rows, width = stream_in.shape
    tokens = seqs * rows
    part = width // sections
    group = HEADS // sections
    ring = dp // group
    total_sel = chosen_rows.shape[1]
    sel = total_sel // dp
    lines = Lines(sections, dp, group)

    def own_columns(value):
        return lax.dynamic_slice_in_dim(value, section * part, part, value.ndim - 1)

    def own_hidden(expand, shrink):
        inner = expand.shape[1] // dp
        share = inner // sections
        cut = expand.reshape(expand.shape[0], dp, sections, share)
        cut = lax.dynamic_index_in_dim(cut, section, 2, keepdims=False).reshape(expand.shape[0], dp * share)
        return cut, lax.dynamic_slice_in_dim(shrink, section * share, share, 0)

    def own_attention(query, keys, values):
        local = query.shape[0]
        pair = jnp.stack(
            [own_columns(keys).reshape(local, group, HDIM), own_columns(values).reshape(local, group, HDIM)],
            axis=2,
        ).reshape(local, 2 * part)
        return jnp.concatenate([pair, own_columns(query)], axis=1)

    def cut(*layers):
        if dense_expand.shape[1] // (dp * sections) % 128 == 0:
            return cut_weights([w for layer in layers for w in layer], sections, dp, group, "cut")
        out = []
        for query, keys, values, output, expand, shrink in layers:
            expand_cut, shrink_cut = own_hidden(expand, shrink)
            rest = jnp.concatenate([own_columns(output), expand_cut, shrink_cut], axis=1)
            out += [own_attention(query, keys, values), rest]
        return out

    def gather(value):
        return lax.all_gather(value, "dp", axis=0, tiled=True)

    def after(value, other):
        return lax.optimization_barrier((value, other))[0]

    hidden_size = dense_expand.shape[1] // sections
    gains = jnp.stack([dense_prenorm, dense_midnorm, routed_prenorm, routed_midnorm, router_weight])
    gains = jnp.pad(gains, ((0, 16 - gains.shape[0]), (0, 0)))
    dense_first, dense_rest, routed_first, routed_rest = cut(
        (dense_query, dense_keys, dense_values, dense_output, dense_expand, dense_shrink),
        (routed_query, routed_keys, routed_values, routed_output, routed_expand, routed_shrink),
    )
    rest = gather(dense_rest)
    routed_rest = gather(routed_rest)

    shape = (seqs, sel, rows, width, part)
    grad_top = cotangent.reshape(tokens, width)
    dense_qkv, gains, queries, pairs, start, mixed_turned, lse, mixed = dense_enter(
        lines,
        1,
        [stream_in.reshape(tokens, width), dense_first, gains, segment_ids],
        (seqs, rows, width),
        "dense_enter",
    )
    dense_qkv = dense_qkv.reshape(width, 3 * part)
    (
        attended,
        slope,
        hidden,
        after_dense,
        r_value,
        r_grad,
        r_normed,
        r_queries,
        r_pairs,
        r_start,
        r_turned,
        r_lse,
        r_mixed,
        routed_qkv,
    ) = dense_feed(
        lines,
        2,
        [stream_in, mixed, gains, rest, cotangent, chosen_rows, segment_ids, routed_first],
        shape + (hidden_size,),
        "dense_feed",
    )
    routed_qkv = routed_qkv.reshape(width, 3 * part)
    after_dense = after_dense.reshape(tokens, part)
    attended, slope, hidden, mixed = (x.reshape(tokens, -1) for x in (attended, slope, hidden, mixed))

    def reduce_dp(value):
        return lax.psum_scatter(value, "dp", scatter_dimension=0, tiled=True)

    routed_grads, r_middle, r_grad_attended, r_sent, r_logit, r_vectors = routed_feed(
        lines,
        4,
        [r_value, r_grad, r_mixed, gains, routed_rest],
        (seqs * sel, width, part, hidden_size),
        "routed_feed",
    )
    routed_shard = reduce_dp(routed_grads)
    fed_low, grad_own, added, routed_grads, r_vectors = routed_leave(
        lines,
        5,
        [
            r_grad_attended,
            routed_rest,
            routed_qkv,
            r_queries,
            r_pairs,
            r_start,
            r_turned,
            r_lse,
            r_value,
            r_normed,
            r_mixed,
            r_middle,
            r_logit,
            r_sent,
            r_vectors,
            gains,
            chosen_rows,
            cotangent,
        ],
        shape,
        "routed_leave",
    )
    dense_grads, grad_middle, grad_heads, d_vectors, routed_shard_in = dense_return(
        lines,
        6,
        [
            fed_low.reshape(tokens, width),
            grad_own.reshape(tokens, part),
            stream_in.reshape(tokens, width),
            attended,
            slope,
            hidden,
            mixed,
            rest,
            gains,
            r_vectors,
            routed_grads,
        ],
        (seqs, rows, width, hidden_size),
        "dense_return",
    )
    dense_shard = reduce_dp(after(dense_grads, routed_shard))
    dense_grads, stream_grad, d_vectors, (routed_all, routed_all_in) = dense_leave(
        lines,
        7,
        [
            grad_heads,
            stream_in.reshape(tokens, width),
            queries,
            pairs,
            start,
            mixed_turned,
            lse,
            dense_qkv,
            grad_middle,
            gains,
            d_vectors,
        ],
        [routed_shard, routed_shard_in],
        (seqs, rows, width),
        "dense_leave",
    )
    added = after(added, d_vectors).reshape(tokens, part)
    stream_out = (after_dense + added.astype(F32)).astype(BF).reshape(seqs, rows, part)
    stream_grad = stream_grad.reshape(seqs, rows, part)
    vectors, (dense_pairs, dense_queries), (dense_all,) = dense_finish(
        lines, 8, d_vectors, dense_grads, [dense_shard], (2 * part, part), "dense_finish"
    )

    share = hidden_size // dp
    local = width // dp
    r_exp, r_shr, r_keys, r_values, r_query, r_out = assemble(
        [
            ("hidden", routed_all, 0, hidden_size),
            ("stack", routed_all, hidden_size, width),
            ("pair", routed_all_in, 0, 2 * part),
            ("columns", routed_all_in, 2 * part, part),
            ("columns", routed_all_in, 3 * part, part),
        ],
        share,
        "routed_places",
    )
    d_exp, d_shr, d_keys, d_values, d_query, d_out = assemble(
        [
            ("hidden", dense_all, 0, hidden_size),
            ("stack", dense_all, hidden_size, width),
            ("pair", dense_pairs, 0, 2 * part),
            ("columns", dense_queries, 0, part),
            ("columns", dense_all, hidden_size + width, part),
        ],
        share,
        "dense_places",
    )
    vectors = lax.dynamic_slice_in_dim(vectors, rank * local, local, 1)
    d_shr = d_shr.reshape(sections * share, width)
    r_shr = r_shr.reshape(sections * share, width)
    return (
        (stream_out, stream_grad)
        + (vectors[0], d_query, d_keys, d_values, d_out, vectors[1], d_exp, d_shr)
        + (vectors[2], r_query, r_keys, r_values, r_out, vectors[3], r_exp, r_shr)
        + (vectors[4],)
    )


def solution(mesh):
    streams, row, vector, copied = P(None, "dp", None), P("dp", None), P("dp"), P()
    layer = (vector, row, row, row, row, vector, row, row)
    outs = (P(None, "dp", "section"),) * 2 + layer + layer + (vector,)
    return jax.shard_map(
        on_device,
        mesh=mesh,
        in_specs=(streams, copied, copied, streams) + layer + layer + (vector,),
        out_specs=outs,
        check_vma=False,
    )
```

```python
import functools

import jax
import jax.numpy as jnp
from jax import lax
from jax.experimental import pallas as pl
from jax.experimental.pallas import tpu as pltpu
from jax.sharding import PartitionSpec as P

HEADS = 16
HDIM = 64
DOCS = 8
EPS = 1e-06
NEG = -1e30
SCALE = HDIM ** (-0.5)
VMEM = 32 * 2**20
MESH = pl.DeviceIdType.MESH
BF = jnp.bfloat16
F32 = jnp.float32


def matmul(left, right):
    return jnp.dot(left, right, preferred_element_type=F32)


def contract(left, right, ldim, rdim):
    return lax.dot_general(left, right, (((ldim,), (rdim,)), ((), ())), preferred_element_type=F32)


class Lines:
    def __init__(self, sections, dp, group):
        self.sizes = {"section": sections, "z": group, "core": dp // group}
        self.ring = dp // group

    def place(self, kind):
        if kind == "section":
            return lax.axis_index("section")
        index = lax.axis_index("dp")
        return index // self.ring if kind == "z" else lax.rem(index, self.ring)

    def device(self, kind, place):
        if kind == "section":
            return {"section": place}
        index = lax.axis_index("dp")
        if kind == "z":
            return {"dp": place * self.ring + lax.rem(index, self.ring)}
        return {"dp": (index // self.ring) * self.ring + place}

    def peers(self, kind):
        size = self.sizes[kind]
        me = self.place(kind)
        return [lax.rem(me + step, size) for step in range(1, size)]


class Copies:
    loads, flush = (), None

    def __init__(self, lines, send, recv):
        self.lines, self.send, self.recv, self.used = lines, send, recv, 0

    def greet(self, kinds):
        barrier = pltpu.get_barrier_semaphore()
        count = 0
        for kind in kinds:
            for peer in self.lines.peers(kind):
                pl.semaphore_signal(
                    barrier, inc=1, device_id=self.lines.device(kind, peer), device_id_type=MESH
                )
                count += 1
        for load in Copies.loads:
            load.wait()
        pl.semaphore_wait(barrier, count)

    def start(self, kind, peer, src, dst):
        assert self.used < self.send.shape[0]
        copy = pltpu.make_async_remote_copy(
            src_ref=src,
            dst_ref=dst,
            send_sem=self.send.at[self.used],
            recv_sem=self.recv.at[self.used],
            device_id=self.lines.device(kind, peer),
            device_id_type=MESH,
        )
        self.used += 1
        copy.start()
        return copy

    def swap(self, kind, src, dst):
        me = self.lines.place(kind)
        return [self.start(kind, peer, src(peer), dst(me)) for peer in self.lines.peers(kind)]


def wait(copies):
    for copy in copies:
        copy.wait()


def semaphores(count):
    return [pltpu.SemaphoreType.DMA((count,)), pltpu.SemaphoreType.DMA((count,))]


def communicate(kernel, ident, arrays, shapes, scratch, name, limit=60 * 2**20, far=()):
    place = pl.BlockSpec(memory_space=pl.ANY)
    near = [i for i in range(len(arrays)) if i not in far]
    many, outs = len(arrays), len(shapes)

    def body(*refs):
        ins, results, refs = list(refs[:many]), refs[many : many + outs], refs[many + outs :]
        inner, refs = refs[: len(scratch)], refs[len(scratch) :]
        in_bufs, out_bufs, (in_sems, out_sems) = refs[: len(near)], refs[len(near) : len(near) + outs], refs[-2:]
        loads = []
        for k, i in enumerate(near):
            loads.append(pltpu.make_async_copy(ins[i], in_bufs[k], in_sems.at[k]))
            loads[-1].start()
            ins[i] = in_bufs[k]
        stores = [pltpu.make_async_copy(out_bufs[k], results[k], out_sems.at[k]) for k in range(outs)]
        started = set()

        def flush(ref):
            k = next(k for k in range(outs) if out_bufs[k] is ref)
            stores[k].start()
            started.add(k)

        Copies.loads, Copies.flush = loads, staticmethod(flush)
        kernel(*ins, *out_bufs, *inner)
        for k in range(outs):
            if k not in started:
                stores[k].start()
        for store in stores:
            store.wait()

    return pl.pallas_call(
        body,
        out_shape=[jax.ShapeDtypeStruct(s, d) for s, d in shapes],
        in_specs=[place] * many,
        out_specs=[place] * outs,
        scratch_shapes=list(scratch)
        + [pltpu.VMEM(arrays[i].shape, arrays[i].dtype) for i in near]
        + [pltpu.VMEM(s, d) for s, d in shapes]
        + [pltpu.SemaphoreType.DMA((max(1, len(near)),)), pltpu.SemaphoreType.DMA((outs,))],
        compiler_params=pltpu.CompilerParams(
            collective_id=ident, has_side_effects=True, vmem_limit_bytes=limit
        ),
        name=name,
    )(*arrays)


def span(place, width):
    return pl.ds(pl.multiple_of(place * width, width), width)


def square(lines):
    me = lines.place("section")
    low, high = lax.rem(me, 2), me // 2
    return high * 2 + 1 - low, (1 - high) * 2 + low, (1 - high) * 2 + 1 - low


def pieces_of(rows):
    half = rows // 2
    return (2, half // 2) if half % 32 == 0 else (1, half)


class SquareGather:
    @staticmethod
    def count(rows):
        return 6 * pieces_of(rows)[0]

    def __init__(self, copies, x_ref, o_ref, pieces=None):
        self.copies, self.x_ref, self.o_ref = copies, x_ref, o_ref
        self.width = x_ref.shape[1]
        self.me = copies.lines.place("section")
        near, far, _ = square(copies.lines)
        half = x_ref.shape[0] // 2
        pieces, step = pieces_of(x_ref.shape[0]) if pieces is None else (pieces, half // pieces)
        self.parts = [
            (pl.ds(h * half + j * step, step), one, two)
            for j in range(pieces)
            for h, (one, two) in enumerate(((near, far), (far, near)))
        ]

    def send(self, at, to):
        dst = self.o_ref.at[at, span(self.me, self.width)]
        return self.copies.start("section", to, self.x_ref.at[at], dst)

    def start(self):
        self.first = [self.send(at, one) for at, one, _ in self.parts]
        self.rest = [self.send(at, two) for at, _, two in self.parts]
        self.o_ref[:, span(self.me, self.width)] = self.x_ref[...]

    def forward(self):
        for (at, one, two), copy in zip(self.parts, self.first):
            copy.wait_recv()
            place = self.o_ref.at[at, span(one, self.width)]
            self.rest.append(self.copies.start("section", two, place, place))

    def finish(self):
        for copy in self.first:
            copy.wait_send()
        wait(self.rest)


class SquareScatter:
    @staticmethod
    def count(rows):
        return 6 * pieces_of(rows)[0]

    @staticmethod
    def scratch(rows, width):
        return [pltpu.VMEM((2, rows, width), BF), pltpu.VMEM((rows, width), BF), pltpu.VMEM((rows, width), BF)]

    def __init__(self, copies, x_ref, got, turn, last, pieces=None):
        self.copies, self.x_ref, self.got, self.turn, self.last = copies, x_ref, got, turn, last
        self.width = turn.shape[1]
        self.me = copies.lines.place("section")
        near, far, self.across = square(copies.lines)
        half = x_ref.shape[0] // 2
        pieces, step = pieces_of(x_ref.shape[0]) if pieces is None else (pieces, half // pieces)
        self.parts = [
            (pl.ds(h * half + j * step, step), one, two)
            for j in range(pieces)
            for h, (one, two) in enumerate(((near, far), (far, near)))
        ]

    def read(self, at, place):
        return self.x_ref[at, span(place, self.width)].astype(F32)

    def start(self):
        self.passed, self.kept = [], []
        for at, one, _ in self.parts:
            for place, k, out in ((self.across, 0, self.passed), (one, 1, self.kept)):
                src = self.x_ref.at[at, span(place, self.width)]
                out.append(self.copies.start("section", one, src, self.got.at[k, at]))

    def forward(self):
        self.second = []
        for (at, _, two), copy in zip(self.parts, self.passed):
            copy.wait_recv()
            self.turn[at] = (self.read(at, two) + self.got[0, at].astype(F32)).astype(BF)
            self.second.append(self.copies.start("section", two, self.turn.at[at], self.last.at[at]))

    def finish(self, o_ref):
        for i, (at, _, _) in enumerate(self.parts):
            self.kept[i].wait_recv()
            self.second[i].wait_recv()
            o_ref[at] = self.read(at, self.me) + self.got[1, at].astype(F32) + self.last[at].astype(F32)
        for copy in self.passed + self.kept + self.second:
            copy.wait_send()


def gather_columns(lines, ident, part, name):
    rows, width = part.shape

    def kernel(x_ref, o_ref, send, recv):
        copies = Copies(lines, send, recv)
        copies.greet(["section"])
        gather = SquareGather(copies, x_ref, o_ref)
        gather.start()
        gather.forward()
        gather.finish()

    shape = ((rows, lines.sizes["section"] * width), part.dtype)
    (out,) = communicate(kernel, ident, [part], [shape], semaphores(SquareGather.count(rows)), name)
    return out


def scalar_block(scalars):
    count = -(-scalars.shape[0] // 128)
    count += -count % 8
    return jnp.pad(scalars, (0, count * 128 - scalars.shape[0])).reshape(count, 128)


def sum_places(ref):
    total = ref[0].astype(F32)
    for i in range(1, ref.shape[0]):
        total = total + ref[i].astype(F32)
    return total


def scatter_columns(lines, ident, part, scalars, name):
    rows, full = part.shape
    sections = lines.sizes["section"]
    width = full // sections
    extra = scalars is not None
    arrays = [part]
    shapes = [((rows, width), F32)]
    scratch = semaphores(SquareScatter.count(rows) + sections - 1) + SquareScatter.scratch(rows, width)
    if extra:
        arrays.append(scalar_block(scalars))
        shapes.append((arrays[1].shape, F32))
        scratch.append(pltpu.VMEM((sections,) + arrays[1].shape, F32))

    def kernel(*refs):
        x_ref, refs = refs[0], refs[1:]
        if extra:
            e_ref, o_ref, eo_ref, send, recv, got, turn, last, e_got = refs
        else:
            o_ref, send, recv, got, turn, last = refs
        copies = Copies(lines, send, recv)
        copies.greet(["section"])
        scatter = SquareScatter(copies, x_ref, got, turn, last)
        scatter.start()
        if extra:
            others = copies.swap("section", lambda peer: e_ref, lambda place: e_got.at[place])
            e_got[lines.place("section")] = e_ref[...]
        scatter.forward()
        scatter.finish(o_ref)
        if extra:
            wait(others)
            eo_ref[...] = sum_places(e_got)

    got = communicate(kernel, ident, arrays, shapes, scratch, name)
    if not extra:
        return got[0]
    return got[0], got[1].reshape(-1)[:rows]


class RowScatter:
    @staticmethod
    def count(group, ring):
        return group * (ring - 1) + group - 1

    @staticmethod
    def scratch(group, ring, local, wide):
        vmem = pltpu.VMEM
        return [vmem((ring, group, local, wide), BF), vmem((group, local, wide), BF), vmem((group, local, wide), BF)]

    def __init__(self, copies, w_ref, buffers):
        self.copies, self.w_ref = copies, w_ref
        self.got, self.turn, self.all = buffers
        lines = copies.lines
        self.zplace, self.ring = lines.place("z"), lines.sizes["core"]
        self.order = lines.peers("z") + [self.zplace]

    def start(self):
        self.around = [
            self.copies.swap(
                "core", lambda peer: self.w_ref.at[g * self.ring + peer], lambda me: self.got.at[me, g]
            )
            for g in self.order
        ]

    def forward(self):
        lines = self.copies.lines
        place = lines.place("core")
        self.along = []
        for i, (g, arrived) in enumerate(zip(self.order, self.around)):
            for copy in arrived:
                copy.wait_recv()
            total = self.w_ref[g * self.ring + place].astype(F32)
            for peer in lines.peers("core"):
                total = total + self.got[peer, g].astype(F32)
            self.turn[g] = total.astype(BF)
            if i < len(self.order) - 1:
                self.along.append(self.copies.start("z", g, self.turn.at[g], self.all.at[self.zplace]))
        self.all[self.zplace] = self.turn[self.zplace]

    def finish(self, out_ref):
        wait(self.along)
        out_ref[...] = sum_places(self.all).astype(BF)
        for arrived in self.around:
            for copy in arrived:
                copy.wait_send()


def dense_finish(lines, ident, vectors, weight, shards, cuts, name):
    group, ring, sections = (lines.sizes[k] for k in ("z", "core", "section"))
    dp = group * ring
    many = len(shards)
    local = weight.shape[0] // dp
    wide = weight.shape[1]
    weight = weight.reshape(dp, local, wide)
    width = vectors.shape[1]
    bounds = [sum(cuts[:i]) for i in range(len(cuts) + 1)]
    parts = [pl.ds(bounds[i], cuts[i]) for i in range(len(cuts))]
    count = len(cuts)

    def kernel(x_ref, w_ref, *refs):
        s_refs, refs = refs[:many], refs[many:]
        v_ref, refs = refs[0], refs[1:]
        wo_refs, refs = refs[:count], refs[count:]
        so_refs, refs = refs[:many], refs[many:]
        send, recv, w_got, w_turn, w_all, v_z, v_core, v_all, *w_own = refs
        copies = Copies(lines, send, recv)
        zplace, place, section = (lines.place(k) for k in ("z", "core", "section"))
        copies.greet(["z", "core", "section"])
        order = lines.peers("z") + [zplace]
        gathers = [SquareGather(copies, x, o) for x, o in zip(s_refs, so_refs)]
        for gather in gathers:
            gather.start()
        around = {}
        for h, at in enumerate(parts):
            for i, g in enumerate(order):
                around[h, i] = copies.swap(
                    "core", lambda peer: w_ref.at[g * ring + peer, :, at], lambda me: w_got.at[me, g, :, at]
                )
        along = {h: [] for h in range(count)}
        for h, at in enumerate(parts):
            for i, g in enumerate(order):
                for copy in around[h, i]:
                    copy.wait_recv()
                total = w_ref[g * ring + place, :, at].astype(F32)
                for peer in lines.peers("core"):
                    total = total + w_got[peer, g, :, at].astype(F32)
                w_turn[g, :, at] = total.astype(BF)
                if i < len(order) - 1:
                    along[h].append(copies.start("z", g, w_turn.at[g, :, at], w_all.at[zplace, :, at]))
        pending = copies.swap("z", lambda peer: x_ref, lambda me: v_z.at[me])
        v_z[zplace] = x_ref[...]
        w_all[zplace] = w_turn[zplace]
        for gather in gathers:
            gather.forward()
        for h, at in enumerate(parts):
            wait(along[h])
            total = w_all[0, :, at].astype(F32)
            for i in range(1, group):
                total = total + w_all[i, :, at].astype(F32)
            w_own[h][...] = total.astype(BF)
            gathers.append(SquareGather(copies, w_own[h], wo_refs[h], 1))
            gathers[-1].start()
            if h > 0:
                gathers[-2].forward()
        wait(pending)
        v_core[place] = sum_places(v_z)
        wait(copies.swap("core", lambda peer: v_core.at[place], lambda me: v_core.at[me]))
        v_all[section] = sum_places(v_core)
        pending = copies.swap("section", lambda peer: v_all.at[section], lambda me: v_all.at[me])
        gathers[-1].forward()
        wait(pending)
        for i in range(sections):
            v_ref[:, i * width : (i + 1) * width] = v_all[i]
        for arrived in around.values():
            for copy in arrived:
                copy.wait_send()
        for gather in gathers:
            gather.finish()

    z, c, s = group - 1, ring - 1, sections - 1
    result = communicate(
        kernel,
        ident,
        [vectors, weight] + shards,
        [((8, sections * width), F32)]
        + [((local, sections * cut), BF) for cut in cuts]
        + [((x.shape[0], sections * x.shape[1]), x.dtype) for x in shards],
        semaphores(
            count * (group * c + z + 6)
            + sum(SquareGather.count(x.shape[0]) for x in shards)
            + z
            + c
            + s
        )
        + [
            pltpu.VMEM((ring, group, local, wide), BF),
            pltpu.VMEM((group, local, wide), BF),
            pltpu.VMEM((group, local, wide), BF),
            pltpu.VMEM((group, 8, width), F32),
            pltpu.VMEM((ring, 8, width), F32),
            pltpu.VMEM((sections, 8, width), F32),
        ]
        + [pltpu.VMEM((local, cut), BF) for cut in cuts],
        name,
        limit=60 * 2**20,
    )
    return result[0], result[1 : 1 + count], result[1 + count :]


def assemble(pieces, share, name):
    arrays = []
    for _, array, _, _ in pieces:
        if not any(array is other for other in arrays):
            arrays.append(array)
    where = [next(i for i, other in enumerate(arrays) if other is array) for _, array, _, _ in pieces]
    local = arrays[0].shape[0]
    steps = local // 32 if local % 32 == 0 else 1
    rows = local // steps
    sections = lax.axis_size("section")
    shapes, specs = [], []
    for kind, _, _, width in pieces:
        many = 2 if kind == "pair" else 1
        for _ in range(many):
            if kind == "stack":
                shapes.append(jax.ShapeDtypeStruct((sections, local, width), F32))
                specs.append(pl.BlockSpec((sections, rows, width), lambda i: (0, i, 0)))
            else:
                total = width if kind == "sum" else sections * width // many
                shapes.append(jax.ShapeDtypeStruct((local, total), F32))
                specs.append(pl.BlockSpec((rows, total), lambda i: (i, 0)))

    def kernel(*refs):
        ins, outs = refs[: len(arrays)], list(refs[len(arrays) :])
        for (kind, array, first, width), i in zip(pieces, where):
            wide = array.shape[1] // sections
            blocks = [ins[i][:, s * wide + first : s * wide + first + width].astype(F32) for s in range(sections)]
            out = outs.pop(0)
            if kind == "columns":
                for s, item in enumerate(blocks):
                    out[:, s * width : (s + 1) * width] = item
            elif kind == "stack":
                for s, item in enumerate(blocks):
                    out[s] = item
            elif kind == "sum":
                total = blocks[0]
                for item in blocks[1:]:
                    total = total + item
                out[...] = total
            elif kind == "hidden":
                for d in range(width // share):
                    out[:, d * share * sections : (d + 1) * share * sections] = jnp.concatenate(
                        [item[:, d * share : (d + 1) * share] for item in blocks], axis=1
                    )
            else:
                other = outs.pop(0)
                half = width // 2
                for s, item in enumerate(blocks):
                    for side, dst in ((0, out), (1, other)):
                        heads = [
                            item[:, (2 * g + side) * HDIM : (2 * g + side + 1) * HDIM]
                            for g in range(width // (2 * HDIM))
                        ]
                        dst[:, s * half : (s + 1) * half] = jnp.concatenate(heads, axis=1)

    return pl.pallas_call(
        kernel,
        grid=(steps,),
        in_specs=[pl.BlockSpec((rows, a.shape[1]), lambda i: (i, 0)) for a in arrays],
        out_specs=specs,
        out_shape=shapes,
        compiler_params=pltpu.CompilerParams(vmem_limit_bytes=60 * 2**20),
        name=name,
    )(*arrays)


def column_to_rows(column):
    return jnp.broadcast_to(column, (column.shape[0], 128)).T[:8]


def row_to_column(row):
    return jnp.broadcast_to(row, (128, row.shape[1])).T[:, :1]


def outer_product(left_ref, right_ref, out_ref, first):
    step = 256
    wide = right_ref.shape[1]

    @pl.loop(0, left_ref.shape[1] // step)
    def _(i):
        at = span(i, step)
        block = contract(left_ref[:, at], right_ref[...], 0, 0)
        out_ref[at, first : first + wide] = block.astype(BF)


def unpack_low(packed):
    lane = lax.broadcasted_iota(jnp.int32, packed.shape, 1)
    zero = jnp.zeros_like(packed)
    low = jnp.where(lane < HDIM, packed, zero)
    turned = jnp.concatenate([packed[:, HDIM:], packed[:, :HDIM]], axis=1)
    high = jnp.where(lane < HDIM, turned, zero)
    return jnp.concatenate([low, high], axis=0)


def unpack_high(packed):
    lane = lax.broadcasted_iota(jnp.int32, packed.shape, 1)
    zero = jnp.zeros_like(packed)
    turned = jnp.concatenate([packed[:, HDIM:], packed[:, :HDIM]], axis=1)
    low = jnp.where(lane >= HDIM, turned, zero)
    high = jnp.where(lane >= HDIM, packed, zero)
    return jnp.concatenate([low, high], axis=0)


def pack_turned(turned):
    half = turned.shape[1] // 2
    return jnp.concatenate([turned[:, :half], turned[:, half:]], axis=0).T


def forward_block(query, pieces, qpos, start, causal):
    scores = []
    peak = None
    for index, (pair, _, first) in enumerate(pieces):
        item = contract(pair, query, 1, 1)
        kpos = first + lax.broadcasted_iota(jnp.int32, item.shape, 0)
        allowed = kpos >= start
        if causal[index]:
            allowed = allowed & (kpos <= qpos)
        item = jnp.where(allowed, item, NEG)
        top = jnp.max(item, axis=0, keepdims=True)
        peak = top if peak is None else jnp.maximum(peak, top)
        scores.append(item)
    total = jnp.zeros_like(peak)
    mixed = None
    for item, (_, turned, _) in zip(scores, pieces):
        weight = jnp.exp(item - peak)
        total = total + jnp.sum(weight, axis=0, keepdims=True)
        part = matmul(turned[HDIM:], weight.astype(BF))
        mixed = part if mixed is None else mixed + part
    return mixed / total, peak + jnp.log(total)


def backward_block(query, grad, grad_turned, mixed_turned, lse, pieces, qpos, start, causal):
    row_sum = jnp.sum(grad_turned.astype(F32) * mixed_turned.astype(F32), axis=0, keepdims=True)
    grad_query = None
    grads = []
    for index, (pair, turned, first) in enumerate(pieces):
        scores = contract(pair, query, 1, 1)
        kpos = first + lax.broadcasted_iota(jnp.int32, scores.shape, 0)
        allowed = kpos >= start
        if causal[index]:
            allowed = allowed & (kpos <= qpos)
        probs = jnp.where(allowed, jnp.exp(scores - lse), 0.0)
        grad_probs = contract(pair, grad, 1, 1)
        grad_scores = (probs * (grad_probs - row_sum)).astype(BF)
        grads.append(matmul(grad_scores, query) + matmul(probs.astype(BF), grad))
        part = matmul(turned[:HDIM], grad_scores)
        grad_query = part if grad_query is None else grad_query + part
    return grad_query * SCALE, grads


def document_starts(ids):
    return [
        jnp.sum((ids < c).astype(F32), axis=1, keepdims=True) if c else jnp.zeros((1, 1), F32) for c in range(DOCS)
    ]


def start_of(documents, firsts):
    start = jnp.zeros(documents.shape, F32)
    for c in range(1, DOCS):
        start = jnp.where(documents >= c, firsts[c], start)
    return start.astype(jnp.int32)


def dense_enter(lines, ident, arrays, shape, name):
    seqs, rows, width = shape
    sections, group, ring = (lines.sizes[k] for k in ("section", "z", "core"))
    dp = group * ring
    part = width // sections
    half = rows // 2
    lanes = 2 * HDIM
    block = ring * rows
    local = width // dp

    def kernel(
        value_ref,
        weights_ref,
        cut_ref,
        ids_ref,
        weights_all,
        gains_ref,
        q_got,
        kv_all,
        start_ref,
        turned_ref,
        lse_ref,
        mixed_ref,
        send,
        recv,
        cut_all,
        kv_buf,
        q_buf,
        o_buf,
        o_got,
        o_own,
    ):
        copies = Copies(lines, send, recv)
        zplace, place = lines.place("z"), lines.place("core")
        rank = lax.axis_index("dp")
        copies.greet(["section", "z", "core"])
        pairs = [(weights_ref, weights_all), (cut_ref, cut_all)]
        along, handed = [], []
        for x_ref, o_ref in pairs:
            along.append(copies.swap("z", lambda peer: x_ref, lambda _: o_ref.at[rank]))
        for x_ref, o_ref in pairs:
            handed += copies.swap("core", lambda peer: x_ref, lambda _: o_ref.at[rank])
            o_ref[rank] = x_ref[...]
        for q in range(seqs):
            firsts = document_starts(ids_ref[q : q + 1])
            for g in range(group):
                at = pl.ds(pl.multiple_of((g * ring + place) * rows, rows), rows)
                start_ref[q, g] = start_of(ids_ref[q : q + 1, at], firsts)
        for step in range(group - 1, 0, -1):
            source = lax.rem(zplace + step, group) * ring + place
            for arrived, (_, o_ref) in zip(along, pairs):
                arrived[group - 1 - step].wait_recv()
                handed += copies.swap("core", lambda peer: o_ref.at[source], lambda _: o_ref.at[source])
        for arrived in along:
            for copy in arrived:
                copy.wait_send()
        wait(handed)
        for d in range(dp):
            gains_ref[:, d * local : (d + 1) * local] = cut_all[d].astype(F32)

        arriving, queries, around, outward, gathers = {}, {}, {}, {}, {}

        def project(q):
            value = value_ref[pl.ds(q * rows, rows)].astype(F32)
            normed = (value * inverse_rms(value) * gains_ref[0:1]).astype(BF)
            qkv = matmul(normed, weights_all[...].reshape(width, 3 * part)).astype(BF)
            for g in range(group):
                kv_buf[g, q] = qkv[:, g * lanes : (g + 1) * lanes]
                at = slice(2 * part + g * HDIM, 2 * part + (g + 1) * HDIM)
                q_buf[g, q] = side_by_side([qkv[:half, at], qkv[half:, at]])
            arriving[q] = copies.swap("z", lambda peer: kv_buf.at[peer, q], lambda me: kv_all.at[place, me, q])
            queries[q] = copies.swap("z", lambda peer: q_buf.at[peer, q], lambda me: q_got.at[me, q])
            q_got[zplace, q] = q_buf[zplace, q]
            kv_all[place, zplace, q] = kv_buf[zplace, q]
            own = kv_all.at[place, zplace, q]
            around[q] = copies.swap("core", lambda peer: own, lambda _: own)

        def hand(q):
            for step in range(group - 1, 0, -1):
                arriving[q][group - 1 - step].wait_recv()
                item = kv_all.at[place, lax.rem(zplace + step, group), q]
                around[q] += copies.swap("core", lambda peer: item, lambda _: item)

        def attend(q):
            for copy in arriving[q]:
                copy.wait_send()
            wait(queries[q])
            wait(around[q])
            pieces = []
            for g in range(group):
                pair = kv_all[:, g, q].reshape(block, lanes)
                pieces.append((pair, pair.T, g * block))
            for g in range(group):
                query = unpack_low(q_got[g, q]) * jnp.asarray(SCALE, BF)
                qpos = g * block + place * rows + lax.broadcasted_iota(jnp.int32, (1, rows), 1)
                mixed, lse = forward_block(
                    query, pieces[: g + 1], qpos, start_ref[q, g], [i == g for i in range(g + 1)]
                )
                turned_ref[q, g] = mixed.astype(BF)
                lse_ref[q, g] = lse
                o_buf[g, q] = pack_turned(mixed).astype(BF)
            outward[q] = copies.swap("z", lambda peer: o_buf.at[peer, q], lambda me: o_got.at[me, q])
            o_got[zplace, q] = o_buf[zplace, q]

        def merge(q):
            wait(outward[q])
            packed = [o_got[g, q] for g in range(group)]
            o_own[q] = side_by_side([jnp.concatenate([p[:, :HDIM], p[:, HDIM:]], axis=0) for p in packed])
            gathers[q] = SquareGather(copies, o_own.at[q], mixed_ref.at[q], 1)
            gathers[q].start()

        for q in range(seqs):
            project(q)
        for q in range(seqs):
            hand(q)
            attend(q)
            if q > 0:
                merge(q - 1)
            if q > 1:
                gathers[q - 2].forward()
        merge(seqs - 1)
        for q in range(max(0, seqs - 2), seqs):
            gathers[q].forward()
        for q in range(seqs):
            gathers[q].finish()

    z, c = group - 1, ring - 1
    vmem = pltpu.VMEM
    packed = ((group, seqs, half, lanes), BF)
    return communicate(
        kernel,
        ident,
        arrays,
        [
            ((dp, local, 3 * part), BF),
            ((16, width), F32),
            packed,
            ((ring, group, seqs, rows, lanes), BF),
            ((seqs, group, 1, rows), jnp.int32),
            ((seqs, group, HDIM, rows), BF),
            ((seqs, group, 1, rows), F32),
            ((seqs, rows, width), BF),
        ],
        semaphores(2 * (z + group * c) + seqs * (3 * z + group * c + 6))
        + [
            vmem((dp, 16, local), BF),
            vmem((group, seqs, rows, lanes), BF),
            vmem(*packed),
            vmem(*packed),
            vmem(*packed),
            vmem((seqs, rows, part), BF),
        ],
        name,
        limit=60 * 2**20,
    )


class SequenceSums:
    @staticmethod
    def count(sections, seqs, scalars):
        return seqs * (6 + (sections - 1 if scalars else 0))

    @staticmethod
    def scratch(sections, seqs, rows, part, scalars):
        vmem = pltpu.VMEM
        buffers = [
            vmem((seqs, rows, sections * part), BF),
            vmem((seqs, 2, rows, part), BF),
            vmem((seqs, rows, part), BF),
            vmem((seqs, rows, part), BF),
            vmem((rows, part), F32),
        ]
        if scalars:
            buffers += [vmem((seqs, 8, rows), F32), vmem((seqs, sections, 8, rows), F32)]
        return buffers

    def __init__(self, copies, buffers):
        self.copies, self.buffers, self.items = copies, buffers, {}

    def start(self, q, value, scalars=None):
        wide, got, turn, last = self.buffers[:4]
        wide[q] = value.astype(BF)
        item = SquareScatter(self.copies, wide.at[q], got.at[q], turn.at[q], last.at[q], 1)
        item.start()
        others = []
        if scalars is not None:
            buf, arrived = self.buffers[5:]
            section = self.copies.lines.place("section")
            buf[q] = column_to_rows(scalars)
            others = self.copies.swap("section", lambda peer: buf.at[q], lambda me: arrived.at[q, me])
            arrived[q, section] = buf[q]
        self.items[q] = (item, others)

    def forward(self, q):
        self.items[q][0].forward()

    def finish(self, q):
        item, others = self.items[q]
        total = self.buffers[4]
        item.finish(total)
        if not others:
            return total[...]
        wait(others)
        return total[...], row_to_column(sum_places(self.buffers[6].at[q])[:1])


class Loads:
    def __init__(self, sems):
        self.sems, self.used = sems, 0

    def start(self, src, dst):
        copy = pltpu.make_async_copy(src, dst, self.sems.at[self.used])
        self.used += 1
        copy.start()
        return copy


def dense_return(lines, ident, arrays, shape, name):
    seqs, rows, width, hidden_size = shape
    sections, group, ring = (lines.sizes[k] for k in ("section", "z", "core"))
    part = width // sections
    half = rows // 2

    def kernel(
        fed_ref,
        own_ref,
        value_ref,
        attended_ref,
        slope_ref,
        hidden_ref,
        mixed_ref,
        rest_ref,
        gains_ref,
        r_vectors_ref,
        r_grads_ref,
        grads_ref,
        middle,
        heads,
        vectors_ref,
        r_shard_ref,
        send,
        recv,
        sems,
        dattended,
        out_w,
        expand_w,
        shrink_w,
        late,
        normed,
        dpre,
        *buffers,
    ):
        loads = Loads(sems)
        shrink_load = loads.start(rest_ref.at[:, part + hidden_size :], shrink_w)
        expand_load = loads.start(rest_ref.at[:, part : part + hidden_size], expand_w)
        out_load = loads.start(rest_ref.at[:, :part], out_w)
        hidden_load = loads.start(hidden_ref, late)
        copies = Copies(lines, send, recv)
        own = span(lines.place("section"), part)
        copies.greet(["section", "z", "core"])
        mids = SequenceSums(copies, buffers[:7])
        outs = SequenceSums(copies, buffers[7:-3])
        r_sum = RowScatter(copies, r_grads_ref, buffers[-3:])
        r_sum.start()

        def middle_of(at):
            return value_ref[at].astype(F32) + attended_ref[at].astype(F32)

        def feed(q):
            at = pl.ds(q * rows, rows)
            grad_hidden = contract(fed_ref[at], shrink_w[...], 1, 1)
            grad_pre = (grad_hidden * slope_ref[at].astype(F32)).astype(BF)
            dpre[at] = grad_pre
            grad_normed = contract(grad_pre, expand_w[...], 1, 1)
            mid = middle_of(at)
            mids.start(q, grad_normed, jnp.sum(grad_normed * mid * gains_ref[1:2], axis=1, keepdims=True))
            normed[at] = (mid * inverse_rms(mid) * gains_ref[1:2]).astype(BF)

        def project(q):
            at = pl.ds(q * rows, rows)
            grad_normed, scalars = mids.finish(q)
            inv = inverse_rms(middle_of(at))
            mid = value_ref[at, own].astype(F32) + attended_ref[at, own].astype(F32)
            vectors_ref[1:2] += jnp.sum(grad_normed * mid * inv, axis=0, keepdims=True)
            grad = (
                inv * (grad_normed * gains_ref[1:2, own])
                - mid * (inv * inv * inv) * (scalars * (1.0 / width))
                + own_ref[at]
            )
            middle[at] = grad
            low = grad.astype(BF)
            dattended[at] = low
            outs.start(q, contract(low, out_w[...], 1, 1))

        def leave(q):
            grad = outs.finish(q).astype(BF)
            for g in range(group):
                columns = slice(g * HDIM, (g + 1) * HDIM)
                heads[g, q] = side_by_side([grad[:half, columns], grad[half:, columns]])

        vectors_ref[...] = r_vectors_ref[...]
        vectors_ref[0:2] = jnp.zeros((2, part), F32)
        shrink_load.wait()
        expand_load.wait()
        out_load.wait()
        last = seqs - 1
        for q in range(seqs):
            feed(q)
            if q == 0:
                r_sum.forward()
            if q > 0:
                mids.forward(q - 1)
            if q > 1:
                project(q - 2)
        mids.forward(last)
        hidden_load.wait()
        outer_product(late, fed_ref, grads_ref, hidden_size)
        mixed_load = loads.start(mixed_ref, late)
        for q in range(max(0, last - 1), seqs):
            project(q)
            outs.forward(q - 1)
        outer_product(normed, dpre, grads_ref, 0)
        outs.forward(last)
        mixed_load.wait()
        outer_product(late, dattended, grads_ref, hidden_size + width)
        Copies.flush(grads_ref)
        for q in range(seqs):
            leave(q)
        r_sum.finish(r_shard_ref)

    tokens = seqs * rows
    vmem = pltpu.VMEM
    r_grads = arrays[-1].reshape(group * ring, -1, arrays[-1].shape[1])
    arrays = arrays[:-1] + [r_grads]
    return communicate(
        kernel,
        ident,
        arrays,
        [
            ((width, hidden_size + width + part), BF),
            ((tokens, part), F32),
            ((group, seqs, half, 2 * HDIM), BF),
            ((8, part), F32),
            (r_grads.shape[1:], BF),
        ],
        semaphores(
            SequenceSums.count(sections, seqs, True)
            + SequenceSums.count(sections, seqs, False)
            + RowScatter.count(group, ring)
        )
        + [
            pltpu.SemaphoreType.DMA((5,)),
            vmem((tokens, part), BF),
            vmem((width, part), BF),
            vmem((width, hidden_size), BF),
            vmem((hidden_size, width), BF),
            vmem((tokens, width), BF),
            vmem((tokens, width), BF),
            vmem((tokens, hidden_size), BF),
        ]
        + SequenceSums.scratch(sections, seqs, rows, part, True)
        + SequenceSums.scratch(sections, seqs, rows, part, False)
        + RowScatter.scratch(group, ring, *r_grads.shape[1:]),
        name,
        limit=60 * 2**20,
        far=(5, 6, 7),
    )


def dense_leave(lines, ident, arrays, shards, shape, name):
    seqs, rows, width = shape
    sections, group, ring = (lines.sizes[k] for k in ("section", "z", "core"))
    part = width // sections
    half = rows // 2
    lanes = 2 * HDIM
    block = ring * rows
    many = len(shards)
    tokens = seqs * rows

    def kernel(
        heads,
        value_ref,
        q_ref,
        kv_ref,
        start_ref,
        turned_ref,
        lse_ref,
        qkv_w,
        middle,
        gains_ref,
        mid_vectors_ref,
        *refs,
    ):
        s_refs, refs = refs[:many], refs[many:]
        (grads_ref, stream_ref, vectors_ref), refs = refs[:3], refs[3:]
        so_refs, refs = refs[:many], refs[many:]
        (
            send,
            recv,
            sems,
            kv,
            normed,
            dqkv,
            heads_got,
            acc,
            pairs,
            pairs_got,
            queries,
            queries_got,
            sums,
            sums_got,
            *buffers,
        ) = refs
        loads = Loads(sems)
        kv_loads = {0: loads.start(kv_ref.at[:, :, 0], kv)}
        copies = Copies(lines, send, recv)
        section, zplace, place = (lines.place(k) for k in ("section", "z", "core"))
        own = span(section, part)
        copies.greet(["section", "z", "core"])
        inner = SequenceSums(copies, buffers)
        arriving, around, along, back = {}, {}, {}, {}
        for q in range(seqs):
            heads_got[zplace, q] = heads[zplace, q]
            arriving[q] = copies.swap("z", lambda peer: heads.at[peer, q], lambda me: heads_got.at[me, q])
        gathers = [SquareGather(copies, x, o) for x, o in zip(s_refs, so_refs)]
        for gather in gathers:
            gather.start()

        def attend(q):
            wait(arriving[q])
            kv_loads[q].wait()
            pieces = []
            for g in range(group):
                pair = kv[:, g].reshape(block, lanes)
                pieces.append((pair, pair.T, g * block))
            for g in reversed(range(group)):
                query = unpack_low(q_ref[g, q]) * jnp.asarray(SCALE, BF)
                packed = heads_got[g, q]
                flat = packed.T
                qpos = g * block + place * rows + lax.broadcasted_iota(jnp.int32, (1, rows), 1)
                grad_query, grads = backward_block(
                    query,
                    unpack_high(packed),
                    side_by_side([flat[:HDIM], flat[HDIM:]]),
                    turned_ref[q, g],
                    lse_ref[q, g],
                    pieces[: g + 1],
                    qpos,
                    start_ref[q, g],
                    [i == g for i in range(g + 1)],
                )
                queries[g, q] = pack_turned(grad_query).astype(BF)
                for i, item in enumerate(grads):
                    if g == group - 1:
                        acc[i] = item
                    else:
                        acc[i] += item
            if q > 0:
                wait(around[q - 1])
            for g in range(group):
                for r in range(ring):
                    pairs[r, g] = acc[g, r * rows : (r + 1) * rows].astype(BF)
            if q + 1 < seqs:
                kv_loads[q + 1] = loads.start(kv_ref.at[:, :, q + 1], kv)
            queries_got[zplace, q] = queries[zplace, q]
            around[q] = copies.swap("core", lambda peer: pairs.at[peer], lambda me: pairs_got.at[me, :, q])
            along[q] = copies.swap("z", lambda peer: queries.at[peer, q], lambda me: queries_got.at[me, q])

        def to_tokens(q):
            wait(around[q])
            around[q] = []
            for g in range(group):
                item = pairs[place, g].astype(F32)
                for peer in lines.peers("core"):
                    item = item + pairs_got[peer, g, q].astype(F32)
                sums[g, q] = item.astype(BF)
            sums_got[zplace, q] = sums[zplace, q]
            back[q] = copies.swap("z", lambda peer: sums.at[peer, q], lambda me: sums_got.at[me, q])

        def enter(q):
            wait(back[q] + along[q])
            at = pl.ds(q * rows, rows)
            packed = [queries_got[g, q] for g in range(group)]
            upright = [jnp.concatenate([p[:, :HDIM], p[:, HDIM:]], axis=0) for p in packed]
            grad = side_by_side([sums_got[g, q] for g in range(group)] + upright)
            dqkv[at] = grad
            grad_normed = contract(grad, qkv_w[...], 1, 1)
            value = value_ref[at].astype(F32)
            inner.start(q, grad_normed, jnp.sum(grad_normed * value * gains_ref[0:1], axis=1, keepdims=True))

        def leave(q):
            at = pl.ds(q * rows, rows)
            grad_normed, scalars = inner.finish(q)
            inv = inverse_rms(value_ref[at].astype(F32))
            value = value_ref[at, own].astype(F32)
            vectors_ref[0:1] += jnp.sum(grad_normed * value * inv, axis=0, keepdims=True)
            grad = (
                inv * (grad_normed * gains_ref[0:1, own])
                - value * (inv * inv * inv) * (scalars * (1.0 / width))
                + middle[at]
            )
            stream_ref[at] = grad.astype(BF)

        vectors_ref[...] = mid_vectors_ref[...]
        last = seqs - 1
        for q in range(seqs):
            attend(q)
            to_tokens(q)
            if q == 0:
                for gather in gathers:
                    gather.forward()
        for q in range(seqs):
            at = pl.ds(q * rows, rows)
            value = value_ref[at].astype(F32)
            normed[at] = (value * inverse_rms(value) * gains_ref[0:1]).astype(BF)
        for q in range(seqs):
            enter(q)
            if q > 0:
                inner.forward(q - 1)
            if q > 1:
                leave(q - 2)
        inner.forward(last)
        outer_product(normed, dqkv, grads_ref, 0)
        Copies.flush(grads_ref)
        for q in range(max(0, last - 1), seqs):
            leave(q)
        for gather in gathers:
            gather.finish()

    z, c = group - 1, ring - 1
    vmem = pltpu.VMEM
    result = communicate(
        kernel,
        ident,
        arrays + shards,
        [
            ((width, 3 * part), BF),
            ((tokens, part), BF),
            ((8, part), F32),
        ]
        + [((x.shape[0], sections * x.shape[1]), x.dtype) for x in shards],
        semaphores(
            seqs * (3 * z + c)
            + SequenceSums.count(sections, seqs, True)
            + sum(SquareGather.count(x.shape[0]) for x in shards)
        )
        + [
            pltpu.SemaphoreType.DMA((seqs + 1,)),
            vmem((ring, group, rows, lanes), BF),
            vmem((tokens, width), BF),
            vmem((tokens, 3 * part), BF),
            vmem((group, seqs, half, lanes), BF),
            vmem((group, block, lanes), F32),
            vmem((ring, group, rows, lanes), BF),
            vmem((ring, group, seqs, rows, lanes), BF),
            vmem((group, seqs, half, lanes), BF),
            vmem((group, seqs, half, lanes), BF),
            vmem((group, seqs, rows, lanes), BF),
            vmem((group, seqs, rows, lanes), BF),
        ]
        + SequenceSums.scratch(sections, seqs, rows, part, True),
        name,
        limit=60 * 2**20,
        far=(3,),
    )
    return result[0], result[1], result[2], result[3:]


def inverse_rms(value):
    return lax.rsqrt(jnp.mean(value * value, axis=-1, keepdims=True) + EPS)


def gelu_terms(value):
    scale = 0.7978845608028654
    square = value * value
    bend = jnp.tanh(scale * (value + 0.044715 * square * value))
    half = 0.5 * (1.0 + bend)
    slope = half + 0.5 * value * (1.0 - bend * bend) * scale * (1.0 + 0.134145 * square)
    return value * half, slope


def side_by_side(blocks):
    return jnp.concatenate(blocks, axis=1)


class ColumnSum:
    @staticmethod
    def count(sections, scalars):
        return (sections - 1) * (2 if scalars else 1)

    @staticmethod
    def scratch(sections, rows, width, scalars):
        buffers = [pltpu.VMEM((rows, sections * width), BF), pltpu.VMEM((sections, rows, width), BF)]
        if scalars:
            wide = rows + -rows % 128
            buffers += [pltpu.VMEM((8, wide), F32), pltpu.VMEM((sections, 8, wide), F32)]
        return buffers

    def __init__(self, copies, buffers):
        self.copies, self.buffers = copies, buffers

    def start(self, value, scalars=None):
        buf, got = self.buffers[:2]
        width = got.shape[2]
        section = self.copies.lines.place("section")
        buf[...] = value.astype(BF)
        self.pending = self.copies.swap(
            "section", lambda peer: buf.at[:, span(peer, width)], lambda me: got.at[me]
        )
        got[section] = buf[:, span(section, width)]
        if scalars is not None:
            sbuf, sgot = self.buffers[2:]
            sbuf[...] = jnp.zeros_like(sbuf)
            sbuf[:, : scalars.shape[0]] = column_to_rows(scalars)
            self.pending += self.copies.swap("section", lambda peer: sbuf, lambda me: sgot.at[me])
            sgot[section] = sbuf[...]

    def finish(self):
        wait(self.pending)
        total = sum_places(self.buffers[1])
        if len(self.buffers) == 2:
            return total
        rows = total.shape[0]
        return total, row_to_column(sum_places(self.buffers[3])[:1, :rows])


class Swaps:
    def __init__(self, copies):
        self.copies, self.lines = copies, copies.lines

    def ring(self, buf, got):
        return self.copies.swap("core", lambda peer: buf.at[peer], lambda me: got.at[me])

    def ring_sum(self, buf, got):
        total = buf[self.lines.place("core")].astype(F32)
        for peer in self.lines.peers("core"):
            total = total + got[peer].astype(F32)
        return total.astype(BF)

    def z(self, buf, got):
        place = self.lines.place("z")
        pending = self.copies.swap("z", lambda peer: buf.at[peer], lambda me: got.at[me])
        got[place] = buf[place]
        return pending

    def share(self, kind, all_ref):
        me = self.lines.place(kind)
        return self.copies.swap(kind, lambda peer: all_ref.at[me], lambda _: all_ref.at[me])


def together(all_ref):
    return side_by_side([all_ref[i] for i in range(all_ref.shape[0])])


def halves(value):
    rows = value.shape[0] // 2
    return side_by_side([value[:rows], value[rows:]])


def upright(packed):
    return jnp.concatenate([packed[:, :HDIM], packed[:, HDIM:]], axis=0)


def slots_of(lines, sel):
    group, ring = lines.sizes["z"], lines.sizes["core"]
    index = lax.broadcasted_iota(jnp.int32, (1, group * sel), 1)
    return (index // sel) * (ring * sel) + lines.place("core") * sel + lax.rem(index, sel)


def slot_sequence(lines, queries_ref, pairs_ref, q, sel):
    group, ring = lines.sizes["z"], lines.sizes["core"]
    at = slice(q * sel, (q + 1) * sel)
    query = jnp.concatenate([queries_ref[g, at] for g in range(group)], axis=0)
    pair = jnp.concatenate([pairs_ref[r, g, at] for g in range(group) for r in range(ring)], axis=0)
    return query * jnp.asarray(SCALE, BF), pair


def dense_feed(lines, ident, arrays, shape, name):
    seqs, sel, rows, width, part, hidden_size = shape
    sections, group, ring = (lines.sizes[k] for k in ("section", "z", "core"))
    dp = group * ring
    slots = seqs * sel
    lanes = 2 * HDIM
    queries = group * sel

    def kernel(
        value_ref,
        mixed_ref,
        gains_ref,
        rest_ref,
        top_ref,
        chosen_ref,
        ids_ref,
        first_ref,
        attended_ref,
        slope_ref,
        hidden_ref,
        out_ref,
        picked_ref,
        grad_ref,
        normed_ref,
        queries_ref,
        pairs_all,
        start_ref,
        turned_ref,
        lse_ref,
        r_mixed_ref,
        weights_all,
        send,
        recv,
        sems,
        out_w,
        expand_w,
        shrink_w,
        top,
        own_buf,
        wide,
        got,
        turn,
        last,
        value_core,
        value_core_got,
        value_z,
        value_z_got,
        value_all,
        grad_core,
        grad_core_got,
        grad_z,
        grad_z_got,
        grad_all,
        heads_buf,
        heads_got,
        o_buf,
        o_got,
        mixed_all,
    ):
        loads = Loads(sems)
        section, place = lines.place("section"), lines.place("core")
        rank = lax.axis_index("dp")
        own = span(section, part)
        out_load = loads.start(rest_ref.at[:, :part], out_w)
        top_load = loads.start(top_ref.at[:, :, own], top)
        expand_load = loads.start(rest_ref.at[:, part : part + hidden_size], expand_w)
        shrink_load = loads.start(rest_ref.at[:, part + hidden_size :], shrink_w)
        copies = Copies(lines, send, recv)
        swaps = Swaps(copies)
        copies.greet(["section", "z", "core"])
        weights_along = copies.swap("z", lambda peer: first_ref, lambda _: weights_all.at[rank])
        weights_handed = copies.swap("core", lambda peer: first_ref, lambda _: weights_all.at[rank])
        weights_all[rank] = first_ref[...]
        out_load.wait()
        gathers, scatters = {}, {}
        position = rank * rows + lax.broadcasted_iota(jnp.int32, (1, rows), 1).astype(F32)

        def table(q):
            chosen = row_to_column(chosen_ref[q : q + 1].astype(F32))
            return (chosen == position).astype(F32).astype(BF)

        def pick(q, source, buf):
            found = matmul(table(q), source).astype(BF)
            for d in range(dp):
                buf[d % ring, d // ring, q * sel : (q + 1) * sel] = found[d * sel : (d + 1) * sel]

        def project(q):
            own_buf[q] = matmul(mixed_ref[q], out_w[...]).astype(BF)
            gathers[q] = SquareGather(copies, own_buf.at[q], attended_ref.at[q], 1)
            gathers[q].start()

        def feed(q):
            gathers[q].finish()
            middle = value_ref[q].astype(F32) + attended_ref[q].astype(F32)
            normed = (middle * inverse_rms(middle) * gains_ref[1:2]).astype(BF)
            hidden, slope = gelu_terms(matmul(normed, expand_w[...]))
            hidden = hidden.astype(BF)
            hidden_ref[q] = hidden
            slope_ref[q] = slope.astype(BF)
            wide[q] = matmul(hidden, shrink_w[...]).astype(BF)
            scatters[q] = SquareScatter(copies, wide.at[q], got.at[q], turn.at[q], last.at[q], 1)
            scatters[q].start()

        def leave(q):
            scatters[q].finish(out_ref.at[q])
            after = out_ref[q] + value_ref[q, :, own].astype(F32) + attended_ref[q, :, own].astype(F32)
            out_ref[q] = after
            pick(q, after.astype(BF), value_core)

        for q in range(seqs):
            project(q)
            if q > 0:
                gathers[q - 1].forward()
        gathers[seqs - 1].forward()
        top_load.wait()
        for q in range(seqs):
            pick(q, top[q], grad_core)
        grad_pending = swaps.ring(grad_core, grad_core_got)
        expand_load.wait()
        shrink_load.wait()
        for q in range(seqs):
            feed(q)
            if q == 0:
                wait(grad_pending)
                grad_z[...] = swaps.ring_sum(grad_core, grad_core_got)
                grad_pending = swaps.z(grad_z, grad_z_got)
            else:
                scatters[q - 1].forward()
            if q > 1:
                leave(q - 2)
        Copies.flush(hidden_ref)
        Copies.flush(slope_ref)
        Copies.flush(attended_ref)
        scatters[seqs - 1].forward()
        for q in range(max(0, seqs - 2), seqs):
            leave(q)
        Copies.flush(out_ref)

        pending = swaps.ring(value_core, value_core_got)
        wait(grad_pending)
        grad_all[section] = sum_places(grad_z_got).astype(BF)
        wait(pending)
        value_z[...] = swaps.ring_sum(value_core, value_core_got)
        pending = swaps.z(value_z, value_z_got)
        grad_pending = swaps.share("section", grad_all)

        def slot_starts(q):
            firsts = document_starts(ids_ref[q : q + 1])
            chosen = chosen_ref[q : q + 1].astype(F32)
            documents = sum((chosen >= firsts[c]).astype(F32) for c in range(1, DOCS))
            column = jnp.broadcast_to(row_to_column(chosen), (dp * sel, queries))
            slot = lax.broadcasted_iota(jnp.int32, column.shape, 0)
            mine = jnp.sum(jnp.where(slot == slots_of(lines, sel), column, 0.0), axis=0, keepdims=True)
            mine = sum((mine >= firsts[c]).astype(F32) for c in range(1, DOCS))
            return start_of(mine, document_starts(documents))

        for q in range(seqs):
            start_ref[q] = slot_starts(q)
        for step in range(group - 1, 0, -1):
            weights_along[group - 1 - step].wait_recv()
            source = lax.rem(lines.place("z") + step, group) * ring + place
            weights_handed += copies.swap(
                "core", lambda peer: weights_all.at[source], lambda _: weights_all.at[source]
            )
        wait(pending)
        value_all[section] = sum_places(value_z_got).astype(BF)
        pending = swaps.share("section", value_all)
        wait(grad_pending)
        grad_ref[...] = together(grad_all)
        wait(pending)
        low = together(value_all)
        picked_ref[...] = low
        picked = low.astype(F32)
        normed = (picked * inverse_rms(picked) * gains_ref[2:3]).astype(BF)
        normed_ref[...] = normed
        for copy in weights_along:
            copy.wait_send()
        wait(weights_handed)
        qkv = matmul(normed, weights_all[...].reshape(width, 3 * part)).astype(BF)
        for g in range(group):
            heads_buf[g, :slots] = qkv[:, g * lanes : (g + 1) * lanes]
            heads_buf[g, slots:] = halves(qkv[:, 2 * part + g * HDIM : 2 * part + (g + 1) * HDIM])
        wait(swaps.z(heads_buf, heads_got))
        pairs_all[place] = heads_got[:, :slots]
        pending = swaps.share("core", pairs_all)
        blank = jnp.zeros((slots, HDIM), BF)
        for g in range(group):
            queries_ref[g] = side_by_side([upright(heads_got[g, slots:]), blank])
        wait(pending)
        turned_all = []
        for q in range(seqs):
            query, pair = slot_sequence(lines, queries_ref, pairs_all, q, sel)
            turned, lse = forward_block(
                query, [(pair, pair.T, 0)], slots_of(lines, sel), start_ref[q], [True]
            )
            turned_ref[q] = turned.astype(BF)
            lse_ref[q] = lse
            turned_all.append(jnp.concatenate([turned, jnp.zeros_like(turned)], axis=0).T.astype(BF)[:, :HDIM])
        for g in range(group):
            o_buf[g] = halves(jnp.concatenate([t[g * sel : (g + 1) * sel] for t in turned_all], axis=0))
        wait(swaps.z(o_buf, o_got))
        mixed_all[section] = side_by_side([upright(o_got[g]) for g in range(group)])
        wait(swaps.share("section", mixed_all))
        r_mixed_ref[...] = together(mixed_all)

    vmem = pltpu.VMEM
    z, s, c = group - 1, sections - 1, ring - 1
    short = ((group, slots, part), BF)
    across = ((sections, slots, part), BF)
    packed = ((group, slots // 2, lanes), BF)
    heads = ((group, slots + slots // 2, lanes), BF)
    row = ((slots, width), BF)
    scratch = [
        ((width, part), BF),
        ((width, hidden_size), BF),
        ((hidden_size, width), BF),
        ((seqs, rows, part), BF),
        ((seqs, rows, part), BF),
        ((seqs, rows, width), BF),
        ((seqs, 2, rows, part), BF),
        ((seqs, rows, part), BF),
        ((seqs, rows, part), BF),
        ((ring,) + short[0], BF),
        ((ring,) + short[0], BF),
        short,
        short,
        across,
        ((ring,) + short[0], BF),
        ((ring,) + short[0], BF),
        short,
        short,
        across,
        heads,
        heads,
        packed,
        packed,
        across,
    ]
    return communicate(
        kernel,
        ident,
        arrays,
        [
            ((seqs, rows, width), BF),
            ((seqs, rows, hidden_size), BF),
            ((seqs, rows, hidden_size), BF),
            ((seqs, rows, part), F32),
            row,
            row,
            row,
            ((group, slots, lanes), BF),
            ((ring, group, slots, lanes), BF),
            ((seqs, 1, queries), jnp.int32),
            ((seqs, HDIM, queries), BF),
            ((seqs, 1, queries), F32),
            row,
            ((dp,) + arrays[-1].shape, BF),
        ],
        semaphores(seqs * 12 + 3 * c + 4 * z + 3 * s + z + group * c)
        + [pltpu.SemaphoreType.DMA((4,))]
        + [vmem(a, b) for a, b in scratch],
        name,
        limit=60 * 2**20,
        far=(3, 4),
    )


def routed_feed(lines, ident, arrays, shape, name):
    slots, width, part, hidden_size = shape
    sections = lines.sizes["section"]

    def kernel(
        value_ref,
        grad_ref,
        mixed_ref,
        gains_ref,
        rest_ref,
        grads_ref,
        middle_ref,
        attended_ref,
        sent_ref,
        logit_ref,
        vectors_ref,
        send,
        recv,
        sems,
        out_w,
        expand_w,
        shrink_w,
        keep,
        mid_keep,
        dpre_keep,
        hidden_keep,
        fed_keep,
        attended_all,
        *buffers,
    ):
        loads = Loads(sems)
        out_load = loads.start(rest_ref.at[:, :part], out_w)
        shrink_load = loads.start(rest_ref.at[:, part + hidden_size :], shrink_w)
        expand_load = loads.start(rest_ref.at[:, part : part + hidden_size], expand_w)
        copies = Copies(lines, send, recv)
        swaps = Swaps(copies)
        section = lines.place("section")
        own = span(section, part)
        copies.greet(["section"])
        back, forth = ColumnSum(copies, buffers[:4]), ColumnSum(copies, buffers[4:])
        gain, router = gains_ref[3:4, :], gains_ref[4:5, :]
        out_load.wait()
        attended_own = matmul(mixed_ref[...], out_w[...]).astype(BF)
        attended_all[section] = attended_own
        pending = swaps.share("section", attended_all)
        picked = value_ref[...].astype(F32)
        grad_sent = grad_ref[...].astype(F32)
        gate = jax.nn.sigmoid(jnp.sum(picked * router, axis=1, keepdims=True))
        grad_delta = gate * grad_sent
        fed_low = grad_delta.astype(BF)
        fed_keep[...] = fed_low
        shrink_load.wait()
        grad_hidden = contract(fed_low, shrink_w[...], 1, 1)
        expand_load.wait()
        wait(pending)
        middle = picked + together(attended_all).astype(F32)
        inv = inverse_rms(middle)
        normed = (middle * inv * gain).astype(BF)
        hidden, slope = gelu_terms(matmul(normed, expand_w[...]))
        hidden = hidden.astype(BF)
        grad_pre = (grad_hidden * slope).astype(BF)
        grad_normed = contract(grad_pre, expand_w[...], 1, 1)
        back.start(grad_normed, jnp.sum(grad_normed * middle * gain, axis=1, keepdims=True))
        mid_keep[...] = normed
        hidden_keep[...] = hidden
        dpre_keep[...] = grad_pre
        fed_part = matmul(hidden, shrink_w[...])
        keep[0] = middle
        keep[1] = grad_delta
        keep[2] = grad_sent
        own_attended = attended_own.astype(F32)
        gate_part = jnp.sum(grad_sent * fed_part, axis=1, keepdims=True) + jnp.sum(
            keep[2, :, own] * own_attended, axis=1, keepdims=True
        )
        forth.start(fed_part, gate_part)
        outer_product(mid_keep, dpre_keep, grads_ref, 0)
        grad_normed, scalar = back.finish()
        middle_own = keep[0, :, own]
        vectors_ref[...] = jnp.zeros_like(vectors_ref)
        vectors_ref[3:4] = jnp.sum(grad_normed * middle_own * inv, axis=0, keepdims=True)
        grad_middle = inv * (grad_normed * gains_ref[3:4, own]) - middle_own * (inv * inv * inv) * (
            scalar * (1.0 / width)
        )
        middle_ref[...] = grad_middle
        attended_ref[...] = (grad_middle + keep[1, :, own]).astype(BF)
        outer_product(hidden_keep, fed_keep, grads_ref, hidden_size)
        Copies.flush(grads_ref)
        fed, grad_gate = forth.finish()
        sent_ref[...] = (gate * (own_attended + fed)).astype(BF)
        grad_logit = grad_gate * gate * (1.0 - gate)
        logit_ref[...] = jnp.broadcast_to(grad_logit, logit_ref.shape)
        vectors_ref[4:5] = jnp.sum(grad_logit * value_ref[:, own].astype(F32), axis=0, keepdims=True)

    vmem = pltpu.VMEM
    return communicate(
        kernel,
        ident,
        arrays,
        [
            ((width, hidden_size + width), BF),
            ((slots, part), F32),
            ((slots, part), BF),
            ((slots, part), BF),
            ((slots, 128), F32),
            ((8, part), F32),
        ],
        semaphores(sections - 1 + 2 * ColumnSum.count(sections, True))
        + [
            pltpu.SemaphoreType.DMA((3,)),
            vmem((width, part), BF),
            vmem((width, hidden_size), BF),
            vmem((hidden_size, width), BF),
            vmem((3, slots, width), F32),
            vmem((slots, width), BF),
            vmem((slots, hidden_size), BF),
            vmem((slots, hidden_size), BF),
            vmem((slots, width), BF),
            vmem((sections, slots, part), BF),
        ]
        + 2 * ColumnSum.scratch(sections, slots, part, True),
        name,
        limit=60 * 2**20,
        far=(4,),
    )


def routed_leave(lines, ident, arrays, shape, name):
    seqs, sel, rows, width, part = shape
    sections, group, ring = (lines.sizes[k] for k in ("section", "z", "core"))
    slots = seqs * sel
    lanes = 2 * HDIM

    def kernel(
        attended_ref,
        rest_ref,
        qkv_w,
        queries_ref,
        pairs_ref,
        start_ref,
        turned_ref,
        lse_ref,
        value_ref,
        normed_ref,
        mixed_ref,
        middle_ref,
        logit_ref,
        sent_ref,
        feed_vectors_ref,
        gains_ref,
        chosen_ref,
        top_ref,
        fed_out,
        own_out,
        added_ref,
        grads_ref,
        vectors_ref,
        send,
        recv,
        sems,
        out_w,
        grad_buf,
        grad_got,
        grad_high,
        turn_buf,
        turn_got,
        back_buf,
        back_got,
        dqkv_keep,
        sent_got,
        sent_all,
        final_buf,
        final_got,
        final_all,
        *buffers,
    ):
        loads = Loads(sems)
        out_load = loads.start(rest_ref.at[:, :part], out_w)
        copies = Copies(lines, send, recv)
        swaps = Swaps(copies)
        section, zplace, place = (lines.place(k) for k in ("section", "z", "core"))
        rank = lax.axis_index("dp")
        own = span(section, part)
        copies.greet(["section", "z", "core"])
        outer, inner = ColumnSum(copies, buffers[:2]), ColumnSum(copies, buffers[2:])
        out_load.wait()
        outer.start(contract(attended_ref[...], out_w[...], 1, 1))
        sent_pending = copies.swap("z", lambda peer: sent_ref, lambda me: sent_got.at[me])
        sent_got[zplace] = sent_ref[...]
        outer_product(mixed_ref, attended_ref, grads_ref, 3 * part)
        slot_of = rank * rows + lax.broadcasted_iota(jnp.int32, (rows, 1), 0)
        tables = [(chosen_ref[q : q + 1] == slot_of).astype(F32).astype(BF) for q in range(seqs)]
        blank = jnp.zeros((slots, HDIM), BF)
        grad_mixed = outer.finish().astype(BF)
        for g in range(group):
            grad_buf[g] = halves(grad_mixed[:, g * HDIM : (g + 1) * HDIM])
        pending = swaps.z(grad_buf, grad_got)
        wait(sent_pending)
        sent_all[place] = sent_got[...]
        sent_pending = swaps.share("core", sent_all)
        wait(pending)
        for g in range(group):
            grad_high[g] = side_by_side([blank, upright(grad_got[g])])
        query_grads = []
        for q in range(seqs):
            at = slice(q * sel, (q + 1) * sel)
            query, pair = slot_sequence(lines, queries_ref, pairs_ref, q, sel)
            grad = jnp.concatenate([grad_high[g, at] for g in range(group)], axis=0)
            grad_query, grad_pairs = backward_block(
                query,
                grad,
                grad.T[HDIM:],
                turned_ref[q],
                lse_ref[q],
                [(pair, pair.T, 0)],
                slots_of(lines, sel),
                start_ref[q],
                [True],
            )
            turned = jnp.concatenate([grad_query, jnp.zeros_like(grad_query)], axis=0).T.astype(BF)
            query_grads.append(turned[:, :HDIM])
            low = grad_pairs[0].astype(BF)
            for g in range(group):
                for r in range(ring):
                    first = (g * ring + r) * sel
                    turn_buf[r, g, at] = low[first : first + sel]
        pending = swaps.ring(turn_buf, turn_got)
        for g in range(group):
            back_buf[g, slots:] = halves(
                jnp.concatenate([t[g * sel : (g + 1) * sel] for t in query_grads], axis=0)
            )
        wait(pending)
        back_buf[:, :slots] = swaps.ring_sum(turn_buf, turn_got)
        pending = swaps.z(back_buf, back_got)
        wait(sent_pending)

        def at_positions(q, all_ref):
            at = slice(q * sel, (q + 1) * sel)
            found = jnp.concatenate([all_ref[r, g, at] for g in range(group) for r in range(ring)], axis=0)
            return matmul(tables[q], found)

        for q in range(seqs):
            added_ref[q] = at_positions(q, sent_all).astype(BF)
        wait(pending)
        dqkv_keep[...] = side_by_side(
            [back_got[g, :slots] for g in range(group)] + [upright(back_got[g, slots:]) for g in range(group)]
        )
        grad_normed = contract(dqkv_keep[...], qkv_w[...], 1, 1)
        picked = value_ref[...].astype(F32)
        inv = inverse_rms(picked)
        inner.start(grad_normed, jnp.sum(grad_normed * picked * gains_ref[2:3], axis=1, keepdims=True))
        outer_product(normed_ref, dqkv_keep, grads_ref, 0)
        picked = value_ref[:, own].astype(F32)
        grad_normed, scalar = inner.finish()
        vectors_ref[...] = feed_vectors_ref[...]
        vectors_ref[2:3] = jnp.sum(grad_normed * picked * inv, axis=0, keepdims=True)
        grad_in = inv * (grad_normed * gains_ref[2:3, own]) - picked * (inv * inv * inv) * (scalar * (1.0 / width))
        final_buf[...] = (middle_ref[...] + grad_in + logit_ref[:, :1] * gains_ref[4:5, own]).astype(BF)

        along = copies.swap("z", lambda peer: final_buf, lambda me: final_got.at[me])
        final_got[zplace] = final_buf[...]

        def hand_on(i):
            dst = final_all.at[place, i, :, own]
            dst[...] = final_got[i]
            return copies.swap("section", lambda peer: final_got.at[i], lambda me: dst)

        spread = hand_on(zplace)
        Copies.flush(grads_ref)
        for step in range(group - 1, 0, -1):
            along[group - 1 - step].wait_recv()
            spread += hand_on(lax.rem(zplace + step, group))
        for copy in along:
            copy.wait_send()
        wait(spread)
        wait(swaps.share("core", final_all))
        for q in range(seqs):
            fed_out[q] = (top_ref[q].astype(F32) + at_positions(q, final_all)).astype(BF)
            returned = jnp.concatenate(
                [final_all[r, g, q * sel : (q + 1) * sel, own] for g in range(group) for r in range(ring)], axis=0
            )
            own_out[q] = top_ref[q, :, own].astype(F32) + matmul(tables[q], returned)

    vmem = pltpu.VMEM
    z, s, c = group - 1, sections - 1, ring - 1
    lane_block = ((group, slots, lanes), BF)
    packed = ((group, slots // 2, lanes), BF)
    heads = ((group, slots + slots // 2, lanes), BF)
    ring_block = ((ring, group, slots, lanes), BF)
    short = ((group, slots, part), BF)
    scratch = [
        ((width, part), BF),
        packed,
        packed,
        lane_block,
        ring_block,
        ring_block,
        heads,
        heads,
        ((slots, 3 * part), BF),
        short,
        ((ring,) + short[0], BF),
        ((slots, part), BF),
        short,
        ((ring, group, slots, width), BF),
    ]
    return communicate(
        kernel,
        ident,
        arrays,
        [
            ((seqs, rows, width), BF),
            ((seqs, rows, part), F32),
            ((seqs, rows, part), BF),
            ((width, 4 * part), BF),
            ((8, part), F32),
        ],
        semaphores(
            3 * c
            + 4 * z
            + ColumnSum.count(sections, True)
            + ColumnSum.count(sections, False)
            + group * s
        )
        + [pltpu.SemaphoreType.DMA((1,))]
        + [vmem(a, b) for a, b in scratch]
        + ColumnSum.scratch(sections, slots, part, False)
        + ColumnSum.scratch(sections, slots, part, True),
        name,
        limit=60 * 2**20,
        far=(1,),
    )


def cut_weights(arrays, sections, dp, group, name):
    local, width = arrays[0].shape
    part = width // sections
    inner = arrays[4].shape[1] // dp
    share = inner // sections
    hidden_size = dp * share
    layers = len(arrays) // 6

    def kernel(*refs):
        ins, outs = refs[: 6 * layers], refs[6 * layers : 8 * layers]
        k_buf, v_buf, sems = refs[8 * layers :]
        section = lax.axis_index("section")
        own = span(section, part)
        moves = []
        for i in range(layers):
            q_ref, k_ref, v_ref, o_ref, e_ref, s_ref = ins[6 * i : 6 * i + 6]
            first_ref, rest_ref = outs[2 * i : 2 * i + 2]
            rows = pl.ds(pl.multiple_of(section * share, share), share)
            moves += [
                (k_ref.at[:, own], k_buf.at[i]),
                (v_ref.at[:, own], v_buf.at[i]),
                (q_ref.at[:, own], first_ref.at[:, 2 * part :]),
                (o_ref.at[:, own], rest_ref.at[:, :part]),
                (s_ref.at[rows], rest_ref.at[:, part + hidden_size :]),
            ]
            for d in range(dp):
                at = pl.ds(pl.multiple_of(d * inner + section * share, 128), share)
                moves.append((e_ref.at[:, at], rest_ref.at[:, part + d * share : part + (d + 1) * share]))
        copies = [pltpu.make_async_copy(src, dst, sems.at[i]) for i, (src, dst) in enumerate(moves)]
        for copy in copies:
            copy.start()
        for copy in copies:
            copy.wait()
        for i in range(layers):
            for g in range(group):
                at = slice(g * HDIM, (g + 1) * HDIM)
                pair = side_by_side([k_buf[i, :, at], v_buf[i, :, at]])
                outs[2 * i][:, 2 * g * HDIM : 2 * (g + 1) * HDIM] = pair

    anywhere, vmem = pl.BlockSpec(memory_space=pl.ANY), pl.BlockSpec(memory_space=pltpu.VMEM)
    shapes = [
        jax.ShapeDtypeStruct((local, 3 * part), BF),
        jax.ShapeDtypeStruct((local, part + hidden_size + width), BF),
    ]
    return pl.pallas_call(
        kernel,
        in_specs=[anywhere] * 6 * layers,
        out_specs=[vmem] * 2 * layers,
        out_shape=shapes * layers,
        scratch_shapes=[
            pltpu.VMEM((layers, local, part), BF),
            pltpu.VMEM((layers, local, part), BF),
            pltpu.SemaphoreType.DMA((layers * (5 + dp),)),
        ],
        compiler_params=pltpu.CompilerParams(vmem_limit_bytes=60 * 2**20),
        name=name,
    )(*arrays)


def on_device(
    stream_in,
    segment_ids,
    chosen_rows,
    cotangent,
    dense_prenorm,
    dense_query,
    dense_keys,
    dense_values,
    dense_output,
    dense_midnorm,
    dense_expand,
    dense_shrink,
    routed_prenorm,
    routed_query,
    routed_keys,
    routed_values,
    routed_output,
    routed_midnorm,
    routed_expand,
    routed_shrink,
    router_weight,
):
    sections, dp = lax.axis_size("section"), lax.axis_size("dp")
    section, rank = lax.axis_index("section"), lax.axis_index("dp")
    seqs, rows, width = stream_in.shape
    tokens = seqs * rows
    part = width // sections
    group = HEADS // sections
    ring = dp // group
    total_sel = chosen_rows.shape[1]
    sel = total_sel // dp
    lines = Lines(sections, dp, group)

    def own_columns(value):
        return lax.dynamic_slice_in_dim(value, section * part, part, value.ndim - 1)

    def own_hidden(expand, shrink):
        inner = expand.shape[1] // dp
        share = inner // sections
        cut = expand.reshape(expand.shape[0], dp, sections, share)
        cut = lax.dynamic_index_in_dim(cut, section, 2, keepdims=False).reshape(expand.shape[0], dp * share)
        return cut, lax.dynamic_slice_in_dim(shrink, section * share, share, 0)

    def own_attention(query, keys, values):
        local = query.shape[0]
        pair = jnp.stack(
            [own_columns(keys).reshape(local, group, HDIM), own_columns(values).reshape(local, group, HDIM)],
            axis=2,
        ).reshape(local, 2 * part)
        return jnp.concatenate([pair, own_columns(query)], axis=1)

    def cut(*layers):
        if dense_expand.shape[1] // (dp * sections) % 128 == 0:
            return cut_weights([w for layer in layers for w in layer], sections, dp, group, "cut")
        out = []
        for query, keys, values, output, expand, shrink in layers:
            expand_cut, shrink_cut = own_hidden(expand, shrink)
            rest = jnp.concatenate([own_columns(output), expand_cut, shrink_cut], axis=1)
            out += [own_attention(query, keys, values), rest]
        return out

    def gather(value):
        return lax.all_gather(value, "dp", axis=0, tiled=True)

    def after(value, other):
        return lax.optimization_barrier((value, other))[0]

    hidden_size = dense_expand.shape[1] // sections
    gains = jnp.stack([dense_prenorm, dense_midnorm, routed_prenorm, routed_midnorm, router_weight])
    gains = jnp.pad(gains, ((0, 16 - gains.shape[0]), (0, 0)))
    dense_first, dense_rest, routed_first, routed_rest = cut(
        (dense_query, dense_keys, dense_values, dense_output, dense_expand, dense_shrink),
        (routed_query, routed_keys, routed_values, routed_output, routed_expand, routed_shrink),
    )
    rest = gather(dense_rest)
    routed_rest = gather(routed_rest)

    shape = (seqs, sel, rows, width, part)
    grad_top = cotangent.reshape(tokens, width)
    dense_qkv, gains, queries, pairs, start, mixed_turned, lse, mixed = dense_enter(
        lines,
        1,
        [stream_in.reshape(tokens, width), dense_first, gains, segment_ids],
        (seqs, rows, width),
        "dense_enter",
    )
    dense_qkv = dense_qkv.reshape(width, 3 * part)
    (
        attended,
        slope,
        hidden,
        after_dense,
        r_value,
        r_grad,
        r_normed,
        r_queries,
        r_pairs,
        r_start,
        r_turned,
        r_lse,
        r_mixed,
        routed_qkv,
    ) = dense_feed(
        lines,
        2,
        [stream_in, mixed, gains, rest, cotangent, chosen_rows, segment_ids, routed_first],
        shape + (hidden_size,),
        "dense_feed",
    )
    routed_qkv = routed_qkv.reshape(width, 3 * part)
    after_dense = after_dense.reshape(tokens, part)
    attended, slope, hidden, mixed = (x.reshape(tokens, -1) for x in (attended, slope, hidden, mixed))

    def reduce_dp(value):
        return lax.psum_scatter(value, "dp", scatter_dimension=0, tiled=True)

    routed_grads, r_middle, r_grad_attended, r_sent, r_logit, r_vectors = routed_feed(
        lines,
        4,
        [r_value, r_grad, r_mixed, gains, routed_rest],
        (seqs * sel, width, part, hidden_size),
        "routed_feed",
    )
    routed_shard = reduce_dp(routed_grads)
    fed_low, grad_own, added, routed_grads, r_vectors = routed_leave(
        lines,
        5,
        [
            r_grad_attended,
            routed_rest,
            routed_qkv,
            r_queries,
            r_pairs,
            r_start,
            r_turned,
            r_lse,
            r_value,
            r_normed,
            r_mixed,
            r_middle,
            r_logit,
            r_sent,
            r_vectors,
            gains,
            chosen_rows,
            cotangent,
        ],
        shape,
        "routed_leave",
    )
    dense_grads, grad_middle, grad_heads, d_vectors, routed_shard_in = dense_return(
        lines,
        6,
        [
            fed_low.reshape(tokens, width),
            grad_own.reshape(tokens, part),
            stream_in.reshape(tokens, width),
            attended,
            slope,
            hidden,
            mixed,
            rest,
            gains,
            r_vectors,
            routed_grads,
        ],
        (seqs, rows, width, hidden_size),
        "dense_return",
    )
    dense_shard = reduce_dp(after(dense_grads, routed_shard))
    dense_grads, stream_grad, d_vectors, (routed_all, routed_all_in) = dense_leave(
        lines,
        7,
        [
            grad_heads,
            stream_in.reshape(tokens, width),
            queries,
            pairs,
            start,
            mixed_turned,
            lse,
            dense_qkv,
            grad_middle,
            gains,
            d_vectors,
        ],
        [routed_shard, routed_shard_in],
        (seqs, rows, width),
        "dense_leave",
    )
    added = after(added, d_vectors).reshape(tokens, part)
    stream_out = (after_dense + added.astype(F32)).astype(BF).reshape(seqs, rows, part)
    stream_grad = stream_grad.reshape(seqs, rows, part)
    vectors, (dense_all_in,), (dense_all,) = dense_finish(
        lines, 8, d_vectors, dense_grads, [dense_shard], (3 * part,), "dense_finish"
    )

    share = hidden_size // dp
    local = width // dp
    r_exp, r_shr, r_keys, r_values, r_query, r_out = assemble(
        [
            ("hidden", routed_all, 0, hidden_size),
            ("stack", routed_all, hidden_size, width),
            ("pair", routed_all_in, 0, 2 * part),
            ("columns", routed_all_in, 2 * part, part),
            ("columns", routed_all_in, 3 * part, part),
        ],
        share,
        "routed_places",
    )
    d_exp, d_shr, d_keys, d_values, d_query, d_out = assemble(
        [
            ("hidden", dense_all, 0, hidden_size),
            ("stack", dense_all, hidden_size, width),
            ("pair", dense_all_in, 0, 2 * part),
            ("columns", dense_all_in, 2 * part, part),
            ("columns", dense_all, hidden_size + width, part),
        ],
        share,
        "dense_places",
    )
    vectors = lax.dynamic_slice_in_dim(vectors, rank * local, local, 1)
    d_shr = d_shr.reshape(sections * share, width)
    r_shr = r_shr.reshape(sections * share, width)
    return (
        (stream_out, stream_grad)
        + (vectors[0], d_query, d_keys, d_values, d_out, vectors[1], d_exp, d_shr)
        + (vectors[2], r_query, r_keys, r_values, r_out, vectors[3], r_exp, r_shr)
        + (vectors[4],)
    )


def solution(mesh):
    streams, row, vector, copied = P(None, "dp", None), P("dp", None), P("dp"), P()
    layer = (vector, row, row, row, row, vector, row, row)
    outs = (P(None, "dp", "section"),) * 2 + layer + layer + (vector,)
    return jax.shard_map(
        on_device,
        mesh=mesh,
        in_specs=(streams, copied, copied, streams) + layer + layer + (vector,),
        out_specs=outs,
        check_vma=False,
    )
```

```python
import functools

import jax
import jax.numpy as jnp
from jax import lax
from jax.experimental import pallas as pl
from jax.experimental.pallas import tpu as pltpu
from jax.sharding import PartitionSpec as P

HEADS = 16
HDIM = 64
DOCS = 8
EPS = 1e-06
NEG = -1e30
SCALE = HDIM ** (-0.5)
VMEM = 32 * 2**20
MESH = pl.DeviceIdType.MESH
BF = jnp.bfloat16
F32 = jnp.float32


def matmul(left, right):
    return jnp.dot(left, right, preferred_element_type=F32)


def contract(left, right, ldim, rdim):
    return lax.dot_general(left, right, (((ldim,), (rdim,)), ((), ())), preferred_element_type=F32)


class Lines:
    def __init__(self, sections, dp, group):
        self.sizes = {"section": sections, "z": group, "core": dp // group}
        self.ring = dp // group

    def place(self, kind):
        if kind == "section":
            return lax.axis_index("section")
        index = lax.axis_index("dp")
        return index // self.ring if kind == "z" else lax.rem(index, self.ring)

    def device(self, kind, place):
        if kind == "section":
            return {"section": place}
        index = lax.axis_index("dp")
        if kind == "z":
            return {"dp": place * self.ring + lax.rem(index, self.ring)}
        return {"dp": (index // self.ring) * self.ring + place}

    def peers(self, kind):
        size = self.sizes[kind]
        me = self.place(kind)
        return [lax.rem(me + step, size) for step in range(1, size)]


class Copies:
    loads, flush = (), None

    def __init__(self, lines, send, recv):
        self.lines, self.send, self.recv, self.used = lines, send, recv, 0

    def greet(self, kinds):
        barrier = pltpu.get_barrier_semaphore()
        count = 0
        for kind in kinds:
            for peer in self.lines.peers(kind):
                pl.semaphore_signal(
                    barrier, inc=1, device_id=self.lines.device(kind, peer), device_id_type=MESH
                )
                count += 1
        for load in Copies.loads:
            load.wait()
        pl.semaphore_wait(barrier, count)

    def start(self, kind, peer, src, dst):
        assert self.used < self.send.shape[0]
        copy = pltpu.make_async_remote_copy(
            src_ref=src,
            dst_ref=dst,
            send_sem=self.send.at[self.used],
            recv_sem=self.recv.at[self.used],
            device_id=self.lines.device(kind, peer),
            device_id_type=MESH,
        )
        self.used += 1
        copy.start()
        return copy

    def swap(self, kind, src, dst):
        me = self.lines.place(kind)
        return [self.start(kind, peer, src(peer), dst(me)) for peer in self.lines.peers(kind)]


def wait(copies):
    for copy in copies:
        copy.wait()


def semaphores(count):
    return [pltpu.SemaphoreType.DMA((count,)), pltpu.SemaphoreType.DMA((count,))]


def communicate(kernel, ident, arrays, shapes, scratch, name, limit=60 * 2**20, far=()):
    place = pl.BlockSpec(memory_space=pl.ANY)
    near = [i for i in range(len(arrays)) if i not in far]
    many, outs = len(arrays), len(shapes)

    def body(*refs):
        ins, results, refs = list(refs[:many]), refs[many : many + outs], refs[many + outs :]
        inner, refs = refs[: len(scratch)], refs[len(scratch) :]
        in_bufs, out_bufs, (in_sems, out_sems) = refs[: len(near)], refs[len(near) : len(near) + outs], refs[-2:]
        loads = []
        for k, i in enumerate(near):
            loads.append(pltpu.make_async_copy(ins[i], in_bufs[k], in_sems.at[k]))
            loads[-1].start()
            ins[i] = in_bufs[k]
        stores = [pltpu.make_async_copy(out_bufs[k], results[k], out_sems.at[k]) for k in range(outs)]
        started = set()

        def flush(ref):
            k = next(k for k in range(outs) if out_bufs[k] is ref)
            stores[k].start()
            started.add(k)

        Copies.loads, Copies.flush = loads, staticmethod(flush)
        kernel(*ins, *out_bufs, *inner)
        for k in range(outs):
            if k not in started:
                stores[k].start()
        for store in stores:
            store.wait()

    return pl.pallas_call(
        body,
        out_shape=[jax.ShapeDtypeStruct(s, d) for s, d in shapes],
        in_specs=[place] * many,
        out_specs=[place] * outs,
        scratch_shapes=list(scratch)
        + [pltpu.VMEM(arrays[i].shape, arrays[i].dtype) for i in near]
        + [pltpu.VMEM(s, d) for s, d in shapes]
        + [pltpu.SemaphoreType.DMA((max(1, len(near)),)), pltpu.SemaphoreType.DMA((outs,))],
        compiler_params=pltpu.CompilerParams(
            collective_id=ident, has_side_effects=True, vmem_limit_bytes=limit
        ),
        name=name,
    )(*arrays)


def span(place, width):
    return pl.ds(pl.multiple_of(place * width, width), width)


def square(lines):
    me = lines.place("section")
    low, high = lax.rem(me, 2), me // 2
    return high * 2 + 1 - low, (1 - high) * 2 + low, (1 - high) * 2 + 1 - low


def pieces_of(rows):
    half = rows // 2
    return (2, half // 2) if half % 32 == 0 else (1, half)


class SquareGather:
    @staticmethod
    def count(rows):
        return 6 * pieces_of(rows)[0]

    def __init__(self, copies, x_ref, o_ref, pieces=None):
        self.copies, self.x_ref, self.o_ref = copies, x_ref, o_ref
        self.width = x_ref.shape[1]
        self.me = copies.lines.place("section")
        near, far, _ = square(copies.lines)
        half = x_ref.shape[0] // 2
        pieces, step = pieces_of(x_ref.shape[0]) if pieces is None else (pieces, half // pieces)
        self.parts = [
            (pl.ds(h * half + j * step, step), one, two)
            for j in range(pieces)
            for h, (one, two) in enumerate(((near, far), (far, near)))
        ]

    def send(self, at, to):
        dst = self.o_ref.at[at, span(self.me, self.width)]
        return self.copies.start("section", to, self.x_ref.at[at], dst)

    def start(self):
        self.first = [self.send(at, one) for at, one, _ in self.parts]
        self.rest = [self.send(at, two) for at, _, two in self.parts]
        self.o_ref[:, span(self.me, self.width)] = self.x_ref[...]

    def forward(self):
        for (at, one, two), copy in zip(self.parts, self.first):
            copy.wait_recv()
            place = self.o_ref.at[at, span(one, self.width)]
            self.rest.append(self.copies.start("section", two, place, place))

    def finish(self):
        for copy in self.first:
            copy.wait_send()
        wait(self.rest)


class SquareScatter:
    @staticmethod
    def count(rows):
        return 6 * pieces_of(rows)[0]

    @staticmethod
    def scratch(rows, width):
        return [pltpu.VMEM((2, rows, width), BF), pltpu.VMEM((rows, width), BF), pltpu.VMEM((rows, width), BF)]

    def __init__(self, copies, x_ref, got, turn, last, pieces=None):
        self.copies, self.x_ref, self.got, self.turn, self.last = copies, x_ref, got, turn, last
        self.width = turn.shape[1]
        self.me = copies.lines.place("section")
        near, far, self.across = square(copies.lines)
        half = x_ref.shape[0] // 2
        pieces, step = pieces_of(x_ref.shape[0]) if pieces is None else (pieces, half // pieces)
        self.parts = [
            (pl.ds(h * half + j * step, step), one, two)
            for j in range(pieces)
            for h, (one, two) in enumerate(((near, far), (far, near)))
        ]

    def read(self, at, place):
        return self.x_ref[at, span(place, self.width)].astype(F32)

    def start(self):
        self.passed, self.kept = [], []
        for at, one, _ in self.parts:
            for place, k, out in ((self.across, 0, self.passed), (one, 1, self.kept)):
                src = self.x_ref.at[at, span(place, self.width)]
                out.append(self.copies.start("section", one, src, self.got.at[k, at]))

    def forward(self):
        self.second = []
        for (at, _, two), copy in zip(self.parts, self.passed):
            copy.wait_recv()
            self.turn[at] = (self.read(at, two) + self.got[0, at].astype(F32)).astype(BF)
            self.second.append(self.copies.start("section", two, self.turn.at[at], self.last.at[at]))

    def finish(self, o_ref):
        for i, (at, _, _) in enumerate(self.parts):
            self.kept[i].wait_recv()
            self.second[i].wait_recv()
            o_ref[at] = self.read(at, self.me) + self.got[1, at].astype(F32) + self.last[at].astype(F32)
        for copy in self.passed + self.kept + self.second:
            copy.wait_send()


def gather_columns(lines, ident, part, name):
    rows, width = part.shape

    def kernel(x_ref, o_ref, send, recv):
        copies = Copies(lines, send, recv)
        copies.greet(["section"])
        gather = SquareGather(copies, x_ref, o_ref)
        gather.start()
        gather.forward()
        gather.finish()

    shape = ((rows, lines.sizes["section"] * width), part.dtype)
    (out,) = communicate(kernel, ident, [part], [shape], semaphores(SquareGather.count(rows)), name)
    return out


def scalar_block(scalars):
    count = -(-scalars.shape[0] // 128)
    count += -count % 8
    return jnp.pad(scalars, (0, count * 128 - scalars.shape[0])).reshape(count, 128)


def sum_places(ref):
    total = ref[0].astype(F32)
    for i in range(1, ref.shape[0]):
        total = total + ref[i].astype(F32)
    return total


def scatter_columns(lines, ident, part, scalars, name):
    rows, full = part.shape
    sections = lines.sizes["section"]
    width = full // sections
    extra = scalars is not None
    arrays = [part]
    shapes = [((rows, width), F32)]
    scratch = semaphores(SquareScatter.count(rows) + sections - 1) + SquareScatter.scratch(rows, width)
    if extra:
        arrays.append(scalar_block(scalars))
        shapes.append((arrays[1].shape, F32))
        scratch.append(pltpu.VMEM((sections,) + arrays[1].shape, F32))

    def kernel(*refs):
        x_ref, refs = refs[0], refs[1:]
        if extra:
            e_ref, o_ref, eo_ref, send, recv, got, turn, last, e_got = refs
        else:
            o_ref, send, recv, got, turn, last = refs
        copies = Copies(lines, send, recv)
        copies.greet(["section"])
        scatter = SquareScatter(copies, x_ref, got, turn, last)
        scatter.start()
        if extra:
            others = copies.swap("section", lambda peer: e_ref, lambda place: e_got.at[place])
            e_got[lines.place("section")] = e_ref[...]
        scatter.forward()
        scatter.finish(o_ref)
        if extra:
            wait(others)
            eo_ref[...] = sum_places(e_got)

    got = communicate(kernel, ident, arrays, shapes, scratch, name)
    if not extra:
        return got[0]
    return got[0], got[1].reshape(-1)[:rows]


class RowScatter:
    @staticmethod
    def count(group, ring):
        return group * (ring - 1) + group - 1

    @staticmethod
    def scratch(group, ring, local, wide):
        vmem = pltpu.VMEM
        return [vmem((ring, group, local, wide), BF), vmem((group, local, wide), BF), vmem((group, local, wide), BF)]

    def __init__(self, copies, w_ref, buffers):
        self.copies, self.w_ref = copies, w_ref
        self.got, self.turn, self.all = buffers
        lines = copies.lines
        self.zplace, self.ring = lines.place("z"), lines.sizes["core"]
        self.order = lines.peers("z") + [self.zplace]

    def start(self):
        self.around = [
            self.copies.swap(
                "core", lambda peer: self.w_ref.at[g * self.ring + peer], lambda me: self.got.at[me, g]
            )
            for g in self.order
        ]

    def forward(self):
        lines = self.copies.lines
        place = lines.place("core")
        self.along = []
        for i, (g, arrived) in enumerate(zip(self.order, self.around)):
            for copy in arrived:
                copy.wait_recv()
            total = self.w_ref[g * self.ring + place].astype(F32)
            for peer in lines.peers("core"):
                total = total + self.got[peer, g].astype(F32)
            self.turn[g] = total.astype(BF)
            if i < len(self.order) - 1:
                self.along.append(self.copies.start("z", g, self.turn.at[g], self.all.at[self.zplace]))
        self.all[self.zplace] = self.turn[self.zplace]

    def finish(self, out_ref):
        wait(self.along)
        out_ref[...] = sum_places(self.all).astype(BF)
        for arrived in self.around:
            for copy in arrived:
                copy.wait_send()


def dense_finish(lines, ident, vectors, weight, shards, cuts, name):
    group, ring, sections = (lines.sizes[k] for k in ("z", "core", "section"))
    dp = group * ring
    many = len(shards)
    local = weight.shape[0] // dp
    wide = weight.shape[1]
    weight = weight.reshape(dp, local, wide)
    width = vectors.shape[1]
    bounds = [sum(cuts[:i]) for i in range(len(cuts) + 1)]
    parts = [pl.ds(bounds[i], cuts[i]) for i in range(len(cuts))]
    count = len(cuts)

    def kernel(x_ref, w_ref, *refs):
        s_refs, refs = refs[:many], refs[many:]
        v_ref, refs = refs[0], refs[1:]
        wo_refs, refs = refs[:count], refs[count:]
        so_refs, refs = refs[:many], refs[many:]
        send, recv, w_got, w_turn, w_all, v_z, v_core, v_all, *w_own = refs
        copies = Copies(lines, send, recv)
        zplace, place, section = (lines.place(k) for k in ("z", "core", "section"))
        copies.greet(["z", "core", "section"])
        order = lines.peers("z") + [zplace]
        gathers = [SquareGather(copies, x, o) for x, o in zip(s_refs, so_refs)]
        for gather in gathers:
            gather.start()
        around = {}
        for h, at in enumerate(parts):
            for i, g in enumerate(order):
                around[h, i] = copies.swap(
                    "core", lambda peer: w_ref.at[g * ring + peer, :, at], lambda me: w_got.at[me, g, :, at]
                )
        along = {h: [] for h in range(count)}
        for h, at in enumerate(parts):
            for i, g in enumerate(order):
                for copy in around[h, i]:
                    copy.wait_recv()
                total = w_ref[g * ring + place, :, at].astype(F32)
                for peer in lines.peers("core"):
                    total = total + w_got[peer, g, :, at].astype(F32)
                w_turn[g, :, at] = total.astype(BF)
                if i < len(order) - 1:
                    along[h].append(copies.start("z", g, w_turn.at[g, :, at], w_all.at[zplace, :, at]))
        pending = copies.swap("z", lambda peer: x_ref, lambda me: v_z.at[me])
        v_z[zplace] = x_ref[...]
        w_all[zplace] = w_turn[zplace]
        for gather in gathers:
            gather.forward()
        for h, at in enumerate(parts):
            wait(along[h])
            total = w_all[0, :, at].astype(F32)
            for i in range(1, group):
                total = total + w_all[i, :, at].astype(F32)
            w_own[h][...] = total.astype(BF)
            gathers.append(SquareGather(copies, w_own[h], wo_refs[h], 1))
            gathers[-1].start()
            if h > 0:
                gathers[-2].forward()
        wait(pending)
        v_core[place] = sum_places(v_z)
        wait(copies.swap("core", lambda peer: v_core.at[place], lambda me: v_core.at[me]))
        v_all[section] = sum_places(v_core)
        pending = copies.swap("section", lambda peer: v_all.at[section], lambda me: v_all.at[me])
        gathers[-1].forward()
        wait(pending)
        for i in range(sections):
            v_ref[:, i * width : (i + 1) * width] = v_all[i]
        for arrived in around.values():
            for copy in arrived:
                copy.wait_send()
        for gather in gathers:
            gather.finish()

    z, c, s = group - 1, ring - 1, sections - 1
    result = communicate(
        kernel,
        ident,
        [vectors, weight] + shards,
        [((8, sections * width), F32)]
        + [((local, sections * cut), BF) for cut in cuts]
        + [((x.shape[0], sections * x.shape[1]), x.dtype) for x in shards],
        semaphores(
            count * (group * c + z + 6)
            + sum(SquareGather.count(x.shape[0]) for x in shards)
            + z
            + c
            + s
        )
        + [
            pltpu.VMEM((ring, group, local, wide), BF),
            pltpu.VMEM((group, local, wide), BF),
            pltpu.VMEM((group, local, wide), BF),
            pltpu.VMEM((group, 8, width), F32),
            pltpu.VMEM((ring, 8, width), F32),
            pltpu.VMEM((sections, 8, width), F32),
        ]
        + [pltpu.VMEM((local, cut), BF) for cut in cuts],
        name,
        limit=60 * 2**20,
    )
    return result[0], result[1 : 1 + count], result[1 + count :]


def assemble(pieces, share, name):
    arrays = []
    for _, array, _, _ in pieces:
        if not any(array is other for other in arrays):
            arrays.append(array)
    where = [next(i for i, other in enumerate(arrays) if other is array) for _, array, _, _ in pieces]
    local = arrays[0].shape[0]
    steps = local // 32 if local % 32 == 0 else 1
    rows = local // steps
    sections = lax.axis_size("section")
    shapes, specs = [], []
    for kind, _, _, width in pieces:
        many = 2 if kind == "pair" else 1
        for _ in range(many):
            if kind == "stack":
                shapes.append(jax.ShapeDtypeStruct((sections, local, width), F32))
                specs.append(pl.BlockSpec((sections, rows, width), lambda i: (0, i, 0)))
            else:
                total = width if kind == "sum" else sections * width // many
                shapes.append(jax.ShapeDtypeStruct((local, total), F32))
                specs.append(pl.BlockSpec((rows, total), lambda i: (i, 0)))

    def kernel(*refs):
        ins, outs = refs[: len(arrays)], list(refs[len(arrays) :])
        for (kind, array, first, width), i in zip(pieces, where):
            wide = array.shape[1] // sections
            blocks = [ins[i][:, s * wide + first : s * wide + first + width].astype(F32) for s in range(sections)]
            out = outs.pop(0)
            if kind == "columns":
                for s, item in enumerate(blocks):
                    out[:, s * width : (s + 1) * width] = item
            elif kind == "stack":
                for s, item in enumerate(blocks):
                    out[s] = item
            elif kind == "sum":
                total = blocks[0]
                for item in blocks[1:]:
                    total = total + item
                out[...] = total
            elif kind == "hidden":
                for d in range(width // share):
                    out[:, d * share * sections : (d + 1) * share * sections] = jnp.concatenate(
                        [item[:, d * share : (d + 1) * share] for item in blocks], axis=1
                    )
            else:
                other = outs.pop(0)
                half = width // 2
                for s, item in enumerate(blocks):
                    for side, dst in ((0, out), (1, other)):
                        heads = [
                            item[:, (2 * g + side) * HDIM : (2 * g + side + 1) * HDIM]
                            for g in range(width // (2 * HDIM))
                        ]
                        dst[:, s * half : (s + 1) * half] = jnp.concatenate(heads, axis=1)

    return pl.pallas_call(
        kernel,
        grid=(steps,),
        in_specs=[pl.BlockSpec((rows, a.shape[1]), lambda i: (i, 0)) for a in arrays],
        out_specs=specs,
        out_shape=shapes,
        compiler_params=pltpu.CompilerParams(vmem_limit_bytes=60 * 2**20),
        name=name,
    )(*arrays)


def column_to_rows(column):
    return jnp.broadcast_to(column, (column.shape[0], 128)).T[:8]


def row_to_column(row):
    return jnp.broadcast_to(row, (128, row.shape[1])).T[:, :1]


def outer_product(left_ref, right_ref, out_ref, first):
    step = 256
    wide = right_ref.shape[1]

    @pl.loop(0, left_ref.shape[1] // step)
    def _(i):
        at = span(i, step)
        block = contract(left_ref[:, at], right_ref[...], 0, 0)
        out_ref[at, first : first + wide] = block.astype(BF)


def unpack_low(packed):
    lane = lax.broadcasted_iota(jnp.int32, packed.shape, 1)
    zero = jnp.zeros_like(packed)
    low = jnp.where(lane < HDIM, packed, zero)
    turned = jnp.concatenate([packed[:, HDIM:], packed[:, :HDIM]], axis=1)
    high = jnp.where(lane < HDIM, turned, zero)
    return jnp.concatenate([low, high], axis=0)


def unpack_high(packed):
    lane = lax.broadcasted_iota(jnp.int32, packed.shape, 1)
    zero = jnp.zeros_like(packed)
    turned = jnp.concatenate([packed[:, HDIM:], packed[:, :HDIM]], axis=1)
    low = jnp.where(lane >= HDIM, turned, zero)
    high = jnp.where(lane >= HDIM, packed, zero)
    return jnp.concatenate([low, high], axis=0)


def pack_turned(turned):
    half = turned.shape[1] // 2
    return jnp.concatenate([turned[:, :half], turned[:, half:]], axis=0).T


def forward_block(query, pieces, qpos, start, causal):
    scores = []
    peak = None
    for index, (pair, _, first) in enumerate(pieces):
        item = contract(pair, query, 1, 1)
        kpos = first + lax.broadcasted_iota(jnp.int32, item.shape, 0)
        allowed = kpos >= start
        if causal[index]:
            allowed = allowed & (kpos <= qpos)
        item = jnp.where(allowed, item, NEG)
        top = jnp.max(item, axis=0, keepdims=True)
        peak = top if peak is None else jnp.maximum(peak, top)
        scores.append(item)
    total = jnp.zeros_like(peak)
    mixed = None
    for item, (_, turned, _) in zip(scores, pieces):
        weight = jnp.exp(item - peak)
        total = total + jnp.sum(weight, axis=0, keepdims=True)
        part = matmul(turned[HDIM:], weight.astype(BF))
        mixed = part if mixed is None else mixed + part
    return mixed / total, peak + jnp.log(total)


def backward_block(query, grad, grad_turned, mixed_turned, lse, pieces, qpos, start, causal):
    row_sum = jnp.sum(grad_turned.astype(F32) * mixed_turned.astype(F32), axis=0, keepdims=True)
    grad_query = None
    grads = []
    for index, (pair, turned, first) in enumerate(pieces):
        scores = contract(pair, query, 1, 1)
        kpos = first + lax.broadcasted_iota(jnp.int32, scores.shape, 0)
        allowed = kpos >= start
        if causal[index]:
            allowed = allowed & (kpos <= qpos)
        probs = jnp.where(allowed, jnp.exp(scores - lse), 0.0)
        grad_probs = contract(pair, grad, 1, 1)
        grad_scores = (probs * (grad_probs - row_sum)).astype(BF)
        grads.append(matmul(grad_scores, query) + matmul(probs.astype(BF), grad))
        part = matmul(turned[:HDIM], grad_scores)
        grad_query = part if grad_query is None else grad_query + part
    return grad_query * SCALE, grads


def document_starts(ids):
    return [
        jnp.sum((ids < c).astype(F32), axis=1, keepdims=True) if c else jnp.zeros((1, 1), F32) for c in range(DOCS)
    ]


def start_of(documents, firsts):
    start = jnp.zeros(documents.shape, F32)
    for c in range(1, DOCS):
        start = jnp.where(documents >= c, firsts[c], start)
    return start.astype(jnp.int32)


def dense_enter(lines, ident, arrays, shape, name):
    seqs, rows, width = shape
    sections, group, ring = (lines.sizes[k] for k in ("section", "z", "core"))
    dp = group * ring
    part = width // sections
    half = rows // 2
    lanes = 2 * HDIM
    block = ring * rows
    local = width // dp

    def kernel(
        value_ref,
        weights_ref,
        cut_ref,
        ids_ref,
        weights_all,
        gains_ref,
        q_got,
        kv_all,
        start_ref,
        turned_ref,
        lse_ref,
        mixed_ref,
        send,
        recv,
        cut_all,
        kv_buf,
        q_buf,
        o_buf,
        o_got,
        o_own,
    ):
        copies = Copies(lines, send, recv)
        zplace, place = lines.place("z"), lines.place("core")
        rank = lax.axis_index("dp")
        copies.greet(["section", "z", "core"])
        pairs = [(weights_ref, weights_all), (cut_ref, cut_all)]
        along, handed = [], []
        for x_ref, o_ref in pairs:
            along.append(copies.swap("z", lambda peer: x_ref, lambda _: o_ref.at[rank]))
        for x_ref, o_ref in pairs:
            handed += copies.swap("core", lambda peer: x_ref, lambda _: o_ref.at[rank])
            o_ref[rank] = x_ref[...]
        for q in range(seqs):
            firsts = document_starts(ids_ref[q : q + 1])
            for g in range(group):
                at = pl.ds(pl.multiple_of((g * ring + place) * rows, rows), rows)
                start_ref[q, g] = start_of(ids_ref[q : q + 1, at], firsts)
        for step in range(group - 1, 0, -1):
            source = lax.rem(zplace + step, group) * ring + place
            for arrived, (_, o_ref) in zip(along, pairs):
                arrived[group - 1 - step].wait_recv()
                handed += copies.swap("core", lambda peer: o_ref.at[source], lambda _: o_ref.at[source])
        for arrived in along:
            for copy in arrived:
                copy.wait_send()
        wait(handed)
        for d in range(dp):
            gains_ref[:, d * local : (d + 1) * local] = cut_all[d].astype(F32)

        arriving, queries, around, outward, gathers = {}, {}, {}, {}, {}

        def project(q):
            value = value_ref[pl.ds(q * rows, rows)].astype(F32)
            normed = (value * inverse_rms(value) * gains_ref[0:1]).astype(BF)
            qkv = matmul(normed, weights_all[...].reshape(width, 3 * part)).astype(BF)
            for g in range(group):
                kv_buf[g, q] = qkv[:, g * lanes : (g + 1) * lanes]
                at = slice(2 * part + g * HDIM, 2 * part + (g + 1) * HDIM)
                q_buf[g, q] = side_by_side([qkv[:half, at], qkv[half:, at]])
            arriving[q] = copies.swap("z", lambda peer: kv_buf.at[peer, q], lambda me: kv_all.at[place, me, q])
            queries[q] = copies.swap("z", lambda peer: q_buf.at[peer, q], lambda me: q_got.at[me, q])
            q_got[zplace, q] = q_buf[zplace, q]
            kv_all[place, zplace, q] = kv_buf[zplace, q]
            own = kv_all.at[place, zplace, q]
            around[q] = copies.swap("core", lambda peer: own, lambda _: own)

        def hand(q):
            for step in range(group - 1, 0, -1):
                arriving[q][group - 1 - step].wait_recv()
                item = kv_all.at[place, lax.rem(zplace + step, group), q]
                around[q] += copies.swap("core", lambda peer: item, lambda _: item)

        def attend(q):
            for copy in arriving[q]:
                copy.wait_send()
            wait(queries[q])
            wait(around[q])
            pieces = []
            for g in range(group):
                pair = kv_all[:, g, q].reshape(block, lanes)
                pieces.append((pair, pair.T, g * block))
            for g in range(group):
                query = unpack_low(q_got[g, q]) * jnp.asarray(SCALE, BF)
                qpos = g * block + place * rows + lax.broadcasted_iota(jnp.int32, (1, rows), 1)
                mixed, lse = forward_block(
                    query, pieces[: g + 1], qpos, start_ref[q, g], [i == g for i in range(g + 1)]
                )
                turned_ref[q, g] = mixed.astype(BF)
                lse_ref[q, g] = lse
                o_buf[g, q] = pack_turned(mixed).astype(BF)
            outward[q] = copies.swap("z", lambda peer: o_buf.at[peer, q], lambda me: o_got.at[me, q])
            o_got[zplace, q] = o_buf[zplace, q]

        def merge(q):
            wait(outward[q])
            packed = [o_got[g, q] for g in range(group)]
            o_own[q] = side_by_side([jnp.concatenate([p[:, :HDIM], p[:, HDIM:]], axis=0) for p in packed])
            gathers[q] = SquareGather(copies, o_own.at[q], mixed_ref.at[q], 1)
            gathers[q].start()

        for q in range(seqs):
            project(q)
        for q in range(seqs):
            hand(q)
            attend(q)
            if q > 0:
                merge(q - 1)
            if q > 1:
                gathers[q - 2].forward()
        merge(seqs - 1)
        for q in range(max(0, seqs - 2), seqs):
            gathers[q].forward()
        for q in range(seqs):
            gathers[q].finish()

    z, c = group - 1, ring - 1
    vmem = pltpu.VMEM
    packed = ((group, seqs, half, lanes), BF)
    return communicate(
        kernel,
        ident,
        arrays,
        [
            ((dp, local, 3 * part), BF),
            ((16, width), F32),
            packed,
            ((ring, group, seqs, rows, lanes), BF),
            ((seqs, group, 1, rows), jnp.int32),
            ((seqs, group, HDIM, rows), BF),
            ((seqs, group, 1, rows), F32),
            ((seqs, rows, width), BF),
        ],
        semaphores(2 * (z + group * c) + seqs * (3 * z + group * c + 6))
        + [
            vmem((dp, 16, local), BF),
            vmem((group, seqs, rows, lanes), BF),
            vmem(*packed),
            vmem(*packed),
            vmem(*packed),
            vmem((seqs, rows, part), BF),
        ],
        name,
        limit=60 * 2**20,
    )


class SequenceSums:
    @staticmethod
    def count(sections, seqs, scalars):
        return seqs * (6 + (sections - 1 if scalars else 0))

    @staticmethod
    def scratch(sections, seqs, rows, part, scalars):
        vmem = pltpu.VMEM
        buffers = [
            vmem((seqs, rows, sections * part), BF),
            vmem((seqs, 2, rows, part), BF),
            vmem((seqs, rows, part), BF),
            vmem((seqs, rows, part), BF),
            vmem((rows, part), F32),
        ]
        if scalars:
            buffers += [vmem((seqs, 8, rows), F32), vmem((seqs, sections, 8, rows), F32)]
        return buffers

    def __init__(self, copies, buffers):
        self.copies, self.buffers, self.items = copies, buffers, {}

    def start(self, q, value, scalars=None):
        wide, got, turn, last = self.buffers[:4]
        wide[q] = value.astype(BF)
        item = SquareScatter(self.copies, wide.at[q], got.at[q], turn.at[q], last.at[q], 1)
        item.start()
        others = []
        if scalars is not None:
            buf, arrived = self.buffers[5:]
            section = self.copies.lines.place("section")
            buf[q] = column_to_rows(scalars)
            others = self.copies.swap("section", lambda peer: buf.at[q], lambda me: arrived.at[q, me])
            arrived[q, section] = buf[q]
        self.items[q] = (item, others)

    def forward(self, q):
        self.items[q][0].forward()

    def finish(self, q):
        item, others = self.items[q]
        total = self.buffers[4]
        item.finish(total)
        if not others:
            return total[...]
        wait(others)
        return total[...], row_to_column(sum_places(self.buffers[6].at[q])[:1])


class Loads:
    def __init__(self, sems):
        self.sems, self.used = sems, 0

    def start(self, src, dst):
        copy = pltpu.make_async_copy(src, dst, self.sems.at[self.used])
        self.used += 1
        copy.start()
        return copy


def dense_return(lines, ident, arrays, shape, name):
    seqs, rows, width, hidden_size = shape
    sections, group, ring = (lines.sizes[k] for k in ("section", "z", "core"))
    part = width // sections
    half = rows // 2

    def kernel(
        fed_ref,
        own_ref,
        value_ref,
        attended_ref,
        slope_ref,
        hidden_ref,
        mixed_ref,
        rest_ref,
        gains_ref,
        r_vectors_ref,
        r_grads_ref,
        grads_ref,
        middle,
        heads_got,
        vectors_ref,
        r_shard_ref,
        send,
        recv,
        sems,
        heads,
        dattended,
        out_w,
        expand_w,
        shrink_w,
        late,
        normed,
        dpre,
        *buffers,
    ):
        loads = Loads(sems)
        shrink_load = loads.start(rest_ref.at[:, part + hidden_size :], shrink_w)
        expand_load = loads.start(rest_ref.at[:, part : part + hidden_size], expand_w)
        out_load = loads.start(rest_ref.at[:, :part], out_w)
        hidden_load = loads.start(hidden_ref, late)
        copies = Copies(lines, send, recv)
        own = span(lines.place("section"), part)
        copies.greet(["section", "z", "core"])
        zplace = lines.place("z")
        mids = SequenceSums(copies, buffers[:7])
        outs = SequenceSums(copies, buffers[7:-3])
        r_sum = RowScatter(copies, r_grads_ref, buffers[-3:])
        r_sum.start()

        def middle_of(at):
            return value_ref[at].astype(F32) + attended_ref[at].astype(F32)

        def feed(q):
            at = pl.ds(q * rows, rows)
            grad_hidden = contract(fed_ref[at], shrink_w[...], 1, 1)
            grad_pre = (grad_hidden * slope_ref[at].astype(F32)).astype(BF)
            dpre[at] = grad_pre
            grad_normed = contract(grad_pre, expand_w[...], 1, 1)
            mid = middle_of(at)
            mids.start(q, grad_normed, jnp.sum(grad_normed * mid * gains_ref[1:2], axis=1, keepdims=True))
            normed[at] = (mid * inverse_rms(mid) * gains_ref[1:2]).astype(BF)

        def project(q):
            at = pl.ds(q * rows, rows)
            grad_normed, scalars = mids.finish(q)
            inv = inverse_rms(middle_of(at))
            mid = value_ref[at, own].astype(F32) + attended_ref[at, own].astype(F32)
            vectors_ref[1:2] += jnp.sum(grad_normed * mid * inv, axis=0, keepdims=True)
            grad = (
                inv * (grad_normed * gains_ref[1:2, own])
                - mid * (inv * inv * inv) * (scalars * (1.0 / width))
                + own_ref[at]
            )
            middle[at] = grad
            low = grad.astype(BF)
            dattended[at] = low
            outs.start(q, contract(low, out_w[...], 1, 1))

        def leave(q):
            grad = outs.finish(q).astype(BF)
            for g in range(group):
                columns = slice(g * HDIM, (g + 1) * HDIM)
                heads[g, q] = side_by_side([grad[:half, columns], grad[half:, columns]])
            heads_got[zplace, q] = heads[zplace, q]
            return copies.swap("z", lambda peer: heads.at[peer, q], lambda me: heads_got.at[me, q])

        vectors_ref[...] = r_vectors_ref[...]
        vectors_ref[0:2] = jnp.zeros((2, part), F32)
        shrink_load.wait()
        expand_load.wait()
        out_load.wait()
        last = seqs - 1
        for q in range(seqs):
            feed(q)
            if q == 0:
                r_sum.forward()
            if q > 0:
                mids.forward(q - 1)
            if q > 1:
                project(q - 2)
        mids.forward(last)
        hidden_load.wait()
        outer_product(late, fed_ref, grads_ref, hidden_size)
        mixed_load = loads.start(mixed_ref, late)
        for q in range(max(0, last - 1), seqs):
            project(q)
            outs.forward(q - 1)
        outer_product(normed, dpre, grads_ref, 0)
        outs.forward(last)
        mixed_load.wait()
        outer_product(late, dattended, grads_ref, hidden_size + width)
        Copies.flush(grads_ref)
        arriving = [leave(q) for q in range(seqs)]
        r_sum.finish(r_shard_ref)
        for pending in arriving:
            wait(pending)

    tokens = seqs * rows
    vmem = pltpu.VMEM
    r_grads = arrays[-1].reshape(group * ring, -1, arrays[-1].shape[1])
    arrays = arrays[:-1] + [r_grads]
    return communicate(
        kernel,
        ident,
        arrays,
        [
            ((width, hidden_size + width + part), BF),
            ((tokens, part), F32),
            ((group, seqs, half, 2 * HDIM), BF),
            ((8, part), F32),
            (r_grads.shape[1:], BF),
        ],
        semaphores(
            SequenceSums.count(sections, seqs, True)
            + SequenceSums.count(sections, seqs, False)
            + RowScatter.count(group, ring)
            + seqs * (group - 1)
        )
        + [
            pltpu.SemaphoreType.DMA((5,)),
            vmem((group, seqs, half, 2 * HDIM), BF),
            vmem((tokens, part), BF),
            vmem((width, part), BF),
            vmem((width, hidden_size), BF),
            vmem((hidden_size, width), BF),
            vmem((tokens, width), BF),
            vmem((tokens, width), BF),
            vmem((tokens, hidden_size), BF),
        ]
        + SequenceSums.scratch(sections, seqs, rows, part, True)
        + SequenceSums.scratch(sections, seqs, rows, part, False)
        + RowScatter.scratch(group, ring, *r_grads.shape[1:]),
        name,
        limit=60 * 2**20,
        far=(5, 6, 7),
    )


def dense_leave(lines, ident, arrays, shards, shape, name):
    seqs, rows, width = shape
    sections, group, ring = (lines.sizes[k] for k in ("section", "z", "core"))
    part = width // sections
    half = rows // 2
    lanes = 2 * HDIM
    block = ring * rows
    many = len(shards)
    tokens = seqs * rows

    def kernel(
        heads_got,
        value_ref,
        q_ref,
        kv_ref,
        start_ref,
        turned_ref,
        lse_ref,
        qkv_w,
        middle,
        gains_ref,
        mid_vectors_ref,
        *refs,
    ):
        s_refs, refs = refs[:many], refs[many:]
        (grads_ref, stream_ref, vectors_ref), refs = refs[:3], refs[3:]
        so_refs, refs = refs[:many], refs[many:]
        (
            send,
            recv,
            sems,
            kv,
            normed,
            dqkv,
            acc,
            pairs,
            pairs_got,
            queries,
            queries_got,
            sums,
            sums_got,
            *buffers,
        ) = refs
        loads = Loads(sems)
        kv_loads = {0: loads.start(kv_ref.at[:, :, 0], kv)}
        copies = Copies(lines, send, recv)
        section, zplace, place = (lines.place(k) for k in ("section", "z", "core"))
        own = span(section, part)
        copies.greet(["section", "z", "core"])
        inner = SequenceSums(copies, buffers)
        around, along, back = {}, {}, {}
        gathers = [SquareGather(copies, x, o) for x, o in zip(s_refs, so_refs)]
        for gather in gathers:
            gather.start()

        def attend(q):
            kv_loads[q].wait()
            pieces = []
            for g in range(group):
                pair = kv[:, g].reshape(block, lanes)
                pieces.append((pair, pair.T, g * block))
            for g in reversed(range(group)):
                query = unpack_low(q_ref[g, q]) * jnp.asarray(SCALE, BF)
                packed = heads_got[g, q]
                flat = packed.T
                qpos = g * block + place * rows + lax.broadcasted_iota(jnp.int32, (1, rows), 1)
                grad_query, grads = backward_block(
                    query,
                    unpack_high(packed),
                    side_by_side([flat[:HDIM], flat[HDIM:]]),
                    turned_ref[q, g],
                    lse_ref[q, g],
                    pieces[: g + 1],
                    qpos,
                    start_ref[q, g],
                    [i == g for i in range(g + 1)],
                )
                queries[g, q] = pack_turned(grad_query).astype(BF)
                for i, item in enumerate(grads):
                    if g == group - 1:
                        acc[i] = item
                    else:
                        acc[i] += item
            if q > 0:
                wait(around[q - 1])
            for g in range(group):
                for r in range(ring):
                    pairs[r, g] = acc[g, r * rows : (r + 1) * rows].astype(BF)
            if q + 1 < seqs:
                kv_loads[q + 1] = loads.start(kv_ref.at[:, :, q + 1], kv)
            queries_got[zplace, q] = queries[zplace, q]
            around[q] = copies.swap("core", lambda peer: pairs.at[peer], lambda me: pairs_got.at[me, :, q])
            along[q] = copies.swap("z", lambda peer: queries.at[peer, q], lambda me: queries_got.at[me, q])

        def to_tokens(q):
            wait(around[q])
            around[q] = []
            for g in range(group):
                item = pairs[place, g].astype(F32)
                for peer in lines.peers("core"):
                    item = item + pairs_got[peer, g, q].astype(F32)
                sums[g, q] = item.astype(BF)
            sums_got[zplace, q] = sums[zplace, q]
            back[q] = copies.swap("z", lambda peer: sums.at[peer, q], lambda me: sums_got.at[me, q])

        def enter(q):
            wait(back[q] + along[q])
            at = pl.ds(q * rows, rows)
            packed = [queries_got[g, q] for g in range(group)]
            upright = [jnp.concatenate([p[:, :HDIM], p[:, HDIM:]], axis=0) for p in packed]
            grad = side_by_side([sums_got[g, q] for g in range(group)] + upright)
            dqkv[at] = grad
            grad_normed = contract(grad, qkv_w[...], 1, 1)
            value = value_ref[at].astype(F32)
            inner.start(q, grad_normed, jnp.sum(grad_normed * value * gains_ref[0:1], axis=1, keepdims=True))

        def leave(q):
            at = pl.ds(q * rows, rows)
            grad_normed, scalars = inner.finish(q)
            inv = inverse_rms(value_ref[at].astype(F32))
            value = value_ref[at, own].astype(F32)
            vectors_ref[0:1] += jnp.sum(grad_normed * value * inv, axis=0, keepdims=True)
            grad = (
                inv * (grad_normed * gains_ref[0:1, own])
                - value * (inv * inv * inv) * (scalars * (1.0 / width))
                + middle[at]
            )
            stream_ref[at] = grad.astype(BF)

        vectors_ref[...] = mid_vectors_ref[...]
        last = seqs - 1
        for q in range(seqs):
            attend(q)
            to_tokens(q)
            if q == 0:
                for gather in gathers:
                    gather.forward()
        for q in range(seqs):
            at = pl.ds(q * rows, rows)
            value = value_ref[at].astype(F32)
            normed[at] = (value * inverse_rms(value) * gains_ref[0:1]).astype(BF)
        for q in range(seqs):
            enter(q)
            if q > 0:
                inner.forward(q - 1)
            if q > 1:
                leave(q - 2)
        inner.forward(last)
        outer_product(normed, dqkv, grads_ref, 0)
        Copies.flush(grads_ref)
        for q in range(max(0, last - 1), seqs):
            leave(q)
        for gather in gathers:
            gather.finish()

    z, c = group - 1, ring - 1
    vmem = pltpu.VMEM
    result = communicate(
        kernel,
        ident,
        arrays + shards,
        [
            ((width, 3 * part), BF),
            ((tokens, part), BF),
            ((8, part), F32),
        ]
        + [((x.shape[0], sections * x.shape[1]), x.dtype) for x in shards],
        semaphores(
            seqs * (2 * z + c)
            + SequenceSums.count(sections, seqs, True)
            + sum(SquareGather.count(x.shape[0]) for x in shards)
        )
        + [
            pltpu.SemaphoreType.DMA((seqs + 1,)),
            vmem((ring, group, rows, lanes), BF),
            vmem((tokens, width), BF),
            vmem((tokens, 3 * part), BF),
            vmem((group, block, lanes), F32),
            vmem((ring, group, rows, lanes), BF),
            vmem((ring, group, seqs, rows, lanes), BF),
            vmem((group, seqs, half, lanes), BF),
            vmem((group, seqs, half, lanes), BF),
            vmem((group, seqs, rows, lanes), BF),
            vmem((group, seqs, rows, lanes), BF),
        ]
        + SequenceSums.scratch(sections, seqs, rows, part, True),
        name,
        limit=60 * 2**20,
        far=(3,),
    )
    return result[0], result[1], result[2], result[3:]


def inverse_rms(value):
    return lax.rsqrt(jnp.mean(value * value, axis=-1, keepdims=True) + EPS)


def gelu_terms(value):
    scale = 0.7978845608028654
    square = value * value
    bend = jnp.tanh(scale * (value + 0.044715 * square * value))
    half = 0.5 * (1.0 + bend)
    slope = half + 0.5 * value * (1.0 - bend * bend) * scale * (1.0 + 0.134145 * square)
    return value * half, slope


def side_by_side(blocks):
    return jnp.concatenate(blocks, axis=1)


class ColumnSum:
    @staticmethod
    def count(sections, scalars):
        return (sections - 1) * (2 if scalars else 1)

    @staticmethod
    def scratch(sections, rows, width, scalars):
        buffers = [pltpu.VMEM((rows, sections * width), BF), pltpu.VMEM((sections, rows, width), BF)]
        if scalars:
            wide = rows + -rows % 128
            buffers += [pltpu.VMEM((8, wide), F32), pltpu.VMEM((sections, 8, wide), F32)]
        return buffers

    def __init__(self, copies, buffers):
        self.copies, self.buffers = copies, buffers

    def start(self, value, scalars=None):
        buf, got = self.buffers[:2]
        width = got.shape[2]
        section = self.copies.lines.place("section")
        buf[...] = value.astype(BF)
        self.pending = self.copies.swap(
            "section", lambda peer: buf.at[:, span(peer, width)], lambda me: got.at[me]
        )
        got[section] = buf[:, span(section, width)]
        if scalars is not None:
            sbuf, sgot = self.buffers[2:]
            sbuf[...] = jnp.zeros_like(sbuf)
            sbuf[:, : scalars.shape[0]] = column_to_rows(scalars)
            self.pending += self.copies.swap("section", lambda peer: sbuf, lambda me: sgot.at[me])
            sgot[section] = sbuf[...]

    def finish(self):
        wait(self.pending)
        total = sum_places(self.buffers[1])
        if len(self.buffers) == 2:
            return total
        rows = total.shape[0]
        return total, row_to_column(sum_places(self.buffers[3])[:1, :rows])


class Swaps:
    def __init__(self, copies):
        self.copies, self.lines = copies, copies.lines

    def ring(self, buf, got):
        return self.copies.swap("core", lambda peer: buf.at[peer], lambda me: got.at[me])

    def ring_sum(self, buf, got):
        total = buf[self.lines.place("core")].astype(F32)
        for peer in self.lines.peers("core"):
            total = total + got[peer].astype(F32)
        return total.astype(BF)

    def z(self, buf, got):
        place = self.lines.place("z")
        pending = self.copies.swap("z", lambda peer: buf.at[peer], lambda me: got.at[me])
        got[place] = buf[place]
        return pending

    def share(self, kind, all_ref):
        me = self.lines.place(kind)
        return self.copies.swap(kind, lambda peer: all_ref.at[me], lambda _: all_ref.at[me])


def together(all_ref):
    return side_by_side([all_ref[i] for i in range(all_ref.shape[0])])


def halves(value):
    rows = value.shape[0] // 2
    return side_by_side([value[:rows], value[rows:]])


def upright(packed):
    return jnp.concatenate([packed[:, :HDIM], packed[:, HDIM:]], axis=0)


def slots_of(lines, sel):
    group, ring = lines.sizes["z"], lines.sizes["core"]
    index = lax.broadcasted_iota(jnp.int32, (1, group * sel), 1)
    return (index // sel) * (ring * sel) + lines.place("core") * sel + lax.rem(index, sel)


def slot_sequence(lines, queries_ref, pairs_ref, q, sel):
    group, ring = lines.sizes["z"], lines.sizes["core"]
    at = slice(q * sel, (q + 1) * sel)
    query = jnp.concatenate([queries_ref[g, at] for g in range(group)], axis=0)
    pair = jnp.concatenate([pairs_ref[r, g, at] for g in range(group) for r in range(ring)], axis=0)
    return query * jnp.asarray(SCALE, BF), pair


def dense_feed(lines, ident, arrays, shape, name):
    seqs, sel, rows, width, part, hidden_size = shape
    sections, group, ring = (lines.sizes[k] for k in ("section", "z", "core"))
    dp = group * ring
    slots = seqs * sel
    lanes = 2 * HDIM
    queries = group * sel

    def kernel(
        value_ref,
        mixed_ref,
        gains_ref,
        rest_ref,
        top_ref,
        chosen_ref,
        ids_ref,
        first_ref,
        attended_ref,
        slope_ref,
        hidden_ref,
        out_ref,
        picked_ref,
        grad_ref,
        normed_ref,
        queries_ref,
        pairs_all,
        start_ref,
        turned_ref,
        lse_ref,
        r_mixed_ref,
        weights_all,
        send,
        recv,
        sems,
        out_w,
        expand_w,
        shrink_w,
        top,
        own_buf,
        wide,
        got,
        turn,
        last,
        value_core,
        value_core_got,
        value_z,
        value_z_got,
        value_all,
        grad_core,
        grad_core_got,
        grad_z,
        grad_z_got,
        grad_all,
        heads_buf,
        heads_got,
        o_buf,
        o_got,
        mixed_all,
    ):
        loads = Loads(sems)
        section, place = lines.place("section"), lines.place("core")
        rank = lax.axis_index("dp")
        own = span(section, part)
        out_load = loads.start(rest_ref.at[:, :part], out_w)
        top_load = loads.start(top_ref.at[:, :, own], top)
        expand_load = loads.start(rest_ref.at[:, part : part + hidden_size], expand_w)
        shrink_load = loads.start(rest_ref.at[:, part + hidden_size :], shrink_w)
        copies = Copies(lines, send, recv)
        swaps = Swaps(copies)
        copies.greet(["section", "z", "core"])
        weights_along = copies.swap("z", lambda peer: first_ref, lambda _: weights_all.at[rank])
        weights_handed = copies.swap("core", lambda peer: first_ref, lambda _: weights_all.at[rank])
        weights_all[rank] = first_ref[...]
        out_load.wait()
        gathers, scatters = {}, {}
        position = rank * rows + lax.broadcasted_iota(jnp.int32, (1, rows), 1).astype(F32)

        def table(q):
            chosen = row_to_column(chosen_ref[q : q + 1].astype(F32))
            return (chosen == position).astype(F32).astype(BF)

        def pick(q, source, buf):
            found = matmul(table(q), source).astype(BF)
            for d in range(dp):
                buf[d % ring, d // ring, q * sel : (q + 1) * sel] = found[d * sel : (d + 1) * sel]

        def project(q):
            own_buf[q] = matmul(mixed_ref[q], out_w[...]).astype(BF)
            gathers[q] = SquareGather(copies, own_buf.at[q], attended_ref.at[q], 1)
            gathers[q].start()

        def feed(q):
            gathers[q].finish()
            middle = value_ref[q].astype(F32) + attended_ref[q].astype(F32)
            normed = (middle * inverse_rms(middle) * gains_ref[1:2]).astype(BF)
            hidden, slope = gelu_terms(matmul(normed, expand_w[...]))
            hidden = hidden.astype(BF)
            hidden_ref[q] = hidden
            slope_ref[q] = slope.astype(BF)
            wide[q] = matmul(hidden, shrink_w[...]).astype(BF)
            scatters[q] = SquareScatter(copies, wide.at[q], got.at[q], turn.at[q], last.at[q], 1)
            scatters[q].start()

        def leave(q):
            scatters[q].finish(out_ref.at[q])
            after = out_ref[q] + value_ref[q, :, own].astype(F32) + attended_ref[q, :, own].astype(F32)
            out_ref[q] = after
            pick(q, after.astype(BF), value_core)

        for q in range(seqs):
            project(q)
            if q > 0:
                gathers[q - 1].forward()
        gathers[seqs - 1].forward()
        top_load.wait()
        for q in range(seqs):
            pick(q, top[q], grad_core)
        grad_pending = swaps.ring(grad_core, grad_core_got)
        expand_load.wait()
        shrink_load.wait()
        for q in range(seqs):
            feed(q)
            if q == 0:
                wait(grad_pending)
                grad_z[...] = swaps.ring_sum(grad_core, grad_core_got)
                grad_pending = swaps.z(grad_z, grad_z_got)
            else:
                scatters[q - 1].forward()
            if q > 1:
                leave(q - 2)
        Copies.flush(hidden_ref)
        Copies.flush(slope_ref)
        Copies.flush(attended_ref)
        scatters[seqs - 1].forward()
        for q in range(max(0, seqs - 2), seqs):
            leave(q)
        Copies.flush(out_ref)

        pending = swaps.ring(value_core, value_core_got)
        wait(grad_pending)
        grad_all[section] = sum_places(grad_z_got).astype(BF)
        wait(pending)
        value_z[...] = swaps.ring_sum(value_core, value_core_got)
        pending = swaps.z(value_z, value_z_got)
        grad_pending = swaps.share("section", grad_all)

        def slot_starts(q):
            firsts = document_starts(ids_ref[q : q + 1])
            chosen = chosen_ref[q : q + 1].astype(F32)
            documents = sum((chosen >= firsts[c]).astype(F32) for c in range(1, DOCS))
            column = jnp.broadcast_to(row_to_column(chosen), (dp * sel, queries))
            slot = lax.broadcasted_iota(jnp.int32, column.shape, 0)
            mine = jnp.sum(jnp.where(slot == slots_of(lines, sel), column, 0.0), axis=0, keepdims=True)
            mine = sum((mine >= firsts[c]).astype(F32) for c in range(1, DOCS))
            return start_of(mine, document_starts(documents))

        for q in range(seqs):
            start_ref[q] = slot_starts(q)
        for step in range(group - 1, 0, -1):
            weights_along[group - 1 - step].wait_recv()
            source = lax.rem(lines.place("z") + step, group) * ring + place
            weights_handed += copies.swap(
                "core", lambda peer: weights_all.at[source], lambda _: weights_all.at[source]
            )
        wait(pending)
        value_all[section] = sum_places(value_z_got).astype(BF)
        pending = swaps.share("section", value_all)
        wait(grad_pending)
        grad_ref[...] = together(grad_all)
        wait(pending)
        low = together(value_all)
        picked_ref[...] = low
        picked = low.astype(F32)
        normed = (picked * inverse_rms(picked) * gains_ref[2:3]).astype(BF)
        normed_ref[...] = normed
        for copy in weights_along:
            copy.wait_send()
        wait(weights_handed)
        qkv = matmul(normed, weights_all[...].reshape(width, 3 * part)).astype(BF)
        for g in range(group):
            heads_buf[g, :slots] = qkv[:, g * lanes : (g + 1) * lanes]
            heads_buf[g, slots:] = halves(qkv[:, 2 * part + g * HDIM : 2 * part + (g + 1) * HDIM])
        wait(swaps.z(heads_buf, heads_got))
        pairs_all[place] = heads_got[:, :slots]
        pending = swaps.share("core", pairs_all)
        blank = jnp.zeros((slots, HDIM), BF)
        for g in range(group):
            queries_ref[g] = side_by_side([upright(heads_got[g, slots:]), blank])
        wait(pending)
        turned_all = []
        for q in range(seqs):
            query, pair = slot_sequence(lines, queries_ref, pairs_all, q, sel)
            turned, lse = forward_block(
                query, [(pair, pair.T, 0)], slots_of(lines, sel), start_ref[q], [True]
            )
            turned_ref[q] = turned.astype(BF)
            lse_ref[q] = lse
            turned_all.append(jnp.concatenate([turned, jnp.zeros_like(turned)], axis=0).T.astype(BF)[:, :HDIM])
        for g in range(group):
            o_buf[g] = halves(jnp.concatenate([t[g * sel : (g + 1) * sel] for t in turned_all], axis=0))
        wait(swaps.z(o_buf, o_got))
        mixed_all[section] = side_by_side([upright(o_got[g]) for g in range(group)])
        wait(swaps.share("section", mixed_all))
        r_mixed_ref[...] = together(mixed_all)

    vmem = pltpu.VMEM
    z, s, c = group - 1, sections - 1, ring - 1
    short = ((group, slots, part), BF)
    across = ((sections, slots, part), BF)
    packed = ((group, slots // 2, lanes), BF)
    heads = ((group, slots + slots // 2, lanes), BF)
    row = ((slots, width), BF)
    scratch = [
        ((width, part), BF),
        ((width, hidden_size), BF),
        ((hidden_size, width), BF),
        ((seqs, rows, part), BF),
        ((seqs, rows, part), BF),
        ((seqs, rows, width), BF),
        ((seqs, 2, rows, part), BF),
        ((seqs, rows, part), BF),
        ((seqs, rows, part), BF),
        ((ring,) + short[0], BF),
        ((ring,) + short[0], BF),
        short,
        short,
        across,
        ((ring,) + short[0], BF),
        ((ring,) + short[0], BF),
        short,
        short,
        across,
        heads,
        heads,
        packed,
        packed,
        across,
    ]
    return communicate(
        kernel,
        ident,
        arrays,
        [
            ((seqs, rows, width), BF),
            ((seqs, rows, hidden_size), BF),
            ((seqs, rows, hidden_size), BF),
            ((seqs, rows, part), F32),
            row,
            row,
            row,
            ((group, slots, lanes), BF),
            ((ring, group, slots, lanes), BF),
            ((seqs, 1, queries), jnp.int32),
            ((seqs, HDIM, queries), BF),
            ((seqs, 1, queries), F32),
            row,
            ((dp,) + arrays[-1].shape, BF),
        ],
        semaphores(seqs * 12 + 3 * c + 4 * z + 3 * s + z + group * c)
        + [pltpu.SemaphoreType.DMA((4,))]
        + [vmem(a, b) for a, b in scratch],
        name,
        limit=60 * 2**20,
        far=(3, 4),
    )


def routed_feed(lines, ident, arrays, shape, name):
    slots, width, part, hidden_size = shape
    sections = lines.sizes["section"]

    def kernel(
        value_ref,
        grad_ref,
        mixed_ref,
        gains_ref,
        rest_ref,
        grads_ref,
        middle_ref,
        attended_ref,
        sent_ref,
        logit_ref,
        vectors_ref,
        send,
        recv,
        sems,
        out_w,
        expand_w,
        shrink_w,
        keep,
        mid_keep,
        dpre_keep,
        hidden_keep,
        fed_keep,
        attended_all,
        *buffers,
    ):
        loads = Loads(sems)
        out_load = loads.start(rest_ref.at[:, :part], out_w)
        shrink_load = loads.start(rest_ref.at[:, part + hidden_size :], shrink_w)
        expand_load = loads.start(rest_ref.at[:, part : part + hidden_size], expand_w)
        copies = Copies(lines, send, recv)
        swaps = Swaps(copies)
        section = lines.place("section")
        own = span(section, part)
        copies.greet(["section"])
        back, forth = ColumnSum(copies, buffers[:4]), ColumnSum(copies, buffers[4:])
        gain, router = gains_ref[3:4, :], gains_ref[4:5, :]
        out_load.wait()
        attended_own = matmul(mixed_ref[...], out_w[...]).astype(BF)
        attended_all[section] = attended_own
        pending = swaps.share("section", attended_all)
        picked = value_ref[...].astype(F32)
        grad_sent = grad_ref[...].astype(F32)
        gate = jax.nn.sigmoid(jnp.sum(picked * router, axis=1, keepdims=True))
        grad_delta = gate * grad_sent
        fed_low = grad_delta.astype(BF)
        fed_keep[...] = fed_low
        shrink_load.wait()
        grad_hidden = contract(fed_low, shrink_w[...], 1, 1)
        expand_load.wait()
        wait(pending)
        middle = picked + together(attended_all).astype(F32)
        inv = inverse_rms(middle)
        normed = (middle * inv * gain).astype(BF)
        hidden, slope = gelu_terms(matmul(normed, expand_w[...]))
        hidden = hidden.astype(BF)
        grad_pre = (grad_hidden * slope).astype(BF)
        grad_normed = contract(grad_pre, expand_w[...], 1, 1)
        back.start(grad_normed, jnp.sum(grad_normed * middle * gain, axis=1, keepdims=True))
        mid_keep[...] = normed
        hidden_keep[...] = hidden
        dpre_keep[...] = grad_pre
        fed_part = matmul(hidden, shrink_w[...])
        keep[0] = middle
        keep[1] = grad_delta
        keep[2] = grad_sent
        own_attended = attended_own.astype(F32)
        gate_part = jnp.sum(grad_sent * fed_part, axis=1, keepdims=True) + jnp.sum(
            keep[2, :, own] * own_attended, axis=1, keepdims=True
        )
        forth.start(fed_part, gate_part)
        outer_product(mid_keep, dpre_keep, grads_ref, 0)
        grad_normed, scalar = back.finish()
        middle_own = keep[0, :, own]
        vectors_ref[...] = jnp.zeros_like(vectors_ref)
        vectors_ref[3:4] = jnp.sum(grad_normed * middle_own * inv, axis=0, keepdims=True)
        grad_middle = inv * (grad_normed * gains_ref[3:4, own]) - middle_own * (inv * inv * inv) * (
            scalar * (1.0 / width)
        )
        middle_ref[...] = grad_middle
        attended_ref[...] = (grad_middle + keep[1, :, own]).astype(BF)
        outer_product(hidden_keep, fed_keep, grads_ref, hidden_size)
        Copies.flush(grads_ref)
        fed, grad_gate = forth.finish()
        sent_ref[...] = (gate * (own_attended + fed)).astype(BF)
        grad_logit = grad_gate * gate * (1.0 - gate)
        logit_ref[...] = jnp.broadcast_to(grad_logit, logit_ref.shape)
        vectors_ref[4:5] = jnp.sum(grad_logit * value_ref[:, own].astype(F32), axis=0, keepdims=True)

    vmem = pltpu.VMEM
    return communicate(
        kernel,
        ident,
        arrays,
        [
            ((width, hidden_size + width), BF),
            ((slots, part), F32),
            ((slots, part), BF),
            ((slots, part), BF),
            ((slots, 128), F32),
            ((8, part), F32),
        ],
        semaphores(sections - 1 + 2 * ColumnSum.count(sections, True))
        + [
            pltpu.SemaphoreType.DMA((3,)),
            vmem((width, part), BF),
            vmem((width, hidden_size), BF),
            vmem((hidden_size, width), BF),
            vmem((3, slots, width), F32),
            vmem((slots, width), BF),
            vmem((slots, hidden_size), BF),
            vmem((slots, hidden_size), BF),
            vmem((slots, width), BF),
            vmem((sections, slots, part), BF),
        ]
        + 2 * ColumnSum.scratch(sections, slots, part, True),
        name,
        limit=60 * 2**20,
        far=(4,),
    )


def routed_leave(lines, ident, arrays, shape, name):
    seqs, sel, rows, width, part = shape
    sections, group, ring = (lines.sizes[k] for k in ("section", "z", "core"))
    slots = seqs * sel
    lanes = 2 * HDIM

    def kernel(
        attended_ref,
        rest_ref,
        qkv_w,
        queries_ref,
        pairs_ref,
        start_ref,
        turned_ref,
        lse_ref,
        value_ref,
        normed_ref,
        mixed_ref,
        middle_ref,
        logit_ref,
        sent_ref,
        feed_vectors_ref,
        gains_ref,
        chosen_ref,
        top_ref,
        fed_out,
        own_out,
        added_ref,
        grads_ref,
        vectors_ref,
        send,
        recv,
        sems,
        out_w,
        grad_buf,
        grad_got,
        grad_high,
        turn_buf,
        turn_got,
        back_buf,
        back_got,
        dqkv_keep,
        sent_got,
        sent_all,
        final_buf,
        final_got,
        final_all,
        *buffers,
    ):
        loads = Loads(sems)
        out_load = loads.start(rest_ref.at[:, :part], out_w)
        copies = Copies(lines, send, recv)
        swaps = Swaps(copies)
        section, zplace, place = (lines.place(k) for k in ("section", "z", "core"))
        rank = lax.axis_index("dp")
        own = span(section, part)
        copies.greet(["section", "z", "core"])
        outer, inner = ColumnSum(copies, buffers[:2]), ColumnSum(copies, buffers[2:])
        out_load.wait()
        outer.start(contract(attended_ref[...], out_w[...], 1, 1))
        sent_pending = copies.swap("z", lambda peer: sent_ref, lambda me: sent_got.at[me])
        sent_got[zplace] = sent_ref[...]
        outer_product(mixed_ref, attended_ref, grads_ref, 3 * part)
        slot_of = rank * rows + lax.broadcasted_iota(jnp.int32, (rows, 1), 0)
        tables = [(chosen_ref[q : q + 1] == slot_of).astype(F32).astype(BF) for q in range(seqs)]
        blank = jnp.zeros((slots, HDIM), BF)
        grad_mixed = outer.finish().astype(BF)
        for g in range(group):
            grad_buf[g] = halves(grad_mixed[:, g * HDIM : (g + 1) * HDIM])
        pending = swaps.z(grad_buf, grad_got)
        wait(sent_pending)
        sent_all[place] = sent_got[...]
        sent_pending = swaps.share("core", sent_all)
        wait(pending)
        for g in range(group):
            grad_high[g] = side_by_side([blank, upright(grad_got[g])])
        query_grads = []
        for q in range(seqs):
            at = slice(q * sel, (q + 1) * sel)
            query, pair = slot_sequence(lines, queries_ref, pairs_ref, q, sel)
            grad = jnp.concatenate([grad_high[g, at] for g in range(group)], axis=0)
            grad_query, grad_pairs = backward_block(
                query,
                grad,
                grad.T[HDIM:],
                turned_ref[q],
                lse_ref[q],
                [(pair, pair.T, 0)],
                slots_of(lines, sel),
                start_ref[q],
                [True],
            )
            turned = jnp.concatenate([grad_query, jnp.zeros_like(grad_query)], axis=0).T.astype(BF)
            query_grads.append(turned[:, :HDIM])
            low = grad_pairs[0].astype(BF)
            for g in range(group):
                for r in range(ring):
                    first = (g * ring + r) * sel
                    turn_buf[r, g, at] = low[first : first + sel]
        pending = swaps.ring(turn_buf, turn_got)
        for g in range(group):
            back_buf[g, slots:] = halves(
                jnp.concatenate([t[g * sel : (g + 1) * sel] for t in query_grads], axis=0)
            )
        wait(pending)
        back_buf[:, :slots] = swaps.ring_sum(turn_buf, turn_got)
        pending = swaps.z(back_buf, back_got)
        wait(sent_pending)

        def at_positions(q, all_ref):
            at = slice(q * sel, (q + 1) * sel)
            found = jnp.concatenate([all_ref[r, g, at] for g in range(group) for r in range(ring)], axis=0)
            return matmul(tables[q], found)

        for q in range(seqs):
            added_ref[q] = at_positions(q, sent_all).astype(BF)
        wait(pending)
        dqkv_keep[...] = side_by_side(
            [back_got[g, :slots] for g in range(group)] + [upright(back_got[g, slots:]) for g in range(group)]
        )
        grad_normed = contract(dqkv_keep[...], qkv_w[...], 1, 1)
        picked = value_ref[...].astype(F32)
        inv = inverse_rms(picked)
        inner.start(grad_normed, jnp.sum(grad_normed * picked * gains_ref[2:3], axis=1, keepdims=True))
        outer_product(normed_ref, dqkv_keep, grads_ref, 0)
        picked = value_ref[:, own].astype(F32)
        grad_normed, scalar = inner.finish()
        vectors_ref[...] = feed_vectors_ref[...]
        vectors_ref[2:3] = jnp.sum(grad_normed * picked * inv, axis=0, keepdims=True)
        grad_in = inv * (grad_normed * gains_ref[2:3, own]) - picked * (inv * inv * inv) * (scalar * (1.0 / width))
        final_buf[...] = (middle_ref[...] + grad_in + logit_ref[:, :1] * gains_ref[4:5, own]).astype(BF)

        along = copies.swap("z", lambda peer: final_buf, lambda me: final_got.at[me])
        final_got[zplace] = final_buf[...]

        def hand_on(i):
            dst = final_all.at[place, i, :, own]
            dst[...] = final_got[i]
            return copies.swap("section", lambda peer: final_got.at[i], lambda me: dst)

        spread = hand_on(zplace)
        Copies.flush(grads_ref)
        for step in range(group - 1, 0, -1):
            along[group - 1 - step].wait_recv()
            spread += hand_on(lax.rem(zplace + step, group))
        for copy in along:
            copy.wait_send()
        wait(spread)
        wait(swaps.share("core", final_all))
        for q in range(seqs):
            fed_out[q] = (top_ref[q].astype(F32) + at_positions(q, final_all)).astype(BF)
            returned = jnp.concatenate(
                [final_all[r, g, q * sel : (q + 1) * sel, own] for g in range(group) for r in range(ring)], axis=0
            )
            own_out[q] = top_ref[q, :, own].astype(F32) + matmul(tables[q], returned)

    vmem = pltpu.VMEM
    z, s, c = group - 1, sections - 1, ring - 1
    lane_block = ((group, slots, lanes), BF)
    packed = ((group, slots // 2, lanes), BF)
    heads = ((group, slots + slots // 2, lanes), BF)
    ring_block = ((ring, group, slots, lanes), BF)
    short = ((group, slots, part), BF)
    scratch = [
        ((width, part), BF),
        packed,
        packed,
        lane_block,
        ring_block,
        ring_block,
        heads,
        heads,
        ((slots, 3 * part), BF),
        short,
        ((ring,) + short[0], BF),
        ((slots, part), BF),
        short,
        ((ring, group, slots, width), BF),
    ]
    return communicate(
        kernel,
        ident,
        arrays,
        [
            ((seqs, rows, width), BF),
            ((seqs, rows, part), F32),
            ((seqs, rows, part), BF),
            ((width, 4 * part), BF),
            ((8, part), F32),
        ],
        semaphores(
            3 * c
            + 4 * z
            + ColumnSum.count(sections, True)
            + ColumnSum.count(sections, False)
            + group * s
        )
        + [pltpu.SemaphoreType.DMA((1,))]
        + [vmem(a, b) for a, b in scratch]
        + ColumnSum.scratch(sections, slots, part, False)
        + ColumnSum.scratch(sections, slots, part, True),
        name,
        limit=60 * 2**20,
        far=(1,),
    )


def cut_weights(arrays, sections, dp, group, name):
    local, width = arrays[0].shape
    part = width // sections
    inner = arrays[4].shape[1] // dp
    share = inner // sections
    hidden_size = dp * share
    layers = len(arrays) // 6

    def kernel(*refs):
        ins, outs = refs[: 6 * layers], refs[6 * layers : 8 * layers]
        k_buf, v_buf, sems = refs[8 * layers :]
        section = lax.axis_index("section")
        own = span(section, part)
        moves = []
        for i in range(layers):
            q_ref, k_ref, v_ref, o_ref, e_ref, s_ref = ins[6 * i : 6 * i + 6]
            first_ref, rest_ref = outs[2 * i : 2 * i + 2]
            rows = pl.ds(pl.multiple_of(section * share, share), share)
            moves += [
                (k_ref.at[:, own], k_buf.at[i]),
                (v_ref.at[:, own], v_buf.at[i]),
                (q_ref.at[:, own], first_ref.at[:, 2 * part :]),
                (o_ref.at[:, own], rest_ref.at[:, :part]),
                (s_ref.at[rows], rest_ref.at[:, part + hidden_size :]),
            ]
            for d in range(dp):
                at = pl.ds(pl.multiple_of(d * inner + section * share, 128), share)
                moves.append((e_ref.at[:, at], rest_ref.at[:, part + d * share : part + (d + 1) * share]))
        copies = [pltpu.make_async_copy(src, dst, sems.at[i]) for i, (src, dst) in enumerate(moves)]
        for copy in copies:
            copy.start()
        for copy in copies:
            copy.wait()
        for i in range(layers):
            for g in range(group):
                at = slice(g * HDIM, (g + 1) * HDIM)
                pair = side_by_side([k_buf[i, :, at], v_buf[i, :, at]])
                outs[2 * i][:, 2 * g * HDIM : 2 * (g + 1) * HDIM] = pair

    anywhere, vmem = pl.BlockSpec(memory_space=pl.ANY), pl.BlockSpec(memory_space=pltpu.VMEM)
    shapes = [
        jax.ShapeDtypeStruct((local, 3 * part), BF),
        jax.ShapeDtypeStruct((local, part + hidden_size + width), BF),
    ]
    return pl.pallas_call(
        kernel,
        in_specs=[anywhere] * 6 * layers,
        out_specs=[vmem] * 2 * layers,
        out_shape=shapes * layers,
        scratch_shapes=[
            pltpu.VMEM((layers, local, part), BF),
            pltpu.VMEM((layers, local, part), BF),
            pltpu.SemaphoreType.DMA((layers * (5 + dp),)),
        ],
        compiler_params=pltpu.CompilerParams(vmem_limit_bytes=60 * 2**20),
        name=name,
    )(*arrays)


def on_device(
    stream_in,
    segment_ids,
    chosen_rows,
    cotangent,
    dense_prenorm,
    dense_query,
    dense_keys,
    dense_values,
    dense_output,
    dense_midnorm,
    dense_expand,
    dense_shrink,
    routed_prenorm,
    routed_query,
    routed_keys,
    routed_values,
    routed_output,
    routed_midnorm,
    routed_expand,
    routed_shrink,
    router_weight,
):
    sections, dp = lax.axis_size("section"), lax.axis_size("dp")
    section, rank = lax.axis_index("section"), lax.axis_index("dp")
    seqs, rows, width = stream_in.shape
    tokens = seqs * rows
    part = width // sections
    group = HEADS // sections
    ring = dp // group
    total_sel = chosen_rows.shape[1]
    sel = total_sel // dp
    lines = Lines(sections, dp, group)

    def own_columns(value):
        return lax.dynamic_slice_in_dim(value, section * part, part, value.ndim - 1)

    def own_hidden(expand, shrink):
        inner = expand.shape[1] // dp
        share = inner // sections
        cut = expand.reshape(expand.shape[0], dp, sections, share)
        cut = lax.dynamic_index_in_dim(cut, section, 2, keepdims=False).reshape(expand.shape[0], dp * share)
        return cut, lax.dynamic_slice_in_dim(shrink, section * share, share, 0)

    def own_attention(query, keys, values):
        local = query.shape[0]
        pair = jnp.stack(
            [own_columns(keys).reshape(local, group, HDIM), own_columns(values).reshape(local, group, HDIM)],
            axis=2,
        ).reshape(local, 2 * part)
        return jnp.concatenate([pair, own_columns(query)], axis=1)

    def cut(*layers):
        if dense_expand.shape[1] // (dp * sections) % 128 == 0:
            return cut_weights([w for layer in layers for w in layer], sections, dp, group, "cut")
        out = []
        for query, keys, values, output, expand, shrink in layers:
            expand_cut, shrink_cut = own_hidden(expand, shrink)
            rest = jnp.concatenate([own_columns(output), expand_cut, shrink_cut], axis=1)
            out += [own_attention(query, keys, values), rest]
        return out

    def gather(value):
        return lax.all_gather(value, "dp", axis=0, tiled=True)

    def after(value, other):
        return lax.optimization_barrier((value, other))[0]

    hidden_size = dense_expand.shape[1] // sections
    gains = jnp.stack([dense_prenorm, dense_midnorm, routed_prenorm, routed_midnorm, router_weight])
    gains = jnp.pad(gains, ((0, 16 - gains.shape[0]), (0, 0)))
    dense_first, dense_rest, routed_first, routed_rest = cut(
        (dense_query, dense_keys, dense_values, dense_output, dense_expand, dense_shrink),
        (routed_query, routed_keys, routed_values, routed_output, routed_expand, routed_shrink),
    )
    rest = gather(dense_rest)
    routed_rest = gather(routed_rest)

    shape = (seqs, sel, rows, width, part)
    grad_top = cotangent.reshape(tokens, width)
    dense_qkv, gains, queries, pairs, start, mixed_turned, lse, mixed = dense_enter(
        lines,
        1,
        [stream_in.reshape(tokens, width), dense_first, gains, segment_ids],
        (seqs, rows, width),
        "dense_enter",
    )
    dense_qkv = dense_qkv.reshape(width, 3 * part)
    (
        attended,
        slope,
        hidden,
        after_dense,
        r_value,
        r_grad,
        r_normed,
        r_queries,
        r_pairs,
        r_start,
        r_turned,
        r_lse,
        r_mixed,
        routed_qkv,
    ) = dense_feed(
        lines,
        2,
        [stream_in, mixed, gains, rest, cotangent, chosen_rows, segment_ids, routed_first],
        shape + (hidden_size,),
        "dense_feed",
    )
    routed_qkv = routed_qkv.reshape(width, 3 * part)
    after_dense = after_dense.reshape(tokens, part)
    attended, slope, hidden, mixed = (x.reshape(tokens, -1) for x in (attended, slope, hidden, mixed))

    def reduce_dp(value):
        return lax.psum_scatter(value, "dp", scatter_dimension=0, tiled=True)

    routed_grads, r_middle, r_grad_attended, r_sent, r_logit, r_vectors = routed_feed(
        lines,
        4,
        [r_value, r_grad, r_mixed, gains, routed_rest],
        (seqs * sel, width, part, hidden_size),
        "routed_feed",
    )
    routed_shard = reduce_dp(routed_grads)
    fed_low, grad_own, added, routed_grads, r_vectors = routed_leave(
        lines,
        5,
        [
            r_grad_attended,
            routed_rest,
            routed_qkv,
            r_queries,
            r_pairs,
            r_start,
            r_turned,
            r_lse,
            r_value,
            r_normed,
            r_mixed,
            r_middle,
            r_logit,
            r_sent,
            r_vectors,
            gains,
            chosen_rows,
            cotangent,
        ],
        shape,
        "routed_leave",
    )
    dense_grads, grad_middle, grad_heads, d_vectors, routed_shard_in = dense_return(
        lines,
        6,
        [
            fed_low.reshape(tokens, width),
            grad_own.reshape(tokens, part),
            stream_in.reshape(tokens, width),
            attended,
            slope,
            hidden,
            mixed,
            rest,
            gains,
            r_vectors,
            routed_grads,
        ],
        (seqs, rows, width, hidden_size),
        "dense_return",
    )
    dense_shard = reduce_dp(after(dense_grads, routed_shard))
    dense_grads, stream_grad, d_vectors, (routed_all, routed_all_in) = dense_leave(
        lines,
        7,
        [
            grad_heads,
            stream_in.reshape(tokens, width),
            queries,
            pairs,
            start,
            mixed_turned,
            lse,
            dense_qkv,
            grad_middle,
            gains,
            d_vectors,
        ],
        [routed_shard, routed_shard_in],
        (seqs, rows, width),
        "dense_leave",
    )
    added = after(added, d_vectors).reshape(tokens, part)
    stream_out = (after_dense + added.astype(F32)).astype(BF).reshape(seqs, rows, part)
    stream_grad = stream_grad.reshape(seqs, rows, part)
    vectors, (dense_all_in,), (dense_all,) = dense_finish(
        lines, 8, d_vectors, dense_grads, [dense_shard], (3 * part,), "dense_finish"
    )

    share = hidden_size // dp
    local = width // dp
    r_exp, r_shr, r_keys, r_values, r_query, r_out = assemble(
        [
            ("hidden", routed_all, 0, hidden_size),
            ("stack", routed_all, hidden_size, width),
            ("pair", routed_all_in, 0, 2 * part),
            ("columns", routed_all_in, 2 * part, part),
            ("columns", routed_all_in, 3 * part, part),
        ],
        share,
        "routed_places",
    )
    d_exp, d_shr, d_keys, d_values, d_query, d_out = assemble(
        [
            ("hidden", dense_all, 0, hidden_size),
            ("stack", dense_all, hidden_size, width),
            ("pair", dense_all_in, 0, 2 * part),
            ("columns", dense_all_in, 2 * part, part),
            ("columns", dense_all, hidden_size + width, part),
        ],
        share,
        "dense_places",
    )
    vectors = lax.dynamic_slice_in_dim(vectors, rank * local, local, 1)
    d_shr = d_shr.reshape(sections * share, width)
    r_shr = r_shr.reshape(sections * share, width)
    return (
        (stream_out, stream_grad)
        + (vectors[0], d_query, d_keys, d_values, d_out, vectors[1], d_exp, d_shr)
        + (vectors[2], r_query, r_keys, r_values, r_out, vectors[3], r_exp, r_shr)
        + (vectors[4],)
    )


def solution(mesh):
    streams, row, vector, copied = P(None, "dp", None), P("dp", None), P("dp"), P()
    layer = (vector, row, row, row, row, vector, row, row)
    outs = (P(None, "dp", "section"),) * 2 + layer + layer + (vector,)
    return jax.shard_map(
        on_device,
        mesh=mesh,
        in_specs=(streams, copied, copied, streams) + layer + layer + (vector,),
        out_specs=outs,
        check_vma=False,
    )
```
